32 devices in a mesh: shard: 8 (over y, x, core), tensor: 4 (over z).
Axes of the slice: x: 2, y: 2, z: 4, core: 2. Of those that a mesh axis runs over, the one named last changes fastest.
Arguments:
- hidden_in: bfloat16 [6144, 8192], P('shard'), may hold values from -720 to 720
- policy_weights: bfloat16 [2, 8192, 1024], P(None, 'shard', 'tensor'), may hold values from -6 to 6
- reference_weights: bfloat16 [2, 8192, 1024], P(None, None, 'tensor'), may hold values from -6 to 6
- policy_queries: bfloat16 [6144, 4096], P('shard', 'tensor'), may hold values from -180 to 180
- reference_queries: bfloat16 [6144, 4096], P('shard', 'tensor'), may hold values from -180 to 180
- readout: bfloat16 [6144, 4096], P('shard', 'tensor'), may hold values from -90 to 90
- lengths: int32 [16], P('shard'), may hold values from 96 to 384, as said below
Outputs:
- new_policy: bfloat16 [2, 8192, 1024], P(None, 'shard', 'tensor')
- new_reference: bfloat16 [2, 8192, 1024], P(None, None, 'tensor')
- margins: float32 [8], P('shard')
The draws below stay inside these ranges and needn't reach their ends.
Inputs may be any that keep to these rules, and one draw needn't show every extreme that they name: The first lengths[s] positions of sequence s are real, the rest padding; some sequence has all 384 real.
All inputs are finite; a program needn't handle non-finite values.
Results may differ from the reference program's by a relative error of at most 0.0087.
Values may be sent and summed in bfloat16 or wider, within the bound.
No kernel may reach another device: no remote copies, remote signals or barrier semaphores. Data moves between devices by JAX's collectives and lax.ppermute only.
A program may use at most 128 MiB of HBM per device.

```python
import math
import jax
import jax.numpy as jnp
from jax import lax

D = 8192
HD = 128
KVH = 8
QH = 32
LEN = 384
SEQS = 16
TOKENS = 6144
N_SHARD = 8


def draw_hidden_in(key, part):
    key = jax.random.fold_in(key, 11)
    first_key, second_key = jax.random.split(key, 2)
    feature_rank = jnp.arange(D).astype(jnp.float32) / D
    column_scale = 10.0 ** jax.random.uniform(first_key, (D,)) * 3.0 ** (0.5 * feature_rank)
    base_values = jnp.clip(jax.random.normal(second_key, (TOKENS, D)), -5.0, 5.0)
    return (base_values * column_scale).astype(jnp.bfloat16)


def draw_policy_queries(key, part):
    key = jax.random.fold_in(key, 21)
    first_key = jax.random.fold_in(key, 0)
    row_width = QH * HD
    return jnp.clip(jax.random.normal(first_key, (TOKENS, row_width)), -5.0, 5.0).astype(jnp.bfloat16)


def draw_reference_queries(key, part):
    key = jax.random.fold_in(key, 27)
    first_key = jax.random.fold_in(key, 0)
    row_width = QH * HD
    return jnp.clip(jax.random.normal(first_key, (TOKENS, row_width)), -5.0, 5.0).astype(jnp.bfloat16)


def draw_readout(key, part):
    key = jax.random.fold_in(key, 31)
    first_key, second_key = jax.random.split(key, 2)
    row_width = QH * HD
    head_rank = (jnp.arange(row_width) // HD).astype(jnp.float32) / QH
    column_scale = 10.0 ** jax.random.uniform(first_key, (row_width,)) * 3.0 ** (0.5 * head_rank)
    base_values = jnp.clip(jax.random.normal(second_key, (TOKENS, row_width)), -5.0, 5.0)
    return (base_values * column_scale).astype(jnp.bfloat16)


def draw_lengths(key, part):
    key = jax.random.fold_in(key, 41)
    first_key, second_key = jax.random.split(key)
    drawn_lengths = jax.random.randint(first_key, (SEQS,), LEN // 4, LEN + 1)
    longest = jax.random.randint(second_key, (), 0, SEQS)
    return drawn_lengths.at[longest].set(LEN).astype(jnp.int32)


def block_scale(key, extent, cuts, low, top_value):
    gain = 1.0
    for axis_at, blocks in cuts:
        steps = jax.random.uniform(jax.random.fold_in(jax.random.fold_in(key, 6), axis_at), (blocks,), jnp.float32, low / len(cuts), top_value / len(cuts))
        gain = gain * jnp.repeat(jnp.exp(steps), extent[axis_at] // blocks).reshape((-1,) + (1,) * (len(extent) - 1 - axis_at))
    return gain


def centred(stream_key, extent, spread, most, shards=(), kind=jnp.bfloat16):
    drawn = spread * jax.random.normal(stream_key, extent, jnp.float32)
    if shards:
        drawn = drawn * block_scale(stream_key, extent, shards, -0.22, 0.18)
    return jnp.clip(drawn, -most, most).astype(kind)


def setup_inputs(seed: int = 0) -> dict:
    key_list = jax.random.split(jax.random.key(seed), 8)
    hidden_in = draw_hidden_in(jax.random.fold_in(key_list[7], 71), 0)
    policy_weights = centred(key_list[1], (2, D, KVH * HD), 1.0, 6.0, ((1, 8), (2, 4)))
    reference_weights = centred(key_list[2], (2, D, KVH * HD), 1.0, 6.0, ((2, 4),))
    policy_queries = draw_policy_queries(jax.random.fold_in(key_list[7], 71), 0)
    reference_queries = draw_reference_queries(jax.random.fold_in(key_list[7], 71), 0)
    readout = draw_readout(jax.random.fold_in(key_list[7], 71), 0)
    lengths = draw_lengths(jax.random.fold_in(key_list[7], 71), 0)
    return dict(hidden_in=hidden_in, policy_weights=policy_weights, reference_weights=reference_weights, policy_queries=policy_queries, reference_queries=reference_queries, readout=readout, lengths=lengths)


rope_base = 1000000.0
dpo_beta = 0.1
learning_rate = 0.2
mix_alpha = 0.6
norm_eps = 1e-06

def rope_tables(seq_count, seq_len, head_size):
    positions = jnp.tile(jnp.arange(seq_len, dtype=jnp.float32), seq_count)
    freq_index = jnp.arange(head_size // 2, dtype=jnp.float32)
    frequency = rope_base ** (-2.0 * freq_index / head_size)
    angles = positions[:, None] * frequency[None, :]
    return (jnp.cos(angles)[:, None, :], jnp.sin(angles)[:, None, :])

def rotate_half(vectors, cosine, sine_table):
    half_size = vectors.shape[-1] // 2
    first_half = vectors[..., :half_size]
    second_half = vectors[..., half_size:]
    return jnp.concatenate([first_half * cosine - second_half * sine_table, second_half * cosine + first_half * sine_table], axis=-1)

def rounded(values):
    return lax.optimization_barrier(values.astype(jnp.bfloat16)).astype(jnp.float32)

def masked_scores(key_rows, value_rows, queries, readout, lengths, seq_len, total_heads):
    seq_count = lengths.shape[0]
    kv_heads = key_rows.shape[1]
    head_size = key_rows.shape[2]
    groups = queries.shape[1] // (kv_heads * head_size)
    query_f = queries.reshape(seq_count, seq_len, kv_heads, groups, head_size).astype(jnp.float32)
    key_f = key_rows.reshape(seq_count, seq_len, kv_heads, head_size).astype(jnp.float32)
    value_f = value_rows.reshape(seq_count, seq_len, kv_heads, head_size).astype(jnp.float32)
    logits = jnp.einsum('sikgd,sjkd->skgij', query_f, key_f) / math.sqrt(head_size)
    positions = jnp.arange(seq_len)
    causal = positions[:, None] >= positions[None, :]
    live_keys = positions[None, :] < lengths[:, None]
    allowed = causal[None, None, None, :, :] & live_keys[:, None, None, None, :]
    logits = jnp.where(allowed, logits, -1e+30)
    row_max = lax.optimization_barrier(jnp.max(logits, axis=-1, keepdims=True))
    exponent = jnp.exp(logits - row_max)
    probability = rounded(exponent / lax.optimization_barrier(jnp.sum(exponent, axis=-1, keepdims=True)))
    attended = rounded(jnp.einsum('skgij,sjkd->sikgd', probability, value_f))
    readout_f = readout.reshape(seq_count, seq_len, kv_heads, groups, head_size).astype(jnp.float32)
    token_logit = lax.optimization_barrier(jnp.sum(attended * readout_f, axis=(2, 3, 4))) / math.sqrt(total_heads * head_size)
    return lax.optimization_barrier(jnp.sum(jnp.where(live_keys, token_logit, 0.0), axis=1))

def reference(hidden_in, policy_weights, reference_weights, policy_queries, reference_queries, readout, lengths):
    hidden_f = hidden_in.astype(jnp.float32)
    inverse = lax.rsqrt(lax.optimization_barrier(jnp.mean(hidden_f * hidden_f, axis=-1, keepdims=True)) + norm_eps)
    normed = (hidden_f * inverse).astype(jnp.bfloat16)
    block_rows = 2 * LEN
    columns = KVH * HD
    cosine, sine_table = rope_tables(2, LEN, HD)
    width_scale = D ** (-0.5)
    policy_f = policy_weights.astype(jnp.float32)
    reference_f = reference_weights.astype(jnp.float32)

    def project(rows_in, weights_f):
        projected = jnp.einsum('td,kdc->tkc', rows_in.astype(jnp.float32), weights_f) * width_scale
        key_rows = rotate_half(projected[:, 0].reshape(block_rows, KVH, HD), cosine, sine_table).astype(jnp.bfloat16)
        value_rows = projected[:, 1].reshape(block_rows, KVH, HD).astype(jnp.bfloat16)
        return (key_rows, value_rows)

    def block_slice(array, block_index, row_count):
        return lax.dynamic_slice_in_dim(array, block_index * row_count, row_count, 0)

    def block_scores(block_index):
        rows_in = block_slice(normed, block_index, block_rows)
        seq_lengths = block_slice(lengths, block_index, 2)
        readout_rows = block_slice(readout, block_index, block_rows)
        ref_keys, ref_values = project(rows_in, reference_f)
        pol_keys, pol_values = project(rows_in, policy_f)
        ref_scores = masked_scores(ref_keys, ref_values, block_slice(reference_queries, block_index, block_rows), readout_rows, seq_lengths, LEN, QH)
        pol_scores = masked_scores(pol_keys, pol_values, block_slice(policy_queries, block_index, block_rows), readout_rows, seq_lengths, LEN, QH)
        return (ref_scores, pol_scores)
    blocks = jnp.arange(N_SHARD, dtype=jnp.int32)
    ref_all, pol_all = lax.map(block_scores, blocks)
    paired = pol_all - ref_all
    margins = dpo_beta * (paired[:, 0] - paired[:, 1])
    weight = jax.nn.sigmoid(-margins)
    coefficient = jnp.stack([-weight, weight], axis=1)

    def add_block(running, block_index):
        rows_in = block_slice(normed, block_index, block_rows)
        seq_lengths = block_slice(lengths, block_index, 2)
        readout_rows = block_slice(readout, block_index, block_rows)
        query_rows = block_slice(policy_queries, block_index, block_rows)
        pol_keys, pol_values = project(rows_in, policy_f)

        def policy_part(key_rows, value_rows):
            return masked_scores(key_rows, value_rows, query_rows, readout_rows, seq_lengths, LEN, QH)
        unused_scores, pullback = jax.vjp(policy_part, pol_keys, pol_values)
        block_coeff = lax.dynamic_index_in_dim(coefficient, block_index, 0, keepdims=False)
        key_grad, value_grad = pullback(block_coeff)
        key_pre = rotate_half(key_grad.astype(jnp.float32), cosine, -sine_table).astype(jnp.bfloat16)
        cotangent = jnp.concatenate([key_pre.reshape(block_rows, columns), value_grad.reshape(block_rows, columns)], axis=1)
        row_term = jnp.dot(rows_in.T, cotangent, preferred_element_type=jnp.float32)
        return (running + rounded(row_term), None)
    gradient_sum, unused_out = lax.scan(add_block, jnp.zeros((D, 2 * columns), jnp.float32), blocks)
    gradient = gradient_sum.reshape(D, 2, columns).transpose(1, 0, 2)
    mean_square = lax.optimization_barrier(jnp.mean(gradient * gradient, axis=(1, 2)))
    scale_factor = lax.rsqrt(mean_square + norm_eps)
    new_policy = (policy_f - learning_rate * scale_factor[:, None, None] * gradient).astype(jnp.bfloat16)
    new_reference = (mix_alpha * new_policy.astype(jnp.float32) + (1.0 - mix_alpha) * reference_f).astype(jnp.bfloat16)
    return (new_policy, new_reference, margins)
```

```python
import functools
import math

import jax
import jax.numpy as jnp
import numpy as np
from jax import lax
from jax.experimental import pallas as pl
from jax.experimental.pallas import tpu as pltpu
from jax.sharding import PartitionSpec as P

D = 8192
HD = 128
KVH = 8
QH = 32
LEN = 384
TILE = 128

rope_base = 1000000.0
dpo_beta = 0.1
learning_rate = 0.2
mix_alpha = 0.6
norm_eps = 1e-06
width_scale = D ** (-0.5)
logit_scale = 1.0 / math.sqrt(HD)
MIB = 1024 * 1024

NT = (((1,), (1,)), ((), ()))
NN = (((1,), (0,)), ((), ()))
TN = (((0,), (0,)), ((), ()))


def dot(a, b, dims):
    return lax.dot_general(a, b, dims, preferred_element_type=jnp.float32)


def params(mib=48):
    return pltpu.CompilerParams(vmem_limit_bytes=mib * MIB)


VMEM = pl.BlockSpec(memory_space=pltpu.VMEM)
SMEM = pl.BlockSpec(memory_space=pltpu.SMEM)
HBM = pl.BlockSpec(memory_space=pl.ANY)


def resident(x):
    return pltpu.with_memory_space_constraint(x, pltpu.VMEM)


def rope_tables():
    frequency = rope_base ** (-2.0 * np.arange(HD // 2) / HD)
    angles = np.arange(LEN)[:, None] * frequency[None, :]
    cosine, sine = np.cos(angles), np.sin(angles)
    return (
        np.concatenate([cosine, cosine], axis=1).astype(np.float32),
        np.concatenate([-sine, sine], axis=1).astype(np.float32),
    )


def store_heads(acc_ref, cos, sin, key_ref, value_ref):
    for s in range(key_ref.shape[0] // LEN):
        rows = slice(s * LEN, (s + 1) * LEN)
        for h in range(key_ref.shape[1] // HD):
            cols = slice(h * HD, (h + 1) * HD)
            k = acc_ref[0, rows, cols] * width_scale
            key_ref[rows, cols] = (k * cos + pltpu.roll(k, HD // 2, 1) * sin).astype(jnp.bfloat16)
    value_ref[...] = (acc_ref[1] * width_scale).astype(jnp.bfloat16)


def norm_project_kernel(hidden_hbm, weight_hbm, cos_ref, sin_ref, normed_ref, key_ref, value_ref, x, w, acc, part, in_sem, w_sem):
    tokens = x.shape[0]
    step, width, span, chunk = 16, 512, 128, 1024
    reads = []
    for i in range(tokens // span):
        at = pl.ds(i * span, span)
        reads.append(pltpu.make_async_copy(hidden_hbm.at[at], x.at[at], in_sem.at[i]))
    loads = []
    for c in range(D // chunk):
        at = pl.ds(c * chunk, chunk)
        loads.append(pltpu.make_async_copy(weight_hbm.at[:, at, :], w.at[:, at, :], w_sem.at[c]))
    for copy in reads + loads:
        copy.start()

    def row_step(i, carry):
        at = pl.ds(pl.multiple_of(i * step, step), step)
        total = jnp.zeros((step, width), jnp.float32)
        for c in range(D // width):
            v = x[at, c * width : (c + 1) * width].astype(jnp.float32)
            total = total + v * v
        part[at, :] = functools.reduce(jnp.add, [total[:, c * 128 : (c + 1) * 128] for c in range(width // 128)])
        return carry

    for i, copy in enumerate(reads):
        copy.wait()
        lax.fori_loop(i * (span // step), (i + 1) * (span // step), row_step, 0)
    for copy in loads:
        copy.wait()
    mean = jnp.sum(part[...], axis=1, keepdims=True) * (1.0 / D)
    part[...] = jnp.broadcast_to(lax.rsqrt(mean + norm_eps), part.shape)

    def normalise(c):
        at = slice(c * chunk, (c + 1) * chunk)
        for i in range(tokens // span):
            rows = slice(i * span, (i + 1) * span)
            scale = jnp.concatenate([part[rows, :]] * (chunk // 128), axis=1)
            normed_ref[rows, at] = (x[rows, at].astype(jnp.float32) * scale).astype(jnp.bfloat16)

    normalise(0)
    for c in range(D // chunk):
        at = slice(c * chunk, (c + 1) * chunk)
        for i in (0, 1):
            term = dot(normed_ref[:, at], w[i, at, :], NN)
            acc[i] = term if c == 0 else acc[i] + term
        if (c + 1) * chunk < D:
            normalise(c + 1)
    store_heads(acc, cos_ref[...], sin_ref[...], key_ref, value_ref)


def norm_project(hidden, weights, cos, sin):
    tokens = hidden.shape[0]
    cols = weights.shape[2]
    return pl.pallas_call(
        norm_project_kernel,
        in_specs=[HBM, HBM, VMEM, VMEM],
        out_specs=[VMEM, VMEM, VMEM],
        out_shape=[
            pltpu.VMEM((tokens, D), jnp.bfloat16),
            jax.ShapeDtypeStruct((tokens, cols), jnp.bfloat16),
            jax.ShapeDtypeStruct((tokens, cols), jnp.bfloat16),
        ],
        scratch_shapes=[
            pltpu.VMEM((tokens, D), jnp.bfloat16),
            pltpu.VMEM((2, D, cols), jnp.bfloat16),
            pltpu.VMEM((2, tokens, cols), jnp.float32),
            pltpu.VMEM((tokens, 128), jnp.float32),
            pltpu.SemaphoreType.DMA((tokens // 128,)),
            pltpu.SemaphoreType.DMA((D // 1024,)),
        ],
        compiler_params=params(),
        cost_estimate=pl.CostEstimate(flops=4 * tokens * D * cols, bytes_accessed=4 * tokens * D + 4 * D * cols, transcendentals=0),
        name="norm_project",
    )(hidden, weights, cos, sin)


def project_kernel(count, first, last, idx_ref, masks_ref, x_ref, *refs):
    refs = list(refs)
    pieces = [refs[:count], refs[count : 2 * count]]
    refs = refs[2 * count :]
    held = None if first else refs.pop(0)
    if last:
        cos_ref, sin_ref, key_ref, value_ref, w, acc, sem = refs
    else:
        acc, w, sem = refs
    depth = w.shape[2]
    copies = [[pltpu.make_async_copy(pieces[i][n], w.at[i, n], sem.at[i, n]) for i in (0, 1)] for n in range(count)]
    for pair in copies:
        for copy in pair:
            copy.start()
    for n in range(count):
        for copy in copies[n]:
            copy.wait()
        col = pl.multiple_of((idx_ref[0] ^ masks_ref[n]) * depth, depth)
        x = x_ref[:, pl.ds(col, depth)]
        for i in (0, 1):
            term = dot(x, w[i, n], NN)
            if n:
                term = acc[i] + term
            elif not first:
                term = held[i] + term
            acc[i] = term
    if last:
        store_heads(acc, cos_ref[...], sin_ref[...], key_ref, value_ref)


def project(idx, normed, masks, pieces, held, tables):
    tokens = normed.shape[0]
    rows, cols = pieces[masks[0]][0].shape
    first, last = held is None, tables is not None
    count = len(masks)
    in_specs = [SMEM, SMEM, VMEM] + [HBM] * (2 * count)
    args = [idx, jnp.asarray(masks, jnp.int32), resident(normed)]
    args += [pieces[m][0] for m in masks] + [pieces[m][1] for m in masks]
    if not first:
        in_specs.append(VMEM)
        args.append(held)
    acc_shape = (2, tokens, cols)
    scratch = [pltpu.VMEM((2, count, rows, cols), jnp.bfloat16), pltpu.SemaphoreType.DMA((2, count))]
    if last:
        in_specs += [VMEM] * 2
        args += list(tables)
        out_specs = [VMEM] * 2
        out_shape = [jax.ShapeDtypeStruct((tokens, cols), jnp.bfloat16)] * 2
        scratch.insert(1, pltpu.VMEM(acc_shape, jnp.float32))
    else:
        out_specs = VMEM
        out_shape = jax.ShapeDtypeStruct(acc_shape, jnp.float32)
    return pl.pallas_call(
        functools.partial(project_kernel, count, first, last),
        in_specs=in_specs,
        out_specs=out_specs,
        out_shape=out_shape,
        scratch_shapes=scratch,
        compiler_params=params(),
        cost_estimate=pl.CostEstimate(
            flops=4 * tokens * rows * cols * count,
            bytes_accessed=count * (2 * tokens * rows + 4 * rows * cols),
            transcendentals=0,
        ),
        name="project",
    )(*args)


def stacked(ref, r, groups):
    rows = slice(r * TILE, (r + 1) * TILE)
    return jnp.concatenate([ref[rows, g * HD : (g + 1) * HD] for g in range(groups)], axis=0)


def live_readout(ref, r, groups, length):
    x = stacked(ref, r, groups).astype(jnp.float32)
    at = lax.broadcasted_iota(jnp.int32, x.shape, 0) % TILE + r * TILE
    return jnp.where(at < length, x, 0.0).astype(jnp.bfloat16)


def attend_kernel(back, len_ref, q_ref, k_ref, v_ref, ro_ref, *rest):
    groups = q_ref.shape[1] // HD
    seq = pl.program_id(0)
    length = len_ref[seq]
    tiles = LEN // TILE
    if back:
        before_ref, cos_ref, sin_ref, margin_ref, grad_ref = rest
    else:
        (margin_ref,) = rest
    side = jnp.where(seq % 2 == 0, 1.0, -1.0) * (dpo_beta / math.sqrt(QH * HD))
    score = jnp.zeros((1, groups * TILE), jnp.float32)
    dk = [None] * tiles
    dv = [None] * tiles
    for r in range(tiles):
        n = (r + 1) * TILE
        q = stacked(q_ref, r, groups)
        ro = live_readout(ro_ref, r, groups, length)
        s = dot(k_ref[0:n, :], q, NT)
        dp = dot(v_ref[0:n, :], ro, NT)
        j = lax.broadcasted_iota(jnp.int32, (TILE, groups * TILE), 0)
        i = lax.broadcasted_iota(jnp.int32, (TILE, groups * TILE), 1) % TILE
        s = [s[b * TILE : (b + 1) * TILE] for b in range(r + 1)]
        s[r] = jnp.where(j <= i, s[r], -1e30)
        top = functools.reduce(jnp.maximum, [jnp.max(x, axis=0, keepdims=True) for x in s])
        e = [jnp.exp2((x - top) * (logit_scale * math.log2(math.e))) for x in s]
        inverse = 1.0 / functools.reduce(jnp.add, [jnp.sum(x, axis=0, keepdims=True) for x in e])
        dp = [dp[b * TILE : (b + 1) * TILE] for b in range(r + 1)]
        p = [(x * inverse).astype(jnp.bfloat16) for x in e]
        wide = [x.astype(jnp.float32) for x in p]
        delta = functools.reduce(jnp.add, [jnp.sum(x * y, axis=0, keepdims=True) for x, y in zip(wide, dp)])
        score = score + delta
        if back:
            ds = jnp.concatenate([(x * (y - delta)).astype(jnp.bfloat16) for x, y in zip(wide, dp)], axis=0)
            tk = dot(ds, q, NN)
            tv = dot(jnp.concatenate(p, axis=0), ro, NN)
            for b in range(r + 1):
                at = slice(b * TILE, (b + 1) * TILE)
                dk[b] = tk[at] if dk[b] is None else dk[b] + tk[at]
                dv[b] = tv[at] if dv[b] is None else dv[b] + tv[at]
    @pl.when((seq == 0) & (pl.program_id(1) == 0))
    def _():
        margin_ref[...] = -before_ref[...] if back else jnp.zeros_like(margin_ref)

    margin_ref[...] += jnp.broadcast_to(jnp.sum(score, axis=1, keepdims=True) * side, margin_ref.shape)
    if back:
        scale = jnp.where(seq % 2 == 0, -1.0, 1.0) * (1.0 / math.sqrt(QH * HD))
        for b in range(tiles):
            at = slice(b * TILE, (b + 1) * TILE)
            k = dk[b] * (scale * logit_scale)
            grad_ref[0, at, :] = (k * cos_ref[at, :] - pltpu.roll(k, HD // 2, 1) * sin_ref[at, :]).astype(jnp.bfloat16)
            grad_ref[1, at, :] = (dv[b] * scale).astype(jnp.bfloat16)


def attend(lengths, queries, keys, values, readout, before=None, tables=None):
    seqs = lengths.shape[0]
    heads = keys.shape[1] // HD
    wide = queries.shape[1] // heads
    back = tables is not None
    at = lambda s, k, lens: (s, k)
    in_specs = [
        pl.BlockSpec((LEN, wide), at),
        pl.BlockSpec((LEN, HD), at),
        pl.BlockSpec((LEN, HD), at),
        pl.BlockSpec((LEN, wide), at),
    ]
    args = [queries, keys, values, readout]
    fixed = lambda s, k, lens: (0, 0)
    out_specs = [pl.BlockSpec((8, 128), fixed)]
    out_shape = [jax.ShapeDtypeStruct((8, 128), jnp.float32)]
    if back:
        in_specs += [pl.BlockSpec((8, 128), fixed)] + [pl.BlockSpec((LEN, HD), fixed)] * 2
        args += [before, *tables]
        out_specs.append(pl.BlockSpec((2, LEN, HD), lambda s, k, lens: (0, s, k)))
        out_shape.append(jax.ShapeDtypeStruct((2,) + keys.shape, jnp.bfloat16))
    return pl.pallas_call(
        functools.partial(attend_kernel, back),
        grid_spec=pltpu.PrefetchScalarGridSpec(num_scalar_prefetch=1, grid=(seqs, heads), in_specs=in_specs, out_specs=out_specs),
        out_shape=out_shape,
        compiler_params=params(),
        cost_estimate=pl.CostEstimate(
            flops=seqs * heads * LEN * LEN * wide * (8 if back else 4),
            bytes_accessed=4 * seqs * LEN * wide * heads,
            transcendentals=seqs * heads * LEN * LEN * wide // HD,
        ),
        name="attend_back" if back else "attend",
    )(lengths, *args)


def gradient_tiles(idx, mask, x_ref, cot_ref, rows):
    both = jnp.concatenate([cot_ref[0], cot_ref[1]], axis=1)
    tile = min(rows, 512)
    for t in range(rows // tile):
        col = pl.multiple_of((idx ^ mask) * rows + t * tile, tile)
        out = dot(x_ref[:, pl.ds(col, tile)], both, TN)
        for i in (0, 1):
            yield i, slice(t * tile, (t + 1) * tile), out[:, i * cot_ref.shape[2] : (i + 1) * cot_ref.shape[2]]


def gradient_kernel(mask, idx_ref, x_ref, cot_ref, out_ref):
    for i, at, value in gradient_tiles(idx_ref[0], mask, x_ref, cot_ref, out_ref.shape[1]):
        out_ref[i, at, :] = value.astype(out_ref.dtype)


def merged_kernel(mask, idx_ref, x_ref, cot_ref, theirs_ref, mine_margin, their_margin, *outs):
    cols = cot_ref.shape[2]
    wide = lambda ref: jnp.concatenate([jax.nn.sigmoid(-ref[0:1, :])] * (cols // 128), axis=1)
    mine, their = wide(mine_margin), wide(their_margin)
    for i, at, value in gradient_tiles(idx_ref[0], mask, x_ref, cot_ref, theirs_ref.shape[1]):
        value = value * mine + theirs_ref[i, at, :].astype(jnp.float32) * their
        outs[i][at, :] = value.astype(outs[i].dtype)


def gradient_block(idx, normed, cot, mask, rows, merge=None):
    _, tokens, cols = cot.shape
    args = [idx, resident(normed), cot]
    if merge is None:
        kernel, name = gradient_kernel, "gradient_block"
        out_shape = jax.ShapeDtypeStruct((2, rows, cols), jnp.bfloat16)
    else:
        kernel, name = merged_kernel, "merged_block"
        args += list(merge)
        out_shape = [jax.ShapeDtypeStruct((rows, cols), jnp.bfloat16 if mask else jnp.float32)] * 2
    return pl.pallas_call(
        functools.partial(kernel, mask),
        in_specs=[SMEM] + [VMEM] * (len(args) - 1),
        out_specs=VMEM if merge is None else [VMEM] * 2,
        out_shape=out_shape,
        compiler_params=params(),
        cost_estimate=pl.CostEstimate(flops=4 * tokens * rows * cols, bytes_accessed=8 * rows * cols, transcendentals=0),
        name=name,
    )(*args)


def finish_kernel(counts, *refs):
    refs = list(refs)
    *outs, square_ref = refs[-3:]
    refs = refs[:-3]
    square_ref[...] = jnp.zeros_like(square_ref)
    for i in (0, 1):
        value = refs.pop(0)[...]
        for _ in range(counts[i]):
            value = value + refs.pop(0)[...].astype(jnp.float32)
        outs[i][...] = value.astype(jnp.bfloat16)
        total = jnp.sum(jnp.sum(value * value, axis=0, keepdims=True), axis=1, keepdims=True)
        square_ref[i : i + 1, :] = jnp.broadcast_to(total, (1, 128))


def finish(base, arrived):
    args = [x for i in (0, 1) for x in (base[i], *arrived[i])]
    return pl.pallas_call(
        functools.partial(finish_kernel, [len(a) for a in arrived]),
        in_specs=[VMEM] * len(args),
        out_specs=[VMEM] * 3,
        out_shape=[jax.ShapeDtypeStruct(base[0].shape, jnp.bfloat16)] * 2 + [jax.ShapeDtypeStruct((8, 128), jnp.float32)],
        compiler_params=params(),
        name="finish",
    )(*args)


def blend_kernel(count, first, idx_ref, masks_ref, square_ref, *refs):
    refs = list(refs)
    pieces = [[refs[(2 * k + i) * count : (2 * k + i + 1) * count] for i in (0, 1)] for k in (0, 1)]
    refs = refs[4 * count :]
    ref_hbm = refs.pop(0)
    if not first:
        refs.pop(0)
    out_hbm, token_ref = refs[:2]
    new_hbm = refs[2] if first else None
    x, r, o, new, sem, out_sem = refs[3 if first else 2 :]
    rows, cols = r.shape[2:]
    token_ref[...] = jnp.zeros_like(token_ref)
    copies, at = [], []
    for n in range(count):
        at.append(pl.ds(pl.multiple_of((idx_ref[0] ^ masks_ref[n]) * rows, rows), rows))
        group = [pltpu.make_async_copy(pieces[k][i][n], x.at[k, i, n], sem.at[2 * k + i, n]) for k in (0, 1) for i in (0, 1)]
        group.append(pltpu.make_async_copy(ref_hbm.at[:, at[n], :], r.at[n], sem.at[4, n]))
        for copy in group:
            copy.start()
        copies.append(group)
    mean = square_ref[...] * (1.0 / (D * KVH * HD))
    scale = jnp.concatenate([learning_rate * lax.rsqrt(mean + norm_eps)] * (cols // 128), axis=1)
    writes = []
    for n in range(count):
        for copy in copies[n]:
            copy.wait()
        for i in (0, 1):
            value = (x[0, i, n].astype(jnp.float32) - scale[i : i + 1, :] * x[1, i, n].astype(jnp.float32)).astype(jnp.bfloat16)
            if first and n == 0:
                new[i] = value
            mixed = mix_alpha * value.astype(jnp.float32) + (1.0 - mix_alpha) * r[n, i].astype(jnp.float32)
            o[n, i] = mixed.astype(jnp.bfloat16)
        writes.append(pltpu.make_async_copy(o.at[n], out_hbm.at[:, at[n], :], out_sem.at[n]))
        if first and n == 0:
            writes.append(pltpu.make_async_copy(new, new_hbm, out_sem.at[count]))
            writes[-1].start()
        writes[len(writes) - 1 - (first and n == 0)].start()
    for copy in writes:
        copy.wait()


def blend(idx, squares, weights, grads, reference, held, masks):
    rows, cols = weights[masks[0]][0].shape
    count = len(masks)
    first = held is None
    args = [idx, jnp.asarray(masks, jnp.int32), squares]
    args += [pieces[m][i] for pieces in (weights, grads) for i in (0, 1) for m in masks] + [reference]
    in_specs = [SMEM, SMEM, VMEM] + [HBM] * (4 * count + 1)
    out_specs = [HBM, VMEM]
    out_shape = [jax.ShapeDtypeStruct(reference.shape, jnp.bfloat16), jax.ShapeDtypeStruct((8, 128), jnp.float32)]
    aliases = {}
    if first:
        out_specs.append(HBM)
        out_shape.append(jax.ShapeDtypeStruct((2, rows, cols), jnp.bfloat16))
    else:
        aliases = {len(args): 0}
        in_specs.append(HBM)
        args.append(held)
    return pl.pallas_call(
        functools.partial(blend_kernel, count, first),
        in_specs=in_specs,
        out_specs=out_specs,
        out_shape=out_shape,
        scratch_shapes=[
            pltpu.VMEM((2, 2, count, rows, cols), jnp.bfloat16),
            pltpu.VMEM((count, 2, rows, cols), jnp.bfloat16),
            pltpu.VMEM((count, 2, rows, cols), jnp.bfloat16),
            pltpu.VMEM((2, rows, cols), jnp.bfloat16),
            pltpu.SemaphoreType.DMA((5, count)),
            pltpu.SemaphoreType.DMA((count + 1,)),
        ],
        input_output_aliases=aliases,
        compiler_params=params(62),
        cost_estimate=pl.CostEstimate(flops=8 * rows * cols * count, bytes_accessed=16 * rows * cols * count, transcendentals=0),
        name="blend",
    )(*args)


def bits_of(mask):
    return [1 << b for b in range(mask.bit_length()) if mask >> b & 1]


def after(value, *earlier):
    return lax.optimization_barrier((value, earlier))[0]


def body(shards, tensors, hidden_in, policy_weights, reference_weights, policy_queries, reference_queries, readout, lengths):
    rows = policy_weights.shape[1]
    idx = lax.axis_index("shard").astype(jnp.int32).reshape(1)
    tables = tuple(jnp.asarray(t) for t in rope_tables())

    def swap(x, bit, axis="shard", size=shards):
        return lax.ppermute(x, axis, [(i, i ^ bit) for i in range(size)])

    def powers(size):
        return [1 << b for b in range(size.bit_length() - 1)]

    chips = sorted(range(0, shards, 2), key=lambda m: (len(bits_of(m)), m))
    near = [m for m in chips if len(bits_of(m)) == 1]
    far = [m for m in chips if len(bits_of(m)) > 1]
    link = lambda i, m: bits_of(m)[-1] if i == 0 else bits_of(m)[0]

    def send_near(own):
        got = {0: list(own)}
        for turn in (0, 1):
            for n, m in enumerate(near):
                i = (turn + n) % 2
                got.setdefault(m, [None, None])[i] = swap(own[i], m)
        got[1] = [swap(g, 1) for g in own]
        return got

    def relay(got, m, *earlier):
        got[m] = [None, None]
        for i in (0, 1):
            via = link(i, m)
            got[m][i] = swap(after(got[m ^ via][i], *earlier), via)

    def to_core(got, m, *earlier):
        got[m | 1] = [swap(after(g, *earlier), 1) for g in got[m]]

    weights = send_near((policy_weights[0], policy_weights[1]))
    normed, ref_keys, ref_values = norm_project(hidden_in, reference_weights, *tables)
    for m in far:
        relay(weights, m, ref_keys)
    for m in near:
        to_core(weights, m, ref_keys)
    (ref_margin,) = attend(lengths, reference_queries, ref_keys, ref_values, readout)
    early = [m | c for m in [0] + near for c in (0, 1)]
    held = project(after(idx, ref_margin), normed, early, weights, None, None if far else tables)
    if far:
        for m in far:
            to_core(weights, m, held)
        held = project(idx, normed, [m | c for m in far for c in (0, 1)], weights, held, tables)
    pol_keys, pol_values = held
    margin, cot = attend(lengths, policy_queries, pol_keys, pol_values, readout, ref_margin, tables)

    theirs = {}
    order = list(reversed(chips))

    def block_for_core(earlier):
        m = order[len(theirs)]
        block = gradient_block(after(idx, earlier), normed, cot, m | 1, rows)
        theirs[m] = swap(block, 1)
        return block

    for bit in powers(tensors):
        received = swap(margin, bit, "tensor", tensors)
        if len(theirs) < len(order) - 1:
            received = after(received, block_for_core(margin))
        margin = margin + received
    other = swap(margin, 1)
    if len(theirs) < len(order) - 1:
        other = after(other, block_for_core(margin))

    chip_sum = {}
    arrived = {m: [[], []] for m in chips}
    waiting = []
    last = other

    def send(m, i):
        payload = chip_sum[m][i]
        if arrived[m][i]:
            payload = payload.astype(jnp.float32)
            for term in arrived[m][i]:
                payload = payload + term.astype(jnp.float32)
            payload = payload.astype(jnp.bfloat16)
        via = link(i, m)
        arrived[m ^ via][i].append(swap(payload, via))
        return payload

    for m in order:
        if m == 0:
            last = [send(*which) for which in waiting]
        if m not in theirs:
            last = block_for_core(last)
        chip_sum[m] = gradient_block(after(idx, last), normed, cot, m, rows, (theirs[m], margin, other))
        last = []
        for i in (0, 1):
            if m and not any(k ^ link(i, k) == m for k in far):
                last.append(send(m, i))
            elif m:
                waiting.append((m, i))
        last = last or chip_sum[m]
    *own, squares = finish(chip_sum[0], arrived[0])

    grads = send_near(own)
    for bit in powers(tensors):
        squares = squares + swap(squares, bit, "tensor", tensors)
    for m in far:
        relay(grads, m, squares)
        squares = after(squares, *[grads[m ^ link(i, m)][i] for i in (0, 1)])
    for bit in powers(shards):
        squares = squares + swap(squares, bit)
    for m in near:
        to_core(grads, m, squares)
    new_reference, token, new_policy = blend(idx, squares, weights, grads, reference_weights, None, [0, 1])
    new_reference, token = blend(idx, squares, weights, grads, reference_weights, new_reference, early[2:])
    for m in far:
        to_core(grads, m, token)
    for masks in (far, [m | 1 for m in far]) if far else ():
        new_reference, token = blend(idx, squares, weights, grads, reference_weights, new_reference, masks)
    return (new_policy, new_reference, margin[0, :1])


def solution(mesh):
    return jax.shard_map(
        functools.partial(body, mesh.shape["shard"], mesh.shape["tensor"]),
        mesh=mesh,
        in_specs=(
            P("shard", None),
            P(None, "shard", "tensor"),
            P(None, None, "tensor"),
            P("shard", "tensor"),
            P("shard", "tensor"),
            P("shard", "tensor"),
            P("shard"),
        ),
        out_specs=(P(None, "shard", "tensor"), P(None, None, "tensor"), P("shard")),
        check_vma=False,
    )
```

```python
import functools
import math

import jax
import jax.numpy as jnp
import numpy as np
from jax import lax
from jax.experimental import pallas as pl
from jax.experimental.pallas import tpu as pltpu
from jax.sharding import PartitionSpec as P

D = 8192
HD = 128
KVH = 8
QH = 32
LEN = 384
TILE = 128

rope_base = 1000000.0
dpo_beta = 0.1
learning_rate = 0.2
mix_alpha = 0.6
norm_eps = 1e-06
width_scale = D ** (-0.5)
logit_scale = 1.0 / math.sqrt(HD)
MIB = 1024 * 1024

NT = (((1,), (1,)), ((), ()))
NN = (((1,), (0,)), ((), ()))
TN = (((0,), (0,)), ((), ()))


def dot(a, b, dims):
    return lax.dot_general(a, b, dims, preferred_element_type=jnp.float32)


def params(mib):
    return pltpu.CompilerParams(vmem_limit_bytes=mib * MIB)


COST = pl.CostEstimate(flops=1, bytes_accessed=1, transcendentals=0)
VMEM = pl.BlockSpec(memory_space=pltpu.VMEM)
SMEM = pl.BlockSpec(memory_space=pltpu.SMEM)
HBM = pl.BlockSpec(memory_space=pl.ANY)


def resident(x):
    return pltpu.with_memory_space_constraint(x, pltpu.VMEM)


def in_hbm(x):
    return pltpu.with_memory_space_constraint(x, pltpu.HBM)


def rope_tables():
    frequency = rope_base ** (-2.0 * np.arange(HD // 2) / HD)
    angles = np.arange(LEN)[:, None] * frequency[None, :]
    cosine, sine = np.cos(angles), np.sin(angles)
    return np.stack([np.concatenate([cosine, cosine], axis=1), np.concatenate([-sine, sine], axis=1)]).astype(np.float32)


def store_heads(acc_ref, cos, sin, key_ref, value_ref):
    for s in range(key_ref.shape[0] // LEN):
        rows = slice(s * LEN, (s + 1) * LEN)
        for h in range(key_ref.shape[1] // HD):
            cols = slice(h * HD, (h + 1) * HD)
            k = acc_ref[0, rows, cols] * width_scale
            key_ref[rows, cols] = (k * cos + pltpu.roll(k, HD // 2, 1) * sin).astype(jnp.bfloat16)
    value_ref[...] = (acc_ref[1] * width_scale).astype(jnp.bfloat16)


def norm_project_kernel(
    hidden_hbm, weight_hbm, table_hbm, normed_ref, key_ref, value_ref, x, w, acc, part, table, in_sem, w_sem, table_sem
):
    tokens = x.shape[0]
    step, width, span, chunk = 16, 512, 128, 1024
    reads = []
    for i in range(tokens // span):
        at = pl.ds(i * span, span)
        reads.append(pltpu.make_async_copy(hidden_hbm.at[at], x.at[at], in_sem.at[i]))
    loads = []
    for c in range(D // chunk):
        at = pl.ds(c * chunk, chunk)
        loads.append(pltpu.make_async_copy(weight_hbm.at[:, at, :], w.at[:, at, :], w_sem.at[c]))
    loads.append(pltpu.make_async_copy(table_hbm, table, table_sem))
    for copy in reads + loads:
        copy.start()

    def row_step(i, carry):
        at = pl.ds(pl.multiple_of(i * step, step), step)
        total = jnp.zeros((step, width), jnp.float32)
        for c in range(D // width):
            v = x[at, c * width : (c + 1) * width].astype(jnp.float32)
            total = total + v * v
        part[at, :] = functools.reduce(jnp.add, [total[:, c * 128 : (c + 1) * 128] for c in range(width // 128)])
        return carry

    for i, copy in enumerate(reads):
        copy.wait()
        lax.fori_loop(i * (span // step), (i + 1) * (span // step), row_step, 0)
    for copy in loads:
        copy.wait()
    mean = jnp.sum(part[...], axis=1, keepdims=True) * (1.0 / D)
    part[...] = jnp.broadcast_to(lax.rsqrt(mean + norm_eps), part.shape)

    def normalise(c):
        at = slice(c * chunk, (c + 1) * chunk)
        for i in range(tokens // step):
            rows = slice(i * step, (i + 1) * step)
            scale = jnp.concatenate([part[rows, :]] * (chunk // 128), axis=1)
            normed_ref[rows, at] = (x[rows, at].astype(jnp.float32) * scale).astype(jnp.bfloat16)

    normalise(0)
    for c in range(D // chunk):
        at = slice(c * chunk, (c + 1) * chunk)
        for i in (0, 1):
            term = dot(normed_ref[:, at], w[i, at, :], NN)
            acc[i] = term if c == 0 else acc[i] + term
        if (c + 1) * chunk < D:
            normalise(c + 1)
    store_heads(acc, table[0], table[1], key_ref, value_ref)


def norm_project(hidden, weights, tables):
    tokens = hidden.shape[0]
    cols = weights.shape[2]
    return pl.pallas_call(
        norm_project_kernel,
        in_specs=[HBM, HBM, HBM],
        out_specs=[VMEM, VMEM, VMEM],
        out_shape=[
            pltpu.VMEM((tokens, D), jnp.bfloat16),
            pltpu.VMEM((tokens, cols), jnp.bfloat16),
            pltpu.VMEM((tokens, cols), jnp.bfloat16),
        ],
        scratch_shapes=[
            pltpu.VMEM((tokens, D), jnp.bfloat16),
            pltpu.VMEM((2, D, cols), jnp.bfloat16),
            pltpu.VMEM((2, tokens, cols), jnp.float32),
            pltpu.VMEM((tokens, 128), jnp.float32),
            pltpu.VMEM(tables.shape, jnp.float32),
            pltpu.SemaphoreType.DMA((tokens // 128,)),
            pltpu.SemaphoreType.DMA((D // 1024,)),
            pltpu.SemaphoreType.DMA,
        ],
        compiler_params=params(29),
        cost_estimate=COST,
        name="norm_project",
    )(in_hbm(hidden), in_hbm(weights), in_hbm(tables))


def project_kernel(masks, first, last, idx_ref, x_ref, *refs):
    refs = list(refs)
    count = len(masks)
    pieces = [refs[:count], refs[count : 2 * count]]
    refs = refs[2 * count :]
    held = None if first else refs.pop(0)
    if last:
        table_hbm, key_ref, value_ref, w, acc, table, sem, table_sem = refs
        table_copy = pltpu.make_async_copy(table_hbm, table, table_sem)
        table_copy.start()
    else:
        acc, w, sem = refs
    depth = w.shape[2]
    copies = [[pltpu.make_async_copy(pieces[i][n], w.at[i, n], sem.at[i, n]) for i in (0, 1)] for n in range(count)]
    for pair in copies:
        for copy in pair:
            copy.start()
    for n in range(count):
        for copy in copies[n]:
            copy.wait()
        col = pl.multiple_of((idx_ref[0] ^ masks[n]) * depth, depth)
        x = x_ref[:, pl.ds(col, depth)]
        for i in (0, 1):
            term = dot(x, w[i, n], NN)
            if n:
                term = acc[i] + term
            elif not first:
                term = held[i] + term
            acc[i] = term
    if last:
        table_copy.wait()
        store_heads(acc, table[0], table[1], key_ref, value_ref)


def project(idx, normed, masks, pieces, held, tables):
    tokens = normed.shape[0]
    rows, cols = pieces[masks[0]][0].shape
    first, last = held is None, tables is not None
    count = len(masks)
    in_specs = [SMEM, VMEM] + [HBM] * (2 * count)
    args = [idx, resident(normed)]
    args += [pieces[m][i] for i in (0, 1) for m in masks]
    if not first:
        in_specs.append(VMEM)
        args.append(resident(held))
    acc_shape = (2, tokens, cols)
    scratch = [pltpu.VMEM((2, count, rows, cols), jnp.bfloat16), pltpu.SemaphoreType.DMA((2, count))]
    if last:
        in_specs.append(HBM)
        args.append(in_hbm(tables))
        out_specs = [VMEM] * 2
        out_shape = [pltpu.VMEM((tokens, cols), jnp.bfloat16)] * 2
        scratch.insert(1, pltpu.VMEM(acc_shape, jnp.float32))
        scratch.insert(2, pltpu.VMEM(tables.shape, jnp.float32))
        scratch.append(pltpu.SemaphoreType.DMA)
    else:
        out_specs = VMEM
        out_shape = pltpu.VMEM(acc_shape, jnp.float32)
    return pl.pallas_call(
        functools.partial(project_kernel, tuple(masks), first, last),
        in_specs=in_specs,
        out_specs=out_specs,
        out_shape=out_shape,
        scratch_shapes=scratch,
        compiler_params=params(10),
        cost_estimate=COST,
        name="project",
    )(*args)


HEADS = 2


def stacked(ref, r, first, count):
    rows = slice(r * TILE, (r + 1) * TILE)
    return jnp.concatenate([ref[rows, g * HD : (g + 1) * HD] for g in range(first, first + count)], axis=0)


def live_readout(ref, r, first, count, length):
    x = stacked(ref, r, first, count).astype(jnp.float32)
    at = lax.broadcasted_iota(jnp.int32, x.shape, 0) % TILE + r * TILE
    return jnp.where(at < length, x, 0.0).astype(jnp.bfloat16)


def attend_kernel(keep, len_ref, q_ref, k_ref, v_ref, ro_ref, *rest):
    groups = q_ref.shape[1] // HD
    count = min(groups, HEADS)
    seq = pl.program_id(0)
    length = len_ref[seq]
    if keep:
        before_ref, margin_ref, prob_ref, delta_ref = rest
    else:
        (margin_ref,) = rest
    score = jnp.zeros((1, count * TILE), jnp.float32)
    j = lax.broadcasted_iota(jnp.int32, (TILE, count * TILE), 0)
    i = lax.broadcasted_iota(jnp.int32, (TILE, count * TILE), 1) % TILE
    base = 0
    for r in range(LEN // TILE):
        n = (r + 1) * TILE
        for g in range(0, groups, count):
            q = stacked(q_ref, r, g, count)
            ro = live_readout(ro_ref, r, g, count, length)
            s = dot(k_ref[0:n, :], q, NT)
            dp = dot(v_ref[0:n, :], ro, NT)
            s = [s[b * TILE : (b + 1) * TILE] for b in range(r + 1)]
            s[r] = jnp.where(j <= i, s[r], -1e30)
            top = functools.reduce(jnp.maximum, [jnp.max(x, axis=0, keepdims=True) for x in s])
            e = [jnp.exp2((x - top) * (logit_scale * math.log2(math.e))) for x in s]
            inverse = 1.0 / functools.reduce(jnp.add, [jnp.sum(x, axis=0, keepdims=True) for x in e])
            cols = slice(g * TILE, (g + count) * TILE)
            delta = jnp.zeros((1, count * TILE), jnp.float32)
            for b in range(r + 1):
                p = (e[b] * inverse).astype(jnp.bfloat16)
                if keep:
                    prob_ref[0, 0, base + b * TILE : base + (b + 1) * TILE, cols] = p
                delta = delta + jnp.sum(p.astype(jnp.float32) * dp[b * TILE : (b + 1) * TILE], axis=0, keepdims=True)
            if keep:
                delta_ref[0, 0, r : r + 1, cols] = delta
            score = score + delta
        base += n
    side = jnp.where(seq % 2 == 0, 1.0, -1.0) * (dpo_beta / math.sqrt(QH * HD))

    @pl.when((seq == 0) & (pl.program_id(1) == 0))
    def _():
        margin_ref[...] = -before_ref[...] if keep else jnp.zeros_like(margin_ref)

    margin_ref[...] += jnp.broadcast_to(jnp.sum(score, axis=1, keepdims=True) * side, margin_ref.shape)


def attend(lengths, queries, keys, values, readout, before=None):
    seqs = lengths.shape[0]
    heads = keys.shape[1] // HD
    wide = queries.shape[1] // heads
    tiles = LEN // TILE
    span = TILE * tiles * (tiles + 1) // 2
    keep = before is not None
    at = lambda s, k, lens: (s, k)
    at4 = lambda s, k, lens: (s, k, 0, 0)
    fixed = lambda s, k, lens: (0, 0)
    in_specs = [pl.BlockSpec((LEN, wide), at), pl.BlockSpec((LEN, HD), at), pl.BlockSpec((LEN, HD), at), pl.BlockSpec((LEN, wide), at)]
    args = [queries, resident(keys), resident(values), readout]
    out_specs = [pl.BlockSpec((8, 128), fixed)]
    out_shape = [jax.ShapeDtypeStruct((8, 128), jnp.float32)]
    if keep:
        in_specs.append(pl.BlockSpec((8, 128), fixed))
        args.append(before)
        out_specs += [pl.BlockSpec((1, 1, span, wide), at4), pl.BlockSpec((1, 1, tiles, wide), at4)]
        out_shape += [pltpu.VMEM((seqs, heads, span, wide), jnp.bfloat16), pltpu.VMEM((seqs, heads, tiles, wide), jnp.float32)]
    return pl.pallas_call(
        functools.partial(attend_kernel, keep),
        grid_spec=pltpu.PrefetchScalarGridSpec(num_scalar_prefetch=1, grid=(seqs, heads), in_specs=in_specs, out_specs=out_specs),
        out_shape=out_shape,
        compiler_params=params(8),
        cost_estimate=COST,
        name="attend",
    )(lengths, *args)


def attend_back_kernel(len_ref, q_ref, v_ref, ro_ref, prob_ref, delta_ref, table_ref, grad_ref):
    groups = q_ref.shape[1] // HD
    count = min(groups, HEADS)
    seq = pl.program_id(0)
    length = len_ref[seq]
    tiles = LEN // TILE
    dk = [None] * tiles
    dv = [None] * tiles
    base = 0
    for r in range(tiles):
        n = (r + 1) * TILE
        for g in range(0, groups, count):
            q = stacked(q_ref, r, g, count)
            ro = live_readout(ro_ref, r, g, count, length)
            cols = slice(g * TILE, (g + count) * TILE)
            p = prob_ref[0, 0, base : base + n, cols]
            dp = dot(v_ref[0:n, :], ro, NT)
            ds = (p.astype(jnp.float32) * (dp - delta_ref[0, 0, r : r + 1, cols])).astype(jnp.bfloat16)
            tk = dot(ds, q, NN)
            tv = dot(p, ro, NN)
            for b in range(r + 1):
                at = slice(b * TILE, (b + 1) * TILE)
                dk[b] = tk[at] if dk[b] is None else dk[b] + tk[at]
                dv[b] = tv[at] if dv[b] is None else dv[b] + tv[at]
        base += n
    scale = jnp.where(seq % 2 == 0, -1.0, 1.0) * (1.0 / math.sqrt(QH * HD))
    for b in range(tiles):
        at = slice(b * TILE, (b + 1) * TILE)
        k = dk[b] * (scale * logit_scale)
        k = k * table_ref[0, at, :] - pltpu.roll(k, HD // 2, 1) * table_ref[1, at, :]
        grad_ref[0, :, at] = k.T.astype(jnp.bfloat16)
        grad_ref[1, :, at] = (dv[b] * scale).T.astype(jnp.bfloat16)


def attend_back(lengths, queries, values, readout, probs, delta, tables):
    seqs, heads, span, wide = probs.shape
    at = lambda s, k, lens: (s, k)
    at4 = lambda s, k, lens: (s, k, 0, 0)
    return pl.pallas_call(
        attend_back_kernel,
        grid_spec=pltpu.PrefetchScalarGridSpec(
            num_scalar_prefetch=1,
            grid=(seqs, heads),
            in_specs=[
                pl.BlockSpec((LEN, wide), at),
                pl.BlockSpec((LEN, HD), at),
                pl.BlockSpec((LEN, wide), at),
                pl.BlockSpec((1, 1, span, wide), at4),
                pl.BlockSpec((1, 1) + delta.shape[2:], at4),
                pl.BlockSpec(tables.shape, lambda s, k, lens: (0, 0, 0)),
            ],
            out_specs=pl.BlockSpec((2, HD, LEN), lambda s, k, lens: (0, k, s)),
        ),
        out_shape=pltpu.VMEM((2,) + values.shape[::-1], jnp.bfloat16),
        compiler_params=params(10),
        cost_estimate=COST,
        name="attend_back",
    )(lengths, queries, resident(values), readout, resident(probs), resident(delta), tables)


def gradient_tiles(idx, mask, x_ref, cot_ref, rows):
    cols = cot_ref.shape[1]
    both = jnp.concatenate([cot_ref[0], cot_ref[1]], axis=0)
    tile = min(rows, 256)
    for t in range(rows // tile):
        col = pl.multiple_of((idx ^ mask) * rows + t * tile, tile)
        out = dot(both, x_ref[:, pl.ds(col, tile)], NN)
        for i in (0, 1):
            yield i, slice(t * tile, (t + 1) * tile), out[i * cols : (i + 1) * cols]


def gradient_kernel(masks, idx_ref, x_ref, cot_ref, *outs):
    for mask, out_ref in zip(masks, outs):
        for i, at, value in gradient_tiles(idx_ref[0], mask, x_ref, cot_ref, out_ref.shape[2]):
            out_ref[i, :, at] = value.astype(out_ref.dtype)


def merged_kernel(masks, idx_ref, x_ref, cot_ref, mine_margin, their_margin, *refs):
    count = len(masks)
    theirs_hbm, outs = refs[:count], refs[count : 3 * count]
    theirs, sem = refs[3 * count :]
    copies = [pltpu.make_async_copy(theirs_hbm[n], theirs.at[n], sem.at[n]) for n in range(count)]
    for copy in copies:
        copy.start()
    weight = lambda ref: jnp.concatenate([jax.nn.sigmoid(-ref[0:1, :])] * 2, axis=1)
    mine, their = weight(mine_margin), weight(their_margin)
    for n, mask in enumerate(masks):
        copies[n].wait()
        for i, at, value in gradient_tiles(idx_ref[0], mask, x_ref, cot_ref, theirs.shape[3]):
            value = value * mine + theirs[n, i, :, at].astype(jnp.float32) * their
            outs[2 * n + i][:, at] = value.astype(outs[2 * n + i].dtype)


def gradient_blocks(idx, normed, cot, masks, rows, merge=None):
    _, cols, tokens = cot.shape
    args = [idx, resident(normed), resident(cot)]
    in_specs = [SMEM, VMEM, VMEM]
    scratch = []
    if merge is None:
        kernel, name = gradient_kernel, "gradient_block"
        out_shape = [jax.ShapeDtypeStruct((2, cols, rows), jnp.bfloat16) for m in masks]
    else:
        kernel, name = merged_kernel, "merged_block"
        margins, theirs = merge
        args += [*margins] + [theirs[m] for m in masks]
        in_specs += [VMEM, VMEM] + [HBM] * len(masks)
        out_shape = [
            jax.ShapeDtypeStruct((cols, rows), jnp.bfloat16) if m else pltpu.VMEM((cols, rows), jnp.float32)
            for m in masks
            for i in (0, 1)
        ]
        scratch = [pltpu.VMEM((len(masks), 2, cols, rows), jnp.bfloat16), pltpu.SemaphoreType.DMA((len(masks),))]
    outs = pl.pallas_call(
        functools.partial(kernel, tuple(masks)),
        in_specs=in_specs,
        out_specs=[VMEM] * len(out_shape),
        out_shape=out_shape,
        scratch_shapes=scratch,
        compiler_params=params(10),
        cost_estimate=COST,
        name=name,
    )(*args)
    return outs if merge is None else [outs[2 * n : 2 * n + 2] for n in range(len(masks))]


def finish_kernel(counts, *refs):
    refs = list(refs)
    out_ref, square_ref = refs[-2:]
    refs = refs[:-2]
    square_ref[...] = jnp.zeros_like(square_ref)
    cols, rows = refs[0].shape
    for i in (0, 1):
        terms = [refs.pop(0) for _ in range(1 + counts[i])]
        squares = jnp.zeros((1, 128), jnp.float32)
        for c in range(cols // 128):
            for r in range(rows // 128):
                at = (slice(c * 128, (c + 1) * 128), slice(r * 128, (r + 1) * 128))
                value = functools.reduce(jnp.add, [t[at].astype(jnp.float32) for t in terms])
                squares = squares + jnp.sum(value * value, axis=0, keepdims=True)
                out_ref[i, at[1], at[0]] = value.T.astype(jnp.bfloat16)
        square_ref[i : i + 1, :] = jnp.broadcast_to(jnp.sum(squares, axis=1, keepdims=True), (1, 128))


def finish(base, arrived):
    args = [x for i in (0, 1) for x in (resident(base[i]), *arrived[i])]
    cols, rows = base[0].shape
    return pl.pallas_call(
        functools.partial(finish_kernel, [len(a) for a in arrived]),
        in_specs=[VMEM] * len(args),
        out_specs=[VMEM] * 2,
        out_shape=[jax.ShapeDtypeStruct((2, rows, cols), jnp.bfloat16), jax.ShapeDtypeStruct((8, 128), jnp.float32)],
        compiler_params=params(8),
        cost_estimate=COST,
        name="finish",
    )(*args)


def fetch_kernel(masks, idx_ref, *refs):
    count = len(masks)
    pieces, (ref_hbm, w, r, sem) = refs[: 2 * count], refs[2 * count :]
    rows = r.shape[2]
    copies = []
    for n, mask in enumerate(masks):
        at = pl.ds(pl.multiple_of((idx_ref[0] ^ mask) * rows, rows), rows)
        copies += [pltpu.make_async_copy(pieces[2 * n + i], w.at[n, i], sem.at[i, n]) for i in (0, 1)]
        copies.append(pltpu.make_async_copy(ref_hbm.at[:, at, :], r.at[n], sem.at[2, n]))
    for copy in copies:
        copy.start()
    for copy in copies:
        copy.wait()


def fetch(idx, weights, reference, masks):
    rows, cols = weights[masks[0]][0].shape
    count = len(masks)
    return pl.pallas_call(
        functools.partial(fetch_kernel, tuple(masks)),
        in_specs=[SMEM] + [HBM] * (2 * count + 1),
        out_specs=[VMEM] * 2,
        out_shape=[pltpu.VMEM((count, 2, rows, cols), jnp.bfloat16)] * 2,
        scratch_shapes=[pltpu.SemaphoreType.DMA((3, count))],
        compiler_params=params(4),
        cost_estimate=COST,
        name="fetch",
    )(idx, *[w for m in masks for w in weights[m]], in_hbm(reference))


def blend_kernel(masks, first, ready, idx_ref, square_ref, *refs):
    refs = list(refs)
    count = len(masks)
    grads = [[refs.pop(0)] if whole else [refs.pop(0), refs.pop(0)] for whole in first_parts(masks, ready)]
    if ready is None:
        weights = [[refs.pop(0), refs.pop(0)] for m in masks]
        ref_hbm = refs.pop(0)
    else:
        w, r = refs.pop(0), refs.pop(0)
    if not first:
        refs.pop(0)
    out_hbm, token_ref = refs.pop(0), refs.pop(0)
    new_hbm = refs.pop(0) if first else None
    if ready is None:
        w, r = refs.pop(0), refs.pop(0)
    g, o, new, sem, out_sem = refs
    rows, cols = g.shape[2:]
    step = 32
    token_ref[...] = jnp.zeros_like(token_ref)
    copies, at = [], []
    for n in range(count):
        at.append(pl.ds(pl.multiple_of((idx_ref[0] ^ masks[n]) * rows, rows), rows))
        if len(grads[n]) == 1:
            group = [pltpu.make_async_copy(grads[n][0], g.at[n], sem.at[0, n])]
        else:
            group = [pltpu.make_async_copy(grads[n][i], g.at[n, i], sem.at[i, n]) for i in (0, 1)]
        if ready is None:
            group += [pltpu.make_async_copy(weights[n][i], w.at[n, i], sem.at[2 + i, n]) for i in (0, 1)]
            group.append(pltpu.make_async_copy(ref_hbm.at[:, at[n], :], r.at[n], sem.at[4, n]))
        for copy in group:
            copy.start()
        copies.append(group)
    mean = square_ref[...] * (1.0 / (D * KVH * HD))
    scale = jnp.concatenate([learning_rate * lax.rsqrt(mean + norm_eps)] * (cols // 128), axis=1)
    writes = []
    half = rows // 2
    for n in range(count):
        from_n = n if ready is None else ready + n
        for copy in copies[n]:
            copy.wait()
        for part in range(2):
            for i in (0, 1):
                for start in range(part * half, (part + 1) * half, step):
                    j = slice(start, start + step)
                    value = w[from_n, i, j].astype(jnp.float32) - scale[i : i + 1, :] * g[n, i, j].astype(jnp.float32)
                    value = value.astype(jnp.bfloat16)
                    if first and n == 0:
                        new[i, j] = value
                    mixed = mix_alpha * value.astype(jnp.float32) + (1.0 - mix_alpha) * r[from_n, i, j].astype(jnp.float32)
                    o[n, i, j] = mixed.astype(jnp.bfloat16)
            at_part = pl.ds(pl.multiple_of((idx_ref[0] ^ masks[n]) * rows + part * half, half), half)
            copy = pltpu.make_async_copy(o.at[n, :, pl.ds(part * half, half), :], out_hbm.at[:, at_part, :], out_sem.at[part, n])
            copy.start()
            writes.append(copy)
        if first and n == 0:
            copy = pltpu.make_async_copy(new, new_hbm, out_sem.at[0, count])
            copy.start()
            writes.append(copy)
    for copy in writes:
        copy.wait()


def first_parts(masks, ready):
    return [len(bits_of(m >> 1)) < 2 for m in masks]


def blend(idx, squares, weights, grads, reference, held, masks, ready=None):
    rows, cols = weights[masks[0]][0].shape
    count = len(masks)
    first = held is None
    args = [idx, squares] + [x for m in masks for x in grads[m]]
    in_specs = [SMEM, VMEM] + [HBM] * (len(args) - 2)
    block = pltpu.VMEM((count, 2, rows, cols), jnp.bfloat16)
    scratch = [block, block, pltpu.VMEM((2, rows, cols) if first else (8, 128), jnp.bfloat16)]
    scratch += [pltpu.SemaphoreType.DMA((5, count)), pltpu.SemaphoreType.DMA((2, count + 1))]
    if ready is None:
        args += [w for m in masks for w in weights[m]] + [in_hbm(reference)]
        in_specs += [HBM] * (2 * count + 1)
        scratch = [block, block] + scratch
    else:
        args += [resident(x) for x in ready[0]]
        in_specs += [VMEM] * 2
    out_specs = [HBM, VMEM]
    out_shape = [jax.ShapeDtypeStruct(reference.shape, jnp.bfloat16), jax.ShapeDtypeStruct((8, 128), jnp.float32)]
    aliases = {}
    if first:
        out_specs.append(HBM)
        out_shape.append(jax.ShapeDtypeStruct((2, rows, cols), jnp.bfloat16))
    else:
        aliases = {len(args): 0}
        in_specs.append(HBM)
        args.append(held)
    return pl.pallas_call(
        functools.partial(blend_kernel, tuple(masks), first, None if ready is None else ready[1]),
        in_specs=in_specs,
        out_specs=out_specs,
        out_shape=out_shape,
        scratch_shapes=scratch,
        input_output_aliases=aliases,
        compiler_params=params(6 + 5 * count),
        cost_estimate=COST,
        name="blend",
    )(*args)


def bits_of(mask):
    return [1 << b for b in range(mask.bit_length()) if mask >> b & 1]


def after(value, *earlier):
    return lax.optimization_barrier((value, earlier))[0]


def body(shards, tensors, hidden_in, policy_weights, reference_weights, policy_queries, reference_queries, readout, lengths):
    rows = policy_weights.shape[1]
    idx = lax.axis_index("shard").astype(jnp.int32).reshape(1)
    tables = jnp.asarray(rope_tables())

    def swap(x, bit, axis="shard", size=shards):
        return lax.ppermute(x, axis, [(i, i ^ bit) for i in range(size)])

    def powers(size):
        return [1 << b for b in range(size.bit_length() - 1)]

    chips = sorted(range(0, shards, 2), key=lambda m: (len(bits_of(m)), m))
    near = [m for m in chips if len(bits_of(m)) == 1]
    far = [m for m in chips if len(bits_of(m)) > 1]
    link = lambda i, m: bits_of(m)[-1] if i == 0 else bits_of(m)[0]

    def send_near(own):
        got = {0: list(own)}
        for turn in (0, 1):
            for n, m in enumerate(near):
                i = (turn + n) % 2
                got.setdefault(m, [None, None])[i] = swap(own[i], m)
        got[1] = [swap(g, 1) for g in own]
        return got

    def send_whole(own):
        got = {m: [swap(own, m)] for m in near}
        got[0] = [own]
        got[1] = [swap(own, 1)]
        return got

    def relay(got, m, *earlier):
        got[m] = [None, None]
        for i in (0, 1):
            via = link(i, m)
            source = got[m ^ via]
            source = source[i] if len(source) == 2 else source[0][i]
            got[m][i] = swap(after(source, *earlier), via)

    def to_core(got, m, *earlier):
        got[m | 1] = [swap(after(g, *earlier), 1) for g in got[m]]

    weights = send_near((policy_weights[0], policy_weights[1]))
    normed, ref_keys, ref_values = norm_project(hidden_in, reference_weights, tables)
    for m in far:
        relay(weights, m, ref_keys)
    (ref_margin,) = attend(lengths, reference_queries, ref_keys, ref_values, readout)
    for m in near:
        to_core(weights, m, ref_margin)
    early = [m | c for m in [0] + near for c in (0, 1)]
    held = project(after(idx, ref_margin), normed, early, weights, None, None if far else tables)
    if far:
        for m in far:
            to_core(weights, m, held)
        held = project(idx, normed, [m | c for m in far for c in (0, 1)], weights, held, tables)
    pol_keys, pol_values = held
    margin, probs, delta = attend(lengths, policy_queries, pol_keys, pol_values, readout, ref_margin)

    theirs = {}
    order = list(reversed(chips))
    split = max(len(far), 1)

    def backward():
        return attend_back(lengths, policy_queries, pol_values, readout, probs, delta, tables)

    def other_blocks():
        done = []
        for masks in (order[:split], order[split:]):
            blocks = gradient_blocks(after(idx, margin), normed, cot, [m | 1 for m in masks], rows)
            theirs.update({m: swap(block, 1) for m, block in zip(masks, blocks)})
            done += blocks
        return done

    cot = None
    for bit in powers(tensors):
        received = swap(margin, bit, "tensor", tensors)
        if cot is None:
            received = after(received, cot := backward())
        elif not theirs:
            received = after(received, other_blocks())
        margin = margin + received
    if cot is None:
        cot = backward()
    if not theirs:
        other_blocks()
    margins = (margin, swap(margin, 1))

    chip_sum = {}
    arrived = {m: [[], []] for m in chips}
    waiting = []

    def send(m, i):
        payload = chip_sum[m][i]
        if arrived[m][i]:
            payload = payload.astype(jnp.float32)
            for term in arrived[m][i]:
                payload = payload + term.astype(jnp.float32)
            payload = payload.astype(jnp.bfloat16)
        via = link(i, m)
        arrived[m ^ via][i].append(swap(payload, via))
        return payload

    last = margins[1]
    for masks in (order[:split], order[split:]):
        blocks = gradient_blocks(after(idx, last), normed, cot, masks, rows, (margins, theirs))
        chip_sum.update(zip(masks, blocks))
        last = blocks
        for m in masks:
            for i in (0, 1):
                if m and not any(k ^ link(i, k) == m for k in far):
                    send(m, i)
                elif m:
                    waiting.append((m, i))
    for m, i in waiting:
        arrived[m][i] = [after(term, last) for term in arrived[m][i]]
        send(m, i)
    own, squares = finish(chip_sum[0], arrived[0])

    grads = send_whole(own)
    for bit in powers(tensors):
        squares = squares + swap(squares, bit, "tensor", tensors)
    for bit in powers(shards):
        squares = squares + swap(squares, bit)
    for m in far:
        relay(grads, m, squares)
    for m in near:
        to_core(grads, m)
    new_reference, token, new_policy = blend(idx, squares, weights, grads, reference_weights, None, early)
    if far:
        ready = fetch(after(idx, token), weights, reference_weights, [m | c for c in (0, 1) for m in far])
        for m in far:
            to_core(grads, m, ready)
        for c in (0, 1):
            masks = [m | c for m in far]
            new_reference, token = blend(idx, squares, weights, grads, reference_weights, new_reference, masks, (ready, c * len(far)))
    return (new_policy, new_reference, margin[0, :1])


def solution(mesh):
    return jax.shard_map(
        functools.partial(body, mesh.shape["shard"], mesh.shape["tensor"]),
        mesh=mesh,
        in_specs=(
            P("shard", None),
            P(None, "shard", "tensor"),
            P(None, None, "tensor"),
            P("shard", "tensor"),
            P("shard", "tensor"),
            P("shard", "tensor"),
            P("shard"),
        ),
        out_specs=(P(None, "shard", "tensor"), P(None, None, "tensor"), P("shard")),
        check_vma=False,
    )
```

```python
import functools
import math

import jax
import jax.numpy as jnp
import numpy as np
from jax import lax
from jax.experimental import pallas as pl
from jax.experimental.pallas import tpu as pltpu
from jax.sharding import PartitionSpec as P

D = 8192
HD = 128
KVH = 8
QH = 32
LEN = 384
TILE = 128

rope_base = 1000000.0
dpo_beta = 0.1
learning_rate = 0.2
mix_alpha = 0.6
norm_eps = 1e-06
width_scale = D ** (-0.5)
logit_scale = 1.0 / math.sqrt(HD)
MIB = 1024 * 1024

NT = (((1,), (1,)), ((), ()))
NN = (((1,), (0,)), ((), ()))
TN = (((0,), (0,)), ((), ()))


def dot(a, b, dims):
    return lax.dot_general(a, b, dims, preferred_element_type=jnp.float32)


def params(mib):
    return pltpu.CompilerParams(vmem_limit_bytes=mib * MIB)


COST = pl.CostEstimate(flops=1, bytes_accessed=1, transcendentals=0)
LONG = pl.CostEstimate(flops=1, bytes_accessed=40 * 1000 * 1000, transcendentals=0)
VMEM = pl.BlockSpec(memory_space=pltpu.VMEM)
SMEM = pl.BlockSpec(memory_space=pltpu.SMEM)
HBM = pl.BlockSpec(memory_space=pl.ANY)


def resident(x):
    return pltpu.with_memory_space_constraint(x, pltpu.VMEM)


def in_hbm(x):
    return pltpu.with_memory_space_constraint(x, pltpu.HBM)


def rope_tables():
    frequency = rope_base ** (-2.0 * np.arange(HD // 2) / HD)
    angles = np.arange(LEN)[:, None] * frequency[None, :]
    cosine, sine = np.cos(angles), np.sin(angles)
    return np.stack([np.concatenate([cosine, cosine], axis=1), np.concatenate([-sine, sine], axis=1)]).astype(np.float32)


def store_heads(acc_ref, cos, sin, key_ref, value_ref):
    for s in range(key_ref.shape[0] // LEN):
        rows = slice(s * LEN, (s + 1) * LEN)
        for h in range(key_ref.shape[1] // HD):
            cols = slice(h * HD, (h + 1) * HD)
            k = acc_ref[0, rows, cols] * width_scale
            key_ref[rows, cols] = (k * cos + pltpu.roll(k, HD // 2, 1) * sin).astype(jnp.bfloat16)
    value_ref[...] = (acc_ref[1] * width_scale).astype(jnp.bfloat16)


def norm_project_kernel(hidden_hbm, weight_hbm, table_hbm, normed_ref, key_ref, value_ref, w, acc, part, table, in_sem, w_sem, table_sem):
    tokens = normed_ref.shape[0]
    step, width, span, chunk = 16, 512, 128, 1024
    reads = []
    for i in range(tokens // span):
        at = pl.ds(i * span, span)
        reads.append(pltpu.make_async_copy(hidden_hbm.at[at], normed_ref.at[at], in_sem.at[i]))
    loads = []
    for c in range(D // chunk):
        at = pl.ds(c * chunk, chunk)
        loads.append(pltpu.make_async_copy(weight_hbm.at[:, at, :], w.at[:, at, :], w_sem.at[c]))
    loads.append(pltpu.make_async_copy(table_hbm, table, table_sem))
    for copy in reads + loads:
        copy.start()

    def row_step(i, carry):
        at = pl.ds(pl.multiple_of(i * step, step), step)
        total = jnp.zeros((step, width), jnp.float32)
        for c in range(D // width):
            v = normed_ref[at, c * width : (c + 1) * width].astype(jnp.float32)
            total = total + v * v
        part[at, :] = functools.reduce(jnp.add, [total[:, c * 128 : (c + 1) * 128] for c in range(width // 128)])
        return carry

    for i, copy in enumerate(reads):
        copy.wait()
        lax.fori_loop(i * (span // step), (i + 1) * (span // step), row_step, 0)
    for copy in loads:
        copy.wait()
    mean = jnp.sum(part[...], axis=1, keepdims=True) * (1.0 / D)
    part[...] = jnp.broadcast_to(lax.rsqrt(mean + norm_eps), part.shape)

    def normalise(c):
        at = slice(c * chunk, (c + 1) * chunk)
        for i in range(tokens // step):
            rows = slice(i * step, (i + 1) * step)
            scale = jnp.concatenate([part[rows, :]] * (chunk // 128), axis=1)
            normed_ref[rows, at] = (normed_ref[rows, at].astype(jnp.float32) * scale).astype(jnp.bfloat16)

    normalise(0)
    for c in range(D // chunk):
        at = slice(c * chunk, (c + 1) * chunk)
        for i in (0, 1):
            term = dot(normed_ref[:, at], w[i, at, :], NN)
            acc[i] = term if c == 0 else acc[i] + term
        if (c + 1) * chunk < D:
            normalise(c + 1)
    store_heads(acc, table[0], table[1], key_ref, value_ref)


def norm_project(hidden, weights, tables):
    tokens = hidden.shape[0]
    cols = weights.shape[2]
    return pl.pallas_call(
        norm_project_kernel,
        in_specs=[HBM, HBM, HBM],
        out_specs=[VMEM, VMEM, VMEM],
        out_shape=[
            pltpu.VMEM((tokens, D), jnp.bfloat16),
            pltpu.VMEM((tokens, cols), jnp.bfloat16),
            pltpu.VMEM((tokens, cols), jnp.bfloat16),
        ],
        scratch_shapes=[
            pltpu.VMEM((2, D, cols), jnp.bfloat16),
            pltpu.VMEM((2, tokens, cols), jnp.float32),
            pltpu.VMEM((tokens, 128), jnp.float32),
            pltpu.VMEM(tables.shape, jnp.float32),
            pltpu.SemaphoreType.DMA((tokens // 128,)),
            pltpu.SemaphoreType.DMA((D // 1024,)),
            pltpu.SemaphoreType.DMA,
        ],
        compiler_params=params(16),
        cost_estimate=COST,
        name="norm_project",
    )(in_hbm(hidden), in_hbm(weights), in_hbm(tables))


def project_kernel(masks, first, last, idx_ref, x_ref, *refs):
    refs = list(refs)
    count = len(masks)
    pieces = [refs[:count], refs[count : 2 * count]]
    refs = refs[2 * count :]
    held = None if first else refs.pop(0)
    if last:
        table_hbm, key_ref, value_ref, w, acc, table, sem, table_sem = refs
        table_copy = pltpu.make_async_copy(table_hbm, table, table_sem)
        table_copy.start()
    else:
        acc, w, sem = refs
    depth = w.shape[2]
    copies = [[pltpu.make_async_copy(pieces[i][n], w.at[i, n], sem.at[i, n]) for i in (0, 1)] for n in range(count)]
    for pair in copies:
        for copy in pair:
            copy.start()
    for n in range(count):
        for copy in copies[n]:
            copy.wait()
        col = pl.multiple_of((idx_ref[0] ^ masks[n]) * depth, depth)
        x = x_ref[:, pl.ds(col, depth)]
        for i in (0, 1):
            term = dot(x, w[i, n], NN)
            if n:
                term = acc[i] + term
            elif not first:
                term = held[i] + term
            acc[i] = term
    if last:
        table_copy.wait()
        store_heads(acc, table[0], table[1], key_ref, value_ref)


def project(idx, normed, masks, pieces, held, tables):
    tokens = normed.shape[0]
    rows, cols = pieces[masks[0]][0].shape
    first, last = held is None, tables is not None
    count = len(masks)
    in_specs = [SMEM, VMEM] + [HBM] * (2 * count)
    args = [idx, resident(normed)]
    args += [pieces[m][i] for i in (0, 1) for m in masks]
    if not first:
        in_specs.append(VMEM)
        args.append(resident(held))
    acc_shape = (2, tokens, cols)
    scratch = [pltpu.VMEM((2, count, rows, cols), jnp.bfloat16), pltpu.SemaphoreType.DMA((2, count))]
    if last:
        in_specs.append(HBM)
        args.append(in_hbm(tables))
        out_specs = [VMEM] * 2
        out_shape = [pltpu.VMEM((tokens, cols), jnp.bfloat16)] * 2
        scratch.insert(1, pltpu.VMEM(acc_shape, jnp.float32))
        scratch.insert(2, pltpu.VMEM(tables.shape, jnp.float32))
        scratch.append(pltpu.SemaphoreType.DMA)
    else:
        out_specs = VMEM
        out_shape = pltpu.VMEM(acc_shape, jnp.float32)
    return pl.pallas_call(
        functools.partial(project_kernel, tuple(masks), first, last),
        in_specs=in_specs,
        out_specs=out_specs,
        out_shape=out_shape,
        scratch_shapes=scratch,
        compiler_params=params(10),
        cost_estimate=COST,
        name="project",
    )(*args)


HEADS = 2


def parts(q_ref, k_ref):
    heads = k_ref.shape[1] // HD
    groups = q_ref.shape[1] // k_ref.shape[1]
    for seq in range(k_ref.shape[0] // LEN):
        for h in range(heads):
            yield seq, seq * LEN, h, h * groups, groups


def stacked(ref, row, r, first, count):
    rows = slice(row + r * TILE, row + (r + 1) * TILE)
    return jnp.concatenate([ref[rows, g * HD : (g + 1) * HD] for g in range(first, first + count)], axis=0)


def live_readout(ref, row, r, first, count, length):
    x = stacked(ref, row, r, first, count).astype(jnp.float32)
    at = lax.broadcasted_iota(jnp.int32, x.shape, 0) % TILE + r * TILE
    return jnp.where(at < length, x, 0.0).astype(jnp.bfloat16)


def attend_kernel(keep, len_ref, q_ref, k_ref, v_ref, ro_ref, *rest):
    if keep:
        before_ref, margin_ref, prob_ref, delta_ref = rest
        margin = -before_ref[0:1, 0:1]
    else:
        (margin_ref,) = rest
        margin = jnp.zeros((1, 1), jnp.float32)
    for seq, row, h, first, groups in parts(q_ref, k_ref):
        count = min(groups, HEADS)
        length = len_ref[seq]
        col = slice(h * HD, (h + 1) * HD)
        score = jnp.zeros((1, count * TILE), jnp.float32)
        j = lax.broadcasted_iota(jnp.int32, (TILE, count * TILE), 0)
        i = lax.broadcasted_iota(jnp.int32, (TILE, count * TILE), 1) % TILE
        base = 0
        for r in range(LEN // TILE):
            n = (r + 1) * TILE
            for g in range(0, groups, count):
                q = stacked(q_ref, row, r, first + g, count)
                ro = live_readout(ro_ref, row, r, first + g, count, length)
                s = dot(k_ref[row : row + n, col], q, NT)
                dp = dot(v_ref[row : row + n, col], ro, NT)
                s = [s[b * TILE : (b + 1) * TILE] for b in range(r + 1)]
                s[r] = jnp.where(j <= i, s[r], -1e30)
                top = functools.reduce(jnp.maximum, [jnp.max(x, axis=0, keepdims=True) for x in s])
                e = [jnp.exp2((x - top) * (logit_scale * math.log2(math.e))) for x in s]
                inverse = 1.0 / functools.reduce(jnp.add, [jnp.sum(x, axis=0, keepdims=True) for x in e])
                cols = slice(g * TILE, (g + count) * TILE)
                delta = jnp.zeros((1, count * TILE), jnp.float32)
                for b in range(r + 1):
                    p = (e[b] * inverse).astype(jnp.bfloat16)
                    if keep:
                        prob_ref[seq, h, base + b * TILE : base + (b + 1) * TILE, cols] = p
                    delta = delta + jnp.sum(p.astype(jnp.float32) * dp[b * TILE : (b + 1) * TILE], axis=0, keepdims=True)
                if keep:
                    delta_ref[seq, h, r : r + 1, cols] = delta
                score = score + delta
            base += n
        side = (1.0 if seq % 2 == 0 else -1.0) * (dpo_beta / math.sqrt(QH * HD))
        margin = margin + jnp.sum(score, axis=1, keepdims=True) * side
    margin_ref[...] = jnp.broadcast_to(margin, margin_ref.shape)


def attend(lengths, queries, keys, values, readout, before=None):
    seqs = lengths.shape[0]
    heads = keys.shape[1] // HD
    wide = queries.shape[1] // heads
    tiles = LEN // TILE
    span = TILE * tiles * (tiles + 1) // 2
    keep = before is not None
    args = [lengths] + [resident(x) for x in (queries, keys, values, readout)]
    out_shape = [jax.ShapeDtypeStruct((8, 128), jnp.float32)]
    if keep:
        args.append(before)
        out_shape += [pltpu.VMEM((seqs, heads, span, wide), jnp.bfloat16), pltpu.VMEM((seqs, heads, tiles, wide), jnp.float32)]
    return pl.pallas_call(
        functools.partial(attend_kernel, keep),
        in_specs=[SMEM] + [VMEM] * (len(args) - 1),
        out_specs=[VMEM] * len(out_shape),
        out_shape=out_shape,
        compiler_params=params(8),
        cost_estimate=COST,
        name="attend",
    )(*args)


def attend_back_kernel(len_ref, q_ref, v_ref, ro_ref, prob_ref, delta_ref, table_ref, grad_ref):
    tiles = LEN // TILE
    for seq, row, h, first, groups in parts(q_ref, v_ref):
        count = min(groups, HEADS)
        length = len_ref[seq]
        col = slice(h * HD, (h + 1) * HD)
        dk = [None] * tiles
        dv = [None] * tiles
        base = 0
        for r in range(tiles):
            n = (r + 1) * TILE
            for g in range(0, groups, count):
                q = stacked(q_ref, row, r, first + g, count)
                ro = live_readout(ro_ref, row, r, first + g, count, length)
                cols = slice(g * TILE, (g + count) * TILE)
                p = prob_ref[seq, h, base : base + n, cols]
                dp = dot(v_ref[row : row + n, col], ro, NT)
                ds = (p.astype(jnp.float32) * (dp - delta_ref[seq, h, r : r + 1, cols])).astype(jnp.bfloat16)
                tk = dot(ds, q, NN)
                tv = dot(p, ro, NN)
                for b in range(r + 1):
                    at = slice(b * TILE, (b + 1) * TILE)
                    dk[b] = tk[at] if dk[b] is None else dk[b] + tk[at]
                    dv[b] = tv[at] if dv[b] is None else dv[b] + tv[at]
            base += n
        scale = (-1.0 if seq % 2 == 0 else 1.0) * (1.0 / math.sqrt(QH * HD))
        for b in range(tiles):
            at = slice(b * TILE, (b + 1) * TILE)
            to = slice(row + b * TILE, row + (b + 1) * TILE)
            k = dk[b] * (scale * logit_scale)
            k = k * table_ref[0, at, :] - pltpu.roll(k, HD // 2, 1) * table_ref[1, at, :]
            grad_ref[0, col, to] = k.T.astype(jnp.bfloat16)
            grad_ref[1, col, to] = (dv[b] * scale).T.astype(jnp.bfloat16)


def attend_back(lengths, queries, values, readout, probs, delta, tables):
    return pl.pallas_call(
        attend_back_kernel,
        in_specs=[SMEM] + [VMEM] * 6,
        out_specs=VMEM,
        out_shape=pltpu.VMEM((2,) + values.shape[::-1], jnp.bfloat16),
        compiler_params=params(8),
        cost_estimate=COST,
        name="attend_back",
    )(lengths, *[resident(x) for x in (queries, values, readout, probs, delta, tables)])


def gradient_tiles(idx, mask, x_ref, cot_ref, rows):
    cols = cot_ref.shape[1]
    both = jnp.concatenate([cot_ref[0], cot_ref[1]], axis=0)
    tile = min(rows, 256)
    for t in range(rows // tile):
        col = pl.multiple_of((idx ^ mask) * rows + t * tile, tile)
        out = dot(both, x_ref[:, pl.ds(col, tile)], NN)
        for i in (0, 1):
            yield i, slice(t * tile, (t + 1) * tile), out[i * cols : (i + 1) * cols]


def gradient_kernel(masks, idx_ref, x_ref, cot_ref, *outs):
    outs = outs[len(outs) - len(masks) :]
    for mask, out_ref in zip(masks, outs):
        for i, at, value in gradient_tiles(idx_ref[0], mask, x_ref, cot_ref, out_ref.shape[2]):
            out_ref[i, :, at] = value.astype(out_ref.dtype)


def merged_kernel(masks, idx_ref, x_ref, cot_ref, mine_margin, their_margin, *refs):
    count = len(masks)
    theirs_hbm, outs = refs[:count], refs[count : 3 * count]
    theirs, sem = refs[3 * count :]
    copies = [pltpu.make_async_copy(theirs_hbm[n], theirs.at[n], sem.at[n]) for n in range(count)]
    for copy in copies:
        copy.start()
    weight = lambda ref: jnp.concatenate([jax.nn.sigmoid(-ref[0:1, :])] * 2, axis=1)
    mine, their = weight(mine_margin), weight(their_margin)
    for n, mask in enumerate(masks):
        copies[n].wait()
        for i, at, value in gradient_tiles(idx_ref[0], mask, x_ref, cot_ref, theirs.shape[3]):
            value = value * mine + theirs[n, i, :, at].astype(jnp.float32) * their
            outs[2 * n + i][:, at] = value.astype(outs[2 * n + i].dtype)


def gradient_blocks(idx, normed, cot, masks, rows, merge=None, earlier=()):
    _, cols, tokens = cot.shape
    args = [idx, resident(normed), resident(cot)]
    in_specs = [SMEM, VMEM, VMEM]
    scratch = []
    if merge is None:
        kernel, name = gradient_kernel, "gradient_block"
        out_shape = [jax.ShapeDtypeStruct((2, cols, rows), jnp.bfloat16) for m in masks]
        args += earlier
        in_specs += [HBM] * len(earlier)
    else:
        kernel, name = merged_kernel, "merged_block"
        margins, theirs = merge
        args += [*margins] + [theirs[m] for m in masks]
        in_specs += [VMEM, VMEM] + [HBM] * len(masks)
        out_shape = [
            jax.ShapeDtypeStruct((cols, rows), jnp.bfloat16) if m else pltpu.VMEM((cols, rows), jnp.float32)
            for m in masks
            for i in (0, 1)
        ]
        scratch = [pltpu.VMEM((len(masks), 2, cols, rows), jnp.bfloat16), pltpu.SemaphoreType.DMA((len(masks),))]
    outs = pl.pallas_call(
        functools.partial(kernel, tuple(masks)),
        in_specs=in_specs,
        out_specs=[VMEM] * len(out_shape),
        out_shape=out_shape,
        scratch_shapes=scratch,
        compiler_params=params(10),
        cost_estimate=COST,
        name=name,
    )(*args)
    return outs if merge is None else [outs[2 * n : 2 * n + 2] for n in range(len(masks))]


def finish_kernel(counts, *refs):
    refs = list(refs)
    out_ref, square_ref = refs[-2:]
    refs = refs[:-2]
    square_ref[...] = jnp.zeros_like(square_ref)
    cols, rows = refs[0].shape
    for i in (0, 1):
        terms = [refs.pop(0) for _ in range(1 + counts[i])]
        squares = jnp.zeros((1, 128), jnp.float32)
        for c in range(cols // 128):
            for r in range(rows // 128):
                at = (slice(c * 128, (c + 1) * 128), slice(r * 128, (r + 1) * 128))
                value = functools.reduce(jnp.add, [t[at].astype(jnp.float32) for t in terms])
                squares = squares + jnp.sum(value * value, axis=0, keepdims=True)
                out_ref[i, at[1], at[0]] = value.T.astype(jnp.bfloat16)
        square_ref[i : i + 1, :] = jnp.broadcast_to(jnp.sum(squares, axis=1, keepdims=True), (1, 128))


def finish(base, arrived):
    args = [x for i in (0, 1) for x in (resident(base[i]), *arrived[i])]
    cols, rows = base[0].shape
    return pl.pallas_call(
        functools.partial(finish_kernel, [len(a) for a in arrived]),
        in_specs=[VMEM] * len(args),
        out_specs=[VMEM] * 2,
        out_shape=[jax.ShapeDtypeStruct((2, rows, cols), jnp.bfloat16), jax.ShapeDtypeStruct((8, 128), jnp.float32)],
        compiler_params=params(8),
        cost_estimate=COST,
        name="finish",
    )(*args)


def spread_kernel(*refs):
    terms, out_ref = refs[:-3], refs[-2]
    out_ref[...] = functools.reduce(jnp.add, [t[...] for t in terms])


def spread(terms, own):
    return pl.pallas_call(
        spread_kernel,
        in_specs=[VMEM] * len(terms) + [HBM],
        out_specs=[VMEM, HBM],
        out_shape=[jax.ShapeDtypeStruct((8, 128), jnp.float32), jax.ShapeDtypeStruct(own.shape, own.dtype)],
        input_output_aliases={len(terms): 1},
        compiler_params=params(4),
        cost_estimate=COST,
        name="spread",
    )(*terms, own)


def fetch_kernel(masks, idx_ref, *refs):
    count = len(masks)
    pieces, (ref_hbm, _, w, r, sem) = refs[: 2 * count], refs[2 * count :]
    rows = r.shape[2]
    copies = []
    for n, mask in enumerate(masks):
        at = pl.ds(pl.multiple_of((idx_ref[0] ^ mask) * rows, rows), rows)
        copies += [pltpu.make_async_copy(pieces[2 * n + i], w.at[n, i], sem.at[i, n]) for i in (0, 1)]
        copies.append(pltpu.make_async_copy(ref_hbm.at[:, at, :], r.at[n], sem.at[2, n]))
    for copy in copies:
        copy.start()
    for copy in copies:
        copy.wait()


def fetch(idx, weights, reference, masks, earlier):
    rows, cols = weights[masks[0]][0].shape
    count = len(masks)
    return pl.pallas_call(
        functools.partial(fetch_kernel, tuple(masks)),
        in_specs=[SMEM] + [HBM] * (2 * count + 2),
        out_specs=[VMEM] * 2,
        out_shape=[pltpu.VMEM((count, 2, rows, cols), jnp.bfloat16)] * 2,
        scratch_shapes=[pltpu.SemaphoreType.DMA((3, count))],
        compiler_params=params(4),
        cost_estimate=COST,
        name="fetch",
    )(idx, *[w for m in masks for w in weights[m]], in_hbm(reference), earlier)


def blend_kernel(masks, first, ready, idx_ref, square_ref, *refs):
    refs = list(refs)
    count = len(masks)
    grads = [[refs.pop(0)] if whole else [refs.pop(0), refs.pop(0)] for whole in first_parts(masks, ready)]
    if ready is None:
        weights = [[refs.pop(0), refs.pop(0)] for m in masks]
        ref_hbm = refs.pop(0)
    else:
        w, r = refs.pop(0), refs.pop(0)
    if not first:
        refs.pop(0)
    out_hbm, token_ref = refs.pop(0), refs.pop(0)
    new_hbm = refs.pop(0) if first else None
    if ready is None:
        w, r = refs.pop(0), refs.pop(0)
    g, o, new, sem, out_sem = refs
    rows, cols = g.shape[2:]
    step = 32
    half = rows // 2
    token_ref[...] = jnp.zeros_like(token_ref)

    def reads(n):
        slot = n % 2
        at = pl.ds(pl.multiple_of((idx_ref[0] ^ masks[n]) * rows, rows), rows)
        if len(grads[n]) == 1:
            group = [pltpu.make_async_copy(grads[n][0], g.at[slot], sem.at[0, slot])]
        else:
            group = [pltpu.make_async_copy(grads[n][i], g.at[slot, i], sem.at[i, slot]) for i in (0, 1)]
        if ready is None:
            group += [pltpu.make_async_copy(weights[n][i], w.at[slot, i], sem.at[2 + i, slot]) for i in (0, 1)]
            group.append(pltpu.make_async_copy(ref_hbm.at[:, at, :], r.at[slot], sem.at[4, slot]))
        for copy in group:
            copy.start()
        return group

    mean = square_ref[...] * (1.0 / (D * KVH * HD))
    scale = jnp.concatenate([learning_rate * lax.rsqrt(mean + norm_eps)] * (cols // 128), axis=1)
    coming = {n: reads(n) for n in range(min(2, count))}
    writes = {}
    for n in range(count):
        slot = n % 2
        held = slot if ready is None else ready + n
        for copy in coming[n] + writes.pop(n - 2, []):
            copy.wait()
        writes[n] = []
        for part in range(2):
            for i in (0, 1):
                for start in range(part * half, (part + 1) * half, step):
                    j = slice(start, start + step)
                    value = w[held, i, j].astype(jnp.float32) - scale[i : i + 1, :] * g[slot, i, j].astype(jnp.float32)
                    value = value.astype(jnp.bfloat16)
                    if first and n == 0:
                        new[i, j] = value
                    mixed = mix_alpha * value.astype(jnp.float32) + (1.0 - mix_alpha) * r[held, i, j].astype(jnp.float32)
                    o[slot, i, j] = mixed.astype(jnp.bfloat16)
            at = pl.ds(pl.multiple_of((idx_ref[0] ^ masks[n]) * rows + part * half, half), half)
            copy = pltpu.make_async_copy(o.at[slot, :, pl.ds(part * half, half), :], out_hbm.at[:, at, :], out_sem.at[part, slot])
            copy.start()
            writes[n].append(copy)
        if first and n == 0:
            copy = pltpu.make_async_copy(new, new_hbm, out_sem.at[0, 2])
            copy.start()
            writes[n].append(copy)
        if n + 2 < count:
            coming[n + 2] = reads(n + 2)
    for group in writes.values():
        for copy in group:
            copy.wait()


def first_parts(masks, ready):
    return [len(bits_of(m >> 1)) < 2 for m in masks]


def blend(idx, squares, weights, grads, reference, held, masks, ready=None):
    rows, cols = weights[masks[0]][0].shape
    count = len(masks)
    first = held is None
    args = [idx, squares] + [x for m in masks for x in grads[m]]
    in_specs = [SMEM, VMEM] + [HBM] * (len(args) - 2)
    block = pltpu.VMEM((min(count, 2), 2, rows, cols), jnp.bfloat16)
    scratch = [block, block, pltpu.VMEM((2, rows, cols) if first else (8, 128), jnp.bfloat16)]
    scratch += [pltpu.SemaphoreType.DMA((5, 2)), pltpu.SemaphoreType.DMA((2, 3))]
    if ready is None:
        args += [w for m in masks for w in weights[m]] + [in_hbm(reference)]
        in_specs += [HBM] * (2 * count + 1)
        scratch = [block, block] + scratch
    else:
        args += [resident(x) for x in ready[0]]
        in_specs += [VMEM] * 2
    out_specs = [HBM, VMEM]
    out_shape = [jax.ShapeDtypeStruct(reference.shape, jnp.bfloat16), jax.ShapeDtypeStruct((8, 128), jnp.float32)]
    aliases = {}
    if first:
        out_specs.append(HBM)
        out_shape.append(jax.ShapeDtypeStruct((2, rows, cols), jnp.bfloat16))
    else:
        aliases = {len(args): 0}
        in_specs.append(HBM)
        args.append(held)
    return pl.pallas_call(
        functools.partial(blend_kernel, tuple(masks), first, None if ready is None else ready[1]),
        in_specs=in_specs,
        out_specs=out_specs,
        out_shape=out_shape,
        scratch_shapes=scratch,
        input_output_aliases=aliases,
        compiler_params=params(14),
        cost_estimate=COST if first else LONG,
        name="blend",
    )(*args)


def bits_of(mask):
    return [1 << b for b in range(mask.bit_length()) if mask >> b & 1]


def after(value, *earlier):
    return lax.optimization_barrier((value, earlier))[0]


def body(shards, tensors, hidden_in, policy_weights, reference_weights, policy_queries, reference_queries, readout, lengths):
    rows = policy_weights.shape[1]
    idx = lax.axis_index("shard").astype(jnp.int32).reshape(1)
    tables = jnp.asarray(rope_tables())

    def swap(x, bit, axis="shard", size=shards):
        return lax.ppermute(x, axis, [(i, i ^ bit) for i in range(size)])

    def powers(size):
        return [1 << b for b in range(size.bit_length() - 1)]

    chips = sorted(range(0, shards, 2), key=lambda m: (len(bits_of(m)), m))
    near = [m for m in chips if len(bits_of(m)) == 1]
    far = [m for m in chips if len(bits_of(m)) > 1]
    link = lambda i, m: bits_of(m)[-1] if i == 0 else bits_of(m)[0]

    def send_near(own):
        got = {0: list(own)}
        for turn in (0, 1):
            for n, m in enumerate(near):
                i = (turn + n) % 2
                got.setdefault(m, [None, None])[i] = swap(own[i], m)
        got[1] = [swap(g, 1) for g in own]
        return got

    def send_whole(own):
        got = {m: [swap(own, m)] for m in near}
        got[0] = [own]
        got[1] = [swap(own, 1)]
        return got

    def relay(got, m, *earlier):
        got[m] = [None, None]
        for i in (0, 1):
            via = link(i, m)
            source = got[m ^ via]
            source = source[i] if len(source) == 2 else source[0][i]
            got[m][i] = swap(after(source, *earlier), via)

    def to_core(got, m, *earlier):
        got[m | 1] = [swap(after(g, *earlier), 1) for g in got[m]]

    weights = send_near((policy_weights[0], policy_weights[1]))
    normed, ref_keys, ref_values = norm_project(hidden_in, reference_weights, tables)
    (ref_margin,) = attend(lengths, reference_queries, ref_keys, ref_values, readout)
    for m in far:
        relay(weights, m, ref_margin, *[weights[k] for k in near])
    for m in near:
        to_core(weights, m, ref_margin)
    held = project(idx, normed, [0, 1], weights, None, None)
    for m in far:
        to_core(weights, m, held)
    held = project(idx, normed, [m | c for m in near + far for c in (0, 1)], weights, held, tables)
    pol_keys, pol_values = held
    margin, probs, delta = attend(lengths, policy_queries, pol_keys, pol_values, readout, ref_margin)

    theirs = {}
    order = list(reversed(chips))
    split = max(len(far), 1)

    def other_blocks(masks, *earlier):
        blocks = gradient_blocks(idx, normed, cot, [m | 1 for m in masks], rows, None, earlier)
        theirs.update({m: swap(block, 1) for m, block in zip(masks, blocks)})
        return blocks

    cot = attend_back(lengths, policy_queries, pol_values, readout, probs, delta, tables)
    beside = [lambda: cot, lambda: other_blocks(order[:split], margin)]
    for bit in powers(tensors):
        received = swap(margin, bit, "tensor", tensors)
        margin = margin + (after(received, beside.pop(0)()) if beside else received)
    for work in beside:
        work()
    received = swap(margin, 1)
    margins = (margin, after(received, other_blocks(order[split:], margin)))

    chip_sum = {}
    arrived = {m: [[], []] for m in chips}
    waiting = []

    def send(m, i):
        payload = chip_sum[m][i]
        if arrived[m][i]:
            payload = payload.astype(jnp.float32)
            for term in arrived[m][i]:
                payload = payload + term.astype(jnp.float32)
            payload = payload.astype(jnp.bfloat16)
        via = link(i, m)
        arrived[m ^ via][i].append(swap(payload, via))
        return payload

    for masks in (order[:split], order[split:]):
        blocks = gradient_blocks(idx, normed, cot, masks, rows, (margins, theirs))
        chip_sum.update(zip(masks, blocks))
        for m in masks:
            for i in (0, 1):
                if m and not any(k ^ link(i, k) == m for k in far):
                    send(m, i)
                elif m:
                    waiting.append((m, i))
    for m, i in waiting:
        send(m, i)
    own, squares = finish(chip_sum[0], arrived[0])

    terms = [squares] + [swap(squares, m) for m in chips[1:]]
    while len(terms) > 4:
        terms = [a + b for a, b in zip(terms[::2], terms[1::2])]
    squares, own = spread(terms, own)
    grads = send_whole(own)
    squares = squares + swap(squares, 1)
    for bit in powers(tensors):
        squares = squares + swap(squares, bit, "tensor", tensors)
    new_reference, token, new_policy = blend(idx, squares, weights, grads, reference_weights, None, [0, 1])
    for m in far:
        relay(grads, m, token)
    for m in near:
        to_core(grads, m, token)
    new_reference, token = blend(idx, squares, weights, grads, reference_weights, new_reference, [m | c for m in near for c in (0, 1)])
    if far:
        ready = fetch(idx, weights, reference_weights, [m | c for c in (0, 1) for m in far], token)
        for m in far:
            to_core(grads, m)
        for c in (0, 1):
            masks = [m | c for m in far]
            new_reference, token = blend(idx, squares, weights, grads, reference_weights, new_reference, masks, (ready, c * len(far)))
    return (new_policy, new_reference, margin[0, :1])


def solution(mesh):
    return jax.shard_map(
        functools.partial(body, mesh.shape["shard"], mesh.shape["tensor"]),
        mesh=mesh,
        in_specs=(
            P("shard", None),
            P(None, "shard", "tensor"),
            P(None, None, "tensor"),
            P("shard", "tensor"),
            P("shard", "tensor"),
            P("shard", "tensor"),
            P("shard"),
        ),
        out_specs=(P(None, "shard", "tensor"), P(None, None, "tensor"), P("shard")),
        check_vma=False,
    )
```

```python
import functools
import math

import jax
import jax.numpy as jnp
import numpy as np
from jax import lax
from jax.experimental import pallas as pl
from jax.experimental.pallas import tpu as pltpu
from jax.sharding import PartitionSpec as P

D = 8192
HD = 128
KVH = 8
QH = 32
LEN = 384
TILE = 128

rope_base = 1000000.0
dpo_beta = 0.1
learning_rate = 0.2
mix_alpha = 0.6
norm_eps = 1e-06
width_scale = D ** (-0.5)
logit_scale = 1.0 / math.sqrt(HD)
MIB = 1024 * 1024

NT = (((1,), (1,)), ((), ()))
NN = (((1,), (0,)), ((), ()))
TN = (((0,), (0,)), ((), ()))


def dot(a, b, dims):
    return lax.dot_general(a, b, dims, preferred_element_type=jnp.float32)


def params(mib):
    return pltpu.CompilerParams(vmem_limit_bytes=mib * MIB)


COST = pl.CostEstimate(flops=1, bytes_accessed=1, transcendentals=0)
LONG = pl.CostEstimate(flops=1, bytes_accessed=40 * 1000 * 1000, transcendentals=0)
VMEM = pl.BlockSpec(memory_space=pltpu.VMEM)
SMEM = pl.BlockSpec(memory_space=pltpu.SMEM)
HBM = pl.BlockSpec(memory_space=pl.ANY)


def resident(x):
    return pltpu.with_memory_space_constraint(x, pltpu.VMEM)


def in_hbm(x):
    return pltpu.with_memory_space_constraint(x, pltpu.HBM)


def rope_tables():
    frequency = rope_base ** (-2.0 * np.arange(HD // 2) / HD)
    angles = np.arange(LEN)[:, None] * frequency[None, :]
    cosine, sine = np.cos(angles), np.sin(angles)
    return np.stack([np.concatenate([cosine, cosine], axis=1), np.concatenate([-sine, sine], axis=1)]).astype(np.float32)


def store_heads(acc_ref, cos, sin, key_ref, value_ref):
    for s in range(key_ref.shape[0] // LEN):
        rows = slice(s * LEN, (s + 1) * LEN)
        for h in range(key_ref.shape[1] // HD):
            cols = slice(h * HD, (h + 1) * HD)
            k = acc_ref[0, rows, cols] * width_scale
            key_ref[rows, cols] = (k * cos + pltpu.roll(k, HD // 2, 1) * sin).astype(jnp.bfloat16)
    value_ref[...] = (acc_ref[1] * width_scale).astype(jnp.bfloat16)


def norm_project_kernel(idx_ref, hidden_hbm, weight_hbm, table_hbm, normed_ref, key_ref, value_ref, w, acc, part, table, in_sem, w_sem, table_sem):
    tokens = normed_ref.shape[0]
    step, width, span, chunk = 16, 512, 128, 1024
    reads = []
    for i in range(tokens // span):
        at = pl.ds(i * span, span)
        reads.append(pltpu.make_async_copy(hidden_hbm.at[at], normed_ref.at[at], in_sem.at[i]))
    loads = []
    for c in range(D // chunk):
        at = pl.ds(c * chunk, chunk)
        loads.append(pltpu.make_async_copy(weight_hbm.at[:, at, :], w.at[:, at, :], w_sem.at[c]))
    loads.append(pltpu.make_async_copy(table_hbm, table, table_sem))
    for copy in reads + loads:
        copy.start()

    def row_step(i, carry):
        at = pl.ds(pl.multiple_of(i * step, step), step)
        total = jnp.zeros((step, width), jnp.float32)
        for c in range(D // width):
            v = normed_ref[at, c * width : (c + 1) * width].astype(jnp.float32)
            total = total + v * v
        part[at, :] = functools.reduce(jnp.add, [total[:, c * 128 : (c + 1) * 128] for c in range(width // 128)])
        return carry

    for i, copy in enumerate(reads):
        copy.wait()
        lax.fori_loop(i * (span // step), (i + 1) * (span // step), row_step, 0)
    for copy in loads:
        copy.wait()
    mean = jnp.sum(part[...], axis=1, keepdims=True) * (1.0 / D)
    part[...] = jnp.broadcast_to(lax.rsqrt(mean + norm_eps), part.shape)

    def normalise(c):
        at = slice(c * chunk, (c + 1) * chunk)
        for i in range(tokens // step):
            rows = slice(i * step, (i + 1) * step)
            scale = jnp.concatenate([part[rows, :]] * (chunk // 128), axis=1)
            normed_ref[rows, at] = (normed_ref[rows, at].astype(jnp.float32) * scale).astype(jnp.bfloat16)

    normalise(0)
    for c in range(D // chunk):
        at = slice(c * chunk, (c + 1) * chunk)
        for i in (0, 1):
            term = dot(normed_ref[:, at], w[i, at, :], NN)
            acc[i] = term if c == 0 else acc[i] + term
        if (c + 1) * chunk < D:
            normalise(c + 1)
    store_heads(acc, table[0], table[1], key_ref, value_ref)


def norm_project(idx, hidden, weights, tables):
    tokens = hidden.shape[0]
    cols = weights.shape[2]
    return pl.pallas_call(
        norm_project_kernel,
        in_specs=[SMEM, HBM, HBM, HBM],
        out_specs=[VMEM, VMEM, VMEM],
        out_shape=[
            pltpu.VMEM((tokens, D), jnp.bfloat16),
            pltpu.VMEM((tokens, cols), jnp.bfloat16),
            pltpu.VMEM((tokens, cols), jnp.bfloat16),
        ],
        scratch_shapes=[
            pltpu.VMEM((2, D, cols), jnp.bfloat16),
            pltpu.VMEM((2, tokens, cols), jnp.float32),
            pltpu.VMEM((tokens, 128), jnp.float32),
            pltpu.VMEM(tables.shape, jnp.float32),
            pltpu.SemaphoreType.DMA((tokens // 128,)),
            pltpu.SemaphoreType.DMA((D // 1024,)),
            pltpu.SemaphoreType.DMA,
        ],
        compiler_params=params(16),
        cost_estimate=COST,
        name="norm_project",
    )(idx, in_hbm(hidden), in_hbm(weights), in_hbm(tables))


def is_whole(mask):
    return len(bits_of(mask >> 1)) < 2


def read_rows(sources, target, sems):
    if len(sources) == 1:
        return [pltpu.make_async_copy(sources[0], target, sems[0])]
    return [pltpu.make_async_copy(sources[i], target.at[i], sems[i]) for i in (0, 1)]


def project_kernel(masks, first, last, idx_ref, x_ref, *refs):
    refs = list(refs)
    count = len(masks)
    pieces = [[refs.pop(0) for _ in range(1 if is_whole(m) else 2)] for m in masks]
    held = None if first else refs.pop(0)
    if last:
        table_hbm, key_ref, value_ref, w, acc, table, sem, table_sem = refs
        table_copy = pltpu.make_async_copy(table_hbm, table, table_sem)
        table_copy.start()
    else:
        acc, w, sem = refs
    depth = w.shape[2]
    copies = [read_rows(pieces[n], w.at[n], [sem.at[i, n] for i in (0, 1)]) for n in range(count)]
    for group in copies:
        for copy in group:
            copy.start()
    for n in range(count):
        for copy in copies[n]:
            copy.wait()
        col = pl.multiple_of((idx_ref[0] ^ masks[n]) * depth, depth)
        x = x_ref[:, pl.ds(col, depth)]
        for i in (0, 1):
            term = dot(x, w[n, i], NN)
            if n:
                term = acc[i] + term
            elif not first:
                term = held[i] + term
            acc[i] = term
    if last:
        table_copy.wait()
        store_heads(acc, table[0], table[1], key_ref, value_ref)


def project(idx, normed, masks, pieces, held, tables):
    tokens = normed.shape[0]
    rows, cols = pieces[masks[0]][0].shape[-2:]
    first, last = held is None, tables is not None
    count = len(masks)
    args = [idx, resident(normed)] + [w for m in masks for w in pieces[m]]
    in_specs = [SMEM, VMEM] + [HBM] * (len(args) - 2)
    if not first:
        in_specs.append(VMEM)
        args.append(resident(held))
    acc_shape = (2, tokens, cols)
    scratch = [pltpu.VMEM((count, 2, rows, cols), jnp.bfloat16), pltpu.SemaphoreType.DMA((2, count))]
    if last:
        in_specs.append(HBM)
        args.append(in_hbm(tables))
        out_specs = [VMEM] * 2
        out_shape = [pltpu.VMEM((tokens, cols), jnp.bfloat16)] * 2
        scratch.insert(1, pltpu.VMEM(acc_shape, jnp.float32))
        scratch.insert(2, pltpu.VMEM(tables.shape, jnp.float32))
        scratch.append(pltpu.SemaphoreType.DMA)
    else:
        out_specs = VMEM
        out_shape = pltpu.VMEM(acc_shape, jnp.float32)
    return pl.pallas_call(
        functools.partial(project_kernel, tuple(masks), first, last),
        in_specs=in_specs,
        out_specs=out_specs,
        out_shape=out_shape,
        scratch_shapes=scratch,
        compiler_params=params(10),
        cost_estimate=COST,
        name="project",
    )(*args)


HEADS = 2


def parts(q_ref, k_ref):
    heads = k_ref.shape[1] // HD
    groups = q_ref.shape[1] // k_ref.shape[1]
    for seq in range(k_ref.shape[0] // LEN):
        for h in range(heads):
            yield seq, seq * LEN, h, h * groups, groups


def stacked(ref, row, r, first, count):
    rows = slice(row + r * TILE, row + (r + 1) * TILE)
    return jnp.concatenate([ref[rows, g * HD : (g + 1) * HD] for g in range(first, first + count)], axis=0)


def live_readout(ref, row, r, first, count, length):
    x = stacked(ref, row, r, first, count).astype(jnp.float32)
    at = lax.broadcasted_iota(jnp.int32, x.shape, 0) % TILE + r * TILE
    return jnp.where(at < length, x, 0.0).astype(jnp.bfloat16)


def attend_kernel(keep, len_ref, q_ref, k_ref, v_ref, ro_ref, *rest):
    if keep:
        before_ref, margin_ref, prob_ref, delta_ref = rest
        margin = -before_ref[0:1, 0:1]
    else:
        (margin_ref,) = rest
        margin = jnp.zeros((1, 1), jnp.float32)
    for seq, row, h, first, groups in parts(q_ref, k_ref):
        count = min(groups, HEADS)
        length = len_ref[seq]
        col = slice(h * HD, (h + 1) * HD)
        score = jnp.zeros((1, count * TILE), jnp.float32)
        j = lax.broadcasted_iota(jnp.int32, (TILE, count * TILE), 0)
        i = lax.broadcasted_iota(jnp.int32, (TILE, count * TILE), 1) % TILE
        base = 0
        for r in range(LEN // TILE):
            n = (r + 1) * TILE
            for g in range(0, groups, count):
                q = stacked(q_ref, row, r, first + g, count)
                ro = live_readout(ro_ref, row, r, first + g, count, length)
                s = dot(k_ref[row : row + n, col], q, NT)
                dp = dot(v_ref[row : row + n, col], ro, NT)
                s = [s[b * TILE : (b + 1) * TILE] for b in range(r + 1)]
                s[r] = jnp.where(j <= i, s[r], -1e30)
                top = functools.reduce(jnp.maximum, [jnp.max(x, axis=0, keepdims=True) for x in s])
                e = [jnp.exp2((x - top) * (logit_scale * math.log2(math.e))) for x in s]
                inverse = 1.0 / functools.reduce(jnp.add, [jnp.sum(x, axis=0, keepdims=True) for x in e])
                cols = slice(g * TILE, (g + count) * TILE)
                delta = jnp.zeros((1, count * TILE), jnp.float32)
                for b in range(r + 1):
                    p = (e[b] * inverse).astype(jnp.bfloat16)
                    if keep:
                        prob_ref[seq, h, base + b * TILE : base + (b + 1) * TILE, cols] = p
                    delta = delta + jnp.sum(p.astype(jnp.float32) * dp[b * TILE : (b + 1) * TILE], axis=0, keepdims=True)
                if keep:
                    delta_ref[seq, h, r : r + 1, cols] = delta
                score = score + delta
            base += n
        side = (1.0 if seq % 2 == 0 else -1.0) * (dpo_beta / math.sqrt(QH * HD))
        margin = margin + jnp.sum(score, axis=1, keepdims=True) * side
    margin_ref[...] = jnp.broadcast_to(margin, margin_ref.shape)


def attend(lengths, queries, keys, values, readout, before=None):
    seqs = lengths.shape[0]
    heads = keys.shape[1] // HD
    wide = queries.shape[1] // heads
    tiles = LEN // TILE
    span = TILE * tiles * (tiles + 1) // 2
    keep = before is not None
    args = [lengths] + [resident(x) for x in (queries, keys, values, readout)]
    out_shape = [jax.ShapeDtypeStruct((8, 128), jnp.float32)]
    if keep:
        args.append(before)
        out_shape += [pltpu.VMEM((seqs, heads, span, wide), jnp.bfloat16), pltpu.VMEM((seqs, heads, tiles, wide), jnp.float32)]
    return pl.pallas_call(
        functools.partial(attend_kernel, keep),
        in_specs=[SMEM] + [VMEM] * (len(args) - 1),
        out_specs=[VMEM] * len(out_shape),
        out_shape=out_shape,
        compiler_params=params(8),
        cost_estimate=COST,
        name="attend",
    )(*args)


def attend_back_kernel(len_ref, q_ref, v_ref, ro_ref, prob_ref, delta_ref, table_ref, grad_ref):
    tiles = LEN // TILE
    for seq, row, h, first, groups in parts(q_ref, v_ref):
        count = min(groups, HEADS)
        length = len_ref[seq]
        col = slice(h * HD, (h + 1) * HD)
        dk = [None] * tiles
        dv = [None] * tiles
        base = 0
        for r in range(tiles):
            n = (r + 1) * TILE
            for g in range(0, groups, count):
                q = stacked(q_ref, row, r, first + g, count)
                ro = live_readout(ro_ref, row, r, first + g, count, length)
                cols = slice(g * TILE, (g + count) * TILE)
                p = prob_ref[seq, h, base : base + n, cols]
                dp = dot(v_ref[row : row + n, col], ro, NT)
                ds = (p.astype(jnp.float32) * (dp - delta_ref[seq, h, r : r + 1, cols])).astype(jnp.bfloat16)
                tk = dot(ds, q, NN)
                tv = dot(p, ro, NN)
                for b in range(r + 1):
                    at = slice(b * TILE, (b + 1) * TILE)
                    dk[b] = tk[at] if dk[b] is None else dk[b] + tk[at]
                    dv[b] = tv[at] if dv[b] is None else dv[b] + tv[at]
            base += n
        scale = (-1.0 if seq % 2 == 0 else 1.0) * (1.0 / math.sqrt(QH * HD))
        for b in range(tiles):
            at = slice(b * TILE, (b + 1) * TILE)
            to = slice(row + b * TILE, row + (b + 1) * TILE)
            k = dk[b] * (scale * logit_scale)
            k = k * table_ref[0, at, :] - pltpu.roll(k, HD // 2, 1) * table_ref[1, at, :]
            grad_ref[0, col, to] = k.T.astype(jnp.bfloat16)
            grad_ref[1, col, to] = (dv[b] * scale).T.astype(jnp.bfloat16)


def attend_back(lengths, queries, values, readout, probs, delta, tables):
    return pl.pallas_call(
        attend_back_kernel,
        in_specs=[SMEM] + [VMEM] * 6,
        out_specs=VMEM,
        out_shape=pltpu.VMEM((2,) + values.shape[::-1], jnp.bfloat16),
        compiler_params=params(8),
        cost_estimate=COST,
        name="attend_back",
    )(lengths, *[resident(x) for x in (queries, values, readout, probs, delta, tables)])


def gradient_tiles(idx, mask, x_ref, cot_ref, rows):
    cols = cot_ref.shape[1]
    both = jnp.concatenate([cot_ref[0], cot_ref[1]], axis=0)
    tile = min(rows, 256)
    for t in range(rows // tile):
        col = pl.multiple_of((idx ^ mask) * rows + t * tile, tile)
        out = dot(both, x_ref[:, pl.ds(col, tile)], NN)
        for i in (0, 1):
            yield i, slice(t * tile, (t + 1) * tile), out[i * cols : (i + 1) * cols]


def gradient_kernel(masks, idx_ref, x_ref, cot_ref, *outs):
    outs = outs[len(outs) - len(masks) :]
    for mask, out_ref in zip(masks, outs):
        for i, at, value in gradient_tiles(idx_ref[0], mask, x_ref, cot_ref, out_ref.shape[2]):
            out_ref[i, :, at] = value.astype(out_ref.dtype)


def merged_kernel(masks, idx_ref, x_ref, cot_ref, margin_ref, *refs):
    count = len(masks)
    theirs_hbm, outs = refs[:count], refs[count : 3 * count]
    theirs, sem = refs[3 * count :]
    copies = [pltpu.make_async_copy(theirs_hbm[n], theirs.at[n], sem.at[n]) for n in range(count)]
    for copy in copies:
        copy.start()
    mine, their = (jnp.concatenate([jax.nn.sigmoid(-margin_ref[i : i + 1, :])] * 2, axis=1) for i in (0, 4))
    for n, mask in enumerate(masks):
        copies[n].wait()
        for i, at, value in gradient_tiles(idx_ref[0], mask, x_ref, cot_ref, theirs.shape[3]):
            value = value * mine + theirs[n, i, :, at].astype(jnp.float32) * their
            outs[2 * n + i][:, at] = value.astype(outs[2 * n + i].dtype)


def gradient_blocks(idx, normed, cot, masks, rows, merge=None, earlier=()):
    _, cols, tokens = cot.shape
    args = [idx, resident(normed), resident(cot)]
    in_specs = [SMEM, VMEM, VMEM]
    scratch = []
    if merge is None:
        kernel, name = gradient_kernel, "gradient_block"
        out_shape = [jax.ShapeDtypeStruct((2, cols, rows), jnp.bfloat16) for m in masks]
        args += earlier
        in_specs += [HBM] * len(earlier)
    else:
        kernel, name = merged_kernel, "merged_block"
        margins, theirs = merge
        args += [margins] + [theirs[m] for m in masks]
        in_specs += [VMEM] + [HBM] * len(masks)
        out_shape = [
            jax.ShapeDtypeStruct((cols, rows), jnp.bfloat16) if m else pltpu.VMEM((cols, rows), jnp.float32)
            for m in masks
            for i in (0, 1)
        ]
        scratch = [pltpu.VMEM((len(masks), 2, cols, rows), jnp.bfloat16), pltpu.SemaphoreType.DMA((len(masks),))]
    outs = pl.pallas_call(
        functools.partial(kernel, tuple(masks)),
        in_specs=in_specs,
        out_specs=[VMEM] * len(out_shape),
        out_shape=out_shape,
        scratch_shapes=scratch,
        compiler_params=params(10),
        cost_estimate=COST,
        name=name,
    )(*args)
    return outs if merge is None else [outs[2 * n : 2 * n + 2] for n in range(len(masks))]


def finish_kernel(counts, *refs):
    refs = list(refs)
    out_ref, square_ref = refs[-2:]
    refs = refs[:-2]
    square_ref[...] = jnp.zeros_like(square_ref)
    cols, rows = refs[0].shape
    for i in (0, 1):
        terms = [refs.pop(0) for _ in range(1 + counts[i])]
        squares = jnp.zeros((1, 128), jnp.float32)
        for c in range(cols // 128):
            for r in range(rows // 128):
                at = (slice(c * 128, (c + 1) * 128), slice(r * 128, (r + 1) * 128))
                value = functools.reduce(jnp.add, [t[at].astype(jnp.float32) for t in terms])
                squares = squares + jnp.sum(value * value, axis=0, keepdims=True)
                out_ref[i, at[1], at[0]] = value.T.astype(jnp.bfloat16)
        square_ref[i : i + 1, :] = jnp.broadcast_to(jnp.sum(squares, axis=1, keepdims=True), (1, 128))


def finish(base, arrived):
    args = [x for i in (0, 1) for x in (resident(base[i]), *arrived[i])]
    cols, rows = base[0].shape
    return pl.pallas_call(
        functools.partial(finish_kernel, [len(a) for a in arrived]),
        in_specs=[VMEM] * len(args),
        out_specs=[VMEM] * 2,
        out_shape=[jax.ShapeDtypeStruct((2, rows, cols), jnp.bfloat16), jax.ShapeDtypeStruct((8, 128), jnp.float32)],
        compiler_params=params(8),
        cost_estimate=COST,
        name="finish",
    )(*args)


def fetch_kernel(masks, idx_ref, *refs):
    refs = list(refs)
    pieces = [[refs.pop(0) for _ in range(1 if is_whole(m) else 2)] for m in masks]
    ref_hbm, _, w, r, sem = refs
    rows = r.shape[2]
    copies = []
    for n, mask in enumerate(masks):
        at = pl.ds(pl.multiple_of((idx_ref[0] ^ mask) * rows, rows), rows)
        copies += read_rows(pieces[n], w.at[n], [sem.at[i, n] for i in (0, 1)])
        copies.append(pltpu.make_async_copy(ref_hbm.at[:, at, :], r.at[n], sem.at[2, n]))
    for copy in copies:
        copy.start()
    for copy in copies:
        copy.wait()


def fetch(idx, weights, reference, masks, earlier):
    rows, cols = weights[masks[0]][0].shape[-2:]
    count = len(masks)
    args = [idx] + [w for m in masks for w in weights[m]] + [in_hbm(reference), earlier]
    return pl.pallas_call(
        functools.partial(fetch_kernel, tuple(masks)),
        in_specs=[SMEM] + [HBM] * (len(args) - 1),
        out_specs=[VMEM] * 2,
        out_shape=[pltpu.VMEM((count, 2, rows, cols), jnp.bfloat16)] * 2,
        scratch_shapes=[pltpu.SemaphoreType.DMA((3, count))],
        compiler_params=params(4),
        cost_estimate=COST,
        name="fetch",
    )(*args)


def blend_kernel(masks, first, ready, idx_ref, square_ref, *refs):
    refs = list(refs)
    count = len(masks)
    grads = [[refs.pop(0) for _ in range(1 if is_whole(m) else 2)] for m in masks]
    if ready is None:
        weights = [[refs.pop(0) for _ in range(1 if is_whole(m) else 2)] for m in masks]
        ref_hbm = refs.pop(0)
    else:
        w, r = refs.pop(0), refs.pop(0)
    if not first:
        refs.pop(0)
    out_hbm, token_ref = refs.pop(0), refs.pop(0)
    new_hbm = refs.pop(0) if first else None
    if ready is None:
        w, r = refs.pop(0), refs.pop(0)
    g, o, new, sem, out_sem = refs
    rows, cols = g.shape[2:]
    step = 32
    half = rows // 2
    token_ref[...] = jnp.zeros_like(token_ref)

    def reads(n):
        slot = n % 2
        at = pl.ds(pl.multiple_of((idx_ref[0] ^ masks[n]) * rows, rows), rows)
        group = read_rows(grads[n], g.at[slot], [sem.at[i, slot] for i in (0, 1)])
        if ready is None:
            group += read_rows(weights[n], w.at[slot], [sem.at[2 + i, slot] for i in (0, 1)])
            group.append(pltpu.make_async_copy(ref_hbm.at[:, at, :], r.at[slot], sem.at[4, slot]))
        for copy in group:
            copy.start()
        return group

    mean = square_ref[...] * (1.0 / (D * KVH * HD))
    scale = jnp.concatenate([learning_rate * lax.rsqrt(mean + norm_eps)] * (cols // 128), axis=1)
    coming = {n: reads(n) for n in range(min(2, count))}
    writes = {}
    for n in range(count):
        slot = n % 2
        held = slot if ready is None else ready + n
        for copy in coming[n] + writes.pop(n - 2, []):
            copy.wait()
        writes[n] = []
        for part in range(2):
            for i in (0, 1):
                for start in range(part * half, (part + 1) * half, step):
                    j = slice(start, start + step)
                    value = w[held, i, j].astype(jnp.float32) - scale[i : i + 1, :] * g[slot, i, j].astype(jnp.float32)
                    value = value.astype(jnp.bfloat16)
                    if first and n == 0:
                        new[i, j] = value
                    mixed = mix_alpha * value.astype(jnp.float32) + (1.0 - mix_alpha) * r[held, i, j].astype(jnp.float32)
                    o[slot, i, j] = mixed.astype(jnp.bfloat16)
            at = pl.ds(pl.multiple_of((idx_ref[0] ^ masks[n]) * rows + part * half, half), half)
            copy = pltpu.make_async_copy(o.at[slot, :, pl.ds(part * half, half), :], out_hbm.at[:, at, :], out_sem.at[part, slot])
            copy.start()
            writes[n].append(copy)
        if first and n == 0:
            copy = pltpu.make_async_copy(new, new_hbm, out_sem.at[0, 2])
            copy.start()
            writes[n].append(copy)
        if n + 2 < count:
            coming[n + 2] = reads(n + 2)
    for group in writes.values():
        for copy in group:
            copy.wait()


def blend(idx, squares, weights, grads, reference, held, masks, ready=None):
    rows, cols = weights[masks[0]][0].shape[-2:]
    count = len(masks)
    first = held is None
    args = [idx, squares] + [x for m in masks for x in grads[m]]
    in_specs = [SMEM, VMEM] + [HBM] * (len(args) - 2)
    block = pltpu.VMEM((min(count, 2), 2, rows, cols), jnp.bfloat16)
    scratch = [block, block, pltpu.VMEM((2, rows, cols) if first else (8, 128), jnp.bfloat16)]
    scratch += [pltpu.SemaphoreType.DMA((5, 2)), pltpu.SemaphoreType.DMA((2, 3))]
    if ready is None:
        extra = [w for m in masks for w in weights[m]] + [in_hbm(reference)]
        args += extra
        in_specs += [HBM] * len(extra)
        scratch = [block, block] + scratch
    else:
        args += [resident(x) for x in ready[0]]
        in_specs += [VMEM] * 2
    out_specs = [HBM, VMEM]
    out_shape = [jax.ShapeDtypeStruct(reference.shape, jnp.bfloat16), jax.ShapeDtypeStruct((8, 128), jnp.float32)]
    aliases = {}
    if first:
        out_specs.append(HBM)
        out_shape.append(jax.ShapeDtypeStruct((2, rows, cols), jnp.bfloat16))
    else:
        aliases = {len(args): 0}
        in_specs.append(HBM)
        args.append(held)
    return pl.pallas_call(
        functools.partial(blend_kernel, tuple(masks), first, None if ready is None else ready[1]),
        in_specs=in_specs,
        out_specs=out_specs,
        out_shape=out_shape,
        scratch_shapes=scratch,
        input_output_aliases=aliases,
        compiler_params=params(14),
        cost_estimate=COST,
        name="blend",
    )(*args)


def bits_of(mask):
    return [1 << b for b in range(mask.bit_length()) if mask >> b & 1]


def after(value, *earlier):
    return lax.optimization_barrier((value, earlier))[0]


def body(shards, tensors, hidden_in, policy_weights, reference_weights, policy_queries, reference_queries, readout, lengths):
    rows = policy_weights.shape[1]
    idx = lax.axis_index("shard").astype(jnp.int32).reshape(1)
    tables = jnp.asarray(rope_tables())

    def swap(x, bit, axis="shard", size=shards):
        return lax.ppermute(x, axis, [(i, i ^ bit) for i in range(size)])

    def powers(size):
        return [1 << b for b in range(size.bit_length() - 1)]

    chips = sorted(range(0, shards, 2), key=lambda m: (len(bits_of(m)), m))
    near = [m for m in chips if len(bits_of(m)) == 1]
    far = [m for m in chips if len(bits_of(m)) > 1]
    link = lambda i, m: bits_of(m)[-1] if i == 0 else bits_of(m)[0]

    def send_near(own):
        got = {m: [swap(own, m)] for m in near}
        got[0] = [own]
        got[1] = [swap(own, 1)]
        return got

    def relay(got, m, *earlier):
        got[m] = [None, None]
        for i in (0, 1):
            via = link(i, m)
            source = got[m ^ via]
            source = source[i] if len(source) == 2 else source[0][i]
            got[m][i] = swap(after(source, *earlier), via)

    def to_core(got, m, *earlier):
        got[m | 1] = [swap(after(g, *earlier), 1) for g in got[m]]

    weights = send_near(policy_weights)
    normed, ref_keys, ref_values = norm_project(idx, hidden_in, reference_weights, tables)
    (ref_margin,) = attend(lengths, reference_queries, ref_keys, ref_values, readout)
    for m in far:
        relay(weights, m, ref_margin, *[weights[k] for k in near])
    for m in near:
        to_core(weights, m, ref_margin)
    held = project(idx, normed, [0, 1], weights, None, None)
    held = project(idx, normed, [m | c for m in near for c in (0, 1)], weights, held, None if far else tables)
    if far:
        for m in far:
            to_core(weights, m, held)
        held = project(idx, normed, [m | c for m in far for c in (0, 1)], weights, held, tables)
    pol_keys, pol_values = held
    margin, probs, delta = attend(lengths, policy_queries, pol_keys, pol_values, readout, ref_margin)

    theirs = {}
    order = list(reversed(chips))
    split = max(len(far), 1)

    def other_blocks(masks, *earlier):
        blocks = gradient_blocks(idx, normed, cot, [m | 1 for m in masks], rows, None, earlier)
        theirs.update({m: swap(block, 1) for m, block in zip(masks, blocks)})
        return blocks

    received = swap(margin, 1)
    cot = attend_back(lengths, policy_queries, pol_values, readout, probs, delta, tables)
    margins = jnp.concatenate([margin[:4], after(received, cot)[4:]], axis=0)
    beside = [order[:split], order[split:]]
    for bit in powers(tensors):
        received = swap(margins, bit, "tensor", tensors)
        margins = margins + (after(received, other_blocks(beside.pop(0), margins)) if beside else received)
    for masks in beside:
        other_blocks(masks)

    chip_sum = {}
    arrived = {m: [[], []] for m in chips}
    waiting = []

    def send(m, i):
        payload = chip_sum[m][i]
        if arrived[m][i]:
            payload = payload.astype(jnp.float32)
            for term in arrived[m][i]:
                payload = payload + term.astype(jnp.float32)
            payload = payload.astype(jnp.bfloat16)
        via = link(i, m)
        arrived[m ^ via][i].append(swap(payload, via))
        return payload

    for masks in (order[:split], order[split:]):
        blocks = gradient_blocks(idx, normed, cot, masks, rows, (margins, theirs))
        chip_sum.update(zip(masks, blocks))
        for m in masks:
            for i in (0, 1):
                if m and not any(k ^ link(i, k) == m for k in far):
                    send(m, i)
                elif m:
                    waiting.append((m, i))
    for m, i in waiting:
        send(m, i)
    own, squares = finish(chip_sum[0], arrived[0])

    grads = send_near(own)
    for bit in powers(tensors):
        squares = squares + swap(squares, bit, "tensor", tensors)
    squares = squares + swap(squares, 1)
    terms = [squares] + [swap(squares, m) for m in chips[1:]]
    while len(terms) > 1:
        terms = [a + b for a, b in zip(terms[::2], terms[1::2])]
    for m in far:
        relay(grads, m, squares, *[grads[k] for k in near])
    (squares,) = terms
    for m in near:
        to_core(grads, m, squares)
    new_reference, token, new_policy = blend(idx, squares, weights, grads, reference_weights, None, [0, 1])
    new_reference, token = blend(idx, squares, weights, grads, reference_weights, new_reference, [m | c for m in near for c in (0, 1)])
    if far:
        ready = fetch(idx, weights, reference_weights, [m | c for c in (0, 1) for m in far], token)
        for m in far:
            to_core(grads, m, ready)
        for c in (0, 1):
            masks = [m | c for m in far]
            new_reference, token = blend(idx, squares, weights, grads, reference_weights, new_reference, masks, (ready, c * len(far)))
    return (new_policy, new_reference, margins[0, :1])


def solution(mesh):
    return jax.shard_map(
        functools.partial(body, mesh.shape["shard"], mesh.shape["tensor"]),
        mesh=mesh,
        in_specs=(
            P("shard", None),
            P(None, "shard", "tensor"),
            P(None, None, "tensor"),
            P("shard", "tensor"),
            P("shard", "tensor"),
            P("shard", "tensor"),
            P("shard"),
        ),
        out_specs=(P(None, "shard", "tensor"), P(None, None, "tensor"), P("shard")),
        check_vma=False,
    )
```

```python
import functools
import math

import jax
import jax.numpy as jnp
import numpy as np
from jax import lax
from jax.experimental import pallas as pl
from jax.experimental.pallas import tpu as pltpu
from jax.sharding import PartitionSpec as P

D = 8192
HD = 128
KVH = 8
QH = 32
LEN = 384
TILE = 128

rope_base = 1000000.0
dpo_beta = 0.1
learning_rate = 0.2
mix_alpha = 0.6
norm_eps = 1e-06
width_scale = D ** (-0.5)
logit_scale = 1.0 / math.sqrt(HD)
MIB = 1024 * 1024

NT = (((1,), (1,)), ((), ()))
NN = (((1,), (0,)), ((), ()))
TN = (((0,), (0,)), ((), ()))


def dot(a, b, dims):
    return lax.dot_general(a, b, dims, preferred_element_type=jnp.float32)


def params(mib):
    return pltpu.CompilerParams(vmem_limit_bytes=mib * MIB)


COST = pl.CostEstimate(flops=1, bytes_accessed=1, transcendentals=0)
LONG = pl.CostEstimate(flops=1, bytes_accessed=40 * 1000 * 1000, transcendentals=0)
VMEM = pl.BlockSpec(memory_space=pltpu.VMEM)
SMEM = pl.BlockSpec(memory_space=pltpu.SMEM)
HBM = pl.BlockSpec(memory_space=pl.ANY)


def resident(x):
    return pltpu.with_memory_space_constraint(x, pltpu.VMEM)


def in_hbm(x):
    return pltpu.with_memory_space_constraint(x, pltpu.HBM)


def rope_tables():
    frequency = rope_base ** (-2.0 * np.arange(HD // 2) / HD)
    angles = np.arange(LEN)[:, None] * frequency[None, :]
    cosine, sine = np.cos(angles), np.sin(angles)
    return np.stack([np.concatenate([cosine, cosine], axis=1), np.concatenate([-sine, sine], axis=1)]).astype(np.float32)


def store_heads(acc_ref, cos, sin, key_ref, value_ref):
    for s in range(key_ref.shape[0] // LEN):
        rows = slice(s * LEN, (s + 1) * LEN)
        for h in range(key_ref.shape[1] // HD):
            cols = slice(h * HD, (h + 1) * HD)
            k = acc_ref[0, rows, cols] * width_scale
            key_ref[rows, cols] = (k * cos + pltpu.roll(k, HD // 2, 1) * sin).astype(jnp.bfloat16)
    value_ref[...] = (acc_ref[1] * width_scale).astype(jnp.bfloat16)


def norm_project_kernel(idx_ref, hidden_hbm, weight_hbm, table_hbm, normed_ref, key_ref, value_ref, w, acc, part, table, in_sem, w_sem, table_sem):
    tokens = normed_ref.shape[0]
    step, width, span, chunk = 16, 512, 128, 1024
    reads = []
    for i in range(tokens // span):
        at = pl.ds(i * span, span)
        reads.append(pltpu.make_async_copy(hidden_hbm.at[at], normed_ref.at[at], in_sem.at[i]))
    loads = []
    for c in range(D // chunk):
        at = pl.ds(c * chunk, chunk)
        loads.append(pltpu.make_async_copy(weight_hbm.at[:, at, :], w.at[:, at, :], w_sem.at[c]))
    loads.append(pltpu.make_async_copy(table_hbm, table, table_sem))
    for copy in reads + loads:
        copy.start()

    def row_step(i, carry):
        at = pl.ds(pl.multiple_of(i * step, step), step)
        total = jnp.zeros((step, width), jnp.float32)
        for c in range(D // width):
            v = normed_ref[at, c * width : (c + 1) * width].astype(jnp.float32)
            total = total + v * v
        part[at, :] = functools.reduce(jnp.add, [total[:, c * 128 : (c + 1) * 128] for c in range(width // 128)])
        return carry

    for i, copy in enumerate(reads):
        copy.wait()
        lax.fori_loop(i * (span // step), (i + 1) * (span // step), row_step, 0)
    for copy in loads:
        copy.wait()
    mean = jnp.sum(part[...], axis=1, keepdims=True) * (1.0 / D)
    part[...] = jnp.broadcast_to(lax.rsqrt(mean + norm_eps), part.shape)

    def columns(c):
        return pl.ds(pl.multiple_of(c * chunk, chunk), chunk)

    def normalise(c):
        for i in range(tokens // step):
            rows = slice(i * step, (i + 1) * step)
            scale = jnp.concatenate([part[rows, :]] * (chunk // 128), axis=1)
            normed_ref[rows, columns(c)] = (normed_ref[rows, columns(c)].astype(jnp.float32) * scale).astype(jnp.bfloat16)

    def multiply(c, carry):
        for i in (0, 1):
            acc[i] += dot(normed_ref[:, columns(c)], w[i, columns(c), :], NN)

        @pl.when(c + 1 < D // chunk)
        def _():
            normalise(c + 1)

        return carry

    acc[...] = jnp.zeros_like(acc)
    normalise(0)
    lax.fori_loop(0, D // chunk, multiply, 0)
    store_heads(acc, table[0], table[1], key_ref, value_ref)


def norm_project(idx, hidden, weights, tables):
    tokens = hidden.shape[0]
    cols = weights.shape[2]
    return pl.pallas_call(
        norm_project_kernel,
        in_specs=[SMEM, HBM, HBM, HBM],
        out_specs=[VMEM, VMEM, VMEM],
        out_shape=[
            pltpu.VMEM((tokens, D), jnp.bfloat16),
            pltpu.VMEM((tokens, cols), jnp.bfloat16),
            pltpu.VMEM((tokens, cols), jnp.bfloat16),
        ],
        scratch_shapes=[
            pltpu.VMEM((2, D, cols), jnp.bfloat16),
            pltpu.VMEM((2, tokens, cols), jnp.float32),
            pltpu.VMEM((tokens, 128), jnp.float32),
            pltpu.VMEM(tables.shape, jnp.float32),
            pltpu.SemaphoreType.DMA((tokens // 128,)),
            pltpu.SemaphoreType.DMA((D // 1024,)),
            pltpu.SemaphoreType.DMA,
        ],
        compiler_params=params(16),
        cost_estimate=COST,
        name="norm_project",
    )(idx, in_hbm(hidden), in_hbm(weights), in_hbm(tables))


def is_whole(mask):
    return len(bits_of(mask >> 1)) < 2


def read_rows(sources, target, sems):
    if len(sources) == 1:
        return [pltpu.make_async_copy(sources[0], target, sems[0])]
    return [pltpu.make_async_copy(sources[i], target.at[i], sems[i]) for i in (0, 1)]


def project_kernel(masks, first, last, idx_ref, x_ref, *refs):
    refs = list(refs)
    count = len(masks)
    pieces = [[refs.pop(0) for _ in range(1 if is_whole(m) else 2)] for m in masks]
    held = None if first else refs.pop(0)
    if last:
        table_hbm, key_ref, value_ref, w, acc, table, sem, table_sem = refs
        table_copy = pltpu.make_async_copy(table_hbm, table, table_sem)
        table_copy.start()
    else:
        acc, w, sem = refs
    depth = w.shape[2]
    copies = [read_rows(pieces[n], w.at[n], [sem.at[i, n] for i in (0, 1)]) for n in range(count)]
    for group in copies:
        for copy in group:
            copy.start()
    for n in range(count):
        for copy in copies[n]:
            copy.wait()
        col = pl.multiple_of((idx_ref[0] ^ masks[n]) * depth, depth)
        x = x_ref[:, pl.ds(col, depth)]
        for i in (0, 1):
            term = dot(x, w[n, i], NN)
            if n:
                term = acc[i] + term
            elif not first:
                term = held[i] + term
            acc[i] = term
    if last:
        table_copy.wait()
        store_heads(acc, table[0], table[1], key_ref, value_ref)


def project(idx, normed, masks, pieces, held, tables):
    tokens = normed.shape[0]
    rows, cols = pieces[masks[0]][0].shape[-2:]
    first, last = held is None, tables is not None
    count = len(masks)
    args = [idx, resident(normed)] + [w for m in masks for w in pieces[m]]
    in_specs = [SMEM, VMEM] + [HBM] * (len(args) - 2)
    if not first:
        in_specs.append(VMEM)
        args.append(resident(held))
    acc_shape = (2, tokens, cols)
    scratch = [pltpu.VMEM((count, 2, rows, cols), jnp.bfloat16), pltpu.SemaphoreType.DMA((2, count))]
    if last:
        in_specs.append(HBM)
        args.append(in_hbm(tables))
        out_specs = [VMEM] * 2
        out_shape = [pltpu.VMEM((tokens, cols), jnp.bfloat16)] * 2
        scratch.insert(1, pltpu.VMEM(acc_shape, jnp.float32))
        scratch.insert(2, pltpu.VMEM(tables.shape, jnp.float32))
        scratch.append(pltpu.SemaphoreType.DMA)
    else:
        out_specs = VMEM
        out_shape = pltpu.VMEM(acc_shape, jnp.float32)
    return pl.pallas_call(
        functools.partial(project_kernel, tuple(masks), first, last),
        in_specs=in_specs,
        out_specs=out_specs,
        out_shape=out_shape,
        scratch_shapes=scratch,
        compiler_params=params(10),
        cost_estimate=COST,
        name="project",
    )(*args)


HEADS = 2


def stacked(ref, row, col, r, first, count):
    rows = pl.ds(pl.multiple_of(row + r * TILE, TILE), TILE)
    at = lambda g: pl.ds(pl.multiple_of(col + g * HD, HD), HD)
    return jnp.concatenate([ref[rows, at(g)] for g in range(first, first + count)], axis=0)


def live_readout(ref, row, col, r, first, count, length):
    x = stacked(ref, row, col, r, first, count).astype(jnp.float32)
    at = lax.broadcasted_iota(jnp.int32, x.shape, 0) % TILE + r * TILE
    return jnp.where(at < length, x, 0.0).astype(jnp.bfloat16)


def places(step, q_ref, k_ref):
    heads = k_ref.shape[1] // HD
    seq, h = step // heads, step % heads
    return seq, h, seq * LEN, pl.multiple_of(h * HD, HD), h * (q_ref.shape[1] // heads)


def attend_kernel(keep, len_ref, q_ref, k_ref, v_ref, ro_ref, *rest):
    groups = q_ref.shape[1] // k_ref.shape[1]
    count = min(groups, HEADS)
    if keep:
        before_ref, margin_ref, prob_ref, delta_ref = rest
    else:
        (margin_ref,) = rest

    def one(step, margin):
        seq, h, row, col, q_col = places(step, q_ref, k_ref)
        length = len_ref[seq]
        score = jnp.zeros((1, count * TILE), jnp.float32)
        j = lax.broadcasted_iota(jnp.int32, (TILE, count * TILE), 0)
        i = lax.broadcasted_iota(jnp.int32, (TILE, count * TILE), 1) % TILE
        base = 0
        for r in range(LEN // TILE):
            n = (r + 1) * TILE
            keys = (pl.ds(pl.multiple_of(row, TILE), n), pl.ds(col, HD))
            for g in range(0, groups, count):
                q = stacked(q_ref, row, q_col, r, g, count)
                ro = live_readout(ro_ref, row, q_col, r, g, count, length)
                s = dot(k_ref[keys], q, NT)
                dp = dot(v_ref[keys], ro, NT)
                s = [s[b * TILE : (b + 1) * TILE] for b in range(r + 1)]
                s[r] = jnp.where(j <= i, s[r], -1e30)
                top = functools.reduce(jnp.maximum, [jnp.max(x, axis=0, keepdims=True) for x in s])
                e = [jnp.exp2((x - top) * (logit_scale * math.log2(math.e))) for x in s]
                inverse = 1.0 / functools.reduce(jnp.add, [jnp.sum(x, axis=0, keepdims=True) for x in e])
                cols = slice(g * TILE, (g + count) * TILE)
                delta = jnp.zeros((1, count * TILE), jnp.float32)
                for b in range(r + 1):
                    p = (e[b] * inverse).astype(jnp.bfloat16)
                    if keep:
                        prob_ref[seq, h, base + b * TILE : base + (b + 1) * TILE, cols] = p
                    delta = delta + jnp.sum(p.astype(jnp.float32) * dp[b * TILE : (b + 1) * TILE], axis=0, keepdims=True)
                if keep:
                    delta_ref[seq, h, r : r + 1, cols] = delta
                score = score + delta
            base += n
        side = jnp.where(seq % 2 == 0, 1.0, -1.0) * (dpo_beta / math.sqrt(QH * HD))
        return margin + jnp.sum(score, axis=1, keepdims=True) * side

    steps = k_ref.shape[0] // LEN * (k_ref.shape[1] // HD)
    start = -before_ref[0:1, 0:1] if keep else jnp.zeros((1, 1), jnp.float32)
    margin_ref[...] = jnp.broadcast_to(lax.fori_loop(0, steps, one, start), margin_ref.shape)


def attend(lengths, queries, keys, values, readout, before=None):
    seqs = lengths.shape[0]
    heads = keys.shape[1] // HD
    wide = queries.shape[1] // heads
    tiles = LEN // TILE
    span = TILE * tiles * (tiles + 1) // 2
    keep = before is not None
    args = [lengths] + [resident(x) for x in (queries, keys, values, readout)]
    out_shape = [jax.ShapeDtypeStruct((8, 128), jnp.float32)]
    if keep:
        args.append(before)
        out_shape += [pltpu.VMEM((seqs, heads, span, wide), jnp.bfloat16), pltpu.VMEM((seqs, heads, tiles, wide), jnp.float32)]
    return pl.pallas_call(
        functools.partial(attend_kernel, keep),
        in_specs=[SMEM] + [VMEM] * (len(args) - 1),
        out_specs=[VMEM] * len(out_shape),
        out_shape=out_shape,
        compiler_params=params(8),
        cost_estimate=COST,
        name="attend",
    )(*args)


def attend_back_kernel(len_ref, q_ref, v_ref, ro_ref, prob_ref, delta_ref, table_ref, grad_ref):
    tiles = LEN // TILE
    groups = q_ref.shape[1] // v_ref.shape[1]
    count = min(groups, HEADS)

    def one(step, carry):
        seq, h, row, col, q_col = places(step, q_ref, v_ref)
        length = len_ref[seq]
        dk = [None] * tiles
        dv = [None] * tiles
        base = 0
        for r in range(tiles):
            n = (r + 1) * TILE
            keys = (pl.ds(pl.multiple_of(row, TILE), n), pl.ds(col, HD))
            for g in range(0, groups, count):
                q = stacked(q_ref, row, q_col, r, g, count)
                ro = live_readout(ro_ref, row, q_col, r, g, count, length)
                cols = slice(g * TILE, (g + count) * TILE)
                p = prob_ref[seq, h, base : base + n, cols]
                dp = dot(v_ref[keys], ro, NT)
                ds = (p.astype(jnp.float32) * (dp - delta_ref[seq, h, r : r + 1, cols])).astype(jnp.bfloat16)
                tk = dot(ds, q, NN)
                tv = dot(p, ro, NN)
                for b in range(r + 1):
                    at = slice(b * TILE, (b + 1) * TILE)
                    dk[b] = tk[at] if dk[b] is None else dk[b] + tk[at]
                    dv[b] = tv[at] if dv[b] is None else dv[b] + tv[at]
            base += n
        scale = jnp.where(seq % 2 == 0, -1.0, 1.0) * (1.0 / math.sqrt(QH * HD))
        for b in range(tiles):
            at = slice(b * TILE, (b + 1) * TILE)
            to = (pl.ds(col, HD), pl.ds(pl.multiple_of(row + b * TILE, TILE), TILE))
            k = dk[b] * (scale * logit_scale)
            k = k * table_ref[0, at, :] - pltpu.roll(k, HD // 2, 1) * table_ref[1, at, :]
            grad_ref[(0, *to)] = k.T.astype(jnp.bfloat16)
            grad_ref[(1, *to)] = (dv[b] * scale).T.astype(jnp.bfloat16)
        return carry

    lax.fori_loop(0, v_ref.shape[0] // LEN * (v_ref.shape[1] // HD), one, 0)


def attend_back(lengths, queries, values, readout, probs, delta, tables):
    return pl.pallas_call(
        attend_back_kernel,
        in_specs=[SMEM] + [VMEM] * 6,
        out_specs=VMEM,
        out_shape=pltpu.VMEM((2,) + values.shape[::-1], jnp.bfloat16),
        compiler_params=params(8),
        cost_estimate=COST,
        name="attend_back",
    )(lengths, *[resident(x) for x in (queries, values, readout, probs, delta, tables)])


def gradient_tiles(idx, mask, x_ref, cot_ref, rows, store):
    cols = cot_ref.shape[1]
    tile = min(rows, 256)

    def one(t, carry):
        col = pl.multiple_of((idx ^ mask) * rows + t * tile, tile)
        at = pl.ds(pl.multiple_of(t * tile, tile), tile)
        both = jnp.concatenate([cot_ref[0], cot_ref[1]], axis=0)
        out = dot(both, x_ref[:, pl.ds(col, tile)], NN)
        for i in (0, 1):
            store(i, at, out[i * cols : (i + 1) * cols])
        return carry

    lax.fori_loop(0, rows // tile, one, 0)


def gradient_kernel(masks, idx_ref, x_ref, cot_ref, *outs):
    outs = outs[len(outs) - len(masks) :]
    for mask, out_ref in zip(masks, outs):

        def store(i, at, value):
            out_ref[i, :, at] = value.astype(out_ref.dtype)

        gradient_tiles(idx_ref[0], mask, x_ref, cot_ref, out_ref.shape[2], store)


def merged_kernel(masks, idx_ref, x_ref, cot_ref, mine_ref, their_ref, *refs):
    count = len(masks)
    theirs_hbm, outs = refs[:count], refs[count : 3 * count]
    theirs, sem = refs[3 * count :]
    copies = [pltpu.make_async_copy(theirs_hbm[n], theirs.at[n], sem.at[n]) for n in range(count)]
    for copy in copies:
        copy.start()
    mine, their = (jnp.concatenate([jax.nn.sigmoid(-ref[0:1, :])] * 2, axis=1) for ref in (mine_ref, their_ref))
    for n, mask in enumerate(masks):
        copies[n].wait()

        def store(i, at, value):
            value = value * mine + theirs[n, i, :, at].astype(jnp.float32) * their
            outs[2 * n + i][:, at] = value.astype(outs[2 * n + i].dtype)

        gradient_tiles(idx_ref[0], mask, x_ref, cot_ref, theirs.shape[3], store)


def gradient_blocks(idx, normed, cot, masks, rows, merge=None, earlier=()):
    _, cols, tokens = cot.shape
    args = [idx, resident(normed), resident(cot)]
    in_specs = [SMEM, VMEM, VMEM]
    scratch = []
    if merge is None:
        kernel, name = gradient_kernel, "gradient_block"
        out_shape = [jax.ShapeDtypeStruct((2, cols, rows), jnp.bfloat16) for m in masks]
        args += earlier
        in_specs += [HBM] * len(earlier)
    else:
        kernel, name = merged_kernel, "merged_block"
        margins, theirs = merge
        args += [*margins] + [theirs[m] for m in masks]
        in_specs += [VMEM] * 2 + [HBM] * len(masks)
        out_shape = [
            jax.ShapeDtypeStruct((cols, rows), jnp.bfloat16) if m else pltpu.VMEM((cols, rows), jnp.float32)
            for m in masks
            for i in (0, 1)
        ]
        scratch = [pltpu.VMEM((len(masks), 2, cols, rows), jnp.bfloat16), pltpu.SemaphoreType.DMA((len(masks),))]
    outs = pl.pallas_call(
        functools.partial(kernel, tuple(masks)),
        in_specs=in_specs,
        out_specs=[VMEM] * len(out_shape),
        out_shape=out_shape,
        scratch_shapes=scratch,
        compiler_params=params(10),
        cost_estimate=COST,
        name=name,
    )(*args)
    return outs if merge is None else [outs[2 * n : 2 * n + 2] for n in range(len(masks))]


def finish_kernel(counts, *refs):
    refs = list(refs)
    out_ref, square_ref = refs[-2:]
    refs = refs[:-2]
    square_ref[...] = jnp.zeros_like(square_ref)
    cols, rows = refs[0].shape
    for i in (0, 1):
        terms = [refs.pop(0) for _ in range(1 + counts[i])]
        squares = jnp.zeros((1, 128), jnp.float32)
        for c in range(cols // 128):
            for r in range(rows // 128):
                at = (slice(c * 128, (c + 1) * 128), slice(r * 128, (r + 1) * 128))
                value = functools.reduce(jnp.add, [t[at].astype(jnp.float32) for t in terms])
                squares = squares + jnp.sum(value * value, axis=0, keepdims=True)
                out_ref[i, at[1], at[0]] = value.T.astype(jnp.bfloat16)
        square_ref[i : i + 1, :] = jnp.broadcast_to(jnp.sum(squares, axis=1, keepdims=True), (1, 128))


def finish(base, arrived):
    args = [x for i in (0, 1) for x in (resident(base[i]), *arrived[i])]
    cols, rows = base[0].shape
    return pl.pallas_call(
        functools.partial(finish_kernel, [len(a) for a in arrived]),
        in_specs=[VMEM] * len(args),
        out_specs=[VMEM] * 2,
        out_shape=[jax.ShapeDtypeStruct((2, rows, cols), jnp.bfloat16), jax.ShapeDtypeStruct((8, 128), jnp.float32)],
        compiler_params=params(8),
        cost_estimate=COST,
        name="finish",
    )(*args)


def fetch_kernel(masks, idx_ref, *refs):
    refs = list(refs)
    pieces = [[refs.pop(0) for _ in range(1 if is_whole(m) else 2)] for m in masks]
    ref_hbm, _, w, r, sem = refs
    rows = r.shape[2]
    copies = []
    for n, mask in enumerate(masks):
        at = pl.ds(pl.multiple_of((idx_ref[0] ^ mask) * rows, rows), rows)
        copies += read_rows(pieces[n], w.at[n], [sem.at[i, n] for i in (0, 1)])
        copies.append(pltpu.make_async_copy(ref_hbm.at[:, at, :], r.at[n], sem.at[2, n]))
    for copy in copies:
        copy.start()
    for copy in copies:
        copy.wait()


def fetch(idx, weights, reference, masks, earlier):
    rows, cols = weights[masks[0]][0].shape[-2:]
    count = len(masks)
    args = [idx] + [w for m in masks for w in weights[m]] + [in_hbm(reference), earlier]
    return pl.pallas_call(
        functools.partial(fetch_kernel, tuple(masks)),
        in_specs=[SMEM] + [HBM] * (len(args) - 1),
        out_specs=[VMEM] * 2,
        out_shape=[pltpu.VMEM((count, 2, rows, cols), jnp.bfloat16)] * 2,
        scratch_shapes=[pltpu.SemaphoreType.DMA((3, count))],
        compiler_params=params(4),
        cost_estimate=COST,
        name="fetch",
    )(*args)


def blend_kernel(masks, first, ready, idx_ref, square_ref, *refs):
    refs = list(refs)
    count = len(masks)
    grads = [[refs.pop(0) for _ in range(1 if is_whole(m) else 2)] for m in masks]
    if ready is None:
        weights = [[refs.pop(0) for _ in range(1 if is_whole(m) else 2)] for m in masks]
        ref_hbm = refs.pop(0)
    else:
        w, r = refs.pop(0), refs.pop(0)
    if not first:
        refs.pop(0)
    out_hbm, token_ref = refs.pop(0), refs.pop(0)
    new_hbm = refs.pop(0) if first else None
    if ready is None:
        w, r = refs.pop(0), refs.pop(0)
    g, o, new, sem, out_sem = refs
    rows, cols = g.shape[2:]
    step = 64
    half = rows // 2
    token_ref[...] = jnp.zeros_like(token_ref)

    def reads(n):
        slot = n % 2
        at = pl.ds(pl.multiple_of((idx_ref[0] ^ masks[n]) * rows, rows), rows)
        group = read_rows(grads[n], g.at[slot], [sem.at[i, slot] for i in (0, 1)])
        if ready is None:
            group += read_rows(weights[n], w.at[slot], [sem.at[2 + i, slot] for i in (0, 1)])
            group.append(pltpu.make_async_copy(ref_hbm.at[:, at, :], r.at[slot], sem.at[4, slot]))
        for copy in group:
            copy.start()
        return group

    mean = square_ref[...] * (1.0 / (D * KVH * HD))
    scale = jnp.concatenate([learning_rate * lax.rsqrt(mean + norm_eps)] * (cols // 128), axis=1)
    coming = {n: reads(n) for n in range(min(2, count))}
    writes = {}
    for n in range(count):
        slot = n % 2
        held = slot if ready is None else ready + n
        for copy in coming[n] + writes.pop(n - 2, []):
            copy.wait()
        writes[n] = []
        for part in range(2):

            def mix(t, carry):
                j = pl.ds(pl.multiple_of(part * half + t * step, step), step)
                for i in (0, 1):
                    value = w[held, i, j].astype(jnp.float32) - scale[i : i + 1, :] * g[slot, i, j].astype(jnp.float32)
                    value = value.astype(jnp.bfloat16)
                    if first and n == 0:
                        new[i, j] = value
                    mixed = mix_alpha * value.astype(jnp.float32) + (1.0 - mix_alpha) * r[held, i, j].astype(jnp.float32)
                    o[slot, i, j] = mixed.astype(jnp.bfloat16)
                return carry

            lax.fori_loop(0, half // step, mix, 0)
            at = pl.ds(pl.multiple_of((idx_ref[0] ^ masks[n]) * rows + part * half, half), half)
            copy = pltpu.make_async_copy(o.at[slot, :, pl.ds(part * half, half), :], out_hbm.at[:, at, :], out_sem.at[part, slot])
            copy.start()
            writes[n].append(copy)
        if first and n == 0:
            copy = pltpu.make_async_copy(new, new_hbm, out_sem.at[0, 2])
            copy.start()
            writes[n].append(copy)
        if n + 2 < count:
            coming[n + 2] = reads(n + 2)
    for group in writes.values():
        for copy in group:
            copy.wait()


def blend(idx, squares, weights, grads, reference, held, masks, ready=None):
    rows, cols = weights[masks[0]][0].shape[-2:]
    count = len(masks)
    first = held is None
    args = [idx, squares] + [x for m in masks for x in grads[m]]
    in_specs = [SMEM, VMEM] + [HBM] * (len(args) - 2)
    block = pltpu.VMEM((min(count, 2), 2, rows, cols), jnp.bfloat16)
    scratch = [block, block, pltpu.VMEM((2, rows, cols) if first else (8, 128), jnp.bfloat16)]
    scratch += [pltpu.SemaphoreType.DMA((5, 2)), pltpu.SemaphoreType.DMA((2, 3))]
    if ready is None:
        extra = [w for m in masks for w in weights[m]] + [in_hbm(reference)]
        args += extra
        in_specs += [HBM] * len(extra)
        scratch = [block, block] + scratch
    else:
        args += [resident(x) for x in ready[0]]
        in_specs += [VMEM] * 2
    out_specs = [HBM, VMEM]
    out_shape = [jax.ShapeDtypeStruct(reference.shape, jnp.bfloat16), jax.ShapeDtypeStruct((8, 128), jnp.float32)]
    aliases = {}
    if first:
        out_specs.append(HBM)
        out_shape.append(jax.ShapeDtypeStruct((2, rows, cols), jnp.bfloat16))
    else:
        aliases = {len(args): 0}
        in_specs.append(HBM)
        args.append(held)
    return pl.pallas_call(
        functools.partial(blend_kernel, tuple(masks), first, None if ready is None else ready[1]),
        in_specs=in_specs,
        out_specs=out_specs,
        out_shape=out_shape,
        scratch_shapes=scratch,
        input_output_aliases=aliases,
        compiler_params=params(14),
        cost_estimate=COST,
        name="blend",
    )(*args)


def bits_of(mask):
    return [1 << b for b in range(mask.bit_length()) if mask >> b & 1]


def after(value, *earlier):
    return lax.optimization_barrier((value, earlier))[0]


def body(shards, tensors, hidden_in, policy_weights, reference_weights, policy_queries, reference_queries, readout, lengths):
    rows = policy_weights.shape[1]
    idx = lax.axis_index("shard").astype(jnp.int32).reshape(1)
    tables = jnp.asarray(rope_tables())

    def swap(x, bit, axis="shard", size=shards):
        return lax.ppermute(x, axis, [(i, i ^ bit) for i in range(size)])

    def powers(size):
        return [1 << b for b in range(size.bit_length() - 1)]

    chips = sorted(range(0, shards, 2), key=lambda m: (len(bits_of(m)), m))
    near = [m for m in chips if len(bits_of(m)) == 1]
    far = [m for m in chips if len(bits_of(m)) > 1]
    link = lambda i, m: bits_of(m)[-1] if i == 0 else bits_of(m)[0]

    def send_near(own):
        got = {m: [swap(own, m)] for m in near}
        got[0] = [own]
        got[1] = [swap(own, 1)]
        return got

    def relay(got, m, *earlier):
        got[m] = [None, None]
        for i in (0, 1):
            via = link(i, m)
            source = got[m ^ via]
            source = source[i] if len(source) == 2 else source[0][i]
            got[m][i] = swap(after(source, *earlier), via)

    def to_core(got, m, *earlier):
        got[m | 1] = [swap(after(g, *earlier), 1) for g in got[m]]

    weights = send_near(policy_weights)
    normed, ref_keys, ref_values = norm_project(idx, hidden_in, reference_weights, tables)
    (ref_margin,) = attend(lengths, reference_queries, ref_keys, ref_values, readout)
    for m in far:
        relay(weights, m, ref_margin, *[weights[k] for k in near])
    for m in near:
        to_core(weights, m, ref_margin)
    held = project(idx, normed, [0, 1], weights, None, None)
    held = project(idx, normed, [m | c for m in near for c in (0, 1)], weights, held, None if far else tables)
    if far:
        for m in far:
            to_core(weights, m, held)
        held = project(idx, normed, [m | c for m in far for c in (0, 1)], weights, held, tables)
    pol_keys, pol_values = held
    margin, probs, delta = attend(lengths, policy_queries, pol_keys, pol_values, readout, ref_margin)

    theirs = {}
    order = list(reversed(chips))
    split = max(len(far), 1)

    def other_blocks(masks, *earlier):
        blocks = gradient_blocks(idx, normed, cot, [m | 1 for m in masks], rows, None, earlier)
        theirs.update({m: swap(block, 1) for m, block in zip(masks, blocks)})
        return blocks

    received = [swap(margin, m, "tensor", tensors) for m in range(1, tensors)]
    cot = attend_back(lengths, policy_queries, pol_values, readout, probs, delta, tables)
    terms = [margin] + [after(x, cot) for x in received]
    while len(terms) > 1:
        terms = [a + b for a, b in zip(terms[::2], terms[1::2])]
    (margin,) = terms
    received = swap(margin, 1)
    margins = (margin, after(received, other_blocks(order[:split], margin)))
    other_blocks(order[split:], margins[1])

    chip_sum = {}
    arrived = {m: [[], []] for m in chips}
    waiting = []

    def send(m, i):
        payload = chip_sum[m][i]
        if arrived[m][i]:
            payload = payload.astype(jnp.float32)
            for term in arrived[m][i]:
                payload = payload + term.astype(jnp.float32)
            payload = payload.astype(jnp.bfloat16)
        via = link(i, m)
        arrived[m ^ via][i].append(swap(payload, via))
        return payload

    for masks in (order[:split], order[split:]):
        blocks = gradient_blocks(idx, normed, cot, masks, rows, (margins, theirs))
        chip_sum.update(zip(masks, blocks))
        for m in masks:
            for i in (0, 1):
                if m and not any(k ^ link(i, k) == m for k in far):
                    send(m, i)
                elif m:
                    waiting.append((m, i))
    for m, i in waiting:
        send(m, i)
    own, squares = finish(chip_sum[0], arrived[0])

    grads = send_near(own)
    for bit in powers(tensors):
        squares = squares + swap(squares, bit, "tensor", tensors)
    squares = squares + swap(squares, 1)
    terms = [squares] + [swap(squares, m) for m in chips[1:]]
    while len(terms) > 1:
        terms = [a + b for a, b in zip(terms[::2], terms[1::2])]
    for m in far:
        relay(grads, m, squares, *[grads[k] for k in near])
    (squares,) = terms
    for m in near:
        to_core(grads, m, squares)
    new_reference, token, new_policy = blend(idx, squares, weights, grads, reference_weights, None, [0, 1])
    new_reference, token = blend(idx, squares, weights, grads, reference_weights, new_reference, [m | c for m in near for c in (0, 1)])
    if far:
        ready = fetch(idx, weights, reference_weights, [m | c for c in (0, 1) for m in far], token)
        for m in far:
            to_core(grads, m, ready)
        for c in (0, 1):
            masks = [m | c for m in far]
            new_reference, token = blend(idx, squares, weights, grads, reference_weights, new_reference, masks, (ready, c * len(far)))
    return (new_policy, new_reference, margin[0, :1])


def solution(mesh):
    return jax.shard_map(
        functools.partial(body, mesh.shape["shard"], mesh.shape["tensor"]),
        mesh=mesh,
        in_specs=(
            P("shard", None),
            P(None, "shard", "tensor"),
            P(None, None, "tensor"),
            P("shard", "tensor"),
            P("shard", "tensor"),
            P("shard", "tensor"),
            P("shard"),
        ),
        out_specs=(P(None, "shard", "tensor"), P(None, None, "tensor"), P("shard")),
        check_vma=False,
    )
```

```python
import functools
import math

import jax
import jax.numpy as jnp
import numpy as np
from jax import lax
from jax.experimental import pallas as pl
from jax.experimental.pallas import tpu as pltpu
from jax.sharding import PartitionSpec as P

D = 8192
HD = 128
KVH = 8
QH = 32
LEN = 384
TILE = 128

rope_base = 1000000.0
dpo_beta = 0.1
learning_rate = 0.2
mix_alpha = 0.6
norm_eps = 1e-06
width_scale = D ** (-0.5)
logit_scale = 1.0 / math.sqrt(HD)
MIB = 1024 * 1024

NT = (((1,), (1,)), ((), ()))
NN = (((1,), (0,)), ((), ()))
TN = (((0,), (0,)), ((), ()))


def dot(a, b, dims):
    return lax.dot_general(a, b, dims, preferred_element_type=jnp.float32)


def params(mib):
    return pltpu.CompilerParams(vmem_limit_bytes=mib * MIB)


COST = pl.CostEstimate(flops=1, bytes_accessed=1, transcendentals=0)
LONG = pl.CostEstimate(flops=1, bytes_accessed=40 * 1000 * 1000, transcendentals=0)
VMEM = pl.BlockSpec(memory_space=pltpu.VMEM)
SMEM = pl.BlockSpec(memory_space=pltpu.SMEM)
HBM = pl.BlockSpec(memory_space=pl.ANY)


def resident(x):
    return pltpu.with_memory_space_constraint(x, pltpu.VMEM)


def in_hbm(x):
    return pltpu.with_memory_space_constraint(x, pltpu.HBM)


def rope_tables():
    frequency = rope_base ** (-2.0 * np.arange(HD // 2) / HD)
    angles = np.arange(LEN)[:, None] * frequency[None, :]
    cosine, sine = np.cos(angles), np.sin(angles)
    return np.stack([np.concatenate([cosine, cosine], axis=1), np.concatenate([-sine, sine], axis=1)]).astype(np.float32)


def store_heads(acc_ref, cos, sin, key_ref, value_ref):
    for s in range(key_ref.shape[0] // LEN):
        rows = slice(s * LEN, (s + 1) * LEN)
        for h in range(key_ref.shape[1] // HD):
            cols = slice(h * HD, (h + 1) * HD)
            k = acc_ref[0, rows, cols] * width_scale
            key_ref[rows, cols] = (k * cos + pltpu.roll(k, HD // 2, 1) * sin).astype(jnp.bfloat16)
    value_ref[...] = (acc_ref[1] * width_scale).astype(jnp.bfloat16)


def norm_project_kernel(idx_ref, hidden_hbm, weight_hbm, table_hbm, normed_ref, key_ref, value_ref, w, acc, part, table, in_sem, w_sem, table_sem):
    tokens = normed_ref.shape[0]
    step, width, span, chunk = 16, 512, 128, 1024
    reads = []
    for i in range(tokens // span):
        at = pl.ds(i * span, span)
        reads.append(pltpu.make_async_copy(hidden_hbm.at[at], normed_ref.at[at], in_sem.at[i]))
    loads = []
    for c in range(D // chunk):
        at = pl.ds(c * chunk, chunk)
        loads.append(pltpu.make_async_copy(weight_hbm.at[:, at, :], w.at[:, at, :], w_sem.at[c]))
    loads.append(pltpu.make_async_copy(table_hbm, table, table_sem))
    for copy in reads + loads:
        copy.start()

    def row_step(i, carry):
        at = pl.ds(pl.multiple_of(i * step, step), step)
        total = jnp.zeros((step, width), jnp.float32)
        for c in range(D // width):
            v = normed_ref[at, c * width : (c + 1) * width].astype(jnp.float32)
            total = total + v * v
        part[at, :] = functools.reduce(jnp.add, [total[:, c * 128 : (c + 1) * 128] for c in range(width // 128)])
        return carry

    for i, copy in enumerate(reads):
        copy.wait()
        lax.fori_loop(i * (span // step), (i + 1) * (span // step), row_step, 0)
    for copy in loads:
        copy.wait()
    mean = jnp.sum(part[...], axis=1, keepdims=True) * (1.0 / D)
    part[...] = jnp.broadcast_to(lax.rsqrt(mean + norm_eps), part.shape)

    def columns(c):
        return pl.ds(pl.multiple_of(c * chunk, chunk), chunk)

    def normalise(c):
        for i in range(tokens // step):
            rows = slice(i * step, (i + 1) * step)
            scale = jnp.concatenate([part[rows, :]] * (chunk // 128), axis=1)
            normed_ref[rows, columns(c)] = (normed_ref[rows, columns(c)].astype(jnp.float32) * scale).astype(jnp.bfloat16)

    def multiply(c, carry):
        for i in (0, 1):
            acc[i] += dot(normed_ref[:, columns(c)], w[i, columns(c), :], NN)

        @pl.when(c + 1 < D // chunk)
        def _():
            normalise(c + 1)

        return carry

    acc[...] = jnp.zeros_like(acc)
    normalise(0)
    lax.fori_loop(0, D // chunk, multiply, 0)
    store_heads(acc, table[0], table[1], key_ref, value_ref)


def norm_project(idx, hidden, weights, tables):
    tokens = hidden.shape[0]
    cols = weights.shape[2]
    return pl.pallas_call(
        norm_project_kernel,
        in_specs=[SMEM, HBM, HBM, HBM],
        out_specs=[VMEM, VMEM, VMEM],
        out_shape=[
            pltpu.VMEM((tokens, D), jnp.bfloat16),
            pltpu.VMEM((tokens, cols), jnp.bfloat16),
            pltpu.VMEM((tokens, cols), jnp.bfloat16),
        ],
        scratch_shapes=[
            pltpu.VMEM((2, D, cols), jnp.bfloat16),
            pltpu.VMEM((2, tokens, cols), jnp.float32),
            pltpu.VMEM((tokens, 128), jnp.float32),
            pltpu.VMEM(tables.shape, jnp.float32),
            pltpu.SemaphoreType.DMA((tokens // 128,)),
            pltpu.SemaphoreType.DMA((D // 1024,)),
            pltpu.SemaphoreType.DMA,
        ],
        compiler_params=params(16),
        cost_estimate=COST,
        name="norm_project",
    )(idx, in_hbm(hidden), in_hbm(weights), in_hbm(tables))


def is_whole(mask):
    return len(bits_of(mask >> 1)) < 2


def read_rows(sources, target, sems):
    if len(sources) == 1:
        return [pltpu.make_async_copy(sources[0], target, sems[0])]
    if len(sources[0].shape) == 2:
        return [pltpu.make_async_copy(sources[i], target.at[i], sems[i]) for i in (0, 1)]
    half = sources[0].shape[1]
    return [pltpu.make_async_copy(sources[h], target.at[:, pl.ds(h * half, half), :], sems[h]) for h in (0, 1)]


def project_kernel(masks, first, last, idx_ref, x_ref, *refs):
    refs = list(refs)
    count = len(masks)
    pieces = [[refs.pop(0) for _ in range(1 if is_whole(m) else 2)] for m in masks]
    held = None if first else refs.pop(0)
    if last:
        table_hbm, key_ref, value_ref, w, acc, table, sem, table_sem = refs
        table_copy = pltpu.make_async_copy(table_hbm, table, table_sem)
        table_copy.start()
    else:
        acc, w, sem = refs
    depth = w.shape[2]
    copies = [read_rows(pieces[n], w.at[n], [sem.at[i, n] for i in (0, 1)]) for n in range(count)]
    for group in copies:
        for copy in group:
            copy.start()
    for n in range(count):
        for copy in copies[n]:
            copy.wait()
        col = pl.multiple_of((idx_ref[0] ^ masks[n]) * depth, depth)
        x = x_ref[:, pl.ds(col, depth)]
        for i in (0, 1):
            term = dot(x, w[n, i], NN)
            if n:
                term = acc[i] + term
            elif not first:
                term = held[i] + term
            acc[i] = term
    if last:
        table_copy.wait()
        store_heads(acc, table[0], table[1], key_ref, value_ref)


def project(idx, normed, masks, pieces, held, tables):
    tokens = normed.shape[0]
    rows, cols = pieces[masks[0]][0].shape[-2:]
    first, last = held is None, tables is not None
    count = len(masks)
    args = [idx, resident(normed)] + [w for m in masks for w in pieces[m]]
    in_specs = [SMEM, VMEM] + [HBM] * (len(args) - 2)
    if not first:
        in_specs.append(VMEM)
        args.append(resident(held))
    acc_shape = (2, tokens, cols)
    scratch = [pltpu.VMEM((count, 2, rows, cols), jnp.bfloat16), pltpu.SemaphoreType.DMA((2, count))]
    if last:
        in_specs.append(HBM)
        args.append(in_hbm(tables))
        out_specs = [VMEM] * 2
        out_shape = [pltpu.VMEM((tokens, cols), jnp.bfloat16)] * 2
        scratch.insert(1, pltpu.VMEM(acc_shape, jnp.float32))
        scratch.insert(2, pltpu.VMEM(tables.shape, jnp.float32))
        scratch.append(pltpu.SemaphoreType.DMA)
    else:
        out_specs = VMEM
        out_shape = pltpu.VMEM(acc_shape, jnp.float32)
    return pl.pallas_call(
        functools.partial(project_kernel, tuple(masks), first, last),
        in_specs=in_specs,
        out_specs=out_specs,
        out_shape=out_shape,
        scratch_shapes=scratch,
        compiler_params=params(10),
        cost_estimate=COST,
        name="project",
    )(*args)


HEADS = 2


def stacked(ref, row, col, r, first, count):
    rows = pl.ds(pl.multiple_of(row + r * TILE, TILE), TILE)
    at = lambda g: pl.ds(pl.multiple_of(col + g * HD, HD), HD)
    return jnp.concatenate([ref[rows, at(g)] for g in range(first, first + count)], axis=0)


def live_readout(ref, row, col, r, first, count, length):
    x = stacked(ref, row, col, r, first, count).astype(jnp.float32)
    at = lax.broadcasted_iota(jnp.int32, x.shape, 0) % TILE + r * TILE
    return jnp.where(at < length, x, 0.0).astype(jnp.bfloat16)


def places(step, q_ref, k_ref):
    heads = k_ref.shape[1] // HD
    seq, h = step // heads, step % heads
    return seq, h, seq * LEN, pl.multiple_of(h * HD, HD), h * (q_ref.shape[1] // heads)


def attend_kernel(keep, len_ref, q_ref, k_ref, v_ref, ro_ref, *rest):
    groups = q_ref.shape[1] // k_ref.shape[1]
    count = min(groups, HEADS)
    if keep:
        before_ref, margin_ref, prob_ref, delta_ref = rest
    else:
        (margin_ref,) = rest

    def one(step, margin):
        seq, h, row, col, q_col = places(step, q_ref, k_ref)
        length = len_ref[seq]
        score = jnp.zeros((1, count * TILE), jnp.float32)
        j = lax.broadcasted_iota(jnp.int32, (TILE, count * TILE), 0)
        i = lax.broadcasted_iota(jnp.int32, (TILE, count * TILE), 1) % TILE
        base = 0
        for r in range(LEN // TILE):
            n = (r + 1) * TILE
            keys = (pl.ds(pl.multiple_of(row, TILE), n), pl.ds(col, HD))
            for g in range(0, groups, count):
                q = stacked(q_ref, row, q_col, r, g, count)
                ro = live_readout(ro_ref, row, q_col, r, g, count, length)
                s = dot(k_ref[keys], q, NT)
                dp = dot(v_ref[keys], ro, NT)
                s = [s[b * TILE : (b + 1) * TILE] for b in range(r + 1)]
                s[r] = jnp.where(j <= i, s[r], -1e30)
                top = functools.reduce(jnp.maximum, [jnp.max(x, axis=0, keepdims=True) for x in s])
                e = [jnp.exp2((x - top) * (logit_scale * math.log2(math.e))) for x in s]
                inverse = 1.0 / functools.reduce(jnp.add, [jnp.sum(x, axis=0, keepdims=True) for x in e])
                cols = slice(g * TILE, (g + count) * TILE)
                delta = jnp.zeros((1, count * TILE), jnp.float32)
                for b in range(r + 1):
                    p = (e[b] * inverse).astype(jnp.bfloat16)
                    if keep:
                        prob_ref[seq, h, base + b * TILE : base + (b + 1) * TILE, cols] = p
                    delta = delta + jnp.sum(p.astype(jnp.float32) * dp[b * TILE : (b + 1) * TILE], axis=0, keepdims=True)
                if keep:
                    delta_ref[seq, h, r : r + 1, cols] = delta
                score = score + delta
            base += n
        side = jnp.where(seq % 2 == 0, 1.0, -1.0) * (dpo_beta / math.sqrt(QH * HD))
        return margin + jnp.sum(score, axis=1, keepdims=True) * side

    steps = k_ref.shape[0] // LEN * (k_ref.shape[1] // HD)
    start = -before_ref[0:1, 0:1] if keep else jnp.zeros((1, 1), jnp.float32)
    margin_ref[...] = jnp.broadcast_to(lax.fori_loop(0, steps, one, start, unroll=min(steps, 2) if keep else 1), margin_ref.shape)


def attend(lengths, queries, keys, values, readout, before=None):
    seqs = lengths.shape[0]
    heads = keys.shape[1] // HD
    wide = queries.shape[1] // heads
    tiles = LEN // TILE
    span = TILE * tiles * (tiles + 1) // 2
    keep = before is not None
    args = [lengths] + [resident(x) for x in (queries, keys, values, readout)]
    out_shape = [jax.ShapeDtypeStruct((8, 128), jnp.float32)]
    if keep:
        args.append(before)
        out_shape += [pltpu.VMEM((seqs, heads, span, wide), jnp.bfloat16), pltpu.VMEM((seqs, heads, tiles, wide), jnp.float32)]
    return pl.pallas_call(
        functools.partial(attend_kernel, keep),
        in_specs=[SMEM] + [VMEM] * (len(args) - 1),
        out_specs=[VMEM] * len(out_shape),
        out_shape=out_shape,
        compiler_params=params(8),
        cost_estimate=COST,
        name="attend",
    )(*args)


def attend_back_kernel(len_ref, q_ref, v_ref, ro_ref, prob_ref, delta_ref, table_ref, grad_ref):
    tiles = LEN // TILE
    groups = q_ref.shape[1] // v_ref.shape[1]
    count = min(groups, HEADS)

    def one(step, carry):
        seq, h, row, col, q_col = places(step, q_ref, v_ref)
        length = len_ref[seq]
        dk = [None] * tiles
        dv = [None] * tiles
        base = 0
        for r in range(tiles):
            n = (r + 1) * TILE
            keys = (pl.ds(pl.multiple_of(row, TILE), n), pl.ds(col, HD))
            for g in range(0, groups, count):
                q = stacked(q_ref, row, q_col, r, g, count)
                ro = live_readout(ro_ref, row, q_col, r, g, count, length)
                cols = slice(g * TILE, (g + count) * TILE)
                p = prob_ref[seq, h, base : base + n, cols]
                dp = dot(v_ref[keys], ro, NT)
                ds = (p.astype(jnp.float32) * (dp - delta_ref[seq, h, r : r + 1, cols])).astype(jnp.bfloat16)
                tk = dot(ds, q, NN)
                tv = dot(p, ro, NN)
                for b in range(r + 1):
                    at = slice(b * TILE, (b + 1) * TILE)
                    dk[b] = tk[at] if dk[b] is None else dk[b] + tk[at]
                    dv[b] = tv[at] if dv[b] is None else dv[b] + tv[at]
            base += n
        scale = jnp.where(seq % 2 == 0, -1.0, 1.0) * (1.0 / math.sqrt(QH * HD))
        for b in range(tiles):
            at = slice(b * TILE, (b + 1) * TILE)
            to = (pl.ds(col, HD), pl.ds(pl.multiple_of(row + b * TILE, TILE), TILE))
            k = dk[b] * (scale * logit_scale)
            k = k * table_ref[0, at, :] - pltpu.roll(k, HD // 2, 1) * table_ref[1, at, :]
            grad_ref[(0, *to)] = k.T.astype(jnp.bfloat16)
            grad_ref[(1, *to)] = (dv[b] * scale).T.astype(jnp.bfloat16)
        return carry

    steps = v_ref.shape[0] // LEN * (v_ref.shape[1] // HD)
    lax.fori_loop(0, steps, one, 0, unroll=min(steps, 2))


def attend_back(lengths, queries, values, readout, probs, delta, tables):
    return pl.pallas_call(
        attend_back_kernel,
        in_specs=[SMEM] + [VMEM] * 6,
        out_specs=VMEM,
        out_shape=pltpu.VMEM((2,) + values.shape[::-1], jnp.bfloat16),
        compiler_params=params(8),
        cost_estimate=COST,
        name="attend_back",
    )(lengths, *[resident(x) for x in (queries, values, readout, probs, delta, tables)])


def gradient_tiles(idx, mask, x_ref, cot_ref, rows):
    cols = cot_ref.shape[1]
    both = jnp.concatenate([cot_ref[0], cot_ref[1]], axis=0)
    tile = min(rows, 256)
    for t in range(rows // tile):
        col = pl.multiple_of((idx ^ mask) * rows + t * tile, tile)
        out = dot(both, x_ref[:, pl.ds(col, tile)], NN)
        for i in (0, 1):
            yield i, t * tile, tile, out[i * cols : (i + 1) * cols]


def gradient_kernel(masks, idx_ref, x_ref, cot_ref, *outs):
    outs = outs[len(outs) - len(masks) :]
    for mask, out_ref in zip(masks, outs):
        for i, start, tile, value in gradient_tiles(idx_ref[0], mask, x_ref, cot_ref, out_ref.shape[2]):
            out_ref[i, :, start : start + tile] = value.astype(out_ref.dtype)


def merged_kernel(masks, idx_ref, x_ref, cot_ref, mine_ref, their_ref, *refs):
    count = len(masks)
    theirs_hbm, outs = refs[:count], refs[count : 3 * count]
    theirs, sem = refs[3 * count :]
    rows = theirs.shape[3]
    copies = [pltpu.make_async_copy(theirs_hbm[n], theirs.at[n], sem.at[n]) for n in range(count)]
    for copy in copies:
        copy.start()
    mine, their = (ref[0:1, :] for ref in (mine_ref, their_ref))
    mine, their = (jax.nn.sigmoid(-x) for x in (mine, their))
    for n, mask in enumerate(masks):
        copies[n].wait()
        for i, start, tile, value in gradient_tiles(idx_ref[0], mask, x_ref, cot_ref, rows):
            wide = lambda x: jnp.concatenate([x] * (tile // 128), axis=1)
            value = value * wide(mine) + theirs[n, i, :, start : start + tile].astype(jnp.float32) * wide(their)
            outs[2 * n + i][:, start : start + tile] = value.astype(outs[2 * n + i].dtype)


def gradient_blocks(idx, normed, cot, masks, rows, merge=None, earlier=()):
    _, cols, tokens = cot.shape
    args = [idx, resident(normed), resident(cot)]
    in_specs = [SMEM, VMEM, VMEM]
    scratch = []
    if merge is None:
        kernel, name = gradient_kernel, "gradient_block"
        out_shape = [jax.ShapeDtypeStruct((2, cols, rows), jnp.bfloat16) for m in masks]
        args += earlier
        in_specs += [HBM] * len(earlier)
    else:
        kernel, name = merged_kernel, "merged_block"
        margins, theirs = merge
        args += [*margins] + [theirs[m] for m in masks]
        in_specs += [VMEM] * 2 + [HBM] * len(masks)
        out_shape = [
            jax.ShapeDtypeStruct((cols, rows), jnp.bfloat16) if m else pltpu.VMEM((cols, rows), jnp.float32)
            for m in masks
            for i in (0, 1)
        ]
        scratch = [pltpu.VMEM((len(masks), 2, cols, rows), jnp.bfloat16), pltpu.SemaphoreType.DMA((len(masks),))]
    outs = pl.pallas_call(
        functools.partial(kernel, tuple(masks)),
        in_specs=in_specs,
        out_specs=[VMEM] * len(out_shape),
        out_shape=out_shape,
        scratch_shapes=scratch,
        compiler_params=params(10),
        cost_estimate=COST,
        name=name,
    )(*args)
    return outs if merge is None else [outs[2 * n : 2 * n + 2] for n in range(len(masks))]


def finish_kernel(half, counts, *refs):
    refs = list(refs)
    out_ref, square_ref = refs[-2:]
    refs = refs[:-2]
    square_ref[...] = jnp.zeros_like(square_ref)
    _, rows, cols = out_ref.shape
    for i in (0, 1):
        terms = [refs.pop(0) for _ in range(1 + counts[i])]
        squares = jnp.zeros((1, 128), jnp.float32)
        for c in range(0, cols, 128):
            for r in range(0, rows, 128):
                at = [slice(x, x + 128) for x in (r if t.shape[1] == rows else half * rows + r for t in terms)]
                value = functools.reduce(jnp.add, [t[c : c + 128, x].astype(jnp.float32) for t, x in zip(terms, at)])
                squares = squares + jnp.sum(value * value, axis=0, keepdims=True)
                out_ref[i, r : r + 128, c : c + 128] = value.T.astype(jnp.bfloat16)
        square_ref[i : i + 1, :] = jnp.broadcast_to(jnp.sum(squares, axis=1, keepdims=True), (1, 128))


def finish(base, arrived, half):
    args = [x for i in (0, 1) for x in (resident(base[i]), *arrived[i])]
    cols, rows = base[0].shape
    return pl.pallas_call(
        functools.partial(finish_kernel, half, [len(a) for a in arrived]),
        in_specs=[VMEM] * len(args),
        out_specs=[VMEM] * 2,
        out_shape=[jax.ShapeDtypeStruct((2, rows // 2, cols), jnp.bfloat16), jax.ShapeDtypeStruct((8, 128), jnp.float32)],
        compiler_params=params(8),
        cost_estimate=COST,
        name="finish",
    )(*args)


def pack_kernel(takes, *refs):
    sources, outs, sem = refs[: 2 * len(takes)], refs[2 * len(takes) + 1 : -1], refs[-1]
    copies = []
    for n, i in enumerate(takes):
        half = sources[2 * n].shape[1]
        for h in (0, 1):
            source, at = sources[2 * n + h], pl.ds(h * half, half)
            if i is None:
                copies.append(pltpu.make_async_copy(source, outs[n].at[:, at, :], sem.at[n, h]))
            else:
                copies.append(pltpu.make_async_copy(source.at[i], outs[n].at[at, :], sem.at[n, h]))
    for copy in copies:
        copy.start()
    for copy in copies:
        copy.wait()


def pack(sources, takes, earlier):
    _, half, cols = sources[0][0].shape
    shapes = [(2, 2 * half, cols) if i is None else (2 * half, cols) for i in takes]
    return pl.pallas_call(
        functools.partial(pack_kernel, tuple(takes)),
        in_specs=[HBM] * (2 * len(takes) + 1),
        out_specs=[HBM] * len(takes),
        out_shape=[jax.ShapeDtypeStruct(shape, jnp.bfloat16) for shape in shapes],
        scratch_shapes=[pltpu.SemaphoreType.DMA((len(takes), 2))],
        compiler_params=params(2),
        cost_estimate=COST,
        name="pack",
    )(*[x for pair in sources for x in pair], earlier)


def fetch_kernel(masks, idx_ref, *refs):
    refs = list(refs)
    pieces = [[refs.pop(0) for _ in range(1 if is_whole(m) else 2)] for m in masks]
    ref_hbm, _, w, r, sem = refs
    rows = r.shape[2]
    copies = []
    for n, mask in enumerate(masks):
        at = pl.ds(pl.multiple_of((idx_ref[0] ^ mask) * rows, rows), rows)
        copies += read_rows(pieces[n], w.at[n], [sem.at[i, n] for i in (0, 1)])
        copies.append(pltpu.make_async_copy(ref_hbm.at[:, at, :], r.at[n], sem.at[2, n]))
    for copy in copies:
        copy.start()
    for copy in copies:
        copy.wait()


def fetch(idx, weights, reference, masks, earlier):
    rows, cols = weights[masks[0]][0].shape[-2:]
    count = len(masks)
    args = [idx] + [w for m in masks for w in weights[m]] + [in_hbm(reference), earlier]
    return pl.pallas_call(
        functools.partial(fetch_kernel, tuple(masks)),
        in_specs=[SMEM] + [HBM] * (len(args) - 1),
        out_specs=[VMEM] * 2,
        out_shape=[pltpu.VMEM((count, 2, rows, cols), jnp.bfloat16)] * 2,
        scratch_shapes=[pltpu.SemaphoreType.DMA((3, count))],
        compiler_params=params(4),
        cost_estimate=COST,
        name="fetch",
    )(*args)


def blend_kernel(masks, first, ready, idx_ref, square_ref, *refs):
    refs = list(refs)
    count = len(masks)
    grads = [[refs.pop(0) for _ in range(1 if m & 1 and is_whole(m) else 2)] for m in masks]
    if ready is None:
        weights = [[refs.pop(0) for _ in range(1 if is_whole(m) else 2)] for m in masks]
        ref_hbm = refs.pop(0)
    else:
        w, r = refs.pop(0), refs.pop(0)
    if not first:
        refs.pop(0)
    out_hbm, token_ref = refs.pop(0), refs.pop(0)
    new_hbm = refs.pop(0) if first else None
    if ready is None:
        w, r = refs.pop(0), refs.pop(0)
    g, o, new, sem, out_sem = refs
    rows, cols = g.shape[2:]
    step = 64
    half = rows // 2
    token_ref[...] = jnp.zeros_like(token_ref)

    def reads(n):
        slot = n % 2
        at = pl.ds(pl.multiple_of((idx_ref[0] ^ masks[n]) * rows, rows), rows)
        group = read_rows(grads[n], g.at[slot], [sem.at[i, slot] for i in (0, 1)])
        if ready is None:
            group += read_rows(weights[n], w.at[slot], [sem.at[2 + i, slot] for i in (0, 1)])
            group.append(pltpu.make_async_copy(ref_hbm.at[:, at, :], r.at[slot], sem.at[4, slot]))
        for copy in group:
            copy.start()
        return group

    mean = square_ref[...] * (1.0 / (D * KVH * HD))
    scale = jnp.concatenate([learning_rate * lax.rsqrt(mean + norm_eps)] * (cols // 128), axis=1)
    coming = {n: reads(n) for n in range(min(2, count))}
    writes = {}
    for n in range(count):
        slot = n % 2
        held = slot if ready is None else ready + n
        for copy in coming[n] + writes.pop(n - 2, []):
            copy.wait()
        writes[n] = []
        for part in range(2):

            def mix(t, carry):
                j = pl.ds(pl.multiple_of(part * half + t * step, step), step)
                for i in (0, 1):
                    value = w[held, i, j].astype(jnp.float32) - scale[i : i + 1, :] * g[slot, i, j].astype(jnp.float32)
                    value = value.astype(jnp.bfloat16)
                    if first and n == 0:
                        new[i, j] = value
                    mixed = mix_alpha * value.astype(jnp.float32) + (1.0 - mix_alpha) * r[held, i, j].astype(jnp.float32)
                    o[slot, i, j] = mixed.astype(jnp.bfloat16)
                return carry

            lax.fori_loop(0, half // step, mix, 0)
            at = pl.ds(pl.multiple_of((idx_ref[0] ^ masks[n]) * rows + part * half, half), half)
            copy = pltpu.make_async_copy(o.at[slot, :, pl.ds(part * half, half), :], out_hbm.at[:, at, :], out_sem.at[part, slot])
            copy.start()
            writes[n].append(copy)
        if first and n == 0:
            copy = pltpu.make_async_copy(new, new_hbm, out_sem.at[0, 2])
            copy.start()
            writes[n].append(copy)
        if n + 2 < count:
            coming[n + 2] = reads(n + 2)
    for group in writes.values():
        for copy in group:
            copy.wait()


def blend(idx, squares, weights, grads, reference, held, masks, ready=None):
    rows, cols = weights[masks[0]][0].shape[-2:]
    count = len(masks)
    first = held is None
    args = [idx, squares] + [x for m in masks for x in grads[m]]
    in_specs = [SMEM, VMEM] + [HBM] * (len(args) - 2)
    block = pltpu.VMEM((min(count, 2), 2, rows, cols), jnp.bfloat16)
    scratch = [block, block, pltpu.VMEM((2, rows, cols) if first else (8, 128), jnp.bfloat16)]
    scratch += [pltpu.SemaphoreType.DMA((5, 2)), pltpu.SemaphoreType.DMA((2, 3))]
    if ready is None:
        extra = [w for m in masks for w in weights[m]] + [in_hbm(reference)]
        args += extra
        in_specs += [HBM] * len(extra)
        scratch = [block, block] + scratch
    else:
        args += [resident(x) for x in ready[0]]
        in_specs += [VMEM] * 2
    out_specs = [HBM, VMEM]
    out_shape = [jax.ShapeDtypeStruct(reference.shape, jnp.bfloat16), jax.ShapeDtypeStruct((8, 128), jnp.float32)]
    aliases = {}
    if first:
        out_specs.append(HBM)
        out_shape.append(jax.ShapeDtypeStruct((2, rows, cols), jnp.bfloat16))
    else:
        aliases = {len(args): 0}
        in_specs.append(HBM)
        args.append(held)
    return pl.pallas_call(
        functools.partial(blend_kernel, tuple(masks), first, None if ready is None else ready[1]),
        in_specs=in_specs,
        out_specs=out_specs,
        out_shape=out_shape,
        scratch_shapes=scratch,
        input_output_aliases=aliases,
        compiler_params=params(14),
        cost_estimate=COST,
        name="blend",
    )(*args)


def bits_of(mask):
    return [1 << b for b in range(mask.bit_length()) if mask >> b & 1]


def after(value, *earlier):
    return lax.optimization_barrier((value, earlier))[0]


def body(shards, tensors, hidden_in, policy_weights, reference_weights, policy_queries, reference_queries, readout, lengths):
    rows = policy_weights.shape[1]
    idx = lax.axis_index("shard").astype(jnp.int32).reshape(1)
    tables = jnp.asarray(rope_tables())

    def swap(x, bit, axis="shard", size=shards):
        return lax.ppermute(x, axis, [(i, i ^ bit) for i in range(size)])

    def powers(size):
        return [1 << b for b in range(size.bit_length() - 1)]

    chips = sorted(range(0, shards, 2), key=lambda m: (len(bits_of(m)), m))
    near = [m for m in chips if len(bits_of(m)) == 1]
    far = [m for m in chips if len(bits_of(m)) > 1]
    link = lambda i, m: bits_of(m)[-1] if i == 0 else bits_of(m)[0]

    def send_near(own):
        got = {m: [swap(own, m)] for m in near}
        got[0] = [own]
        got[1] = [swap(own, 1)]
        return got

    def relay(got, m, *earlier):
        got[m] = [None, None]
        for i in (0, 1):
            via = link(i, m)
            source = got[m ^ via]
            source = source[i] if source[0].ndim == 2 else source[0][i]
            got[m][i] = swap(after(source, *earlier), via)

    def to_core(got, m, *earlier):
        got[m | 1] = [swap(after(g, *earlier), 1) for g in got[m]]

    weights = send_near(policy_weights)
    normed, ref_keys, ref_values = norm_project(idx, hidden_in, reference_weights, tables)
    (ref_margin,) = attend(lengths, reference_queries, ref_keys, ref_values, readout)
    for m in far:
        relay(weights, m, ref_margin, *[weights[k] for k in near])
    for m in near:
        to_core(weights, m, ref_margin)
    held = project(idx, normed, [0, 1], weights, None, None)
    held = project(idx, normed, [m | c for m in near for c in (0, 1)], weights, held, None if far else tables)
    if far:
        for m in far:
            to_core(weights, m, held)
        held = project(idx, normed, [m | c for m in far for c in (0, 1)], weights, held, tables)
    pol_keys, pol_values = held
    margin, probs, delta = attend(lengths, policy_queries, pol_keys, pol_values, readout, ref_margin)

    theirs = {}
    order = list(reversed(chips))
    split = max(len(far), 1)

    def other_blocks(masks, *earlier):
        blocks = gradient_blocks(idx, normed, cot, [m | 1 for m in masks], rows, None, earlier)
        theirs.update({m: swap(block, 1) for m, block in zip(masks, blocks)})
        return blocks

    received = [swap(margin, m, "tensor", tensors) for m in range(1, tensors)]
    cot = attend_back(lengths, policy_queries, pol_values, readout, probs, delta, tables)
    terms = [margin] + [after(x, cot) for x in received]
    while len(terms) > 1:
        terms = [a + b for a, b in zip(terms[::2], terms[1::2])]
    (margin,) = terms
    received = swap(margin, 1)
    margins = (margin, after(received, other_blocks(order[:split], margin)))
    other_blocks(order[split:], margins[1])

    chip_sum = {}
    arrived = {m: ([], []) for m in chips}
    halves = ([[], []], [[], []])
    waiting = []

    def send(m, i, half=None):
        terms = [chip_sum[m][i], *arrived[m][i]]
        if half is not None:
            terms = [t[:, half * rows // 2 : (half + 1) * rows // 2] for t in terms]
        payload = terms[0]
        if len(terms) > 1:
            payload = sum(t.astype(jnp.float32) for t in terms).astype(jnp.bfloat16)
        via = link(i, m)
        received = swap(payload, via)
        if half is None:
            arrived[m ^ via][i].append(received)
        else:
            halves[half][i].append(received)

    for masks in (order[:split], order[split:]):
        chip_sum.update(zip(masks, gradient_blocks(idx, normed, cot, masks, rows, (margins, theirs))))
        for m in masks:
            for i in (0, 1):
                if m and not any(k ^ link(i, k) == m for k in far):
                    send(m, i)
                elif m:
                    waiting.append((m, i))
    for m, i in waiting:
        if m in far:
            send(m, i)

    for half in (0, 1):
        for m, i in waiting:
            if m in near:
                send(m, i, half)
    grads = {m: [] for m in [0] + near}
    parts = []
    for half in (0, 1):
        own, part = finish(chip_sum[0], [arrived[0][i] + halves[half][i] for i in (0, 1)], half)
        parts.append(part)
        grads[0].append(own)
        for m in near:
            grads[m].append(swap(own, m))
    squares = parts[0] + parts[1]
    for bit in powers(tensors):
        squares = squares + swap(squares, bit, "tensor", tensors)
    squares = squares + swap(squares, 1)
    total = squares
    for bit in powers(shards)[1:]:
        total = total + swap(total, bit)
    squares = total
    two = [m for m in far if len(bits_of(m)) == 2]
    ends = [(m, i) for m in two for i in (0, 1)]
    whole = [0] + near
    packed = pack([grads[m ^ link(i, m)] for m, i in ends] + [grads[m] for m in whole], [i for m, i in ends] + [None] * len(whole), total)
    packed = dict(zip(ends + whole, packed))
    for m in far:
        grads[m] = [swap(packed[m, i] if m in two else grads[m ^ link(i, m)][i], link(i, m)) for i in (0, 1)]
    for m in whole:
        grads[m | 1] = [swap(packed[m], 1)]
    new_reference, token, new_policy = blend(idx, squares, weights, grads, reference_weights, None, [0, 1])
    new_reference, token = blend(idx, squares, weights, grads, reference_weights, new_reference, [m | c for m in near for c in (0, 1)])
    if far:
        ready = fetch(idx, weights, reference_weights, [m | c for c in (0, 1) for m in far], token)
        for m in far:
            to_core(grads, m, ready)
        for c in (0, 1):
            masks = [m | c for m in far]
            new_reference, token = blend(idx, squares, weights, grads, reference_weights, new_reference, masks, (ready, c * len(far)))
    return (new_policy, new_reference, margin[0, :1])


def solution(mesh):
    return jax.shard_map(
        functools.partial(body, mesh.shape["shard"], mesh.shape["tensor"]),
        mesh=mesh,
        in_specs=(
            P("shard", None),
            P(None, "shard", "tensor"),
            P(None, None, "tensor"),
            P("shard", "tensor"),
            P("shard", "tensor"),
            P("shard", "tensor"),
            P("shard"),
        ),
        out_specs=(P(None, "shard", "tensor"), P(None, None, "tensor"), P("shard")),
        check_vma=False,
    )
```

```python
import functools
import math

import jax
import jax.numpy as jnp
import numpy as np
from jax import lax
from jax.experimental import pallas as pl
from jax.experimental.pallas import tpu as pltpu
from jax.sharding import PartitionSpec as P

D = 8192
HD = 128
KVH = 8
QH = 32
LEN = 384
TILE = 128

rope_base = 1000000.0
dpo_beta = 0.1
learning_rate = 0.2
mix_alpha = 0.6
norm_eps = 1e-06
width_scale = D ** (-0.5)
logit_scale = 1.0 / math.sqrt(HD)
MIB = 1024 * 1024

NT = (((1,), (1,)), ((), ()))
NN = (((1,), (0,)), ((), ()))
TN = (((0,), (0,)), ((), ()))


def dot(a, b, dims):
    return lax.dot_general(a, b, dims, preferred_element_type=jnp.float32)


def params(mib):
    return pltpu.CompilerParams(vmem_limit_bytes=mib * MIB)


COST = pl.CostEstimate(flops=1, bytes_accessed=1, transcendentals=0)
LONG = pl.CostEstimate(flops=1, bytes_accessed=40 * 1000 * 1000, transcendentals=0)
VMEM = pl.BlockSpec(memory_space=pltpu.VMEM)
SMEM = pl.BlockSpec(memory_space=pltpu.SMEM)
HBM = pl.BlockSpec(memory_space=pl.ANY)


def resident(x):
    return pltpu.with_memory_space_constraint(x, pltpu.VMEM)


def in_hbm(x):
    return pltpu.with_memory_space_constraint(x, pltpu.HBM)


def rope_tables():
    frequency = rope_base ** (-2.0 * np.arange(HD // 2) / HD)
    angles = np.arange(LEN)[:, None] * frequency[None, :]
    cosine, sine = np.cos(angles), np.sin(angles)
    return np.stack([np.concatenate([cosine, cosine], axis=1), np.concatenate([-sine, sine], axis=1)]).astype(np.float32)


def store_heads(acc_ref, cos, sin, key_ref, value_ref):
    for s in range(key_ref.shape[0] // LEN):
        rows = slice(s * LEN, (s + 1) * LEN)
        for h in range(key_ref.shape[1] // HD):
            cols = slice(h * HD, (h + 1) * HD)
            k = acc_ref[0, rows, cols] * width_scale
            key_ref[rows, cols] = (k * cos + pltpu.roll(k, HD // 2, 1) * sin).astype(jnp.bfloat16)
    value_ref[...] = (acc_ref[1] * width_scale).astype(jnp.bfloat16)


def norm_project_kernel(idx_ref, hidden_hbm, weight_hbm, table_hbm, normed_ref, key_ref, value_ref, w, acc, part, table, in_sem, w_sem, table_sem):
    tokens = normed_ref.shape[0]
    step, width, span, chunk = 16, 512, 128, 1024
    reads = []
    for i in range(tokens // span):
        at = pl.ds(i * span, span)
        reads.append(pltpu.make_async_copy(hidden_hbm.at[at], normed_ref.at[at], in_sem.at[i]))
    loads = []
    for c in range(D // chunk):
        at = pl.ds(c * chunk, chunk)
        loads.append(pltpu.make_async_copy(weight_hbm.at[:, at, :], w.at[:, at, :], w_sem.at[c]))
    loads.append(pltpu.make_async_copy(table_hbm, table, table_sem))
    for copy in reads + loads:
        copy.start()

    def row_step(i, carry):
        at = pl.ds(pl.multiple_of(i * step, step), step)
        total = jnp.zeros((step, width), jnp.float32)
        for c in range(D // width):
            v = normed_ref[at, c * width : (c + 1) * width].astype(jnp.float32)
            total = total + v * v
        part[at, :] = functools.reduce(jnp.add, [total[:, c * 128 : (c + 1) * 128] for c in range(width // 128)])
        return carry

    for i, copy in enumerate(reads):
        copy.wait()
        lax.fori_loop(i * (span // step), (i + 1) * (span // step), row_step, 0)
    for copy in loads:
        copy.wait()
    mean = jnp.sum(part[...], axis=1, keepdims=True) * (1.0 / D)
    part[...] = jnp.broadcast_to(lax.rsqrt(mean + norm_eps), part.shape)

    def columns(c):
        return pl.ds(pl.multiple_of(c * chunk, chunk), chunk)

    def normalise(c):
        for i in range(tokens // step):
            rows = slice(i * step, (i + 1) * step)
            scale = jnp.concatenate([part[rows, :]] * (chunk // 128), axis=1)
            normed_ref[rows, columns(c)] = (normed_ref[rows, columns(c)].astype(jnp.float32) * scale).astype(jnp.bfloat16)

    def multiply(c, carry):
        for i in (0, 1):
            acc[i] += dot(normed_ref[:, columns(c)], w[i, columns(c), :], NN)

        @pl.when(c + 1 < D // chunk)
        def _():
            normalise(c + 1)

        return carry

    acc[...] = jnp.zeros_like(acc)
    normalise(0)
    lax.fori_loop(0, D // chunk, multiply, 0)
    store_heads(acc, table[0], table[1], key_ref, value_ref)


def norm_project(idx, hidden, weights, tables):
    tokens = hidden.shape[0]
    cols = weights.shape[2]
    return pl.pallas_call(
        norm_project_kernel,
        in_specs=[SMEM, HBM, HBM, HBM],
        out_specs=[VMEM, VMEM, VMEM],
        out_shape=[
            pltpu.VMEM((tokens, D), jnp.bfloat16),
            pltpu.VMEM((tokens, cols), jnp.bfloat16),
            pltpu.VMEM((tokens, cols), jnp.bfloat16),
        ],
        scratch_shapes=[
            pltpu.VMEM((2, D, cols), jnp.bfloat16),
            pltpu.VMEM((2, tokens, cols), jnp.float32),
            pltpu.VMEM((tokens, 128), jnp.float32),
            pltpu.VMEM(tables.shape, jnp.float32),
            pltpu.SemaphoreType.DMA((tokens // 128,)),
            pltpu.SemaphoreType.DMA((D // 1024,)),
            pltpu.SemaphoreType.DMA,
        ],
        compiler_params=params(16),
        cost_estimate=COST,
        name="norm_project",
    )(idx, in_hbm(hidden), in_hbm(weights), in_hbm(tables))


def is_whole(mask):
    return len(bits_of(mask >> 1)) < 2


def read_rows(sources, target, sems):
    if len(sources) == 1:
        return [pltpu.make_async_copy(sources[0], target, sems[0])]
    if len(sources[0].shape) == 2:
        return [pltpu.make_async_copy(sources[i], target.at[i], sems[i]) for i in (0, 1)]
    half = sources[0].shape[1]
    return [pltpu.make_async_copy(sources[h], target.at[:, pl.ds(h * half, half), :], sems[h]) for h in (0, 1)]


def project_kernel(masks, first, last, idx_ref, x_ref, *refs):
    refs = list(refs)
    count = len(masks)
    pieces = [[refs.pop(0) for _ in range(1 if is_whole(m) else 2)] for m in masks]
    held = None if first else refs.pop(0)
    if last:
        table_hbm, key_ref, value_ref, w, acc, table, sem, table_sem = refs
        table_copy = pltpu.make_async_copy(table_hbm, table, table_sem)
        table_copy.start()
    else:
        acc, w, sem = refs
    depth = w.shape[2]
    copies = [read_rows(pieces[n], w.at[n], [sem.at[i, n] for i in (0, 1)]) for n in range(count)]
    for group in copies:
        for copy in group:
            copy.start()
    for n in range(count):
        for copy in copies[n]:
            copy.wait()
        col = pl.multiple_of((idx_ref[0] ^ masks[n]) * depth, depth)
        x = x_ref[:, pl.ds(col, depth)]
        for i in (0, 1):
            term = dot(x, w[n, i], NN)
            if n:
                term = acc[i] + term
            elif not first:
                term = held[i] + term
            acc[i] = term
    if last:
        table_copy.wait()
        store_heads(acc, table[0], table[1], key_ref, value_ref)


def project(idx, normed, masks, pieces, held, tables):
    tokens = normed.shape[0]
    rows, cols = pieces[masks[0]][0].shape[-2:]
    first, last = held is None, tables is not None
    count = len(masks)
    args = [idx, resident(normed)] + [w for m in masks for w in pieces[m]]
    in_specs = [SMEM, VMEM] + [HBM] * (len(args) - 2)
    if not first:
        in_specs.append(VMEM)
        args.append(resident(held))
    acc_shape = (2, tokens, cols)
    scratch = [pltpu.VMEM((count, 2, rows, cols), jnp.bfloat16), pltpu.SemaphoreType.DMA((2, count))]
    if last:
        in_specs.append(HBM)
        args.append(in_hbm(tables))
        out_specs = [VMEM] * 2
        out_shape = [pltpu.VMEM((tokens, cols), jnp.bfloat16)] * 2
        scratch.insert(1, pltpu.VMEM(acc_shape, jnp.float32))
        scratch.insert(2, pltpu.VMEM(tables.shape, jnp.float32))
        scratch.append(pltpu.SemaphoreType.DMA)
    else:
        out_specs = VMEM
        out_shape = pltpu.VMEM(acc_shape, jnp.float32)
    return pl.pallas_call(
        functools.partial(project_kernel, tuple(masks), first, last),
        in_specs=in_specs,
        out_specs=out_specs,
        out_shape=out_shape,
        scratch_shapes=scratch,
        compiler_params=params(10),
        cost_estimate=COST,
        name="project",
    )(*args)


HEADS = 2


def stacked(ref, row, col, r, first, count):
    rows = pl.ds(pl.multiple_of(row + r * TILE, TILE), TILE)
    at = lambda g: pl.ds(pl.multiple_of(col + g * HD, HD), HD)
    return jnp.concatenate([ref[rows, at(g)] for g in range(first, first + count)], axis=0)


def live_readout(ref, row, col, r, first, count, length):
    x = stacked(ref, row, col, r, first, count).astype(jnp.float32)
    at = lax.broadcasted_iota(jnp.int32, x.shape, 0) % TILE + r * TILE
    return jnp.where(at < length, x, 0.0).astype(jnp.bfloat16)


def places(step, q_ref, k_ref):
    heads = k_ref.shape[1] // HD
    seq, h = step // heads, step % heads
    return seq, h, seq * LEN, pl.multiple_of(h * HD, HD), h * (q_ref.shape[1] // heads)


def attend_kernel(keep, len_ref, q_ref, k_ref, v_ref, ro_ref, *rest):
    groups = q_ref.shape[1] // k_ref.shape[1]
    count = min(groups, HEADS)
    if keep:
        before_ref, margin_ref, prob_ref, delta_ref = rest
    else:
        (margin_ref,) = rest

    def one(step, margin):
        seq, h, row, col, q_col = places(step, q_ref, k_ref)
        length = len_ref[seq]
        score = jnp.zeros((1, count * TILE), jnp.float32)
        j = lax.broadcasted_iota(jnp.int32, (TILE, count * TILE), 0)
        i = lax.broadcasted_iota(jnp.int32, (TILE, count * TILE), 1) % TILE
        base = 0
        for r in range(LEN // TILE):
            n = (r + 1) * TILE
            keys = (pl.ds(pl.multiple_of(row, TILE), n), pl.ds(col, HD))
            for g in range(0, groups, count):
                q = stacked(q_ref, row, q_col, r, g, count)
                ro = live_readout(ro_ref, row, q_col, r, g, count, length)
                s = dot(k_ref[keys], q, NT)
                dp = dot(v_ref[keys], ro, NT)
                s = [s[b * TILE : (b + 1) * TILE] for b in range(r + 1)]
                s[r] = jnp.where(j <= i, s[r], -1e30)
                top = functools.reduce(jnp.maximum, [jnp.max(x, axis=0, keepdims=True) for x in s])
                e = [jnp.exp2((x - top) * (logit_scale * math.log2(math.e))) for x in s]
                inverse = 1.0 / functools.reduce(jnp.add, [jnp.sum(x, axis=0, keepdims=True) for x in e])
                cols = slice(g * TILE, (g + count) * TILE)
                delta = jnp.zeros((1, count * TILE), jnp.float32)
                for b in range(r + 1):
                    p = (e[b] * inverse).astype(jnp.bfloat16)
                    if keep:
                        prob_ref[seq, h, base + b * TILE : base + (b + 1) * TILE, cols] = p
                    delta = delta + jnp.sum(p.astype(jnp.float32) * dp[b * TILE : (b + 1) * TILE], axis=0, keepdims=True)
                if keep:
                    delta_ref[seq, h, r : r + 1, cols] = delta
                score = score + delta
            base += n
        side = jnp.where(seq % 2 == 0, 1.0, -1.0) * (dpo_beta / math.sqrt(QH * HD))
        return margin + jnp.sum(score, axis=1, keepdims=True) * side

    steps = k_ref.shape[0] // LEN * (k_ref.shape[1] // HD)
    start = -before_ref[0:1, 0:1] if keep else jnp.zeros((1, 1), jnp.float32)
    margin_ref[...] = jnp.broadcast_to(lax.fori_loop(0, steps, one, start, unroll=min(steps, 2) if keep else 1), margin_ref.shape)


def attend(lengths, queries, keys, values, readout, before=None):
    seqs = lengths.shape[0]
    heads = keys.shape[1] // HD
    wide = queries.shape[1] // heads
    tiles = LEN // TILE
    span = TILE * tiles * (tiles + 1) // 2
    keep = before is not None
    args = [lengths] + [resident(x) for x in (queries, keys, values, readout)]
    out_shape = [jax.ShapeDtypeStruct((8, 128), jnp.float32)]
    if keep:
        args.append(before)
        out_shape += [pltpu.VMEM((seqs, heads, span, wide), jnp.bfloat16), pltpu.VMEM((seqs, heads, tiles, wide), jnp.float32)]
    return pl.pallas_call(
        functools.partial(attend_kernel, keep),
        in_specs=[SMEM] + [VMEM] * (len(args) - 1),
        out_specs=[VMEM] * len(out_shape),
        out_shape=out_shape,
        compiler_params=params(8),
        cost_estimate=COST,
        name="attend",
    )(*args)


def attend_back_kernel(len_ref, q_ref, v_ref, ro_ref, prob_ref, delta_ref, table_ref, grad_ref):
    tiles = LEN // TILE
    groups = q_ref.shape[1] // v_ref.shape[1]
    count = min(groups, HEADS)

    def one(step, carry):
        seq, h, row, col, q_col = places(step, q_ref, v_ref)
        length = len_ref[seq]
        dk = [None] * tiles
        dv = [None] * tiles
        base = 0
        for r in range(tiles):
            n = (r + 1) * TILE
            keys = (pl.ds(pl.multiple_of(row, TILE), n), pl.ds(col, HD))
            for g in range(0, groups, count):
                q = stacked(q_ref, row, q_col, r, g, count)
                ro = live_readout(ro_ref, row, q_col, r, g, count, length)
                cols = slice(g * TILE, (g + count) * TILE)
                p = prob_ref[seq, h, base : base + n, cols]
                dp = dot(v_ref[keys], ro, NT)
                ds = (p.astype(jnp.float32) * (dp - delta_ref[seq, h, r : r + 1, cols])).astype(jnp.bfloat16)
                tk = dot(ds, q, NN)
                tv = dot(p, ro, NN)
                for b in range(r + 1):
                    at = slice(b * TILE, (b + 1) * TILE)
                    dk[b] = tk[at] if dk[b] is None else dk[b] + tk[at]
                    dv[b] = tv[at] if dv[b] is None else dv[b] + tv[at]
            base += n
        scale = jnp.where(seq % 2 == 0, -1.0, 1.0) * (1.0 / math.sqrt(QH * HD))
        for b in range(tiles):
            at = slice(b * TILE, (b + 1) * TILE)
            to = (pl.ds(col, HD), pl.ds(pl.multiple_of(row + b * TILE, TILE), TILE))
            k = dk[b] * (scale * logit_scale)
            k = k * table_ref[0, at, :] - pltpu.roll(k, HD // 2, 1) * table_ref[1, at, :]
            grad_ref[(0, *to)] = k.T.astype(jnp.bfloat16)
            grad_ref[(1, *to)] = (dv[b] * scale).T.astype(jnp.bfloat16)
        return carry

    steps = v_ref.shape[0] // LEN * (v_ref.shape[1] // HD)
    lax.fori_loop(0, steps, one, 0, unroll=True)


def attend_back(lengths, queries, values, readout, probs, delta, tables):
    return pl.pallas_call(
        attend_back_kernel,
        in_specs=[SMEM] + [VMEM] * 6,
        out_specs=VMEM,
        out_shape=pltpu.VMEM((2,) + values.shape[::-1], jnp.bfloat16),
        compiler_params=params(8),
        cost_estimate=COST,
        name="attend_back",
    )(lengths, *[resident(x) for x in (queries, values, readout, probs, delta, tables)])


def gradient_tiles(idx, mask, x_ref, cot_ref, rows):
    cols = cot_ref.shape[1]
    both = jnp.concatenate([cot_ref[0], cot_ref[1]], axis=0)
    tile = min(rows, 256)
    for t in range(rows // tile):
        col = pl.multiple_of((idx ^ mask) * rows + t * tile, tile)
        out = dot(both, x_ref[:, pl.ds(col, tile)], NN)
        for i in (0, 1):
            yield i, t * tile, tile, out[i * cols : (i + 1) * cols]


def gradient_kernel(masks, idx_ref, x_ref, cot_ref, *outs):
    outs = outs[len(outs) - len(masks) :]
    for mask, out_ref in zip(masks, outs):
        for i, start, tile, value in gradient_tiles(idx_ref[0], mask, x_ref, cot_ref, out_ref.shape[2]):
            out_ref[i, :, start : start + tile] = value.astype(out_ref.dtype)


def merged_kernel(masks, idx_ref, x_ref, cot_ref, mine_ref, their_ref, *refs):
    count = len(masks)
    theirs_hbm, outs = refs[:count], refs[count : 3 * count]
    theirs, sem = refs[3 * count :]
    rows = theirs.shape[3]
    copies = [pltpu.make_async_copy(theirs_hbm[n], theirs.at[n], sem.at[n]) for n in range(count)]
    for copy in copies:
        copy.start()
    mine, their = (ref[0:1, :] for ref in (mine_ref, their_ref))
    mine, their = (jax.nn.sigmoid(-x) for x in (mine, their))
    for n, mask in enumerate(masks):
        copies[n].wait()
        for i, start, tile, value in gradient_tiles(idx_ref[0], mask, x_ref, cot_ref, rows):
            wide = lambda x: jnp.concatenate([x] * (tile // 128), axis=1)
            value = value * wide(mine) + theirs[n, i, :, start : start + tile].astype(jnp.float32) * wide(their)
            outs[2 * n + i][:, start : start + tile] = value.astype(outs[2 * n + i].dtype)


def gradient_blocks(idx, normed, cot, masks, rows, merge=None, earlier=()):
    _, cols, tokens = cot.shape
    args = [idx, resident(normed), resident(cot)]
    in_specs = [SMEM, VMEM, VMEM]
    scratch = []
    if merge is None:
        kernel, name = gradient_kernel, "gradient_block"
        out_shape = [jax.ShapeDtypeStruct((2, cols, rows), jnp.bfloat16) for m in masks]
        args += earlier
        in_specs += [HBM] * len(earlier)
    else:
        kernel, name = merged_kernel, "merged_block"
        margins, theirs = merge
        args += [*margins] + [theirs[m] for m in masks]
        in_specs += [VMEM] * 2 + [HBM] * len(masks)
        out_shape = [
            jax.ShapeDtypeStruct((cols, rows), jnp.bfloat16) if m else pltpu.VMEM((cols, rows), jnp.float32)
            for m in masks
            for i in (0, 1)
        ]
        scratch = [pltpu.VMEM((len(masks), 2, cols, rows), jnp.bfloat16), pltpu.SemaphoreType.DMA((len(masks),))]
    outs = pl.pallas_call(
        functools.partial(kernel, tuple(masks)),
        in_specs=in_specs,
        out_specs=[VMEM] * len(out_shape),
        out_shape=out_shape,
        scratch_shapes=scratch,
        compiler_params=params(10),
        cost_estimate=COST,
        name=name,
    )(*args)
    return outs if merge is None else [outs[2 * n : 2 * n + 2] for n in range(len(masks))]


def finish_kernel(half, counts, *refs):
    refs = list(refs)
    out_ref, square_ref = refs[-2:]
    refs = refs[:-2]
    square_ref[...] = jnp.zeros_like(square_ref)
    _, rows, cols = out_ref.shape
    for i in (0, 1):
        terms = [refs.pop(0) for _ in range(1 + counts[i])]
        squares = jnp.zeros((1, 128), jnp.float32)
        for c in range(0, cols, 128):
            for r in range(0, rows, 128):
                at = [slice(x, x + 128) for x in (r if t.shape[1] == rows else half * rows + r for t in terms)]
                value = functools.reduce(jnp.add, [t[c : c + 128, x].astype(jnp.float32) for t, x in zip(terms, at)])
                squares = squares + jnp.sum(value * value, axis=0, keepdims=True)
                out_ref[i, r : r + 128, c : c + 128] = value.T.astype(jnp.bfloat16)
        square_ref[i : i + 1, :] = jnp.broadcast_to(jnp.sum(squares, axis=1, keepdims=True), (1, 128))


def finish(base, arrived, half):
    args = [x for i in (0, 1) for x in (resident(base[i]), *arrived[i])]
    cols, rows = base[0].shape
    return pl.pallas_call(
        functools.partial(finish_kernel, half, [len(a) for a in arrived]),
        in_specs=[VMEM] * len(args),
        out_specs=[VMEM] * 2,
        out_shape=[jax.ShapeDtypeStruct((2, rows // 2, cols), jnp.bfloat16), jax.ShapeDtypeStruct((8, 128), jnp.float32)],
        compiler_params=params(8),
        cost_estimate=COST,
        name="finish",
    )(*args)


def gate_kernel(value_ref, margin_ref, *refs):
    out_ref, first_ref = refs[-2:]
    out_ref[...] = value_ref[...]
    first_ref[0] = margin_ref[0, 0]


def gate(value, margin, *earlier):
    return pl.pallas_call(
        gate_kernel,
        in_specs=[VMEM, VMEM] + [HBM] * len(earlier),
        out_specs=[VMEM, SMEM],
        out_shape=[jax.ShapeDtypeStruct(value.shape, value.dtype), jax.ShapeDtypeStruct((1,), jnp.float32)],
        compiler_params=params(2),
        cost_estimate=COST,
        name="gate",
    )(value, margin, *earlier)


def pack_kernel(takes, *refs):
    sources, outs, sem = refs[: 2 * len(takes)], refs[-1 - len(takes) : -1], refs[-1]
    copies = []
    for n, i in enumerate(takes):
        half = sources[2 * n].shape[1]
        for h in (0, 1):
            source, at = sources[2 * n + h], pl.ds(h * half, half)
            if i is None:
                copies.append(pltpu.make_async_copy(source, outs[n].at[:, at, :], sem.at[n, h]))
            else:
                copies.append(pltpu.make_async_copy(source.at[i], outs[n].at[at, :], sem.at[n, h]))
    for copy in copies:
        copy.start()
    for copy in copies:
        copy.wait()


def pack(sources, takes, *earlier):
    _, half, cols = sources[0][0].shape
    shapes = [(2, 2 * half, cols) if i is None else (2 * half, cols) for i in takes]
    return pl.pallas_call(
        functools.partial(pack_kernel, tuple(takes)),
        in_specs=[HBM] * (2 * len(takes) + len(earlier)),
        out_specs=[HBM] * len(takes),
        out_shape=[jax.ShapeDtypeStruct(shape, jnp.bfloat16) for shape in shapes],
        scratch_shapes=[pltpu.SemaphoreType.DMA((len(takes), 2))],
        compiler_params=params(2),
        cost_estimate=COST,
        name="pack",
    )(*[x for pair in sources for x in pair], *earlier)


def fetch_kernel(masks, idx_ref, *refs):
    refs = list(refs)
    pieces = [[refs.pop(0) for _ in range(1 if is_whole(m) else 2)] for m in masks]
    ref_hbm, _, w, r, sem = refs
    rows = r.shape[2]
    copies = []
    for n, mask in enumerate(masks):
        at = pl.ds(pl.multiple_of((idx_ref[0] ^ mask) * rows, rows), rows)
        copies += read_rows(pieces[n], w.at[n], [sem.at[i, n] for i in (0, 1)])
        copies.append(pltpu.make_async_copy(ref_hbm.at[:, at, :], r.at[n], sem.at[2, n]))
    for copy in copies:
        copy.start()
    for copy in copies:
        copy.wait()


def fetch(idx, weights, reference, masks, earlier):
    rows, cols = weights[masks[0]][0].shape[-2:]
    count = len(masks)
    args = [idx] + [w for m in masks for w in weights[m]] + [in_hbm(reference), earlier]
    return pl.pallas_call(
        functools.partial(fetch_kernel, tuple(masks)),
        in_specs=[SMEM] + [HBM] * (len(args) - 1),
        out_specs=[VMEM] * 2,
        out_shape=[pltpu.VMEM((count, 2, rows, cols), jnp.bfloat16)] * 2,
        scratch_shapes=[pltpu.SemaphoreType.DMA((3, count))],
        compiler_params=params(4),
        cost_estimate=COST,
        name="fetch",
    )(*args)


def blend_kernel(masks, first, offset, idx_ref, square_ref, *refs):
    refs = list(refs)
    count = len(masks)
    grads = [[refs.pop(0) for _ in range(1 if m & 1 and is_whole(m) else 2)] for m in masks]
    w, r = refs.pop(0), refs.pop(0)
    if not first:
        refs.pop(0)
    out_hbm, token_ref = refs.pop(0), refs.pop(0)
    new_hbm = refs.pop(0) if first else None
    g, o, new, sem, out_sem = refs
    rows, cols = g.shape[2:]
    step = 64
    half = rows // 2
    token_ref[...] = jnp.zeros_like(token_ref)
    coming = [read_rows(grads[n], g.at[n], [sem.at[i, n] for i in (0, 1)]) for n in range(count)]
    for group in coming:
        for copy in group:
            copy.start()
    mean = square_ref[...] * (1.0 / (D * KVH * HD))
    scale = jnp.concatenate([learning_rate * lax.rsqrt(mean + norm_eps)] * (cols // 128), axis=1)
    writes = []
    for n in range(count):
        for copy in coming[n]:
            copy.wait()
        for part in range(2):

            def mix(t, carry):
                j = pl.ds(pl.multiple_of(part * half + t * step, step), step)
                for i in (0, 1):
                    value = w[offset + n, i, j].astype(jnp.float32) - scale[i : i + 1, :] * g[n, i, j].astype(jnp.float32)
                    value = value.astype(jnp.bfloat16)
                    if first and n == 0:
                        new[i, j] = value
                    mixed = mix_alpha * value.astype(jnp.float32) + (1.0 - mix_alpha) * r[offset + n, i, j].astype(jnp.float32)
                    o[n, i, j] = mixed.astype(jnp.bfloat16)
                return carry

            lax.fori_loop(0, half // step, mix, 0, unroll=2)
            at = pl.ds(pl.multiple_of((idx_ref[0] ^ masks[n]) * rows + part * half, half), half)
            writes.append(pltpu.make_async_copy(o.at[n, :, pl.ds(part * half, half), :], out_hbm.at[:, at, :], out_sem.at[part, n]))
            writes[-1].start()
        if first and n == 0:
            writes.append(pltpu.make_async_copy(new, new_hbm, out_sem.at[0, count]))
            writes[-1].start()
    for copy in writes:
        copy.wait()


def blend(idx, squares, grads, reference, held, masks, ready, offset):
    w, r = ready
    _, _, rows, cols = w.shape
    count = len(masks)
    first = held is None
    args = [idx, squares] + [x for m in masks for x in grads[m]]
    in_specs = [SMEM, VMEM] + [HBM] * (len(args) - 2)
    args += [resident(w), resident(r)]
    in_specs += [VMEM] * 2
    out_specs = [HBM, VMEM]
    out_shape = [jax.ShapeDtypeStruct(reference.shape, jnp.bfloat16), jax.ShapeDtypeStruct((8, 128), jnp.float32)]
    aliases = {}
    if first:
        out_specs.append(HBM)
        out_shape.append(jax.ShapeDtypeStruct((2, rows, cols), jnp.bfloat16))
    else:
        aliases = {len(args): 0}
        in_specs.append(HBM)
        args.append(held)
    block = pltpu.VMEM((count, 2, rows, cols), jnp.bfloat16)
    return pl.pallas_call(
        functools.partial(blend_kernel, tuple(masks), first, offset),
        in_specs=in_specs,
        out_specs=out_specs,
        out_shape=out_shape,
        scratch_shapes=[
            block,
            block,
            pltpu.VMEM((2, rows, cols) if first else (8, 128), jnp.bfloat16),
            pltpu.SemaphoreType.DMA((2, count)),
            pltpu.SemaphoreType.DMA((2, count + 1)),
        ],
        input_output_aliases=aliases,
        compiler_params=params(12),
        cost_estimate=COST,
        name="blend",
    )(*args)


def bits_of(mask):
    return [1 << b for b in range(mask.bit_length()) if mask >> b & 1]


def after(value, *earlier):
    return lax.optimization_barrier((value, earlier))[0]


def body(shards, tensors, hidden_in, policy_weights, reference_weights, policy_queries, reference_queries, readout, lengths):
    rows = policy_weights.shape[1]
    idx = lax.axis_index("shard").astype(jnp.int32).reshape(1)
    tables = jnp.asarray(rope_tables())

    def swap(x, bit, axis="shard", size=shards):
        return lax.ppermute(x, axis, [(i, i ^ bit) for i in range(size)])

    def powers(size):
        return [1 << b for b in range(size.bit_length() - 1)]

    chips = sorted(range(0, shards, 2), key=lambda m: (len(bits_of(m)), m))
    near = [m for m in chips if len(bits_of(m)) == 1]
    far = [m for m in chips if len(bits_of(m)) > 1]
    link = lambda i, m: bits_of(m)[-1] if i == 0 else bits_of(m)[0]

    def send_near(own):
        got = {m: [swap(own, m)] for m in near}
        got[0] = [own]
        got[1] = [swap(own, 1)]
        return got

    def relay(got, m, *earlier):
        got[m] = [None, None]
        for i in (0, 1):
            via = link(i, m)
            source = got[m ^ via]
            source = source[i] if source[0].ndim == 2 else source[0][i]
            got[m][i] = swap(after(source, *earlier), via)

    def to_core(got, m, *earlier):
        got[m | 1] = [swap(after(g, *earlier), 1) for g in got[m]]

    weights = send_near(policy_weights)
    normed, ref_keys, ref_values = norm_project(idx, hidden_in, reference_weights, tables)
    (ref_margin,) = attend(lengths, reference_queries, ref_keys, ref_values, readout)
    for m in far:
        relay(weights, m, ref_margin, *[weights[k] for k in near])
    for m in near:
        to_core(weights, m, ref_margin)
    held = project(idx, normed, [0, 1], weights, None, None)
    held = project(idx, normed, [m | c for m in near for c in (0, 1)], weights, held, None if far else tables)
    if far:
        for m in far:
            to_core(weights, m, held)
        held = project(idx, normed, [m | c for m in far for c in (0, 1)], weights, held, tables)
    pol_keys, pol_values = held
    margin, probs, delta = attend(lengths, policy_queries, pol_keys, pol_values, readout, ref_margin)

    theirs = {}
    order = list(reversed(chips))
    split = max(len(far), 1)

    def other_blocks(masks, *earlier):
        blocks = gradient_blocks(idx, normed, cot, [m | 1 for m in masks], rows, None, earlier)
        theirs.update({m: swap(block, 1) for m, block in zip(masks, blocks)})
        return blocks

    received = [swap(margin, m, "tensor", tensors) for m in range(1, tensors)]
    cot = attend_back(lengths, policy_queries, pol_values, readout, probs, delta, tables)
    terms = [margin] + [after(x, cot) for x in received]
    while len(terms) > 1:
        terms = [a + b for a, b in zip(terms[::2], terms[1::2])]
    (margin,) = terms
    received = swap(margin, 1)
    margins = (margin, after(received, other_blocks(order[:split], margin)))
    other_blocks(order[split:], margins[1])

    chip_sum = {}
    arrived = {m: ([], []) for m in chips}
    halves = ([[], []], [[], []])
    waiting = []

    def send(m, i, half=None):
        terms = [chip_sum[m][i], *arrived[m][i]]
        if half is not None:
            terms = [t[:, half * rows // 2 : (half + 1) * rows // 2] for t in terms]
        payload = terms[0]
        if len(terms) > 1:
            payload = sum(t.astype(jnp.float32) for t in terms).astype(jnp.bfloat16)
        via = link(i, m)
        received = swap(payload, via)
        if half is None:
            arrived[m ^ via][i].append(received)
        else:
            halves[half][i].append(received)

    for masks in (order[:split], order[split:]):
        chip_sum.update(zip(masks, gradient_blocks(idx, normed, cot, masks, rows, (margins, theirs))))
        for m in masks:
            for i in (0, 1):
                if m and not any(k ^ link(i, k) == m for k in far):
                    send(m, i)
                elif m:
                    waiting.append((m, i))
    for m, i in waiting:
        if m in far:
            send(m, i)

    for half in (0, 1):
        for m, i in waiting:
            if m in near:
                send(m, i, half)
    grads = {m: [] for m in [0] + near}
    parts = []
    for half in (0, 1):
        own, part = finish(chip_sum[0], [arrived[0][i] + halves[half][i] for i in (0, 1)], half)
        parts.append(part)
        grads[0].append(own)
        for m in near:
            grads[m].append(swap(own, m))
    squares = parts[0] + parts[1]
    for bit in powers(tensors):
        squares = squares + swap(squares, bit, "tensor", tensors)
    squares = squares + swap(squares, 1)
    squares, margin_out = gate(squares, margin, *[grads[m][0] for m in near])
    masks = [m | c for m in [0] + near for c in (0, 1)] + [m | c for c in (0, 1) for m in far]
    ready = fetch(idx, weights, reference_weights, masks, squares)
    terms = [squares] + [swap(squares, m) for m in chips[1:]]
    while len(terms) > 1:
        terms = [a + b for a, b in zip(terms[::2], terms[1::2])]
    (squares,) = terms
    two = [m for m in far if len(bits_of(m)) == 2]
    ends = [(m, i) for m in two for i in (0, 1)]
    whole = [0] + near
    packed = pack([grads[m ^ link(i, m)] for m, i in ends] + [grads[m] for m in whole], [i for m, i in ends] + [None] * len(whole), squares, ready[0])
    packed = dict(zip(ends + whole, packed))
    for m in far:
        grads[m] = [swap(packed[m, i] if m in two else grads[m ^ link(i, m)][i], link(i, m)) for i in (0, 1)]
    for m in whole:
        grads[m | 1] = [swap(packed[m], 1)]
    groups = [[0, 1], [m | c for m in near for c in (0, 1)]] + [[m | c for m in far] for c in (0, 1)]
    new_reference, at = None, 0
    for group in groups:
        if group == far and far:
            for m in far:
                to_core(grads, m, token)
        if group:
            outs = blend(idx, squares, grads, reference_weights, new_reference, group, ready, at)
            new_reference, token = outs[:2]
            new_policy = outs[2] if at == 0 else new_policy
            at += len(group)
    return (new_policy, new_reference, margin_out)


def solution(mesh):
    return jax.shard_map(
        functools.partial(body, mesh.shape["shard"], mesh.shape["tensor"]),
        mesh=mesh,
        in_specs=(
            P("shard", None),
            P(None, "shard", "tensor"),
            P(None, None, "tensor"),
            P("shard", "tensor"),
            P("shard", "tensor"),
            P("shard", "tensor"),
            P("shard"),
        ),
        out_specs=(P(None, "shard", "tensor"), P(None, None, "tensor"), P("shard")),
        check_vma=False,
    )
```

```python
import functools
import math

import jax
import jax.numpy as jnp
import numpy as np
from jax import lax
from jax.experimental import pallas as pl
from jax.experimental.pallas import tpu as pltpu
from jax.sharding import PartitionSpec as P

D = 8192
HD = 128
KVH = 8
QH = 32
LEN = 384
TILE = 128

rope_base = 1000000.0
dpo_beta = 0.1
learning_rate = 0.2
mix_alpha = 0.6
norm_eps = 1e-06
width_scale = D ** (-0.5)
logit_scale = 1.0 / math.sqrt(HD)
MIB = 1024 * 1024

NT = (((1,), (1,)), ((), ()))
NN = (((1,), (0,)), ((), ()))
TN = (((0,), (0,)), ((), ()))


def dot(a, b, dims):
    return lax.dot_general(a, b, dims, preferred_element_type=jnp.float32)


def params(mib):
    return pltpu.CompilerParams(vmem_limit_bytes=mib * MIB)


COST = pl.CostEstimate(flops=1, bytes_accessed=1, transcendentals=0)
LONG = pl.CostEstimate(flops=1, bytes_accessed=40 * 1000 * 1000, transcendentals=0)
VMEM = pl.BlockSpec(memory_space=pltpu.VMEM)
SMEM = pl.BlockSpec(memory_space=pltpu.SMEM)
HBM = pl.BlockSpec(memory_space=pl.ANY)


def resident(x):
    return pltpu.with_memory_space_constraint(x, pltpu.VMEM)


def in_hbm(x):
    return pltpu.with_memory_space_constraint(x, pltpu.HBM)


def rope_tables():
    frequency = rope_base ** (-2.0 * np.arange(HD // 2) / HD)
    angles = np.arange(LEN)[:, None] * frequency[None, :]
    cosine, sine = np.cos(angles), np.sin(angles)
    return np.stack([np.concatenate([cosine, cosine], axis=1), np.concatenate([-sine, sine], axis=1)]).astype(np.float32)


def store_heads(acc_ref, cos, sin, key_ref, value_ref):
    for s in range(key_ref.shape[0] // LEN):
        rows = slice(s * LEN, (s + 1) * LEN)
        for h in range(key_ref.shape[1] // HD):
            cols = slice(h * HD, (h + 1) * HD)
            k = acc_ref[0, rows, cols] * width_scale
            key_ref[rows, cols] = (k * cos + pltpu.roll(k, HD // 2, 1) * sin).astype(jnp.bfloat16)
    value_ref[...] = (acc_ref[1] * width_scale).astype(jnp.bfloat16)


def norm_project_kernel(idx_ref, hidden_hbm, weight_hbm, table_hbm, normed_ref, key_ref, value_ref, w, acc, part, table, in_sem, w_sem, table_sem):
    tokens = normed_ref.shape[0]
    step, width, span, chunk = 16, 512, 128, 1024
    reads = []
    for i in range(tokens // span):
        at = pl.ds(i * span, span)
        reads.append(pltpu.make_async_copy(hidden_hbm.at[at], normed_ref.at[at], in_sem.at[i]))
    loads = []
    for c in range(D // chunk):
        at = pl.ds(c * chunk, chunk)
        loads.append(pltpu.make_async_copy(weight_hbm.at[:, at, :], w.at[:, at, :], w_sem.at[c]))
    loads.append(pltpu.make_async_copy(table_hbm, table, table_sem))
    for copy in reads + loads:
        copy.start()

    def row_step(i, carry):
        at = pl.ds(pl.multiple_of(i * step, step), step)
        total = jnp.zeros((step, width), jnp.float32)
        for c in range(D // width):
            v = normed_ref[at, c * width : (c + 1) * width].astype(jnp.float32)
            total = total + v * v
        part[at, :] = functools.reduce(jnp.add, [total[:, c * 128 : (c + 1) * 128] for c in range(width // 128)])
        return carry

    for i, copy in enumerate(reads):
        copy.wait()
        lax.fori_loop(i * (span // step), (i + 1) * (span // step), row_step, 0)
    for copy in loads:
        copy.wait()
    mean = jnp.sum(part[...], axis=1, keepdims=True) * (1.0 / D)
    part[...] = jnp.broadcast_to(lax.rsqrt(mean + norm_eps), part.shape)

    def columns(c):
        return pl.ds(pl.multiple_of(c * chunk, chunk), chunk)

    def normalise(c):
        for i in range(tokens // step):
            rows = slice(i * step, (i + 1) * step)
            scale = jnp.concatenate([part[rows, :]] * (chunk // 128), axis=1)
            normed_ref[rows, columns(c)] = (normed_ref[rows, columns(c)].astype(jnp.float32) * scale).astype(jnp.bfloat16)

    def multiply(c, carry):
        for i in (0, 1):
            acc[i] += dot(normed_ref[:, columns(c)], w[i, columns(c), :], NN)

        @pl.when(c + 1 < D // chunk)
        def _():
            normalise(c + 1)

        return carry

    acc[...] = jnp.zeros_like(acc)
    normalise(0)
    lax.fori_loop(0, D // chunk, multiply, 0)
    store_heads(acc, table[0], table[1], key_ref, value_ref)


def norm_project(idx, hidden, weights, tables):
    tokens = hidden.shape[0]
    cols = weights.shape[2]
    return pl.pallas_call(
        norm_project_kernel,
        in_specs=[SMEM, HBM, HBM, HBM],
        out_specs=[VMEM, VMEM, VMEM],
        out_shape=[
            pltpu.VMEM((tokens, D), jnp.bfloat16),
            pltpu.VMEM((tokens, cols), jnp.bfloat16),
            pltpu.VMEM((tokens, cols), jnp.bfloat16),
        ],
        scratch_shapes=[
            pltpu.VMEM((2, D, cols), jnp.bfloat16),
            pltpu.VMEM((2, tokens, cols), jnp.float32),
            pltpu.VMEM((tokens, 128), jnp.float32),
            pltpu.VMEM(tables.shape, jnp.float32),
            pltpu.SemaphoreType.DMA((tokens // 128,)),
            pltpu.SemaphoreType.DMA((D // 1024,)),
            pltpu.SemaphoreType.DMA,
        ],
        compiler_params=params(16),
        cost_estimate=COST,
        name="norm_project",
    )(idx, in_hbm(hidden), in_hbm(weights), in_hbm(tables))


def is_whole(mask):
    return len(bits_of(mask >> 1)) < 2


def read_rows(sources, target, sems):
    if len(sources) == 1:
        return [pltpu.make_async_copy(sources[0], target, sems[0])]
    if len(sources[0].shape) == 2:
        return [pltpu.make_async_copy(sources[i], target.at[i], sems[i]) for i in (0, 1)]
    half = sources[0].shape[1]
    return [pltpu.make_async_copy(sources[h], target.at[:, pl.ds(h * half, half), :], sems[h]) for h in (0, 1)]


def project_kernel(masks, first, last, idx_ref, x_ref, *refs):
    refs = list(refs)
    count = len(masks)
    pieces = [[refs.pop(0) for _ in range(1 if is_whole(m) else 2)] for m in masks]
    held = None if first else refs.pop(0)
    if last:
        table_hbm, key_ref, value_ref, w, acc, table, sem, table_sem = refs
        table_copy = pltpu.make_async_copy(table_hbm, table, table_sem)
        table_copy.start()
    else:
        acc, w, sem = refs
    depth = w.shape[2]
    copies = [read_rows(pieces[n], w.at[n], [sem.at[i, n] for i in (0, 1)]) for n in range(count)]
    for group in copies:
        for copy in group:
            copy.start()
    for n in range(count):
        for copy in copies[n]:
            copy.wait()
        col = pl.multiple_of((idx_ref[0] ^ masks[n]) * depth, depth)
        x = x_ref[:, pl.ds(col, depth)]
        for i in (0, 1):
            term = dot(x, w[n, i], NN)
            if n:
                term = acc[i] + term
            elif not first:
                term = held[i] + term
            acc[i] = term
    if last:
        table_copy.wait()
        store_heads(acc, table[0], table[1], key_ref, value_ref)


def project(idx, normed, masks, pieces, held, tables):
    tokens = normed.shape[0]
    rows, cols = pieces[masks[0]][0].shape[-2:]
    first, last = held is None, tables is not None
    count = len(masks)
    args = [idx, resident(normed)] + [w for m in masks for w in pieces[m]]
    in_specs = [SMEM, VMEM] + [HBM] * (len(args) - 2)
    if not first:
        in_specs.append(VMEM)
        args.append(resident(held))
    acc_shape = (2, tokens, cols)
    scratch = [pltpu.VMEM((count, 2, rows, cols), jnp.bfloat16), pltpu.SemaphoreType.DMA((2, count))]
    if last:
        in_specs.append(HBM)
        args.append(in_hbm(tables))
        out_specs = [VMEM] * 2
        out_shape = [pltpu.VMEM((tokens, cols), jnp.bfloat16)] * 2
        scratch.insert(1, pltpu.VMEM(acc_shape, jnp.float32))
        scratch.insert(2, pltpu.VMEM(tables.shape, jnp.float32))
        scratch.append(pltpu.SemaphoreType.DMA)
    else:
        out_specs = VMEM
        out_shape = pltpu.VMEM(acc_shape, jnp.float32)
    return pl.pallas_call(
        functools.partial(project_kernel, tuple(masks), first, last),
        in_specs=in_specs,
        out_specs=out_specs,
        out_shape=out_shape,
        scratch_shapes=scratch,
        compiler_params=params(10),
        cost_estimate=COST,
        name="project",
    )(*args)


HEADS = 2


def stacked(ref, row, col, r, first, count):
    rows = pl.ds(pl.multiple_of(row + r * TILE, TILE), TILE)
    at = lambda g: pl.ds(pl.multiple_of(col + g * HD, HD), HD)
    return jnp.concatenate([ref[rows, at(g)] for g in range(first, first + count)], axis=0)


def live_readout(ref, row, col, r, first, count, length):
    x = stacked(ref, row, col, r, first, count).astype(jnp.float32)
    at = lax.broadcasted_iota(jnp.int32, x.shape, 0) % TILE + r * TILE
    return jnp.where(at < length, x, 0.0).astype(jnp.bfloat16)


def places(step, q_ref, k_ref):
    heads = k_ref.shape[1] // HD
    seq, h = step // heads, step % heads
    return seq, h, seq * LEN, pl.multiple_of(h * HD, HD), h * (q_ref.shape[1] // heads)


def attend_kernel(keep, len_ref, q_ref, k_ref, v_ref, ro_ref, *rest):
    groups = q_ref.shape[1] // k_ref.shape[1]
    count = min(groups, HEADS)
    if keep:
        before_ref, margin_ref, prob_ref, delta_ref = rest
    else:
        (margin_ref,) = rest

    def one(step, margin):
        seq, h, row, col, q_col = places(step, q_ref, k_ref)
        length = len_ref[seq]
        score = jnp.zeros((1, count * TILE), jnp.float32)
        j = lax.broadcasted_iota(jnp.int32, (TILE, count * TILE), 0)
        i = lax.broadcasted_iota(jnp.int32, (TILE, count * TILE), 1) % TILE
        base = 0
        for r in range(LEN // TILE):
            n = (r + 1) * TILE
            keys = (pl.ds(pl.multiple_of(row, TILE), n), pl.ds(col, HD))
            for g in range(0, groups, count):
                q = stacked(q_ref, row, q_col, r, g, count)
                ro = live_readout(ro_ref, row, q_col, r, g, count, length)
                s = dot(k_ref[keys], q, NT)
                dp = dot(v_ref[keys], ro, NT)
                s = [s[b * TILE : (b + 1) * TILE] for b in range(r + 1)]
                s[r] = jnp.where(j <= i, s[r], -1e30)
                top = functools.reduce(jnp.maximum, [jnp.max(x, axis=0, keepdims=True) for x in s])
                e = [jnp.exp2((x - top) * (logit_scale * math.log2(math.e))) for x in s]
                inverse = 1.0 / functools.reduce(jnp.add, [jnp.sum(x, axis=0, keepdims=True) for x in e])
                cols = slice(g * TILE, (g + count) * TILE)
                delta = jnp.zeros((1, count * TILE), jnp.float32)
                for b in range(r + 1):
                    p = (e[b] * inverse).astype(jnp.bfloat16)
                    if keep:
                        prob_ref[seq, h, base + b * TILE : base + (b + 1) * TILE, cols] = p
                    delta = delta + jnp.sum(p.astype(jnp.float32) * dp[b * TILE : (b + 1) * TILE], axis=0, keepdims=True)
                if keep:
                    delta_ref[seq, h, r : r + 1, cols] = delta
                score = score + delta
            base += n
        side = jnp.where(seq % 2 == 0, 1.0, -1.0) * (dpo_beta / math.sqrt(QH * HD))
        return margin + jnp.sum(score, axis=1, keepdims=True) * side

    steps = k_ref.shape[0] // LEN * (k_ref.shape[1] // HD)
    start = -before_ref[0:1, 0:1] if keep else jnp.zeros((1, 1), jnp.float32)
    margin_ref[...] = jnp.broadcast_to(lax.fori_loop(0, steps, one, start, unroll=keep), margin_ref.shape)


def attend(lengths, queries, keys, values, readout, before=None):
    seqs = lengths.shape[0]
    heads = keys.shape[1] // HD
    wide = queries.shape[1] // heads
    tiles = LEN // TILE
    span = TILE * tiles * (tiles + 1) // 2
    keep = before is not None
    args = [lengths] + [resident(x) for x in (queries, keys, values, readout)]
    out_shape = [jax.ShapeDtypeStruct((8, 128), jnp.float32)]
    if keep:
        args.append(before)
        out_shape += [pltpu.VMEM((seqs, heads, span, wide), jnp.bfloat16), pltpu.VMEM((seqs, heads, tiles, wide), jnp.float32)]
    return pl.pallas_call(
        functools.partial(attend_kernel, keep),
        in_specs=[SMEM] + [VMEM] * (len(args) - 1),
        out_specs=[VMEM] * len(out_shape),
        out_shape=out_shape,
        compiler_params=params(8),
        cost_estimate=COST,
        name="attend",
    )(*args)


def attend_back_kernel(len_ref, q_ref, v_ref, ro_ref, prob_ref, delta_ref, table_ref, grad_ref):
    tiles = LEN // TILE
    groups = q_ref.shape[1] // v_ref.shape[1]
    count = min(groups, HEADS)

    def one(step, carry):
        seq, h, row, col, q_col = places(step, q_ref, v_ref)
        length = len_ref[seq]
        dk = [None] * tiles
        dv = [None] * tiles
        base = 0
        for r in range(tiles):
            n = (r + 1) * TILE
            keys = (pl.ds(pl.multiple_of(row, TILE), n), pl.ds(col, HD))
            for g in range(0, groups, count):
                q = stacked(q_ref, row, q_col, r, g, count)
                ro = live_readout(ro_ref, row, q_col, r, g, count, length)
                cols = slice(g * TILE, (g + count) * TILE)
                p = prob_ref[seq, h, base : base + n, cols]
                dp = dot(v_ref[keys], ro, NT)
                ds = (p.astype(jnp.float32) * (dp - delta_ref[seq, h, r : r + 1, cols])).astype(jnp.bfloat16)
                tk = dot(ds, q, NN)
                tv = dot(p, ro, NN)
                for b in range(r + 1):
                    at = slice(b * TILE, (b + 1) * TILE)
                    dk[b] = tk[at] if dk[b] is None else dk[b] + tk[at]
                    dv[b] = tv[at] if dv[b] is None else dv[b] + tv[at]
            base += n
        scale = jnp.where(seq % 2 == 0, -1.0, 1.0) * (1.0 / math.sqrt(QH * HD))
        for b in range(tiles):
            at = slice(b * TILE, (b + 1) * TILE)
            to = (pl.ds(col, HD), pl.ds(pl.multiple_of(row + b * TILE, TILE), TILE))
            k = dk[b] * (scale * logit_scale)
            k = k * table_ref[0, at, :] - pltpu.roll(k, HD // 2, 1) * table_ref[1, at, :]
            grad_ref[(0, *to)] = k.T.astype(jnp.bfloat16)
            grad_ref[(1, *to)] = (dv[b] * scale).T.astype(jnp.bfloat16)
        return carry

    steps = v_ref.shape[0] // LEN * (v_ref.shape[1] // HD)
    lax.fori_loop(0, steps, one, 0, unroll=True)


def attend_back(lengths, queries, values, readout, probs, delta, tables):
    return pl.pallas_call(
        attend_back_kernel,
        in_specs=[SMEM] + [VMEM] * 6,
        out_specs=VMEM,
        out_shape=pltpu.VMEM((2,) + values.shape[::-1], jnp.bfloat16),
        compiler_params=params(8),
        cost_estimate=COST,
        name="attend_back",
    )(lengths, *[resident(x) for x in (queries, values, readout, probs, delta, tables)])


def gradient_tiles(idx, mask, x_ref, cot_ref, rows):
    cols = cot_ref.shape[1]
    both = jnp.concatenate([cot_ref[0], cot_ref[1]], axis=0)
    tile = min(rows, 256)
    for t in range(rows // tile):
        col = pl.multiple_of((idx ^ mask) * rows + t * tile, tile)
        out = dot(both, x_ref[:, pl.ds(col, tile)], NN)
        for i in (0, 1):
            yield i, t * tile, tile, out[i * cols : (i + 1) * cols]


def gradient_kernel(masks, idx_ref, x_ref, cot_ref, *outs):
    outs = outs[len(outs) - len(masks) :]
    for mask, out_ref in zip(masks, outs):
        for i, start, tile, value in gradient_tiles(idx_ref[0], mask, x_ref, cot_ref, out_ref.shape[2]):
            out_ref[i, :, start : start + tile] = value.astype(out_ref.dtype)


def merged_kernel(masks, idx_ref, x_ref, cot_ref, mine_ref, their_ref, *refs):
    count = len(masks)
    theirs_hbm, outs = refs[:count], refs[count : 3 * count]
    theirs, sem = refs[3 * count :]
    rows = theirs.shape[3]
    copies = [pltpu.make_async_copy(theirs_hbm[n], theirs.at[n], sem.at[n]) for n in range(count)]
    for copy in copies:
        copy.start()
    mine, their = (ref[0:1, :] for ref in (mine_ref, their_ref))
    mine, their = (jax.nn.sigmoid(-x) for x in (mine, their))
    for n, mask in enumerate(masks):
        copies[n].wait()
        for i, start, tile, value in gradient_tiles(idx_ref[0], mask, x_ref, cot_ref, rows):
            wide = lambda x: jnp.concatenate([x] * (tile // 128), axis=1)
            value = value * wide(mine) + theirs[n, i, :, start : start + tile].astype(jnp.float32) * wide(their)
            outs[2 * n + i][:, start : start + tile] = value.astype(outs[2 * n + i].dtype)


def gradient_blocks(idx, normed, cot, masks, rows, merge=None, earlier=()):
    _, cols, tokens = cot.shape
    args = [idx, resident(normed), resident(cot)]
    in_specs = [SMEM, VMEM, VMEM]
    scratch = []
    if merge is None:
        kernel, name = gradient_kernel, "gradient_block"
        out_shape = [jax.ShapeDtypeStruct((2, cols, rows), jnp.bfloat16) for m in masks]
        args += earlier
        in_specs += [HBM] * len(earlier)
    else:
        kernel, name = merged_kernel, "merged_block"
        margins, theirs = merge
        args += [*margins] + [theirs[m] for m in masks]
        in_specs += [VMEM] * 2 + [HBM] * len(masks)
        out_shape = [
            jax.ShapeDtypeStruct((cols, rows), jnp.bfloat16) if m else pltpu.VMEM((cols, rows), jnp.float32)
            for m in masks
            for i in (0, 1)
        ]
        scratch = [pltpu.VMEM((len(masks), 2, cols, rows), jnp.bfloat16), pltpu.SemaphoreType.DMA((len(masks),))]
    outs = pl.pallas_call(
        functools.partial(kernel, tuple(masks)),
        in_specs=in_specs,
        out_specs=[VMEM] * len(out_shape),
        out_shape=out_shape,
        scratch_shapes=scratch,
        compiler_params=params(10),
        cost_estimate=COST,
        name=name,
    )(*args)
    return outs if merge is None else [outs[2 * n : 2 * n + 2] for n in range(len(masks))]


def finish_kernel(half, counts, *refs):
    refs = list(refs)
    out_ref, square_ref = refs[-2:]
    refs = refs[:-2]
    square_ref[...] = jnp.zeros_like(square_ref)
    _, rows, cols = out_ref.shape
    for i in (0, 1):
        terms = [refs.pop(0) for _ in range(1 + counts[i])]
        squares = jnp.zeros((1, 128), jnp.float32)
        for c in range(0, cols, 128):
            for r in range(0, rows, 128):
                at = [slice(x, x + 128) for x in (r if t.shape[1] == rows else half * rows + r for t in terms)]
                value = functools.reduce(jnp.add, [t[c : c + 128, x].astype(jnp.float32) for t, x in zip(terms, at)])
                squares = squares + jnp.sum(value * value, axis=0, keepdims=True)
                out_ref[i, r : r + 128, c : c + 128] = value.T.astype(jnp.bfloat16)
        square_ref[i : i + 1, :] = jnp.broadcast_to(jnp.sum(squares, axis=1, keepdims=True), (1, 128))


def finish(base, arrived, half):
    args = [x for i in (0, 1) for x in (resident(base[i]), *arrived[i])]
    cols, rows = base[0].shape
    return pl.pallas_call(
        functools.partial(finish_kernel, half, [len(a) for a in arrived]),
        in_specs=[VMEM] * len(args),
        out_specs=[VMEM] * 2,
        out_shape=[jax.ShapeDtypeStruct((2, rows // 2, cols), jnp.bfloat16), jax.ShapeDtypeStruct((8, 128), jnp.float32)],
        compiler_params=params(8),
        cost_estimate=COST,
        name="finish",
    )(*args)


def hand_on_kernel(count, *refs):
    pass


def hand_on(arrays, earlier):
    count = len(arrays)
    return pl.pallas_call(
        functools.partial(hand_on_kernel, count),
        in_specs=[HBM] * (count + 1),
        out_specs=[HBM] * count,
        out_shape=[jax.ShapeDtypeStruct(x.shape, x.dtype) for x in arrays],
        input_output_aliases={n: n for n in range(count)},
        compiler_params=params(2),
        cost_estimate=COST,
        name="hand_on",
    )(*arrays, earlier)


def gate_kernel(value_ref, margin_ref, *refs):
    out_ref, first_ref = refs[-2:]
    out_ref[...] = value_ref[...]
    first_ref[0] = margin_ref[0, 0]


def gate(value, margin, *earlier):
    return pl.pallas_call(
        gate_kernel,
        in_specs=[VMEM, VMEM] + [HBM] * len(earlier),
        out_specs=[VMEM, SMEM],
        out_shape=[jax.ShapeDtypeStruct(value.shape, value.dtype), jax.ShapeDtypeStruct((1,), jnp.float32)],
        compiler_params=params(2),
        cost_estimate=COST,
        name="gate",
    )(value, margin, *earlier)


def pack_kernel(takes, parts, *refs):
    sources, outs, sem = refs[: parts * len(takes)], refs[-1 - len(takes) : -1], refs[-1]
    copies = []
    for n, i in enumerate(takes):
        half = sources[parts * n].shape[1]
        for h in range(parts):
            source, at = sources[parts * n + h], pl.ds(h * half, half)
            if i is None:
                copies.append(pltpu.make_async_copy(source, outs[n].at[:, at, :], sem.at[n, h]))
            else:
                copies.append(pltpu.make_async_copy(source.at[i], outs[n].at[at, :], sem.at[n, h]))
    for copy in copies:
        copy.start()
    for copy in copies:
        copy.wait()


def pack(sources, takes, *earlier):
    parts = len(sources[0])
    _, half, cols = sources[0][0].shape
    shapes = [(2, parts * half, cols) if i is None else (parts * half, cols) for i in takes]
    return pl.pallas_call(
        functools.partial(pack_kernel, tuple(takes), parts),
        in_specs=[HBM] * (parts * len(takes) + len(earlier)),
        out_specs=[HBM] * len(takes),
        out_shape=[jax.ShapeDtypeStruct(shape, jnp.bfloat16) for shape in shapes],
        scratch_shapes=[pltpu.SemaphoreType.DMA((len(takes), 2))],
        compiler_params=params(2),
        cost_estimate=COST,
        name="pack",
    )(*[x for pair in sources for x in pair], *earlier)


def fetch_kernel(masks, idx_ref, *refs):
    refs = list(refs)
    pieces = [[refs.pop(0) for _ in range(1 if is_whole(m) else 2)] for m in masks]
    ref_hbm, _, w, r, sem = refs
    rows = r.shape[2]
    copies = []
    for n, mask in enumerate(masks):
        at = pl.ds(pl.multiple_of((idx_ref[0] ^ mask) * rows, rows), rows)
        copies += read_rows(pieces[n], w.at[n], [sem.at[i, n] for i in (0, 1)])
        copies.append(pltpu.make_async_copy(ref_hbm.at[:, at, :], r.at[n], sem.at[2, n]))
    for copy in copies:
        copy.start()
    for copy in copies:
        copy.wait()


def fetch(idx, weights, reference, masks, earlier):
    rows, cols = weights[masks[0]][0].shape[-2:]
    count = len(masks)
    args = [idx] + [w for m in masks for w in weights[m]] + [in_hbm(reference), earlier]
    return pl.pallas_call(
        functools.partial(fetch_kernel, tuple(masks)),
        in_specs=[SMEM] + [HBM] * (len(args) - 1),
        out_specs=[VMEM] * 2,
        out_shape=[pltpu.VMEM((count, 2, rows, cols), jnp.bfloat16)] * 2,
        scratch_shapes=[pltpu.SemaphoreType.DMA((3, count))],
        compiler_params=params(4),
        cost_estimate=COST,
        name="fetch",
    )(*args)


def blend_kernel(masks, first, offset, idx_ref, square_ref, *refs):
    refs = list(refs)
    count = len(masks)
    grads = [[refs.pop(0) for _ in range(1 if m & 1 and is_whole(m) else 2)] for m in masks]
    w, r = refs.pop(0), refs.pop(0)
    if not first:
        refs.pop(0)
    out_hbm, token_ref = refs.pop(0), refs.pop(0)
    new_hbm = refs.pop(0) if first else None
    g, o, new, sem, out_sem = refs
    rows, cols = g.shape[2:]
    step = 64
    half = rows // 2
    token_ref[...] = jnp.zeros_like(token_ref)
    here = [not is_whole(m) for m in masks]
    coming = [[] if here[n] else read_rows(grads[n], g.at[n], [sem.at[i, n] for i in (0, 1)]) for n in range(count)]
    for group in coming:
        for copy in group:
            copy.start()
    mean = square_ref[...] * (1.0 / (D * KVH * HD))
    scale = jnp.concatenate([learning_rate * lax.rsqrt(mean + norm_eps)] * (cols // 128), axis=1)
    writes = []
    for n in range(count):
        for copy in coming[n]:
            copy.wait()
        for part in range(2):

            def mix(t, carry):
                j = pl.ds(pl.multiple_of(part * half + t * step, step), step)
                for i in (0, 1):
                    slope = grads[n][i][j, :] if here[n] else g[n, i, j]
                    value = w[offset + n, i, j].astype(jnp.float32) - scale[i : i + 1, :] * slope.astype(jnp.float32)
                    value = value.astype(jnp.bfloat16)
                    if first and n == 0:
                        new[i, j] = value
                    mixed = mix_alpha * value.astype(jnp.float32) + (1.0 - mix_alpha) * r[offset + n, i, j].astype(jnp.float32)
                    o[n, i, j] = mixed.astype(jnp.bfloat16)
                return carry

            lax.fori_loop(0, half // step, mix, 0, unroll=2)
            at = pl.ds(pl.multiple_of((idx_ref[0] ^ masks[n]) * rows + part * half, half), half)
            writes.append(pltpu.make_async_copy(o.at[n, :, pl.ds(part * half, half), :], out_hbm.at[:, at, :], out_sem.at[part, n]))
            writes[-1].start()
        if first and n == 0:
            writes.append(pltpu.make_async_copy(new, new_hbm, out_sem.at[0, count]))
            writes[-1].start()
    for copy in writes:
        copy.wait()


def blend(idx, squares, grads, reference, held, masks, ready, offset):
    w, r = ready
    _, _, rows, cols = w.shape
    count = len(masks)
    first = held is None
    args = [idx, squares] + [x if is_whole(m) else resident(x) for m in masks for x in grads[m]]
    in_specs = [SMEM, VMEM] + [HBM if is_whole(m) else VMEM for m in masks for x in grads[m]]
    args += [resident(w), resident(r)]
    in_specs += [VMEM] * 2
    out_specs = [HBM, VMEM]
    out_shape = [jax.ShapeDtypeStruct(reference.shape, jnp.bfloat16), jax.ShapeDtypeStruct((8, 128), jnp.float32)]
    aliases = {}
    if first:
        out_specs.append(HBM)
        out_shape.append(jax.ShapeDtypeStruct((2, rows, cols), jnp.bfloat16))
    else:
        aliases = {len(args): 0}
        in_specs.append(HBM)
        args.append(held)
    block = pltpu.VMEM((count, 2, rows, cols), jnp.bfloat16)
    return pl.pallas_call(
        functools.partial(blend_kernel, tuple(masks), first, offset),
        in_specs=in_specs,
        out_specs=out_specs,
        out_shape=out_shape,
        scratch_shapes=[
            block,
            block,
            pltpu.VMEM((2, rows, cols) if first else (8, 128), jnp.bfloat16),
            pltpu.SemaphoreType.DMA((2, count)),
            pltpu.SemaphoreType.DMA((2, count + 1)),
        ],
        input_output_aliases=aliases,
        compiler_params=params(12),
        cost_estimate=COST,
        name="blend",
    )(*args)


def bits_of(mask):
    return [1 << b for b in range(mask.bit_length()) if mask >> b & 1]


def after(value, *earlier):
    return lax.optimization_barrier((value, earlier))[0]


def body(shards, tensors, hidden_in, policy_weights, reference_weights, policy_queries, reference_queries, readout, lengths):
    rows = policy_weights.shape[1]
    idx = lax.axis_index("shard").astype(jnp.int32).reshape(1)
    tables = jnp.asarray(rope_tables())

    def swap(x, bit, axis="shard", size=shards):
        return lax.ppermute(x, axis, [(i, i ^ bit) for i in range(size)])

    def powers(size):
        return [1 << b for b in range(size.bit_length() - 1)]

    chips = sorted(range(0, shards, 2), key=lambda m: (len(bits_of(m)), m))
    near = [m for m in chips if len(bits_of(m)) == 1]
    far = [m for m in chips if len(bits_of(m)) > 1]
    link = lambda i, m: bits_of(m)[-1] if i == 0 else bits_of(m)[0]

    def send_near(own):
        got = {m: [swap(own, m)] for m in near}
        got[0] = [own]
        got[1] = [swap(own, 1)]
        return got

    def relay(got, m, *earlier):
        got[m] = [None, None]
        for i in (0, 1):
            via = link(i, m)
            source = got[m ^ via]
            source = source[i] if source[0].ndim == 2 else source[0][i]
            got[m][i] = swap(after(source, *earlier), via)

    def to_core(got, m, *earlier):
        got[m | 1] = [swap(after(g, *earlier), 1) for g in got[m]]

    weights = send_near(policy_weights)
    normed, ref_keys, ref_values = norm_project(idx, hidden_in, reference_weights, tables)
    (ref_margin,) = attend(lengths, reference_queries, ref_keys, ref_values, readout)
    two = [m for m in far if len(bits_of(m)) == 2]
    ends = [(m, i) for m in two for i in (0, 1)]
    packed = {}
    if two:
        packed = dict(zip(ends, pack([weights[m ^ link(i, m)] for m, i in ends], [i for m, i in ends], ref_margin)))
    for m in far:
        weights[m] = [swap(packed[m, i] if m in two else weights[m ^ link(i, m)][i], link(i, m)) for i in (0, 1)]
    for m in near:
        to_core(weights, m, ref_margin)
    held = project(idx, normed, [0, 1], weights, None, None)
    held = project(idx, normed, [m | c for m in near for c in (0, 1)], weights, held, None if far else tables)
    if far:
        for m in far:
            to_core(weights, m, held)
        held = project(idx, normed, [m | c for m in far for c in (0, 1)], weights, held, tables)
    pol_keys, pol_values = held
    margin, probs, delta = attend(lengths, policy_queries, pol_keys, pol_values, readout, ref_margin)

    theirs = {}
    order = list(reversed(chips))
    split = max(len(far), 1)

    def other_blocks(masks, margin, other=None):
        blocks = gradient_blocks(idx, normed, cot, [m | 1 for m in masks], rows, None, (margin,))
        if other is not None:
            blocks = hand_on(blocks, other)
        theirs.update({m: swap(block, 1) for m, block in zip(masks, blocks)})
        return blocks

    received = [swap(margin, m, "tensor", tensors) for m in range(1, tensors)]
    cot = attend_back(lengths, policy_queries, pol_values, readout, probs, delta, tables)
    terms = [margin] + [after(x, cot) for x in received]
    while len(terms) > 1:
        terms = [a + b for a, b in zip(terms[::2], terms[1::2])]
    (margin,) = terms
    received = swap(margin, 1)
    margins = (margin, after(received, other_blocks(order[:split], margin)))
    other_blocks(order[split:], margin, margins[1])

    chip_sum = {}
    arrived = {m: ([], []) for m in chips}
    halves = ([[], []], [[], []])
    waiting = []

    def send(m, i, half=None):
        terms = [chip_sum[m][i], *arrived[m][i]]
        if half is not None:
            terms = [t[:, half * rows // 2 : (half + 1) * rows // 2] for t in terms]
        payload = terms[0]
        if len(terms) > 1:
            payload = sum(t.astype(jnp.float32) for t in terms).astype(jnp.bfloat16)
        via = link(i, m)
        received = swap(payload, via)
        if half is None:
            arrived[m ^ via][i].append(received)
        else:
            halves[half][i].append(received)

    for masks in (order[:split], order[split:]):
        chip_sum.update(zip(masks, gradient_blocks(idx, normed, cot, masks, rows, (margins, theirs))))
        for m in masks:
            for i in (0, 1):
                if m and not any(k ^ link(i, k) == m for k in far):
                    send(m, i)
                elif m:
                    waiting.append((m, i))
    for m, i in waiting:
        if m in far:
            send(m, i)

    for half in (0, 1):
        for m, i in waiting:
            if m in near:
                send(m, i, half)
    grads = {m: [] for m in [0] + near}
    parts = []
    for half in (0, 1):
        own, part = finish(chip_sum[0], [arrived[0][i] + halves[half][i] for i in (0, 1)], half)
        parts.append(part)
        grads[0].append(own)
        for m in near:
            grads[m].append(swap(own, m))
    squares = parts[0] + parts[1]
    for bit in powers(tensors):
        squares = squares + swap(squares, bit, "tensor", tensors)
    squares = squares + swap(squares, 1)
    squares, margin_out = gate(squares, margin, *[grads[m][0] for m in near])
    masks = [m | c for m in [0] + near for c in (0, 1)] + [m | c for c in (0, 1) for m in far]
    ready = fetch(idx, weights, reference_weights, masks, squares)
    terms = [squares] + [swap(squares, m) for m in chips[1:]]
    while len(terms) > 1:
        terms = [a + b for a, b in zip(terms[::2], terms[1::2])]
    (squares,) = terms
    two = [m for m in far if len(bits_of(m)) == 2]
    ends = [(m, i) for m in two for i in (0, 1)]
    whole = [0] + near
    packed = pack([grads[m ^ link(i, m)] for m, i in ends] + [grads[m] for m in whole], [i for m, i in ends] + [None] * len(whole), squares, ready[0])
    packed = dict(zip(ends + whole, packed))
    for m in far:
        grads[m] = [swap(packed[m, i] if m in two else grads[m ^ link(i, m)][i], link(i, m)) for i in (0, 1)]
    for m in whole:
        grads[m | 1] = [swap(packed[m], 1)]
    groups = [[0, 1], [m | c for m in near for c in (0, 1)]] + [[m | c for m in far] for c in (0, 1)]
    new_reference, at = None, 0
    for group in groups:
        if group == far and far:
            for m in far:
                to_core(grads, m, token)
        if group:
            outs = blend(idx, squares, grads, reference_weights, new_reference, group, ready, at)
            new_reference, token = outs[:2]
            new_policy = outs[2] if at == 0 else new_policy
            at += len(group)
    return (new_policy, new_reference, margin_out)


def solution(mesh):
    return jax.shard_map(
        functools.partial(body, mesh.shape["shard"], mesh.shape["tensor"]),
        mesh=mesh,
        in_specs=(
            P("shard", None),
            P(None, "shard", "tensor"),
            P(None, None, "tensor"),
            P("shard", "tensor"),
            P("shard", "tensor"),
            P("shard", "tensor"),
            P("shard"),
        ),
        out_specs=(P(None, "shard", "tensor"), P(None, None, "tensor"), P("shard")),
        check_vma=False,
    )
```

```python
import functools
import math

import jax
import jax.numpy as jnp
import numpy as np
from jax import lax
from jax.experimental import pallas as pl
from jax.experimental.pallas import tpu as pltpu
from jax.sharding import PartitionSpec as P

D = 8192
HD = 128
KVH = 8
QH = 32
LEN = 384
TILE = 128

rope_base = 1000000.0
dpo_beta = 0.1
learning_rate = 0.2
mix_alpha = 0.6
norm_eps = 1e-06
width_scale = D ** (-0.5)
logit_scale = 1.0 / math.sqrt(HD)
MIB = 1024 * 1024

NT = (((1,), (1,)), ((), ()))
NN = (((1,), (0,)), ((), ()))
TN = (((0,), (0,)), ((), ()))


def dot(a, b, dims):
    return lax.dot_general(a, b, dims, preferred_element_type=jnp.float32)


def params(mib):
    return pltpu.CompilerParams(vmem_limit_bytes=mib * MIB)


COST = pl.CostEstimate(flops=1, bytes_accessed=1, transcendentals=0)
LONG = pl.CostEstimate(flops=1, bytes_accessed=40 * 1000 * 1000, transcendentals=0)
VMEM = pl.BlockSpec(memory_space=pltpu.VMEM)
SMEM = pl.BlockSpec(memory_space=pltpu.SMEM)
HBM = pl.BlockSpec(memory_space=pl.ANY)


def resident(x):
    return pltpu.with_memory_space_constraint(x, pltpu.VMEM)


def in_hbm(x):
    return pltpu.with_memory_space_constraint(x, pltpu.HBM)


def rope_tables():
    frequency = rope_base ** (-2.0 * np.arange(HD // 2) / HD)
    angles = np.arange(LEN)[:, None] * frequency[None, :]
    cosine, sine = np.cos(angles), np.sin(angles)
    return np.stack([np.concatenate([cosine, cosine], axis=1), np.concatenate([-sine, sine], axis=1)]).astype(np.float32)


def store_heads(acc_ref, cos, sin, key_ref, value_ref):
    for s in range(key_ref.shape[0] // LEN):
        rows = slice(s * LEN, (s + 1) * LEN)
        for h in range(key_ref.shape[1] // HD):
            cols = slice(h * HD, (h + 1) * HD)
            k = acc_ref[0, rows, cols] * width_scale
            key_ref[rows, cols] = (k * cos + pltpu.roll(k, HD // 2, 1) * sin).astype(jnp.bfloat16)
    value_ref[...] = (acc_ref[1] * width_scale).astype(jnp.bfloat16)


def norm_project_kernel(idx_ref, hidden_hbm, weight_hbm, table_hbm, normed_ref, key_ref, value_ref, w, acc, part, table, in_sem, w_sem, table_sem):
    tokens = normed_ref.shape[0]
    step, width, span, chunk = 16, 512, 128, 1024
    reads = []
    for i in range(tokens // span):
        at = pl.ds(i * span, span)
        reads.append(pltpu.make_async_copy(hidden_hbm.at[at], normed_ref.at[at], in_sem.at[i]))
    loads = []
    for c in range(D // chunk):
        at = pl.ds(c * chunk, chunk)
        loads.append(pltpu.make_async_copy(weight_hbm.at[:, at, :], w.at[:, at, :], w_sem.at[c]))
    loads.append(pltpu.make_async_copy(table_hbm, table, table_sem))
    for copy in reads + loads:
        copy.start()

    def row_step(i, carry):
        at = pl.ds(pl.multiple_of(i * step, step), step)
        total = jnp.zeros((step, width), jnp.float32)
        for c in range(D // width):
            v = normed_ref[at, c * width : (c + 1) * width].astype(jnp.float32)
            total = total + v * v
        part[at, :] = functools.reduce(jnp.add, [total[:, c * 128 : (c + 1) * 128] for c in range(width // 128)])
        return carry

    for i, copy in enumerate(reads):
        copy.wait()
        lax.fori_loop(i * (span // step), (i + 1) * (span // step), row_step, 0)
    for copy in loads:
        copy.wait()
    mean = jnp.sum(part[...], axis=1, keepdims=True) * (1.0 / D)
    part[...] = jnp.broadcast_to(lax.rsqrt(mean + norm_eps), part.shape)

    def columns(c):
        return pl.ds(pl.multiple_of(c * chunk, chunk), chunk)

    def normalise(c):
        for i in range(tokens // step):
            rows = slice(i * step, (i + 1) * step)
            scale = jnp.concatenate([part[rows, :]] * (chunk // 128), axis=1)
            normed_ref[rows, columns(c)] = (normed_ref[rows, columns(c)].astype(jnp.float32) * scale).astype(jnp.bfloat16)

    def multiply(c, carry):
        for i in (0, 1):
            acc[i] += dot(normed_ref[:, columns(c)], w[i, columns(c), :], NN)

        @pl.when(c + 1 < D // chunk)
        def _():
            normalise(c + 1)

        return carry

    acc[...] = jnp.zeros_like(acc)
    normalise(0)
    lax.fori_loop(0, D // chunk, multiply, 0)
    store_heads(acc, table[0], table[1], key_ref, value_ref)


def norm_project(idx, hidden, weights, tables):
    tokens = hidden.shape[0]
    cols = weights.shape[2]
    return pl.pallas_call(
        norm_project_kernel,
        in_specs=[SMEM, HBM, HBM, HBM],
        out_specs=[VMEM, VMEM, VMEM],
        out_shape=[
            pltpu.VMEM((tokens, D), jnp.bfloat16),
            pltpu.VMEM((tokens, cols), jnp.bfloat16),
            pltpu.VMEM((tokens, cols), jnp.bfloat16),
        ],
        scratch_shapes=[
            pltpu.VMEM((2, D, cols), jnp.bfloat16),
            pltpu.VMEM((2, tokens, cols), jnp.float32),
            pltpu.VMEM((tokens, 128), jnp.float32),
            pltpu.VMEM(tables.shape, jnp.float32),
            pltpu.SemaphoreType.DMA((tokens // 128,)),
            pltpu.SemaphoreType.DMA((D // 1024,)),
            pltpu.SemaphoreType.DMA,
        ],
        compiler_params=params(16),
        cost_estimate=COST,
        name="norm_project",
    )(idx, in_hbm(hidden), in_hbm(weights), in_hbm(tables))


def is_whole(mask):
    return len(bits_of(mask >> 1)) < 2


def read_rows(sources, target, sems):
    if len(sources) == 1:
        return [pltpu.make_async_copy(sources[0], target, sems[0])]
    if len(sources[0].shape) == 2:
        return [pltpu.make_async_copy(sources[i], target.at[i], sems[i]) for i in (0, 1)]
    half = sources[0].shape[1]
    return [pltpu.make_async_copy(sources[h], target.at[:, pl.ds(h * half, half), :], sems[h]) for h in (0, 1)]


def project_kernel(masks, first, last, idx_ref, x_ref, *refs):
    refs = list(refs)
    count = len(masks)
    pieces = [[refs.pop(0) for _ in range(1 if is_whole(m) else 2)] for m in masks]
    held = None if first else refs.pop(0)
    if last:
        table_hbm, key_ref, value_ref, w, acc, table, sem, table_sem = refs
        table_copy = pltpu.make_async_copy(table_hbm, table, table_sem)
        table_copy.start()
    else:
        acc, w, sem = refs
    depth = w.shape[2]
    copies = [read_rows(pieces[n], w.at[n], [sem.at[i, n] for i in (0, 1)]) for n in range(count)]
    for group in copies:
        for copy in group:
            copy.start()
    for n in range(count):
        for copy in copies[n]:
            copy.wait()
        col = pl.multiple_of((idx_ref[0] ^ masks[n]) * depth, depth)
        x = x_ref[:, pl.ds(col, depth)]
        for i in (0, 1):
            term = dot(x, w[n, i], NN)
            if n:
                term = acc[i] + term
            elif not first:
                term = held[i] + term
            acc[i] = term
    if last:
        table_copy.wait()
        store_heads(acc, table[0], table[1], key_ref, value_ref)


def project(idx, normed, masks, pieces, held, tables):
    tokens = normed.shape[0]
    rows, cols = pieces[masks[0]][0].shape[-2:]
    first, last = held is None, tables is not None
    count = len(masks)
    args = [idx, resident(normed)] + [w for m in masks for w in pieces[m]]
    in_specs = [SMEM, VMEM] + [HBM] * (len(args) - 2)
    if not first:
        in_specs.append(VMEM)
        args.append(resident(held))
    acc_shape = (2, tokens, cols)
    scratch = [pltpu.VMEM((count, 2, rows, cols), jnp.bfloat16), pltpu.SemaphoreType.DMA((2, count))]
    if last:
        in_specs.append(HBM)
        args.append(in_hbm(tables))
        out_specs = [VMEM] * 2
        out_shape = [pltpu.VMEM((tokens, cols), jnp.bfloat16)] * 2
        scratch.insert(1, pltpu.VMEM(acc_shape, jnp.float32))
        scratch.insert(2, pltpu.VMEM(tables.shape, jnp.float32))
        scratch.append(pltpu.SemaphoreType.DMA)
    else:
        out_specs = VMEM
        out_shape = pltpu.VMEM(acc_shape, jnp.float32)
    return pl.pallas_call(
        functools.partial(project_kernel, tuple(masks), first, last),
        in_specs=in_specs,
        out_specs=out_specs,
        out_shape=out_shape,
        scratch_shapes=scratch,
        compiler_params=params(10),
        cost_estimate=COST,
        name="project",
    )(*args)


HEADS = 1


def stacked(ref, row, col, r, first, count):
    rows = pl.ds(pl.multiple_of(row + r * TILE, TILE), TILE)
    at = lambda g: pl.ds(pl.multiple_of(col + g * HD, HD), HD)
    return jnp.concatenate([ref[rows, at(g)] for g in range(first, first + count)], axis=0)


def live_readout(ref, row, col, r, first, count, length):
    x = stacked(ref, row, col, r, first, count).astype(jnp.float32)
    at = lax.broadcasted_iota(jnp.int32, x.shape, 0) % TILE + r * TILE
    return jnp.where(at < length, x, 0.0).astype(jnp.bfloat16)


def places(step, q_ref, k_ref):
    heads = k_ref.shape[1] // HD
    seq, h = step // heads, step % heads
    return seq, h, seq * LEN, pl.multiple_of(h * HD, HD), h * (q_ref.shape[1] // heads)


def attend_kernel(keep, len_ref, q_ref, k_ref, v_ref, ro_ref, *rest):
    groups = q_ref.shape[1] // k_ref.shape[1]
    count = min(groups, HEADS)
    if keep:
        before_ref, margin_ref, prob_ref, delta_ref = rest
    else:
        (margin_ref,) = rest

    def one(step, margin):
        seq, h, row, col, q_col = places(step, q_ref, k_ref)
        length = len_ref[seq]
        score = jnp.zeros((1, count * TILE), jnp.float32)
        j = lax.broadcasted_iota(jnp.int32, (TILE, count * TILE), 0)
        i = lax.broadcasted_iota(jnp.int32, (TILE, count * TILE), 1) % TILE
        base = 0
        for r in range(LEN // TILE):
            n = (r + 1) * TILE
            keys = (pl.ds(pl.multiple_of(row, TILE), n), pl.ds(col, HD))
            for g in range(0, groups, count):
                q = stacked(q_ref, row, q_col, r, g, count)
                ro = live_readout(ro_ref, row, q_col, r, g, count, length)
                s = dot(k_ref[keys], q, NT)
                dp = dot(v_ref[keys], ro, NT)
                s = [s[b * TILE : (b + 1) * TILE] for b in range(r + 1)]
                s[r] = jnp.where(j <= i, s[r], -1e30)
                top = functools.reduce(jnp.maximum, [jnp.max(x, axis=0, keepdims=True) for x in s])
                e = [jnp.exp2((x - top) * (logit_scale * math.log2(math.e))) for x in s]
                inverse = 1.0 / functools.reduce(jnp.add, [jnp.sum(x, axis=0, keepdims=True) for x in e])
                cols = slice(g * TILE, (g + count) * TILE)
                delta = jnp.zeros((1, count * TILE), jnp.float32)
                for b in range(r + 1):
                    p = (e[b] * inverse).astype(jnp.bfloat16)
                    if keep:
                        prob_ref[seq, h, base + b * TILE : base + (b + 1) * TILE, cols] = p
                    delta = delta + jnp.sum(p.astype(jnp.float32) * dp[b * TILE : (b + 1) * TILE], axis=0, keepdims=True)
                if keep:
                    delta_ref[seq, h, r : r + 1, cols] = delta
                score = score + delta
            base += n
        side = jnp.where(seq % 2 == 0, 1.0, -1.0) * (dpo_beta / math.sqrt(QH * HD))
        return margin + jnp.sum(score, axis=1, keepdims=True) * side

    steps = k_ref.shape[0] // LEN * (k_ref.shape[1] // HD)
    start = -before_ref[0:1, 0:1] if keep else jnp.zeros((1, 1), jnp.float32)
    margin_ref[...] = jnp.broadcast_to(lax.fori_loop(0, steps, one, start, unroll=keep), margin_ref.shape)


def attend(lengths, queries, keys, values, readout, before=None):
    seqs = lengths.shape[0]
    heads = keys.shape[1] // HD
    wide = queries.shape[1] // heads
    tiles = LEN // TILE
    span = TILE * tiles * (tiles + 1) // 2
    keep = before is not None
    args = [lengths] + [resident(x) for x in (queries, keys, values, readout)]
    out_shape = [jax.ShapeDtypeStruct((8, 128), jnp.float32)]
    if keep:
        args.append(before)
        out_shape += [pltpu.VMEM((seqs, heads, span, wide), jnp.bfloat16), pltpu.VMEM((seqs, heads, tiles, wide), jnp.float32)]
    return pl.pallas_call(
        functools.partial(attend_kernel, keep),
        in_specs=[SMEM] + [VMEM] * (len(args) - 1),
        out_specs=[VMEM] * len(out_shape),
        out_shape=out_shape,
        compiler_params=params(8),
        cost_estimate=COST,
        name="attend",
    )(*args)


def attend_back_kernel(len_ref, q_ref, v_ref, ro_ref, prob_ref, delta_ref, table_ref, grad_ref):
    tiles = LEN // TILE
    groups = q_ref.shape[1] // v_ref.shape[1]
    count = min(groups, HEADS)

    def one(step, carry):
        seq, h, row, col, q_col = places(step, q_ref, v_ref)
        length = len_ref[seq]
        dk = [None] * tiles
        dv = [None] * tiles
        base = 0
        for r in range(tiles):
            n = (r + 1) * TILE
            keys = (pl.ds(pl.multiple_of(row, TILE), n), pl.ds(col, HD))
            for g in range(0, groups, count):
                q = stacked(q_ref, row, q_col, r, g, count)
                ro = live_readout(ro_ref, row, q_col, r, g, count, length)
                cols = slice(g * TILE, (g + count) * TILE)
                p = prob_ref[seq, h, base : base + n, cols]
                dp = dot(v_ref[keys], ro, NT)
                ds = (p.astype(jnp.float32) * (dp - delta_ref[seq, h, r : r + 1, cols])).astype(jnp.bfloat16)
                tk = dot(ds, q, NN)
                tv = dot(p, ro, NN)
                for b in range(r + 1):
                    at = slice(b * TILE, (b + 1) * TILE)
                    dk[b] = tk[at] if dk[b] is None else dk[b] + tk[at]
                    dv[b] = tv[at] if dv[b] is None else dv[b] + tv[at]
            base += n
        scale = jnp.where(seq % 2 == 0, -1.0, 1.0) * (1.0 / math.sqrt(QH * HD))
        for b in range(tiles):
            at = slice(b * TILE, (b + 1) * TILE)
            to = (pl.ds(col, HD), pl.ds(pl.multiple_of(row + b * TILE, TILE), TILE))
            k = dk[b] * (scale * logit_scale)
            k = k * table_ref[0, at, :] - pltpu.roll(k, HD // 2, 1) * table_ref[1, at, :]
            grad_ref[(0, *to)] = k.T.astype(jnp.bfloat16)
            grad_ref[(1, *to)] = (dv[b] * scale).T.astype(jnp.bfloat16)
        return carry

    steps = v_ref.shape[0] // LEN * (v_ref.shape[1] // HD)
    lax.fori_loop(0, steps, one, 0, unroll=True)


def attend_back(lengths, queries, values, readout, probs, delta, tables):
    return pl.pallas_call(
        attend_back_kernel,
        in_specs=[SMEM] + [VMEM] * 6,
        out_specs=VMEM,
        out_shape=pltpu.VMEM((2,) + values.shape[::-1], jnp.bfloat16),
        compiler_params=params(8),
        cost_estimate=COST,
        name="attend_back",
    )(lengths, *[resident(x) for x in (queries, values, readout, probs, delta, tables)])


def gradient_tiles(idx, mask, x_ref, cot_ref, rows):
    cols = cot_ref.shape[1]
    both = jnp.concatenate([cot_ref[0], cot_ref[1]], axis=0)
    tile = min(rows, 256)
    for t in range(rows // tile):
        col = pl.multiple_of((idx ^ mask) * rows + t * tile, tile)
        out = dot(both, x_ref[:, pl.ds(col, tile)], NN)
        for i in (0, 1):
            yield i, t * tile, tile, out[i * cols : (i + 1) * cols]


def gradient_kernel(masks, idx_ref, x_ref, cot_ref, *outs):
    outs = outs[len(outs) - len(masks) :]
    for mask, out_ref in zip(masks, outs):
        for i, start, tile, value in gradient_tiles(idx_ref[0], mask, x_ref, cot_ref, out_ref.shape[2]):
            out_ref[i, :, start : start + tile] = value.astype(out_ref.dtype)


def merged_kernel(masks, idx_ref, x_ref, cot_ref, mine_ref, their_ref, *refs):
    count = len(masks)
    theirs_hbm, outs = refs[:count], refs[count : 3 * count]
    theirs, sem = refs[3 * count :]
    rows = theirs.shape[3]
    copies = [pltpu.make_async_copy(theirs_hbm[n], theirs.at[n], sem.at[n]) for n in range(count)]
    for copy in copies:
        copy.start()
    mine, their = (ref[0:1, :] for ref in (mine_ref, their_ref))
    mine, their = (jax.nn.sigmoid(-x) for x in (mine, their))
    for n, mask in enumerate(masks):
        copies[n].wait()
        for i, start, tile, value in gradient_tiles(idx_ref[0], mask, x_ref, cot_ref, rows):
            wide = lambda x: jnp.concatenate([x] * (tile // 128), axis=1)
            value = value * wide(mine) + theirs[n, i, :, start : start + tile].astype(jnp.float32) * wide(their)
            outs[2 * n + i][:, start : start + tile] = value.astype(outs[2 * n + i].dtype)


def gradient_blocks(idx, normed, cot, masks, rows, merge=None, earlier=()):
    _, cols, tokens = cot.shape
    args = [idx, resident(normed), resident(cot)]
    in_specs = [SMEM, VMEM, VMEM]
    scratch = []
    if merge is None:
        kernel, name = gradient_kernel, "gradient_block"
        out_shape = [jax.ShapeDtypeStruct((2, cols, rows), jnp.bfloat16) for m in masks]
        args += earlier
        in_specs += [HBM] * len(earlier)
    else:
        kernel, name = merged_kernel, "merged_block"
        margins, theirs = merge
        args += [*margins] + [theirs[m] for m in masks]
        in_specs += [VMEM] * 2 + [HBM] * len(masks)
        out_shape = [
            jax.ShapeDtypeStruct((cols, rows), jnp.bfloat16) if m else pltpu.VMEM((cols, rows), jnp.float32)
            for m in masks
            for i in (0, 1)
        ]
        scratch = [pltpu.VMEM((len(masks), 2, cols, rows), jnp.bfloat16), pltpu.SemaphoreType.DMA((len(masks),))]
    outs = pl.pallas_call(
        functools.partial(kernel, tuple(masks)),
        in_specs=in_specs,
        out_specs=[VMEM] * len(out_shape),
        out_shape=out_shape,
        scratch_shapes=scratch,
        compiler_params=params(10),
        cost_estimate=COST,
        name=name,
    )(*args)
    return outs if merge is None else [outs[2 * n : 2 * n + 2] for n in range(len(masks))]


def finish_kernel(half, counts, *refs):
    refs = list(refs)
    out_ref, square_ref = refs[-2:]
    refs = refs[:-2]
    square_ref[...] = jnp.zeros_like(square_ref)
    _, rows, cols = out_ref.shape
    for i in (0, 1):
        terms = [refs.pop(0) for _ in range(1 + counts[i])]
        squares = jnp.zeros((1, 128), jnp.float32)
        for c in range(0, cols, 128):
            for r in range(0, rows, 128):
                at = [slice(x, x + 128) for x in (r if t.shape[1] == rows else half * rows + r for t in terms)]
                value = functools.reduce(jnp.add, [t[c : c + 128, x].astype(jnp.float32) for t, x in zip(terms, at)])
                squares = squares + jnp.sum(value * value, axis=0, keepdims=True)
                out_ref[i, r : r + 128, c : c + 128] = value.T.astype(jnp.bfloat16)
        square_ref[i : i + 1, :] = jnp.broadcast_to(jnp.sum(squares, axis=1, keepdims=True), (1, 128))


def finish(base, arrived, half):
    args = [x for i in (0, 1) for x in (resident(base[i]), *arrived[i])]
    cols, rows = base[0].shape
    return pl.pallas_call(
        functools.partial(finish_kernel, half, [len(a) for a in arrived]),
        in_specs=[VMEM] * len(args),
        out_specs=[VMEM] * 2,
        out_shape=[jax.ShapeDtypeStruct((2, rows // 2, cols), jnp.bfloat16), jax.ShapeDtypeStruct((8, 128), jnp.float32)],
        compiler_params=params(8),
        cost_estimate=COST,
        name="finish",
    )(*args)


def hand_on_kernel(count, *refs):
    pass


def hand_on(arrays, earlier):
    count = len(arrays)
    return pl.pallas_call(
        functools.partial(hand_on_kernel, count),
        in_specs=[HBM] * (count + 1),
        out_specs=[HBM] * count,
        out_shape=[jax.ShapeDtypeStruct(x.shape, x.dtype) for x in arrays],
        input_output_aliases={n: n for n in range(count)},
        compiler_params=params(2),
        cost_estimate=COST,
        name="hand_on",
    )(*arrays, earlier)


def gate_kernel(value_ref, margin_ref, *refs):
    out_ref, first_ref = refs[-2:]
    out_ref[...] = value_ref[...]
    first_ref[0] = margin_ref[0, 0]


def gate(value, margin, *earlier):
    return pl.pallas_call(
        gate_kernel,
        in_specs=[VMEM, VMEM] + [HBM] * len(earlier),
        out_specs=[VMEM, SMEM],
        out_shape=[jax.ShapeDtypeStruct(value.shape, value.dtype), jax.ShapeDtypeStruct((1,), jnp.float32)],
        compiler_params=params(2),
        cost_estimate=COST,
        name="gate",
    )(value, margin, *earlier)


def pack_kernel(takes, parts, *refs):
    sources, outs, sem = refs[: parts * len(takes)], refs[-1 - len(takes) : -1], refs[-1]
    copies = []
    for n, i in enumerate(takes):
        half = sources[parts * n].shape[1]
        for h in range(parts):
            source, at = sources[parts * n + h], pl.ds(h * half, half)
            if i is None:
                copies.append(pltpu.make_async_copy(source, outs[n].at[:, at, :], sem.at[n, h]))
            else:
                copies.append(pltpu.make_async_copy(source.at[i], outs[n].at[at, :], sem.at[n, h]))
    for copy in copies:
        copy.start()
    for copy in copies:
        copy.wait()


def pack(sources, takes, *earlier):
    parts = len(sources[0])
    _, half, cols = sources[0][0].shape
    shapes = [(2, parts * half, cols) if i is None else (parts * half, cols) for i in takes]
    return pl.pallas_call(
        functools.partial(pack_kernel, tuple(takes), parts),
        in_specs=[HBM] * (parts * len(takes) + len(earlier)),
        out_specs=[HBM] * len(takes),
        out_shape=[jax.ShapeDtypeStruct(shape, jnp.bfloat16) for shape in shapes],
        scratch_shapes=[pltpu.SemaphoreType.DMA((len(takes), 2))],
        compiler_params=params(2),
        cost_estimate=COST,
        name="pack",
    )(*[x for pair in sources for x in pair], *earlier)


def fetch_kernel(masks, idx_ref, *refs):
    refs = list(refs)
    pieces = [[refs.pop(0) for _ in range(1 if is_whole(m) else 2)] for m in masks]
    ref_hbm, _, w, r, sem = refs
    rows = r.shape[2]
    copies = []
    for n, mask in enumerate(masks):
        at = pl.ds(pl.multiple_of((idx_ref[0] ^ mask) * rows, rows), rows)
        copies += read_rows(pieces[n], w.at[n], [sem.at[i, n] for i in (0, 1)])
        copies.append(pltpu.make_async_copy(ref_hbm.at[:, at, :], r.at[n], sem.at[2, n]))
    for copy in copies:
        copy.start()
    for copy in copies:
        copy.wait()


def fetch(idx, weights, reference, masks, earlier):
    rows, cols = weights[masks[0]][0].shape[-2:]
    count = len(masks)
    args = [idx] + [w for m in masks for w in weights[m]] + [in_hbm(reference), earlier]
    return pl.pallas_call(
        functools.partial(fetch_kernel, tuple(masks)),
        in_specs=[SMEM] + [HBM] * (len(args) - 1),
        out_specs=[VMEM] * 2,
        out_shape=[pltpu.VMEM((count, 2, rows, cols), jnp.bfloat16)] * 2,
        scratch_shapes=[pltpu.SemaphoreType.DMA((3, count))],
        compiler_params=params(4),
        cost_estimate=COST,
        name="fetch",
    )(*args)


def blend_kernel(masks, first, offset, idx_ref, square_ref, *refs):
    refs = list(refs)
    count = len(masks)
    grads = [[refs.pop(0) for _ in range(1 if m & 1 and is_whole(m) else 2)] for m in masks]
    w, r = refs.pop(0), refs.pop(0)
    if not first:
        refs.pop(0)
    out_hbm, token_ref = refs.pop(0), refs.pop(0)
    new_hbm = refs.pop(0) if first else None
    g, o, new, sem, out_sem = refs
    rows, cols = g.shape[2:]
    step = 64
    half = rows // 2
    token_ref[...] = jnp.zeros_like(token_ref)
    here = [not is_whole(m) for m in masks]
    coming = [[] if here[n] else read_rows(grads[n], g.at[n], [sem.at[i, n] for i in (0, 1)]) for n in range(count)]
    for group in coming:
        for copy in group:
            copy.start()
    mean = square_ref[...] * (1.0 / (D * KVH * HD))
    scale = jnp.concatenate([learning_rate * lax.rsqrt(mean + norm_eps)] * (cols // 128), axis=1)
    writes = []
    for n in range(count):
        for copy in coming[n]:
            copy.wait()
        for part in range(2):

            def mix(t, carry):
                j = pl.ds(pl.multiple_of(part * half + t * step, step), step)
                for i in (0, 1):
                    slope = grads[n][i][j, :] if here[n] else g[n, i, j]
                    value = w[offset + n, i, j].astype(jnp.float32) - scale[i : i + 1, :] * slope.astype(jnp.float32)
                    value = value.astype(jnp.bfloat16)
                    if first and n == 0:
                        new[i, j] = value
                    mixed = mix_alpha * value.astype(jnp.float32) + (1.0 - mix_alpha) * r[offset + n, i, j].astype(jnp.float32)
                    o[n, i, j] = mixed.astype(jnp.bfloat16)
                return carry

            lax.fori_loop(0, half // step, mix, 0, unroll=2)
            at = pl.ds(pl.multiple_of((idx_ref[0] ^ masks[n]) * rows + part * half, half), half)
            writes.append(pltpu.make_async_copy(o.at[n, :, pl.ds(part * half, half), :], out_hbm.at[:, at, :], out_sem.at[part, n]))
            writes[-1].start()
        if first and n == 0:
            writes.append(pltpu.make_async_copy(new, new_hbm, out_sem.at[0, count]))
            writes[-1].start()
    for copy in writes:
        copy.wait()


def blend(idx, squares, grads, reference, held, masks, ready, offset):
    w, r = ready
    _, _, rows, cols = w.shape
    count = len(masks)
    first = held is None
    args = [idx, squares] + [x if is_whole(m) else resident(x) for m in masks for x in grads[m]]
    in_specs = [SMEM, VMEM] + [HBM if is_whole(m) else VMEM for m in masks for x in grads[m]]
    args += [resident(w), resident(r)]
    in_specs += [VMEM] * 2
    out_specs = [HBM, VMEM]
    out_shape = [jax.ShapeDtypeStruct(reference.shape, jnp.bfloat16), jax.ShapeDtypeStruct((8, 128), jnp.float32)]
    aliases = {}
    if first:
        out_specs.append(HBM)
        out_shape.append(jax.ShapeDtypeStruct((2, rows, cols), jnp.bfloat16))
    else:
        aliases = {len(args): 0}
        in_specs.append(HBM)
        args.append(held)
    block = pltpu.VMEM((count, 2, rows, cols), jnp.bfloat16)
    return pl.pallas_call(
        functools.partial(blend_kernel, tuple(masks), first, offset),
        in_specs=in_specs,
        out_specs=out_specs,
        out_shape=out_shape,
        scratch_shapes=[
            block,
            block,
            pltpu.VMEM((2, rows, cols) if first else (8, 128), jnp.bfloat16),
            pltpu.SemaphoreType.DMA((2, count)),
            pltpu.SemaphoreType.DMA((2, count + 1)),
        ],
        input_output_aliases=aliases,
        compiler_params=params(12),
        cost_estimate=COST,
        name="blend",
    )(*args)


def bits_of(mask):
    return [1 << b for b in range(mask.bit_length()) if mask >> b & 1]


def after(value, *earlier):
    return lax.optimization_barrier((value, earlier))[0]


def body(shards, tensors, hidden_in, policy_weights, reference_weights, policy_queries, reference_queries, readout, lengths):
    rows = policy_weights.shape[1]
    idx = lax.axis_index("shard").astype(jnp.int32).reshape(1)
    tables = jnp.asarray(rope_tables())

    def swap(x, bit, axis="shard", size=shards):
        return lax.ppermute(x, axis, [(i, i ^ bit) for i in range(size)])

    def powers(size):
        return [1 << b for b in range(size.bit_length() - 1)]

    chips = sorted(range(0, shards, 2), key=lambda m: (len(bits_of(m)), m))
    near = [m for m in chips if len(bits_of(m)) == 1]
    far = [m for m in chips if len(bits_of(m)) > 1]
    link = lambda i, m: bits_of(m)[-1] if i == 0 else bits_of(m)[0]

    def send_near(own):
        got = {m: [swap(own, m)] for m in near}
        got[0] = [own]
        got[1] = [swap(own, 1)]
        return got

    def relay(got, m, *earlier):
        got[m] = [None, None]
        for i in (0, 1):
            via = link(i, m)
            source = got[m ^ via]
            source = source[i] if source[0].ndim == 2 else source[0][i]
            got[m][i] = swap(after(source, *earlier), via)

    def to_core(got, m, *earlier):
        got[m | 1] = [swap(after(g, *earlier), 1) for g in got[m]]

    weights = send_near(policy_weights)
    normed, ref_keys, ref_values = norm_project(idx, hidden_in, reference_weights, tables)
    (ref_margin,) = attend(lengths, reference_queries, ref_keys, ref_values, readout)
    two = [m for m in far if len(bits_of(m)) == 2]
    ends = [(m, i) for m in two for i in (0, 1)]
    packed = {}
    if two:
        packed = dict(zip(ends, pack([weights[m ^ link(i, m)] for m, i in ends], [i for m, i in ends], ref_margin)))
    for m in far:
        weights[m] = [swap(packed[m, i] if m in two else weights[m ^ link(i, m)][i], link(i, m)) for i in (0, 1)]
    for m in near:
        to_core(weights, m, ref_margin)
    held = project(idx, normed, [0, 1], weights, None, None)
    held = project(idx, normed, [m | c for m in near for c in (0, 1)], weights, held, None if far else tables)
    if far:
        for m in far:
            to_core(weights, m, held)
        held = project(idx, normed, far, weights, held, None)
        held = project(idx, normed, [m | 1 for m in far], weights, held, tables)
    pol_keys, pol_values = held
    margin, probs, delta = attend(lengths, policy_queries, pol_keys, pol_values, readout, ref_margin)

    theirs = {}
    order = list(reversed(chips))
    split = max(len(far), 1)

    def other_blocks(masks, margin, other=None):
        blocks = gradient_blocks(idx, normed, cot, [m | 1 for m in masks], rows, None, (margin,))
        if other is not None:
            blocks = hand_on(blocks, other)
        theirs.update({m: swap(block, 1) for m, block in zip(masks, blocks)})
        return blocks

    received = [swap(margin, m, "tensor", tensors) for m in range(1, tensors)]
    cot = attend_back(lengths, policy_queries, pol_values, readout, probs, delta, tables)
    terms = [margin] + [after(x, cot) for x in received]
    while len(terms) > 1:
        terms = [a + b for a, b in zip(terms[::2], terms[1::2])]
    (margin,) = terms
    received = swap(margin, 1)
    margins = (margin, after(received, other_blocks(order[:split], margin)))
    other_blocks(order[split:], margin, margins[1])

    chip_sum = {}
    arrived = {m: ([], []) for m in chips}
    halves = ([[], []], [[], []])
    waiting = []

    def send(m, i, half=None):
        terms = [chip_sum[m][i], *arrived[m][i]]
        if half is not None:
            terms = [t[:, half * rows // 2 : (half + 1) * rows // 2] for t in terms]
        payload = terms[0]
        if len(terms) > 1:
            payload = sum(t.astype(jnp.float32) for t in terms).astype(jnp.bfloat16)
        via = link(i, m)
        received = swap(payload, via)
        if half is None:
            arrived[m ^ via][i].append(received)
        else:
            halves[half][i].append(received)

    for masks in (order[:split], order[split:]):
        chip_sum.update(zip(masks, gradient_blocks(idx, normed, cot, masks, rows, (margins, theirs))))
        for m in masks:
            for i in (0, 1):
                if m and not any(k ^ link(i, k) == m for k in far):
                    send(m, i)
                elif m:
                    waiting.append((m, i))
    for m, i in waiting:
        if m in far:
            send(m, i)

    for half in (0, 1):
        for m, i in waiting:
            if m in near:
                send(m, i, half)
    grads = {m: [] for m in [0] + near}
    parts = []
    for half in (0, 1):
        own, part = finish(chip_sum[0], [arrived[0][i] + halves[half][i] for i in (0, 1)], half)
        parts.append(part)
        grads[0].append(own)
        for m in near:
            grads[m].append(swap(own, m))
    squares = parts[0] + parts[1]
    for bit in powers(tensors):
        squares = squares + swap(squares, bit, "tensor", tensors)
    squares = squares + swap(squares, 1)
    squares, margin_out = gate(squares, margin, *[grads[m][0] for m in near])
    masks = [m | c for m in [0] + near for c in (0, 1)] + [m | c for c in (0, 1) for m in far]
    ready = fetch(idx, weights, reference_weights, masks, squares)
    terms = [squares] + [swap(squares, m) for m in chips[1:]]
    while len(terms) > 1:
        terms = [a + b for a, b in zip(terms[::2], terms[1::2])]
    (squares,) = terms
    two = [m for m in far if len(bits_of(m)) == 2]
    ends = [(m, i) for m in two for i in (0, 1)]
    whole = [0] + near
    packed = pack([grads[m ^ link(i, m)] for m, i in ends] + [grads[m] for m in whole], [i for m, i in ends] + [None] * len(whole), squares, ready[0])
    packed = dict(zip(ends + whole, packed))
    for m in far:
        grads[m] = [swap(packed[m, i] if m in two else grads[m ^ link(i, m)][i], link(i, m)) for i in (0, 1)]
    for m in whole:
        grads[m | 1] = [swap(packed[m], 1)]
    groups = [[0, 1], [m | c for m in near for c in (0, 1)]] + [[m | c for m in far] for c in (0, 1)]
    new_reference, at = None, 0
    for group in groups:
        if group == far and far:
            for m in far:
                to_core(grads, m, token)
        if group:
            outs = blend(idx, squares, grads, reference_weights, new_reference, group, ready, at)
            new_reference, token = outs[:2]
            new_policy = outs[2] if at == 0 else new_policy
            at += len(group)
    return (new_policy, new_reference, margin_out)


def solution(mesh):
    return jax.shard_map(
        functools.partial(body, mesh.shape["shard"], mesh.shape["tensor"]),
        mesh=mesh,
        in_specs=(
            P("shard", None),
            P(None, "shard", "tensor"),
            P(None, None, "tensor"),
            P("shard", "tensor"),
            P("shard", "tensor"),
            P("shard", "tensor"),
            P("shard"),
        ),
        out_specs=(P(None, "shard", "tensor"), P(None, None, "tensor"), P("shard")),
        check_vma=False,
    )
```

```python
import functools
import math

import jax
import jax.numpy as jnp
import numpy as np
from jax import lax
from jax.experimental import pallas as pl
from jax.experimental.pallas import tpu as pltpu
from jax.sharding import PartitionSpec as P

D = 8192
HD = 128
KVH = 8
QH = 32
LEN = 384
TILE = 128

rope_base = 1000000.0
dpo_beta = 0.1
learning_rate = 0.2
mix_alpha = 0.6
norm_eps = 1e-06
width_scale = D ** (-0.5)
logit_scale = 1.0 / math.sqrt(HD)
MIB = 1024 * 1024

NT = (((1,), (1,)), ((), ()))
NN = (((1,), (0,)), ((), ()))
TN = (((0,), (0,)), ((), ()))


def dot(a, b, dims):
    return lax.dot_general(a, b, dims, preferred_element_type=jnp.float32)


def params(mib):
    return pltpu.CompilerParams(vmem_limit_bytes=mib * MIB)


COST = pl.CostEstimate(flops=1, bytes_accessed=1, transcendentals=0)
LONG = pl.CostEstimate(flops=1, bytes_accessed=40 * 1000 * 1000, transcendentals=0)
VMEM = pl.BlockSpec(memory_space=pltpu.VMEM)
SMEM = pl.BlockSpec(memory_space=pltpu.SMEM)
HBM = pl.BlockSpec(memory_space=pl.ANY)


def resident(x):
    return pltpu.with_memory_space_constraint(x, pltpu.VMEM)


def in_hbm(x):
    return pltpu.with_memory_space_constraint(x, pltpu.HBM)


def rope_tables():
    frequency = rope_base ** (-2.0 * np.arange(HD // 2) / HD)
    angles = np.arange(LEN)[:, None] * frequency[None, :]
    cosine, sine = np.cos(angles), np.sin(angles)
    return np.stack([np.concatenate([cosine, cosine], axis=1), np.concatenate([-sine, sine], axis=1)]).astype(np.float32)


def store_heads(acc_ref, cos, sin, key_ref, value_ref):
    for s in range(key_ref.shape[0] // LEN):
        rows = slice(s * LEN, (s + 1) * LEN)
        for h in range(key_ref.shape[1] // HD):
            cols = slice(h * HD, (h + 1) * HD)
            k = acc_ref[0, rows, cols] * width_scale
            key_ref[rows, cols] = (k * cos + pltpu.roll(k, HD // 2, 1) * sin).astype(jnp.bfloat16)
    value_ref[...] = (acc_ref[1] * width_scale).astype(jnp.bfloat16)


def norm_project_kernel(idx_ref, hidden_hbm, weight_hbm, table_hbm, normed_ref, key_ref, value_ref, w, acc, part, table, in_sem, w_sem, table_sem):
    tokens = normed_ref.shape[0]
    step, width, span, chunk = 16, 512, 128, 1024
    reads = []
    for i in range(tokens // span):
        at = pl.ds(i * span, span)
        reads.append(pltpu.make_async_copy(hidden_hbm.at[at], normed_ref.at[at], in_sem.at[i]))
    loads = []
    for c in range(D // chunk):
        at = pl.ds(c * chunk, chunk)
        loads.append(pltpu.make_async_copy(weight_hbm.at[:, at, :], w.at[:, at, :], w_sem.at[c]))
    loads.append(pltpu.make_async_copy(table_hbm, table, table_sem))
    for copy in reads + loads:
        copy.start()

    def row_step(i, carry):
        at = pl.ds(pl.multiple_of(i * step, step), step)
        total = jnp.zeros((step, width), jnp.float32)
        for c in range(D // width):
            v = normed_ref[at, c * width : (c + 1) * width].astype(jnp.float32)
            total = total + v * v
        part[at, :] = functools.reduce(jnp.add, [total[:, c * 128 : (c + 1) * 128] for c in range(width // 128)])
        return carry

    for i, copy in enumerate(reads):
        copy.wait()
        lax.fori_loop(i * (span // step), (i + 1) * (span // step), row_step, 0)
    for copy in loads:
        copy.wait()
    mean = jnp.sum(part[...], axis=1, keepdims=True) * (1.0 / D)
    part[...] = jnp.broadcast_to(lax.rsqrt(mean + norm_eps), part.shape)

    def columns(c):
        return pl.ds(pl.multiple_of(c * chunk, chunk), chunk)

    def normalise(c):
        for i in range(tokens // step):
            rows = slice(i * step, (i + 1) * step)
            scale = jnp.concatenate([part[rows, :]] * (chunk // 128), axis=1)
            normed_ref[rows, columns(c)] = (normed_ref[rows, columns(c)].astype(jnp.float32) * scale).astype(jnp.bfloat16)

    def multiply(c, carry):
        for i in (0, 1):
            acc[i] += dot(normed_ref[:, columns(c)], w[i, columns(c), :], NN)

        @pl.when(c + 1 < D // chunk)
        def _():
            normalise(c + 1)

        return carry

    acc[...] = jnp.zeros_like(acc)
    normalise(0)
    lax.fori_loop(0, D // chunk, multiply, 0)
    store_heads(acc, table[0], table[1], key_ref, value_ref)


def norm_project(idx, hidden, weights, tables):
    tokens = hidden.shape[0]
    cols = weights.shape[2]
    return pl.pallas_call(
        norm_project_kernel,
        in_specs=[SMEM, HBM, HBM, HBM],
        out_specs=[VMEM, VMEM, VMEM],
        out_shape=[
            pltpu.VMEM((tokens, D), jnp.bfloat16),
            pltpu.VMEM((tokens, cols), jnp.bfloat16),
            pltpu.VMEM((tokens, cols), jnp.bfloat16),
        ],
        scratch_shapes=[
            pltpu.VMEM((2, D, cols), jnp.bfloat16),
            pltpu.VMEM((2, tokens, cols), jnp.float32),
            pltpu.VMEM((tokens, 128), jnp.float32),
            pltpu.VMEM(tables.shape, jnp.float32),
            pltpu.SemaphoreType.DMA((tokens // 128,)),
            pltpu.SemaphoreType.DMA((D // 1024,)),
            pltpu.SemaphoreType.DMA,
        ],
        compiler_params=params(16),
        cost_estimate=COST,
        name="norm_project",
    )(idx, in_hbm(hidden), in_hbm(weights), in_hbm(tables))


def is_whole(mask):
    return len(bits_of(mask >> 1)) < 2


def read_rows(sources, target, sems):
    if len(sources) == 1:
        return [pltpu.make_async_copy(sources[0], target, sems[0])]
    if len(sources[0].shape) == 2:
        return [pltpu.make_async_copy(sources[i], target.at[i], sems[i]) for i in (0, 1)]
    half = sources[0].shape[1]
    return [pltpu.make_async_copy(sources[h], target.at[:, pl.ds(h * half, half), :], sems[h]) for h in (0, 1)]


def project_kernel(masks, first, last, idx_ref, x_ref, *refs):
    refs = list(refs)
    count = len(masks)
    pieces = [[refs.pop(0) for _ in range(1 if is_whole(m) else 2)] for m in masks]
    held = None if first else refs.pop(0)
    if last:
        table_hbm, key_ref, value_ref, w, acc, table, sem, table_sem = refs
        table_copy = pltpu.make_async_copy(table_hbm, table, table_sem)
        table_copy.start()
    else:
        acc, w, sem = refs
    depth = w.shape[2]
    copies = [read_rows(pieces[n], w.at[n], [sem.at[i, n] for i in (0, 1)]) for n in range(count)]
    for group in copies:
        for copy in group:
            copy.start()
    for n in range(count):
        for copy in copies[n]:
            copy.wait()
        col = pl.multiple_of((idx_ref[0] ^ masks[n]) * depth, depth)
        x = x_ref[:, pl.ds(col, depth)]
        for i in (0, 1):
            term = dot(x, w[n, i], NN)
            if n:
                term = acc[i] + term
            elif not first:
                term = held[i] + term
            acc[i] = term
    if last:
        table_copy.wait()
        store_heads(acc, table[0], table[1], key_ref, value_ref)


def project(idx, normed, masks, pieces, held, tables):
    tokens = normed.shape[0]
    rows, cols = pieces[masks[0]][0].shape[-2:]
    first, last = held is None, tables is not None
    count = len(masks)
    args = [idx, resident(normed)] + [w for m in masks for w in pieces[m]]
    in_specs = [SMEM, VMEM] + [HBM] * (len(args) - 2)
    if not first:
        in_specs.append(VMEM)
        args.append(resident(held))
    acc_shape = (2, tokens, cols)
    scratch = [pltpu.VMEM((count, 2, rows, cols), jnp.bfloat16), pltpu.SemaphoreType.DMA((2, count))]
    if last:
        in_specs.append(HBM)
        args.append(in_hbm(tables))
        out_specs = [VMEM] * 2
        out_shape = [pltpu.VMEM((tokens, cols), jnp.bfloat16)] * 2
        scratch.insert(1, pltpu.VMEM(acc_shape, jnp.float32))
        scratch.insert(2, pltpu.VMEM(tables.shape, jnp.float32))
        scratch.append(pltpu.SemaphoreType.DMA)
    else:
        out_specs = VMEM
        out_shape = pltpu.VMEM(acc_shape, jnp.float32)
    return pl.pallas_call(
        functools.partial(project_kernel, tuple(masks), first, last),
        in_specs=in_specs,
        out_specs=out_specs,
        out_shape=out_shape,
        scratch_shapes=scratch,
        compiler_params=params(10),
        cost_estimate=COST,
        name="project",
    )(*args)


FORWARD_HEADS = 1
BACKWARD_HEADS = 4


def stacked(ref, row, col, r, first, count):
    rows = pl.ds(pl.multiple_of(row + r * TILE, TILE), TILE)
    at = lambda g: pl.ds(pl.multiple_of(col + g * HD, HD), HD)
    return jnp.concatenate([ref[rows, at(g)] for g in range(first, first + count)], axis=0)


def live_readout(ref, row, col, r, first, count, length):
    x = stacked(ref, row, col, r, first, count).astype(jnp.float32)
    at = lax.broadcasted_iota(jnp.int32, x.shape, 0) % TILE + r * TILE
    return jnp.where(at < length, x, 0.0).astype(jnp.bfloat16)


def places(step, q_ref, k_ref):
    heads = k_ref.shape[1] // HD
    seq, h = step // heads, step % heads
    return seq, h, seq * LEN, pl.multiple_of(h * HD, HD), h * (q_ref.shape[1] // heads)


def attend_kernel(keep, len_ref, q_ref, k_ref, v_ref, ro_ref, *rest):
    groups = q_ref.shape[1] // k_ref.shape[1]
    count = min(groups, FORWARD_HEADS)
    if keep:
        before_ref, margin_ref, prob_ref, delta_ref = rest
    else:
        (margin_ref,) = rest

    def one(step, margin):
        seq, h, row, col, q_col = places(step, q_ref, k_ref)
        length = len_ref[seq]
        score = jnp.zeros((1, count * TILE), jnp.float32)
        j = lax.broadcasted_iota(jnp.int32, (TILE, count * TILE), 0)
        i = lax.broadcasted_iota(jnp.int32, (TILE, count * TILE), 1) % TILE
        base = 0
        for r in range(LEN // TILE):
            n = (r + 1) * TILE
            keys = (pl.ds(pl.multiple_of(row, TILE), n), pl.ds(col, HD))
            for g in range(0, groups, count):
                q = stacked(q_ref, row, q_col, r, g, count)
                ro = live_readout(ro_ref, row, q_col, r, g, count, length)
                s = dot(k_ref[keys], q, NT)
                dp = dot(v_ref[keys], ro, NT)
                s = [s[b * TILE : (b + 1) * TILE] for b in range(r + 1)]
                s[r] = jnp.where(j <= i, s[r], -1e30)
                top = functools.reduce(jnp.maximum, [jnp.max(x, axis=0, keepdims=True) for x in s])
                e = [jnp.exp2((x - top) * (logit_scale * math.log2(math.e))) for x in s]
                inverse = 1.0 / functools.reduce(jnp.add, [jnp.sum(x, axis=0, keepdims=True) for x in e])
                cols = slice(g * TILE, (g + count) * TILE)
                delta = jnp.zeros((1, count * TILE), jnp.float32)
                for b in range(r + 1):
                    p = (e[b] * inverse).astype(jnp.bfloat16)
                    if keep:
                        prob_ref[seq, h, base + b * TILE : base + (b + 1) * TILE, cols] = p
                    delta = delta + jnp.sum(p.astype(jnp.float32) * dp[b * TILE : (b + 1) * TILE], axis=0, keepdims=True)
                if keep:
                    delta_ref[seq, h, r : r + 1, cols] = delta
                score = score + delta
            base += n
        side = jnp.where(seq % 2 == 0, 1.0, -1.0) * (dpo_beta / math.sqrt(QH * HD))
        return margin + jnp.sum(score, axis=1, keepdims=True) * side

    steps = k_ref.shape[0] // LEN * (k_ref.shape[1] // HD)
    start = -before_ref[0:1, 0:1] if keep else jnp.zeros((1, 1), jnp.float32)
    margin_ref[...] = jnp.broadcast_to(lax.fori_loop(0, steps, one, start, unroll=keep), margin_ref.shape)


def attend(lengths, queries, keys, values, readout, before=None):
    seqs = lengths.shape[0]
    heads = keys.shape[1] // HD
    wide = queries.shape[1] // heads
    tiles = LEN // TILE
    span = TILE * tiles * (tiles + 1) // 2
    keep = before is not None
    args = [lengths] + [resident(x) for x in (queries, keys, values, readout)]
    out_shape = [jax.ShapeDtypeStruct((8, 128), jnp.float32)]
    if keep:
        args.append(before)
        out_shape += [pltpu.VMEM((seqs, heads, span, wide), jnp.bfloat16), pltpu.VMEM((seqs, heads, tiles, wide), jnp.float32)]
    return pl.pallas_call(
        functools.partial(attend_kernel, keep),
        in_specs=[SMEM] + [VMEM] * (len(args) - 1),
        out_specs=[VMEM] * len(out_shape),
        out_shape=out_shape,
        compiler_params=params(8),
        cost_estimate=COST,
        name="attend",
    )(*args)


def attend_back_kernel(len_ref, q_ref, v_ref, ro_ref, prob_ref, delta_ref, table_ref, grad_ref):
    tiles = LEN // TILE
    groups = q_ref.shape[1] // v_ref.shape[1]
    count = min(groups, BACKWARD_HEADS)

    def one(step, carry):
        seq, h, row, col, q_col = places(step, q_ref, v_ref)
        length = len_ref[seq]
        dk = [None] * tiles
        dv = [None] * tiles
        base = 0
        for r in range(tiles):
            n = (r + 1) * TILE
            keys = (pl.ds(pl.multiple_of(row, TILE), n), pl.ds(col, HD))
            for g in range(0, groups, count):
                q = stacked(q_ref, row, q_col, r, g, count)
                ro = live_readout(ro_ref, row, q_col, r, g, count, length)
                cols = slice(g * TILE, (g + count) * TILE)
                p = prob_ref[seq, h, base : base + n, cols]
                dp = dot(v_ref[keys], ro, NT)
                ds = (p.astype(jnp.float32) * (dp - delta_ref[seq, h, r : r + 1, cols])).astype(jnp.bfloat16)
                tk = dot(ds, q, NN)
                tv = dot(p, ro, NN)
                for b in range(r + 1):
                    at = slice(b * TILE, (b + 1) * TILE)
                    dk[b] = tk[at] if dk[b] is None else dk[b] + tk[at]
                    dv[b] = tv[at] if dv[b] is None else dv[b] + tv[at]
            base += n
        scale = jnp.where(seq % 2 == 0, -1.0, 1.0) * (1.0 / math.sqrt(QH * HD))
        for b in range(tiles):
            at = slice(b * TILE, (b + 1) * TILE)
            to = (pl.ds(col, HD), pl.ds(pl.multiple_of(row + b * TILE, TILE), TILE))
            k = dk[b] * (scale * logit_scale)
            k = k * table_ref[0, at, :] - pltpu.roll(k, HD // 2, 1) * table_ref[1, at, :]
            grad_ref[(0, *to)] = k.T.astype(jnp.bfloat16)
            grad_ref[(1, *to)] = (dv[b] * scale).T.astype(jnp.bfloat16)
        return carry

    steps = v_ref.shape[0] // LEN * (v_ref.shape[1] // HD)
    lax.fori_loop(0, steps, one, 0, unroll=True)


def attend_back(lengths, queries, values, readout, probs, delta, tables):
    return pl.pallas_call(
        attend_back_kernel,
        in_specs=[SMEM] + [VMEM] * 6,
        out_specs=VMEM,
        out_shape=pltpu.VMEM((2,) + values.shape[::-1], jnp.bfloat16),
        compiler_params=params(8),
        cost_estimate=COST,
        name="attend_back",
    )(lengths, *[resident(x) for x in (queries, values, readout, probs, delta, tables)])


def gradient_tiles(idx, mask, x_ref, cot_ref, rows):
    cols = cot_ref.shape[1]
    both = jnp.concatenate([cot_ref[0], cot_ref[1]], axis=0)
    tile = min(rows, 256)
    for t in range(rows // tile):
        col = pl.multiple_of((idx ^ mask) * rows + t * tile, tile)
        out = dot(both, x_ref[:, pl.ds(col, tile)], NN)
        for i in (0, 1):
            yield i, t * tile, tile, out[i * cols : (i + 1) * cols]


def gradient_kernel(masks, idx_ref, x_ref, cot_ref, *outs):
    outs = outs[len(outs) - len(masks) :]
    for mask, out_ref in zip(masks, outs):
        for i, start, tile, value in gradient_tiles(idx_ref[0], mask, x_ref, cot_ref, out_ref.shape[2]):
            out_ref[i, :, start : start + tile] = value.astype(out_ref.dtype)


def merged_kernel(masks, idx_ref, x_ref, cot_ref, mine_ref, their_ref, *refs):
    count = len(masks)
    theirs_hbm, outs = refs[:count], refs[count : 3 * count]
    theirs, sem = refs[3 * count :]
    rows = theirs.shape[3]
    copies = [pltpu.make_async_copy(theirs_hbm[n], theirs.at[n], sem.at[n]) for n in range(count)]
    for copy in copies:
        copy.start()
    mine, their = (ref[0:1, :] for ref in (mine_ref, their_ref))
    mine, their = (jax.nn.sigmoid(-x) for x in (mine, their))
    for n, mask in enumerate(masks):
        copies[n].wait()
        for i, start, tile, value in gradient_tiles(idx_ref[0], mask, x_ref, cot_ref, rows):
            wide = lambda x: jnp.concatenate([x] * (tile // 128), axis=1)
            value = value * wide(mine) + theirs[n, i, :, start : start + tile].astype(jnp.float32) * wide(their)
            outs[2 * n + i][:, start : start + tile] = value.astype(outs[2 * n + i].dtype)


def gradient_blocks(idx, normed, cot, masks, rows, merge=None, earlier=()):
    _, cols, tokens = cot.shape
    args = [idx, resident(normed), resident(cot)]
    in_specs = [SMEM, VMEM, VMEM]
    scratch = []
    if merge is None:
        kernel, name = gradient_kernel, "gradient_block"
        out_shape = [jax.ShapeDtypeStruct((2, cols, rows), jnp.bfloat16) for m in masks]
        args += earlier
        in_specs += [HBM] * len(earlier)
    else:
        kernel, name = merged_kernel, "merged_block"
        margins, theirs = merge
        args += [*margins] + [theirs[m] for m in masks]
        in_specs += [VMEM] * 2 + [HBM] * len(masks)
        out_shape = [
            jax.ShapeDtypeStruct((cols, rows), jnp.bfloat16) if m else pltpu.VMEM((cols, rows), jnp.float32)
            for m in masks
            for i in (0, 1)
        ]
        scratch = [pltpu.VMEM((len(masks), 2, cols, rows), jnp.bfloat16), pltpu.SemaphoreType.DMA((len(masks),))]
    outs = pl.pallas_call(
        functools.partial(kernel, tuple(masks)),
        in_specs=in_specs,
        out_specs=[VMEM] * len(out_shape),
        out_shape=out_shape,
        scratch_shapes=scratch,
        compiler_params=params(10),
        cost_estimate=COST,
        name=name,
    )(*args)
    return outs if merge is None else [outs[2 * n : 2 * n + 2] for n in range(len(masks))]


def finish_kernel(half, counts, *refs):
    refs = list(refs)
    out_ref, square_ref = refs[-2:]
    refs = refs[:-2]
    square_ref[...] = jnp.zeros_like(square_ref)
    _, rows, cols = out_ref.shape
    for i in (0, 1):
        terms = [refs.pop(0) for _ in range(1 + counts[i])]
        squares = jnp.zeros((1, 128), jnp.float32)
        for c in range(0, cols, 128):
            for r in range(0, rows, 128):
                at = [slice(x, x + 128) for x in (r if t.shape[1] == rows else half * rows + r for t in terms)]
                value = functools.reduce(jnp.add, [t[c : c + 128, x].astype(jnp.float32) for t, x in zip(terms, at)])
                squares = squares + jnp.sum(value * value, axis=0, keepdims=True)
                out_ref[i, r : r + 128, c : c + 128] = value.T.astype(jnp.bfloat16)
        square_ref[i : i + 1, :] = jnp.broadcast_to(jnp.sum(squares, axis=1, keepdims=True), (1, 128))


def finish(base, arrived, half):
    args = [x for i in (0, 1) for x in (resident(base[i]), *arrived[i])]
    cols, rows = base[0].shape
    return pl.pallas_call(
        functools.partial(finish_kernel, half, [len(a) for a in arrived]),
        in_specs=[VMEM] * len(args),
        out_specs=[VMEM] * 2,
        out_shape=[jax.ShapeDtypeStruct((2, rows // 2, cols), jnp.bfloat16), jax.ShapeDtypeStruct((8, 128), jnp.float32)],
        compiler_params=params(8),
        cost_estimate=COST,
        name="finish",
    )(*args)


def hand_on_kernel(count, *refs):
    pass


def hand_on(arrays, earlier):
    count = len(arrays)
    return pl.pallas_call(
        functools.partial(hand_on_kernel, count),
        in_specs=[HBM] * (count + 1),
        out_specs=[HBM] * count,
        out_shape=[jax.ShapeDtypeStruct(x.shape, x.dtype) for x in arrays],
        input_output_aliases={n: n for n in range(count)},
        compiler_params=params(2),
        cost_estimate=COST,
        name="hand_on",
    )(*arrays, earlier)


def gate_kernel(value_ref, margin_ref, *refs):
    out_ref, first_ref = refs[-2:]
    out_ref[...] = value_ref[...]
    first_ref[0] = margin_ref[0, 0]


def gate(value, margin, *earlier):
    return pl.pallas_call(
        gate_kernel,
        in_specs=[VMEM, VMEM] + [HBM] * len(earlier),
        out_specs=[VMEM, SMEM],
        out_shape=[jax.ShapeDtypeStruct(value.shape, value.dtype), jax.ShapeDtypeStruct((1,), jnp.float32)],
        compiler_params=params(2),
        cost_estimate=COST,
        name="gate",
    )(value, margin, *earlier)


def pack_kernel(takes, parts, *refs):
    sources, outs, sem = refs[: parts * len(takes)], refs[-1 - len(takes) : -1], refs[-1]
    copies = []
    for n, i in enumerate(takes):
        half = sources[parts * n].shape[1]
        for h in range(parts):
            source, at = sources[parts * n + h], pl.ds(h * half, half)
            if i is None:
                copies.append(pltpu.make_async_copy(source, outs[n].at[:, at, :], sem.at[n, h]))
            else:
                copies.append(pltpu.make_async_copy(source.at[i], outs[n].at[at, :], sem.at[n, h]))
    for copy in copies:
        copy.start()
    for copy in copies:
        copy.wait()


def pack(sources, takes, *earlier):
    parts = len(sources[0])
    _, half, cols = sources[0][0].shape
    shapes = [(2, parts * half, cols) if i is None else (parts * half, cols) for i in takes]
    return pl.pallas_call(
        functools.partial(pack_kernel, tuple(takes), parts),
        in_specs=[HBM] * (parts * len(takes) + len(earlier)),
        out_specs=[HBM] * len(takes),
        out_shape=[jax.ShapeDtypeStruct(shape, jnp.bfloat16) for shape in shapes],
        scratch_shapes=[pltpu.SemaphoreType.DMA((len(takes), 2))],
        compiler_params=params(2),
        cost_estimate=COST,
        name="pack",
    )(*[x for pair in sources for x in pair], *earlier)


def fetch_kernel(masks, idx_ref, *refs):
    refs = list(refs)
    pieces = [[refs.pop(0) for _ in range(1 if is_whole(m) else 2)] for m in masks]
    ref_hbm, _, w, r, sem = refs
    rows = r.shape[2]
    copies = []
    for n, mask in enumerate(masks):
        at = pl.ds(pl.multiple_of((idx_ref[0] ^ mask) * rows, rows), rows)
        copies += read_rows(pieces[n], w.at[n], [sem.at[i, n] for i in (0, 1)])
        copies.append(pltpu.make_async_copy(ref_hbm.at[:, at, :], r.at[n], sem.at[2, n]))
    for copy in copies:
        copy.start()
    for copy in copies:
        copy.wait()


def fetch(idx, weights, reference, masks, earlier):
    rows, cols = weights[masks[0]][0].shape[-2:]
    count = len(masks)
    args = [idx] + [w for m in masks for w in weights[m]] + [in_hbm(reference), earlier]
    return pl.pallas_call(
        functools.partial(fetch_kernel, tuple(masks)),
        in_specs=[SMEM] + [HBM] * (len(args) - 1),
        out_specs=[VMEM] * 2,
        out_shape=[pltpu.VMEM((count, 2, rows, cols), jnp.bfloat16)] * 2,
        scratch_shapes=[pltpu.SemaphoreType.DMA((3, count))],
        compiler_params=params(4),
        cost_estimate=COST,
        name="fetch",
    )(*args)


def blend_kernel(masks, first, offset, idx_ref, square_ref, *refs):
    refs = list(refs)
    count = len(masks)
    grads = [[refs.pop(0) for _ in range(1 if m & 1 and is_whole(m) else 2)] for m in masks]
    w, r = refs.pop(0), refs.pop(0)
    if not first:
        refs.pop(0)
    out_hbm, token_ref = refs.pop(0), refs.pop(0)
    new_hbm = refs.pop(0) if first else None
    g, o, new, sem, out_sem = refs
    rows, cols = g.shape[2:]
    step = 64
    half = rows // 2
    token_ref[...] = jnp.zeros_like(token_ref)
    here = [not is_whole(m) for m in masks]
    coming = [[] if here[n] else read_rows(grads[n], g.at[n], [sem.at[i, n] for i in (0, 1)]) for n in range(count)]
    for group in coming:
        for copy in group:
            copy.start()
    mean = square_ref[...] * (1.0 / (D * KVH * HD))
    scale = jnp.concatenate([learning_rate * lax.rsqrt(mean + norm_eps)] * (cols // 128), axis=1)
    writes = []
    for n in range(count):
        for copy in coming[n]:
            copy.wait()
        for part in range(2):

            def mix(t, carry):
                j = pl.ds(pl.multiple_of(part * half + t * step, step), step)
                for i in (0, 1):
                    slope = grads[n][i][j, :] if here[n] else g[n, i, j]
                    value = w[offset + n, i, j].astype(jnp.float32) - scale[i : i + 1, :] * slope.astype(jnp.float32)
                    value = value.astype(jnp.bfloat16)
                    if first and n == 0:
                        new[i, j] = value
                    mixed = mix_alpha * value.astype(jnp.float32) + (1.0 - mix_alpha) * r[offset + n, i, j].astype(jnp.float32)
                    o[n, i, j] = mixed.astype(jnp.bfloat16)
                return carry

            lax.fori_loop(0, half // step, mix, 0, unroll=2)
            at = pl.ds(pl.multiple_of((idx_ref[0] ^ masks[n]) * rows + part * half, half), half)
            writes.append(pltpu.make_async_copy(o.at[n, :, pl.ds(part * half, half), :], out_hbm.at[:, at, :], out_sem.at[part, n]))
            writes[-1].start()
        if first and n == 0:
            writes.append(pltpu.make_async_copy(new, new_hbm, out_sem.at[0, count]))
            writes[-1].start()
    for copy in writes:
        copy.wait()


def blend(idx, squares, grads, reference, held, masks, ready, offset):
    w, r = ready
    _, _, rows, cols = w.shape
    count = len(masks)
    first = held is None
    args = [idx, squares] + [x if is_whole(m) else resident(x) for m in masks for x in grads[m]]
    in_specs = [SMEM, VMEM] + [HBM if is_whole(m) else VMEM for m in masks for x in grads[m]]
    args += [resident(w), resident(r)]
    in_specs += [VMEM] * 2
    out_specs = [HBM, VMEM]
    out_shape = [jax.ShapeDtypeStruct(reference.shape, jnp.bfloat16), jax.ShapeDtypeStruct((8, 128), jnp.float32)]
    aliases = {}
    if first:
        out_specs.append(HBM)
        out_shape.append(jax.ShapeDtypeStruct((2, rows, cols), jnp.bfloat16))
    else:
        aliases = {len(args): 0}
        in_specs.append(HBM)
        args.append(held)
    block = pltpu.VMEM((count, 2, rows, cols), jnp.bfloat16)
    return pl.pallas_call(
        functools.partial(blend_kernel, tuple(masks), first, offset),
        in_specs=in_specs,
        out_specs=out_specs,
        out_shape=out_shape,
        scratch_shapes=[
            block,
            block,
            pltpu.VMEM((2, rows, cols) if first else (8, 128), jnp.bfloat16),
            pltpu.SemaphoreType.DMA((2, count)),
            pltpu.SemaphoreType.DMA((2, count + 1)),
        ],
        input_output_aliases=aliases,
        compiler_params=params(12),
        cost_estimate=COST,
        name="blend",
    )(*args)


def bits_of(mask):
    return [1 << b for b in range(mask.bit_length()) if mask >> b & 1]


def after(value, *earlier):
    return lax.optimization_barrier((value, earlier))[0]


def body(shards, tensors, hidden_in, policy_weights, reference_weights, policy_queries, reference_queries, readout, lengths):
    rows = policy_weights.shape[1]
    idx = lax.axis_index("shard").astype(jnp.int32).reshape(1)
    tables = jnp.asarray(rope_tables())

    def swap(x, bit, axis="shard", size=shards):
        return lax.ppermute(x, axis, [(i, i ^ bit) for i in range(size)])

    def powers(size):
        return [1 << b for b in range(size.bit_length() - 1)]

    chips = sorted(range(0, shards, 2), key=lambda m: (len(bits_of(m)), m))
    near = [m for m in chips if len(bits_of(m)) == 1]
    far = [m for m in chips if len(bits_of(m)) > 1]
    link = lambda i, m: bits_of(m)[-1] if i == 0 else bits_of(m)[0]

    def send_near(own):
        got = {m: [swap(own, m)] for m in near}
        got[0] = [own]
        got[1] = [swap(own, 1)]
        return got

    def relay(got, m, *earlier):
        got[m] = [None, None]
        for i in (0, 1):
            via = link(i, m)
            source = got[m ^ via]
            source = source[i] if source[0].ndim == 2 else source[0][i]
            got[m][i] = swap(after(source, *earlier), via)

    def to_core(got, m, *earlier):
        got[m | 1] = [swap(after(g, *earlier), 1) for g in got[m]]

    weights = send_near(policy_weights)
    normed, ref_keys, ref_values = norm_project(idx, hidden_in, reference_weights, tables)
    (ref_margin,) = attend(lengths, reference_queries, ref_keys, ref_values, readout)
    two = [m for m in far if len(bits_of(m)) == 2]
    ends = [(m, i) for m in two for i in (0, 1)]
    packed = {}
    if two:
        packed = dict(zip(ends, pack([weights[m ^ link(i, m)] for m, i in ends], [i for m, i in ends], ref_margin)))
    for m in far:
        weights[m] = [swap(packed[m, i] if m in two else weights[m ^ link(i, m)][i], link(i, m)) for i in (0, 1)]
    for m in near:
        to_core(weights, m, ref_margin)
    held = project(idx, normed, [0, 1], weights, None, None)
    held = project(idx, normed, [m | c for m in near for c in (0, 1)], weights, held, None if far else tables)
    if far:
        for m in far:
            to_core(weights, m, held)
        held = project(idx, normed, far, weights, held, None)
        held = project(idx, normed, [m | 1 for m in far], weights, held, tables)
    pol_keys, pol_values = held
    margin, probs, delta = attend(lengths, policy_queries, pol_keys, pol_values, readout, ref_margin)

    theirs = {}
    order = list(reversed(chips))
    split = max(len(far), 1)

    def other_blocks(masks, margin, other=None):
        blocks = gradient_blocks(idx, normed, cot, [m | 1 for m in masks], rows, None, (margin,))
        if other is not None:
            blocks = hand_on(blocks, other)
        theirs.update({m: swap(block, 1) for m, block in zip(masks, blocks)})
        return blocks

    received = [swap(margin, m, "tensor", tensors) for m in range(1, tensors)]
    cot = attend_back(lengths, policy_queries, pol_values, readout, probs, delta, tables)
    terms = [margin] + [after(x, cot) for x in received]
    while len(terms) > 1:
        terms = [a + b for a, b in zip(terms[::2], terms[1::2])]
    (margin,) = terms
    received = swap(margin, 1)
    margins = (margin, after(received, other_blocks(order[:split], margin)))
    other_blocks(order[split:], margin, margins[1])

    chip_sum = {}
    arrived = {m: ([], []) for m in chips}
    halves = ([[], []], [[], []])
    waiting = []

    def send(m, i, half=None):
        terms = [chip_sum[m][i], *arrived[m][i]]
        if half is not None:
            terms = [t[:, half * rows // 2 : (half + 1) * rows // 2] for t in terms]
        payload = terms[0]
        if len(terms) > 1:
            payload = sum(t.astype(jnp.float32) for t in terms).astype(jnp.bfloat16)
        via = link(i, m)
        received = swap(payload, via)
        if half is None:
            arrived[m ^ via][i].append(received)
        else:
            halves[half][i].append(received)

    for masks in (order[:split], order[split:]):
        chip_sum.update(zip(masks, gradient_blocks(idx, normed, cot, masks, rows, (margins, theirs))))
        for m in masks:
            for i in (0, 1):
                if m and not any(k ^ link(i, k) == m for k in far):
                    send(m, i)
                elif m:
                    waiting.append((m, i))
    for m, i in waiting:
        if m in far:
            send(m, i)

    for half in (0, 1):
        for m, i in waiting:
            if m in near:
                send(m, i, half)
    grads = {m: [] for m in [0] + near}
    parts = []
    for half in (0, 1):
        own, part = finish(chip_sum[0], [arrived[0][i] + halves[half][i] for i in (0, 1)], half)
        parts.append(part)
        grads[0].append(own)
        for m in near:
            grads[m].append(swap(own, m))
    squares = parts[0] + parts[1]
    for bit in powers(tensors):
        squares = squares + swap(squares, bit, "tensor", tensors)
    squares = squares + swap(squares, 1)
    squares, margin_out = gate(squares, margin, *[grads[m][0] for m in near])
    masks = [m | c for m in [0] + near for c in (0, 1)] + [m | c for c in (0, 1) for m in far]
    ready = fetch(idx, weights, reference_weights, masks, squares)
    terms = [squares] + [swap(squares, m) for m in chips[1:]]
    while len(terms) > 1:
        terms = [a + b for a, b in zip(terms[::2], terms[1::2])]
    (squares,) = terms
    two = [m for m in far if len(bits_of(m)) == 2]
    ends = [(m, i) for m in two for i in (0, 1)]
    whole = [0] + near
    packed = pack([grads[m ^ link(i, m)] for m, i in ends] + [grads[m] for m in whole], [i for m, i in ends] + [None] * len(whole), squares, ready[0])
    packed = dict(zip(ends + whole, packed))
    for m in far:
        grads[m] = [swap(packed[m, i] if m in two else grads[m ^ link(i, m)][i], link(i, m)) for i in (0, 1)]
    for m in whole:
        grads[m | 1] = [swap(packed[m], 1)]
    groups = [[0, 1], [m | c for m in near for c in (0, 1)]] + [[m | c for m in far] for c in (0, 1)]
    new_reference, at = None, 0
    for group in groups:
        if group == far and far:
            for m in far:
                to_core(grads, m, token)
        if group:
            outs = blend(idx, squares, grads, reference_weights, new_reference, group, ready, at)
            new_reference, token = outs[:2]
            new_policy = outs[2] if at == 0 else new_policy
            at += len(group)
    return (new_policy, new_reference, margin_out)


def solution(mesh):
    return jax.shard_map(
        functools.partial(body, mesh.shape["shard"], mesh.shape["tensor"]),
        mesh=mesh,
        in_specs=(
            P("shard", None),
            P(None, "shard", "tensor"),
            P(None, None, "tensor"),
            P("shard", "tensor"),
            P("shard", "tensor"),
            P("shard", "tensor"),
            P("shard"),
        ),
        out_specs=(P(None, "shard", "tensor"), P(None, None, "tensor"), P("shard")),
        check_vma=False,
    )
```

```python
import functools
import math

import jax
import jax.numpy as jnp
import numpy as np
from jax import lax
from jax.experimental import pallas as pl
from jax.experimental.pallas import tpu as pltpu
from jax.sharding import PartitionSpec as P

D = 8192
HD = 128
KVH = 8
QH = 32
LEN = 384
TILE = 128

rope_base = 1000000.0
dpo_beta = 0.1
learning_rate = 0.2
mix_alpha = 0.6
norm_eps = 1e-06
width_scale = D ** (-0.5)
logit_scale = 1.0 / math.sqrt(HD)
MIB = 1024 * 1024

NT = (((1,), (1,)), ((), ()))
NN = (((1,), (0,)), ((), ()))
TN = (((0,), (0,)), ((), ()))


def dot(a, b, dims):
    return lax.dot_general(a, b, dims, preferred_element_type=jnp.float32)


def params(mib):
    return pltpu.CompilerParams(vmem_limit_bytes=mib * MIB)


COST = pl.CostEstimate(flops=1, bytes_accessed=1, transcendentals=0)
LONG = pl.CostEstimate(flops=1, bytes_accessed=40 * 1000 * 1000, transcendentals=0)
VMEM = pl.BlockSpec(memory_space=pltpu.VMEM)
SMEM = pl.BlockSpec(memory_space=pltpu.SMEM)
HBM = pl.BlockSpec(memory_space=pl.ANY)


def resident(x):
    return pltpu.with_memory_space_constraint(x, pltpu.VMEM)


def in_hbm(x):
    return pltpu.with_memory_space_constraint(x, pltpu.HBM)


def rope_tables():
    frequency = rope_base ** (-2.0 * np.arange(HD // 2) / HD)
    angles = np.arange(LEN)[:, None] * frequency[None, :]
    cosine, sine = np.cos(angles), np.sin(angles)
    return np.stack([np.concatenate([cosine, cosine], axis=1), np.concatenate([-sine, sine], axis=1)]).astype(np.float32)


def store_heads(acc_ref, cos, sin, key_ref, value_ref):
    for s in range(key_ref.shape[0] // LEN):
        rows = slice(s * LEN, (s + 1) * LEN)
        for h in range(key_ref.shape[1] // HD):
            cols = slice(h * HD, (h + 1) * HD)
            k = acc_ref[0, rows, cols] * width_scale
            key_ref[rows, cols] = (k * cos + pltpu.roll(k, HD // 2, 1) * sin).astype(jnp.bfloat16)
    value_ref[...] = (acc_ref[1] * width_scale).astype(jnp.bfloat16)


def norm_project_kernel(idx_ref, hidden_hbm, weight_hbm, table_hbm, normed_ref, key_ref, value_ref, w, acc, part, table, in_sem, w_sem, table_sem):
    tokens = normed_ref.shape[0]
    step, width, span, chunk = 16, 512, 128, 1024
    reads = []
    for i in range(tokens // span):
        at = pl.ds(i * span, span)
        reads.append(pltpu.make_async_copy(hidden_hbm.at[at], normed_ref.at[at], in_sem.at[i]))
    loads = []
    for c in range(D // chunk):
        at = pl.ds(c * chunk, chunk)
        loads.append(pltpu.make_async_copy(weight_hbm.at[:, at, :], w.at[:, at, :], w_sem.at[c]))
    loads.append(pltpu.make_async_copy(table_hbm, table, table_sem))
    for copy in reads + loads:
        copy.start()

    def row_step(i, carry):
        at = pl.ds(pl.multiple_of(i * step, step), step)
        total = jnp.zeros((step, width), jnp.float32)
        for c in range(D // width):
            v = normed_ref[at, c * width : (c + 1) * width].astype(jnp.float32)
            total = total + v * v
        part[at, :] = functools.reduce(jnp.add, [total[:, c * 128 : (c + 1) * 128] for c in range(width // 128)])
        return carry

    for i, copy in enumerate(reads):
        copy.wait()
        lax.fori_loop(i * (span // step), (i + 1) * (span // step), row_step, 0)
    for copy in loads:
        copy.wait()
    mean = jnp.sum(part[...], axis=1, keepdims=True) * (1.0 / D)
    part[...] = jnp.broadcast_to(lax.rsqrt(mean + norm_eps), part.shape)

    def columns(c):
        return pl.ds(pl.multiple_of(c * chunk, chunk), chunk)

    def normalise(c):
        for i in range(tokens // step):
            rows = slice(i * step, (i + 1) * step)
            scale = jnp.concatenate([part[rows, :]] * (chunk // 128), axis=1)
            normed_ref[rows, columns(c)] = (normed_ref[rows, columns(c)].astype(jnp.float32) * scale).astype(jnp.bfloat16)

    def multiply(c, carry):
        for i in (0, 1):
            acc[i] += dot(normed_ref[:, columns(c)], w[i, columns(c), :], NN)

        @pl.when(c + 1 < D // chunk)
        def _():
            normalise(c + 1)

        return carry

    acc[...] = jnp.zeros_like(acc)
    normalise(0)
    lax.fori_loop(0, D // chunk, multiply, 0)
    store_heads(acc, table[0], table[1], key_ref, value_ref)


def norm_project(idx, hidden, weights, tables):
    tokens = hidden.shape[0]
    cols = weights.shape[2]
    return pl.pallas_call(
        norm_project_kernel,
        in_specs=[SMEM, HBM, HBM, HBM],
        out_specs=[VMEM, VMEM, VMEM],
        out_shape=[
            pltpu.VMEM((tokens, D), jnp.bfloat16),
            pltpu.VMEM((tokens, cols), jnp.bfloat16),
            pltpu.VMEM((tokens, cols), jnp.bfloat16),
        ],
        scratch_shapes=[
            pltpu.VMEM((2, D, cols), jnp.bfloat16),
            pltpu.VMEM((2, tokens, cols), jnp.float32),
            pltpu.VMEM((tokens, 128), jnp.float32),
            pltpu.VMEM(tables.shape, jnp.float32),
            pltpu.SemaphoreType.DMA((tokens // 128,)),
            pltpu.SemaphoreType.DMA((D // 1024,)),
            pltpu.SemaphoreType.DMA,
        ],
        compiler_params=params(16),
        cost_estimate=COST,
        name="norm_project",
    )(idx, in_hbm(hidden), in_hbm(weights), in_hbm(tables))


def is_whole(mask):
    return len(bits_of(mask >> 1)) < 2


def read_rows(sources, target, sems):
    if len(sources) == 1:
        return [pltpu.make_async_copy(sources[0], target, sems[0])]
    if len(sources[0].shape) == 2:
        return [pltpu.make_async_copy(sources[i], target.at[i], sems[i]) for i in (0, 1)]
    half = sources[0].shape[1]
    return [pltpu.make_async_copy(sources[h], target.at[:, pl.ds(h * half, half), :], sems[h]) for h in (0, 1)]


def project_kernel(masks, first, last, idx_ref, x_ref, *refs):
    refs = list(refs)
    count = len(masks)
    pieces = [[refs.pop(0) for _ in range(1 if is_whole(m) else 2)] for m in masks]
    held = None if first else refs.pop(0)
    if last:
        table_hbm, key_ref, value_ref, w, acc, table, sem, table_sem = refs
        table_copy = pltpu.make_async_copy(table_hbm, table, table_sem)
        table_copy.start()
    else:
        acc, w, sem = refs
    depth = w.shape[2]
    copies = [read_rows(pieces[n], w.at[n], [sem.at[i, n] for i in (0, 1)]) for n in range(count)]
    for group in copies:
        for copy in group:
            copy.start()
    for n in range(count):
        for copy in copies[n]:
            copy.wait()
        col = pl.multiple_of((idx_ref[0] ^ masks[n]) * depth, depth)
        x = x_ref[:, pl.ds(col, depth)]
        for i in (0, 1):
            term = dot(x, w[n, i], NN)
            if n:
                term = acc[i] + term
            elif not first:
                term = held[i] + term
            acc[i] = term
    if last:
        table_copy.wait()
        store_heads(acc, table[0], table[1], key_ref, value_ref)


def project(idx, normed, masks, pieces, held, tables):
    tokens = normed.shape[0]
    rows, cols = pieces[masks[0]][0].shape[-2:]
    first, last = held is None, tables is not None
    count = len(masks)
    args = [idx, resident(normed)] + [w for m in masks for w in pieces[m]]
    in_specs = [SMEM, VMEM] + [HBM] * (len(args) - 2)
    if not first:
        in_specs.append(VMEM)
        args.append(resident(held))
    acc_shape = (2, tokens, cols)
    scratch = [pltpu.VMEM((count, 2, rows, cols), jnp.bfloat16), pltpu.SemaphoreType.DMA((2, count))]
    if last:
        in_specs.append(HBM)
        args.append(in_hbm(tables))
        out_specs = [VMEM] * 2
        out_shape = [pltpu.VMEM((tokens, cols), jnp.bfloat16)] * 2
        scratch.insert(1, pltpu.VMEM(acc_shape, jnp.float32))
        scratch.insert(2, pltpu.VMEM(tables.shape, jnp.float32))
        scratch.append(pltpu.SemaphoreType.DMA)
    else:
        out_specs = VMEM
        out_shape = pltpu.VMEM(acc_shape, jnp.float32)
    return pl.pallas_call(
        functools.partial(project_kernel, tuple(masks), first, last),
        in_specs=in_specs,
        out_specs=out_specs,
        out_shape=out_shape,
        scratch_shapes=scratch,
        compiler_params=params(10),
        cost_estimate=COST,
        name="project",
    )(*args)


FORWARD_HEADS = 2
BACKWARD_HEADS = 4


def stacked(ref, row, col, r, first, count):
    rows = pl.ds(pl.multiple_of(row + r * TILE, TILE), TILE)
    at = lambda g: pl.ds(pl.multiple_of(col + g * HD, HD), HD)
    return jnp.concatenate([ref[rows, at(g)] for g in range(first, first + count)], axis=0)


def live_readout(ref, row, col, r, first, count, length):
    x = stacked(ref, row, col, r, first, count).astype(jnp.float32)
    at = lax.broadcasted_iota(jnp.int32, x.shape, 0) % TILE + r * TILE
    return jnp.where(at < length, x, 0.0).astype(jnp.bfloat16)


def places(step, q_ref, k_ref):
    heads = k_ref.shape[1] // HD
    seq, h = step // heads, step % heads
    return seq, h, seq * LEN, pl.multiple_of(h * HD, HD), h * (q_ref.shape[1] // heads)


def attend_kernel(keep, len_ref, q_ref, k_ref, v_ref, ro_ref, *rest):
    groups = q_ref.shape[1] // k_ref.shape[1]
    count = min(groups, FORWARD_HEADS)
    if keep:
        before_ref, margin_ref, prob_ref, delta_ref = rest
    else:
        (margin_ref,) = rest

    def one(step, margin):
        seq, h, row, col, q_col = places(step, q_ref, k_ref)
        length = len_ref[seq]
        score = jnp.zeros((1, TILE), jnp.float32)
        j = lax.broadcasted_iota(jnp.int32, (TILE, TILE), 0)
        i = lax.broadcasted_iota(jnp.int32, (TILE, TILE), 1)
        base = 0
        for r in range(LEN // TILE):
            n = (r + 1) * TILE
            keys = (pl.ds(pl.multiple_of(row, TILE), n), pl.ds(col, HD))
            for g in range(0, groups, count):
                q = stacked(q_ref, row, q_col, r, g, count)
                ro = live_readout(ro_ref, row, q_col, r, g, count, length)
                logits = dot(k_ref[keys], q, NT)
                gains = dot(v_ref[keys], ro, NT)
                for c in range(count):
                    own = slice(c * TILE, (c + 1) * TILE)
                    cols = slice((g + c) * TILE, (g + c + 1) * TILE)
                    s = [logits[b * TILE : (b + 1) * TILE, own] for b in range(r + 1)]
                    s[r] = jnp.where(j <= i, s[r], -1e30)
                    top = functools.reduce(jnp.maximum, [jnp.max(x, axis=0, keepdims=True) for x in s])
                    e = [jnp.exp2((x - top) * (logit_scale * math.log2(math.e))) for x in s]
                    inverse = 1.0 / functools.reduce(jnp.add, [jnp.sum(x, axis=0, keepdims=True) for x in e])
                    delta = jnp.zeros((1, TILE), jnp.float32)
                    for b in range(r + 1):
                        p = (e[b] * inverse).astype(jnp.bfloat16)
                        if keep:
                            prob_ref[seq, h, base + b * TILE : base + (b + 1) * TILE, cols] = p
                        gain = gains[b * TILE : (b + 1) * TILE, own]
                        delta = delta + jnp.sum(p.astype(jnp.float32) * gain, axis=0, keepdims=True)
                    if keep:
                        delta_ref[seq, h, r : r + 1, cols] = delta
                    score = score + delta
            base += n
        side = jnp.where(seq % 2 == 0, 1.0, -1.0) * (dpo_beta / math.sqrt(QH * HD))
        return margin + jnp.sum(score, axis=1, keepdims=True) * side

    steps = k_ref.shape[0] // LEN * (k_ref.shape[1] // HD)
    start = -before_ref[0:1, 0:1] if keep else jnp.zeros((1, 1), jnp.float32)
    margin_ref[...] = jnp.broadcast_to(lax.fori_loop(0, steps, one, start, unroll=keep), margin_ref.shape)


def attend(lengths, queries, keys, values, readout, before=None):
    seqs = lengths.shape[0]
    heads = keys.shape[1] // HD
    wide = queries.shape[1] // heads
    tiles = LEN // TILE
    span = TILE * tiles * (tiles + 1) // 2
    keep = before is not None
    args = [lengths] + [resident(x) for x in (queries, keys, values, readout)]
    out_shape = [jax.ShapeDtypeStruct((8, 128), jnp.float32)]
    if keep:
        args.append(before)
        out_shape += [pltpu.VMEM((seqs, heads, span, wide), jnp.bfloat16), pltpu.VMEM((seqs, heads, tiles, wide), jnp.float32)]
    return pl.pallas_call(
        functools.partial(attend_kernel, keep),
        in_specs=[SMEM] + [VMEM] * (len(args) - 1),
        out_specs=[VMEM] * len(out_shape),
        out_shape=out_shape,
        compiler_params=params(8),
        cost_estimate=COST,
        name="attend",
    )(*args)


def attend_back_kernel(len_ref, q_ref, v_ref, ro_ref, prob_ref, delta_ref, table_ref, grad_ref):
    tiles = LEN // TILE
    groups = q_ref.shape[1] // v_ref.shape[1]
    count = min(groups, BACKWARD_HEADS)

    def one(step, carry):
        seq, h, row, col, q_col = places(step, q_ref, v_ref)
        length = len_ref[seq]
        dk = [None] * tiles
        dv = [None] * tiles
        base = 0
        for r in range(tiles):
            n = (r + 1) * TILE
            keys = (pl.ds(pl.multiple_of(row, TILE), n), pl.ds(col, HD))
            for g in range(0, groups, count):
                q = stacked(q_ref, row, q_col, r, g, count)
                ro = live_readout(ro_ref, row, q_col, r, g, count, length)
                cols = slice(g * TILE, (g + count) * TILE)
                p = prob_ref[seq, h, base : base + n, cols]
                dp = dot(v_ref[keys], ro, NT)
                ds = []
                for c in range(count):
                    own = slice(c * TILE, (c + 1) * TILE)
                    delta = delta_ref[seq, h, r : r + 1, (g + c) * TILE : (g + c + 1) * TILE]
                    ds.append((p[:, own].astype(jnp.float32) * (dp[:, own] - delta)).astype(jnp.bfloat16))
                ds = jnp.concatenate(ds, axis=1)
                tk = dot(ds, q, NN)
                tv = dot(p, ro, NN)
                for b in range(r + 1):
                    at = slice(b * TILE, (b + 1) * TILE)
                    dk[b] = tk[at] if dk[b] is None else dk[b] + tk[at]
                    dv[b] = tv[at] if dv[b] is None else dv[b] + tv[at]
            base += n
        scale = jnp.where(seq % 2 == 0, -1.0, 1.0) * (1.0 / math.sqrt(QH * HD))
        for b in range(tiles):
            at = slice(b * TILE, (b + 1) * TILE)
            to = (pl.ds(col, HD), pl.ds(pl.multiple_of(row + b * TILE, TILE), TILE))
            k = dk[b] * (scale * logit_scale)
            k = k * table_ref[0, at, :] - pltpu.roll(k, HD // 2, 1) * table_ref[1, at, :]
            grad_ref[(0, *to)] = k.T.astype(jnp.bfloat16)
            grad_ref[(1, *to)] = (dv[b] * scale).T.astype(jnp.bfloat16)
        return carry

    steps = v_ref.shape[0] // LEN * (v_ref.shape[1] // HD)
    lax.fori_loop(0, steps, one, 0, unroll=True)


def attend_back(lengths, queries, values, readout, probs, delta, tables):
    return pl.pallas_call(
        attend_back_kernel,
        in_specs=[SMEM] + [VMEM] * 6,
        out_specs=VMEM,
        out_shape=pltpu.VMEM((2,) + values.shape[::-1], jnp.bfloat16),
        compiler_params=params(8),
        cost_estimate=COST,
        name="attend_back",
    )(lengths, *[resident(x) for x in (queries, values, readout, probs, delta, tables)])


def gradient_tiles(idx, mask, x_ref, cot_ref, rows):
    cols = cot_ref.shape[1]
    both = jnp.concatenate([cot_ref[0], cot_ref[1]], axis=0)
    tile = min(rows, 256)
    for t in range(rows // tile):
        col = pl.multiple_of((idx ^ mask) * rows + t * tile, tile)
        out = dot(both, x_ref[:, pl.ds(col, tile)], NN)
        for i in (0, 1):
            yield i, t * tile, tile, out[i * cols : (i + 1) * cols]


def gradient_kernel(masks, idx_ref, x_ref, cot_ref, *outs):
    outs = outs[len(outs) - len(masks) :]
    for mask, out_ref in zip(masks, outs):
        for i, start, tile, value in gradient_tiles(idx_ref[0], mask, x_ref, cot_ref, out_ref.shape[2]):
            out_ref[i, :, start : start + tile] = value.astype(out_ref.dtype)


def merged_kernel(masks, idx_ref, x_ref, cot_ref, mine_ref, their_ref, *refs):
    count = len(masks)
    theirs_hbm, outs = refs[:count], refs[count : 3 * count]
    theirs, sem = refs[3 * count :]
    rows = theirs.shape[3]
    copies = [pltpu.make_async_copy(theirs_hbm[n], theirs.at[n], sem.at[n]) for n in range(count)]
    for copy in copies:
        copy.start()
    mine, their = (ref[0:1, :] for ref in (mine_ref, their_ref))
    mine, their = (jax.nn.sigmoid(-x) for x in (mine, their))
    for n, mask in enumerate(masks):
        copies[n].wait()
        for i, start, tile, value in gradient_tiles(idx_ref[0], mask, x_ref, cot_ref, rows):
            wide = lambda x: jnp.concatenate([x] * (tile // 128), axis=1)
            value = value * wide(mine) + theirs[n, i, :, start : start + tile].astype(jnp.float32) * wide(their)
            outs[2 * n + i][:, start : start + tile] = value.astype(outs[2 * n + i].dtype)


def gradient_blocks(idx, normed, cot, masks, rows, merge=None, earlier=()):
    _, cols, tokens = cot.shape
    args = [idx, resident(normed), resident(cot)]
    in_specs = [SMEM, VMEM, VMEM]
    scratch = []
    if merge is None:
        kernel, name = gradient_kernel, "gradient_block"
        out_shape = [jax.ShapeDtypeStruct((2, cols, rows), jnp.bfloat16) for m in masks]
        args += earlier
        in_specs += [HBM] * len(earlier)
    else:
        kernel, name = merged_kernel, "merged_block"
        margins, theirs = merge
        args += [*margins] + [theirs[m] for m in masks]
        in_specs += [VMEM] * 2 + [HBM] * len(masks)
        out_shape = [
            jax.ShapeDtypeStruct((cols, rows), jnp.bfloat16) if m else pltpu.VMEM((cols, rows), jnp.float32)
            for m in masks
            for i in (0, 1)
        ]
        scratch = [pltpu.VMEM((len(masks), 2, cols, rows), jnp.bfloat16), pltpu.SemaphoreType.DMA((len(masks),))]
    outs = pl.pallas_call(
        functools.partial(kernel, tuple(masks)),
        in_specs=in_specs,
        out_specs=[VMEM] * len(out_shape),
        out_shape=out_shape,
        scratch_shapes=scratch,
        compiler_params=params(10),
        cost_estimate=COST,
        name=name,
    )(*args)
    return outs if merge is None else [outs[2 * n : 2 * n + 2] for n in range(len(masks))]


def finish_kernel(half, counts, *refs):
    refs = list(refs)
    out_ref, square_ref = refs[-2:]
    refs = refs[:-2]
    square_ref[...] = jnp.zeros_like(square_ref)
    _, rows, cols = out_ref.shape
    for i in (0, 1):
        terms = [refs.pop(0) for _ in range(1 + counts[i])]
        squares = jnp.zeros((1, 128), jnp.float32)
        for c in range(0, cols, 128):
            for r in range(0, rows, 128):
                at = [slice(x, x + 128) for x in (r if t.shape[1] == rows else half * rows + r for t in terms)]
                value = functools.reduce(jnp.add, [t[c : c + 128, x].astype(jnp.float32) for t, x in zip(terms, at)])
                squares = squares + jnp.sum(value * value, axis=0, keepdims=True)
                out_ref[i, r : r + 128, c : c + 128] = value.T.astype(jnp.bfloat16)
        square_ref[i : i + 1, :] = jnp.broadcast_to(jnp.sum(squares, axis=1, keepdims=True), (1, 128))


def finish(base, arrived, half):
    args = [x for i in (0, 1) for x in (resident(base[i]), *arrived[i])]
    cols, rows = base[0].shape
    return pl.pallas_call(
        functools.partial(finish_kernel, half, [len(a) for a in arrived]),
        in_specs=[VMEM] * len(args),
        out_specs=[VMEM] * 2,
        out_shape=[jax.ShapeDtypeStruct((2, rows // 2, cols), jnp.bfloat16), jax.ShapeDtypeStruct((8, 128), jnp.float32)],
        compiler_params=params(8),
        cost_estimate=COST,
        name="finish",
    )(*args)


def hand_on_kernel(count, *refs):
    pass


def hand_on(arrays, earlier):
    count = len(arrays)
    return pl.pallas_call(
        functools.partial(hand_on_kernel, count),
        in_specs=[HBM] * (count + 1),
        out_specs=[HBM] * count,
        out_shape=[jax.ShapeDtypeStruct(x.shape, x.dtype) for x in arrays],
        input_output_aliases={n: n for n in range(count)},
        compiler_params=params(2),
        cost_estimate=COST,
        name="hand_on",
    )(*arrays, earlier)


def gate_kernel(value_ref, margin_ref, *refs):
    out_ref, first_ref = refs[-2:]
    out_ref[...] = value_ref[...]
    first_ref[0] = margin_ref[0, 0]


def gate(value, margin, *earlier):
    return pl.pallas_call(
        gate_kernel,
        in_specs=[VMEM, VMEM] + [HBM] * len(earlier),
        out_specs=[VMEM, SMEM],
        out_shape=[jax.ShapeDtypeStruct(value.shape, value.dtype), jax.ShapeDtypeStruct((1,), jnp.float32)],
        compiler_params=params(2),
        cost_estimate=COST,
        name="gate",
    )(value, margin, *earlier)


def pack_kernel(takes, parts, *refs):
    sources, outs, sem = refs[: parts * len(takes)], refs[-1 - len(takes) : -1], refs[-1]
    copies = []
    for n, i in enumerate(takes):
        half = sources[parts * n].shape[1]
        for h in range(parts):
            source, at = sources[parts * n + h], pl.ds(h * half, half)
            if i is None:
                copies.append(pltpu.make_async_copy(source, outs[n].at[:, at, :], sem.at[n, h]))
            else:
                copies.append(pltpu.make_async_copy(source.at[i], outs[n].at[at, :], sem.at[n, h]))
    for copy in copies:
        copy.start()
    for copy in copies:
        copy.wait()


def pack(sources, takes, *earlier):
    parts = len(sources[0])
    _, half, cols = sources[0][0].shape
    shapes = [(2, parts * half, cols) if i is None else (parts * half, cols) for i in takes]
    return pl.pallas_call(
        functools.partial(pack_kernel, tuple(takes), parts),
        in_specs=[HBM] * (parts * len(takes) + len(earlier)),
        out_specs=[HBM] * len(takes),
        out_shape=[jax.ShapeDtypeStruct(shape, jnp.bfloat16) for shape in shapes],
        scratch_shapes=[pltpu.SemaphoreType.DMA((len(takes), 2))],
        compiler_params=params(2),
        cost_estimate=COST,
        name="pack",
    )(*[x for pair in sources for x in pair], *earlier)


def fetch_kernel(masks, idx_ref, *refs):
    refs = list(refs)
    pieces = [[refs.pop(0) for _ in range(1 if is_whole(m) else 2)] for m in masks]
    ref_hbm, _, w, r, sem = refs
    rows = r.shape[2]
    copies = []
    for n, mask in enumerate(masks):
        at = pl.ds(pl.multiple_of((idx_ref[0] ^ mask) * rows, rows), rows)
        copies += read_rows(pieces[n], w.at[n], [sem.at[i, n] for i in (0, 1)])
        copies.append(pltpu.make_async_copy(ref_hbm.at[:, at, :], r.at[n], sem.at[2, n]))
    for copy in copies:
        copy.start()
    for copy in copies:
        copy.wait()


def fetch(idx, weights, reference, masks, earlier):
    rows, cols = weights[masks[0]][0].shape[-2:]
    count = len(masks)
    args = [idx] + [w for m in masks for w in weights[m]] + [in_hbm(reference), earlier]
    return pl.pallas_call(
        functools.partial(fetch_kernel, tuple(masks)),
        in_specs=[SMEM] + [HBM] * (len(args) - 1),
        out_specs=[VMEM] * 2,
        out_shape=[pltpu.VMEM((count, 2, rows, cols), jnp.bfloat16)] * 2,
        scratch_shapes=[pltpu.SemaphoreType.DMA((3, count))],
        compiler_params=params(4),
        cost_estimate=COST,
        name="fetch",
    )(*args)


def blend_kernel(masks, first, offset, idx_ref, square_ref, *refs):
    refs = list(refs)
    count = len(masks)
    grads = [[refs.pop(0) for _ in range(1 if m & 1 and is_whole(m) else 2)] for m in masks]
    w, r = refs.pop(0), refs.pop(0)
    if not first:
        refs.pop(0)
    out_hbm, token_ref = refs.pop(0), refs.pop(0)
    new_hbm = refs.pop(0) if first else None
    g, o, new, sem, out_sem = refs
    rows, cols = g.shape[2:]
    step = 64
    half = rows // 2
    token_ref[...] = jnp.zeros_like(token_ref)
    here = [not is_whole(m) for m in masks]
    coming = [[] if here[n] else read_rows(grads[n], g.at[n], [sem.at[i, n] for i in (0, 1)]) for n in range(count)]
    for group in coming:
        for copy in group:
            copy.start()
    mean = square_ref[...] * (1.0 / (D * KVH * HD))
    scale = jnp.concatenate([learning_rate * lax.rsqrt(mean + norm_eps)] * (cols // 128), axis=1)
    writes = []
    for n in range(count):
        for copy in coming[n]:
            copy.wait()
        for part in range(2):

            def mix(t, carry):
                j = pl.ds(pl.multiple_of(part * half + t * step, step), step)
                for i in (0, 1):
                    slope = grads[n][i][j, :] if here[n] else g[n, i, j]
                    value = w[offset + n, i, j].astype(jnp.float32) - scale[i : i + 1, :] * slope.astype(jnp.float32)
                    value = value.astype(jnp.bfloat16)
                    if first and n == 0:
                        new[i, j] = value
                    mixed = mix_alpha * value.astype(jnp.float32) + (1.0 - mix_alpha) * r[offset + n, i, j].astype(jnp.float32)
                    o[n, i, j] = mixed.astype(jnp.bfloat16)
                return carry

            lax.fori_loop(0, half // step, mix, 0, unroll=2)
            at = pl.ds(pl.multiple_of((idx_ref[0] ^ masks[n]) * rows + part * half, half), half)
            writes.append(pltpu.make_async_copy(o.at[n, :, pl.ds(part * half, half), :], out_hbm.at[:, at, :], out_sem.at[part, n]))
            writes[-1].start()
        if first and n == 0:
            writes.append(pltpu.make_async_copy(new, new_hbm, out_sem.at[0, count]))
            writes[-1].start()
    for copy in writes:
        copy.wait()


def blend(idx, squares, grads, reference, held, masks, ready, offset):
    w, r = ready
    _, _, rows, cols = w.shape
    count = len(masks)
    first = held is None
    args = [idx, squares] + [x if is_whole(m) else resident(x) for m in masks for x in grads[m]]
    in_specs = [SMEM, VMEM] + [HBM if is_whole(m) else VMEM for m in masks for x in grads[m]]
    args += [resident(w), resident(r)]
    in_specs += [VMEM] * 2
    out_specs = [HBM, VMEM]
    out_shape = [jax.ShapeDtypeStruct(reference.shape, jnp.bfloat16), jax.ShapeDtypeStruct((8, 128), jnp.float32)]
    aliases = {}
    if first:
        out_specs.append(HBM)
        out_shape.append(jax.ShapeDtypeStruct((2, rows, cols), jnp.bfloat16))
    else:
        aliases = {len(args): 0}
        in_specs.append(HBM)
        args.append(held)
    block = pltpu.VMEM((count, 2, rows, cols), jnp.bfloat16)
    return pl.pallas_call(
        functools.partial(blend_kernel, tuple(masks), first, offset),
        in_specs=in_specs,
        out_specs=out_specs,
        out_shape=out_shape,
        scratch_shapes=[
            block,
            block,
            pltpu.VMEM((2, rows, cols) if first else (8, 128), jnp.bfloat16),
            pltpu.SemaphoreType.DMA((2, count)),
            pltpu.SemaphoreType.DMA((2, count + 1)),
        ],
        input_output_aliases=aliases,
        compiler_params=params(12),
        cost_estimate=COST,
        name="blend",
    )(*args)


def bits_of(mask):
    return [1 << b for b in range(mask.bit_length()) if mask >> b & 1]


def after(value, *earlier):
    return lax.optimization_barrier((value, earlier))[0]


def body(shards, tensors, hidden_in, policy_weights, reference_weights, policy_queries, reference_queries, readout, lengths):
    rows = policy_weights.shape[1]
    idx = lax.axis_index("shard").astype(jnp.int32).reshape(1)
    tables = jnp.asarray(rope_tables())

    def swap(x, bit, axis="shard", size=shards):
        return lax.ppermute(x, axis, [(i, i ^ bit) for i in range(size)])

    def powers(size):
        return [1 << b for b in range(size.bit_length() - 1)]

    chips = sorted(range(0, shards, 2), key=lambda m: (len(bits_of(m)), m))
    near = [m for m in chips if len(bits_of(m)) == 1]
    far = [m for m in chips if len(bits_of(m)) > 1]
    link = lambda i, m: bits_of(m)[-1] if i == 0 else bits_of(m)[0]

    def send_near(own):
        got = {m: [swap(own, m)] for m in near}
        got[0] = [own]
        got[1] = [swap(own, 1)]
        return got

    def relay(got, m, *earlier):
        got[m] = [None, None]
        for i in (0, 1):
            via = link(i, m)
            source = got[m ^ via]
            source = source[i] if source[0].ndim == 2 else source[0][i]
            got[m][i] = swap(after(source, *earlier), via)

    def to_core(got, m, *earlier):
        got[m | 1] = [swap(after(g, *earlier), 1) for g in got[m]]

    weights = send_near(policy_weights)
    normed, ref_keys, ref_values = norm_project(idx, hidden_in, reference_weights, tables)
    (ref_margin,) = attend(lengths, reference_queries, ref_keys, ref_values, readout)
    two = [m for m in far if len(bits_of(m)) == 2]
    ends = [(m, i) for m in two for i in (0, 1)]
    packed = {}
    if two:
        packed = dict(zip(ends, pack([weights[m ^ link(i, m)] for m, i in ends], [i for m, i in ends], ref_margin)))
    for m in far:
        weights[m] = [swap(packed[m, i] if m in two else weights[m ^ link(i, m)][i], link(i, m)) for i in (0, 1)]
    for m in near:
        to_core(weights, m, ref_margin)
    held = project(idx, normed, [0, 1], weights, None, None)
    held = project(idx, normed, [m | c for m in near for c in (0, 1)], weights, held, None if far else tables)
    if far:
        for m in far:
            to_core(weights, m, held)
        held = project(idx, normed, far, weights, held, None)
        held = project(idx, normed, [m | 1 for m in far], weights, held, tables)
    pol_keys, pol_values = held
    margin, probs, delta = attend(lengths, policy_queries, pol_keys, pol_values, readout, ref_margin)

    theirs = {}
    order = list(reversed(chips))
    split = max(len(far), 1)

    def other_blocks(masks, margin, other=None):
        blocks = gradient_blocks(idx, normed, cot, [m | 1 for m in masks], rows, None, (margin,))
        if other is not None:
            blocks = hand_on(blocks, other)
        theirs.update({m: swap(block, 1) for m, block in zip(masks, blocks)})
        return blocks

    received = [swap(margin, m, "tensor", tensors) for m in range(1, tensors)]
    cot = attend_back(lengths, policy_queries, pol_values, readout, probs, delta, tables)
    terms = [margin] + [after(x, cot) for x in received]
    while len(terms) > 1:
        terms = [a + b for a, b in zip(terms[::2], terms[1::2])]
    (margin,) = terms
    received = swap(margin, 1)
    margins = (margin, after(received, other_blocks(order[:split], margin)))
    other_blocks(order[split:], margin, margins[1])

    chip_sum = {}
    arrived = {m: ([], []) for m in chips}
    halves = ([[], []], [[], []])
    waiting = []

    def send(m, i, half=None):
        terms = [chip_sum[m][i], *arrived[m][i]]
        if half is not None:
            terms = [t[:, half * rows // 2 : (half + 1) * rows // 2] for t in terms]
        payload = terms[0]
        if len(terms) > 1:
            payload = sum(t.astype(jnp.float32) for t in terms).astype(jnp.bfloat16)
        via = link(i, m)
        received = swap(payload, via)
        if half is None:
            arrived[m ^ via][i].append(received)
        else:
            halves[half][i].append(received)

    for masks in (order[:split], order[split:]):
        chip_sum.update(zip(masks, gradient_blocks(idx, normed, cot, masks, rows, (margins, theirs))))
        for m in masks:
            for i in (0, 1):
                if m and not any(k ^ link(i, k) == m for k in far):
                    send(m, i)
                elif m:
                    waiting.append((m, i))
    for m, i in waiting:
        if m in far:
            send(m, i)

    for half in (0, 1):
        for m, i in waiting:
            if m in near:
                send(m, i, half)
    grads = {m: [] for m in [0] + near}
    parts = []
    for half in (0, 1):
        own, part = finish(chip_sum[0], [arrived[0][i] + halves[half][i] for i in (0, 1)], half)
        parts.append(part)
        grads[0].append(own)
        for m in near:
            grads[m].append(swap(own, m))
    squares = parts[0] + parts[1]
    for bit in powers(tensors):
        squares = squares + swap(squares, bit, "tensor", tensors)
    squares = squares + swap(squares, 1)
    squares, margin_out = gate(squares, margin, *[grads[m][0] for m in near])
    masks = [m | c for m in [0] + near for c in (0, 1)] + [m | c for c in (0, 1) for m in far]
    ready = fetch(idx, weights, reference_weights, masks, squares)
    terms = [squares] + [swap(squares, m) for m in chips[1:]]
    while len(terms) > 1:
        terms = [a + b for a, b in zip(terms[::2], terms[1::2])]
    (squares,) = terms
    two = [m for m in far if len(bits_of(m)) == 2]
    ends = [(m, i) for m in two for i in (0, 1)]
    whole = [0] + near
    packed = pack([grads[m ^ link(i, m)] for m, i in ends] + [grads[m] for m in whole], [i for m, i in ends] + [None] * len(whole), squares, ready[0])
    packed = dict(zip(ends + whole, packed))
    for m in far:
        grads[m] = [swap(packed[m, i] if m in two else grads[m ^ link(i, m)][i], link(i, m)) for i in (0, 1)]
    for m in whole:
        grads[m | 1] = [swap(packed[m], 1)]
    groups = [[0, 1], [m | c for m in near for c in (0, 1)]] + [[m | c for m in far] for c in (0, 1)]
    new_reference, at = None, 0
    for group in groups:
        if group == far and far:
            for m in far:
                to_core(grads, m, token)
        if group:
            outs = blend(idx, squares, grads, reference_weights, new_reference, group, ready, at)
            new_reference, token = outs[:2]
            new_policy = outs[2] if at == 0 else new_policy
            at += len(group)
    return (new_policy, new_reference, margin_out)


def solution(mesh):
    return jax.shard_map(
        functools.partial(body, mesh.shape["shard"], mesh.shape["tensor"]),
        mesh=mesh,
        in_specs=(
            P("shard", None),
            P(None, "shard", "tensor"),
            P(None, None, "tensor"),
            P("shard", "tensor"),
            P("shard", "tensor"),
            P("shard", "tensor"),
            P("shard"),
        ),
        out_specs=(P(None, "shard", "tensor"), P(None, None, "tensor"), P("shard")),
        check_vma=False,
    )
```

```python
import functools
import math

import jax
import jax.numpy as jnp
import numpy as np
from jax import lax
from jax.experimental import pallas as pl
from jax.experimental.pallas import tpu as pltpu
from jax.sharding import PartitionSpec as P

D = 8192
HD = 128
KVH = 8
QH = 32
LEN = 384
TILE = 128

rope_base = 1000000.0
dpo_beta = 0.1
learning_rate = 0.2
mix_alpha = 0.6
norm_eps = 1e-06
width_scale = D ** (-0.5)
logit_scale = 1.0 / math.sqrt(HD)
MIB = 1024 * 1024

NT = (((1,), (1,)), ((), ()))
NN = (((1,), (0,)), ((), ()))
TN = (((0,), (0,)), ((), ()))


def dot(a, b, dims):
    return lax.dot_general(a, b, dims, preferred_element_type=jnp.float32)


def params(mib):
    return pltpu.CompilerParams(vmem_limit_bytes=mib * MIB)


COST = pl.CostEstimate(flops=1, bytes_accessed=1, transcendentals=0)
LONG = pl.CostEstimate(flops=1, bytes_accessed=40 * 1000 * 1000, transcendentals=0)
VMEM = pl.BlockSpec(memory_space=pltpu.VMEM)
SMEM = pl.BlockSpec(memory_space=pltpu.SMEM)
HBM = pl.BlockSpec(memory_space=pl.ANY)


def resident(x):
    return pltpu.with_memory_space_constraint(x, pltpu.VMEM)


def in_hbm(x):
    return pltpu.with_memory_space_constraint(x, pltpu.HBM)


def rope_tables():
    frequency = rope_base ** (-2.0 * np.arange(HD // 2) / HD)
    angles = np.arange(LEN)[:, None] * frequency[None, :]
    cosine, sine = np.cos(angles), np.sin(angles)
    return np.stack([np.concatenate([cosine, cosine], axis=1), np.concatenate([-sine, sine], axis=1)]).astype(np.float32)


def store_heads(acc_ref, cos, sin, key_ref, value_ref):
    for s in range(key_ref.shape[0] // LEN):
        rows = slice(s * LEN, (s + 1) * LEN)
        for h in range(key_ref.shape[1] // HD):
            cols = slice(h * HD, (h + 1) * HD)
            k = acc_ref[0, rows, cols] * width_scale
            key_ref[rows, cols] = (k * cos + pltpu.roll(k, HD // 2, 1) * sin).astype(jnp.bfloat16)
    value_ref[...] = (acc_ref[1] * width_scale).astype(jnp.bfloat16)


def norm_project_kernel(idx_ref, hidden_hbm, weight_hbm, table_hbm, normed_ref, key_ref, value_ref, w, acc, part, table, in_sem, w_sem, table_sem):
    tokens = normed_ref.shape[0]
    step, width, span, chunk = 16, 512, 128, 1024
    reads = []
    for i in range(tokens // span):
        at = pl.ds(i * span, span)
        reads.append(pltpu.make_async_copy(hidden_hbm.at[at], normed_ref.at[at], in_sem.at[i]))
    loads = []
    for c in range(D // chunk):
        at = pl.ds(c * chunk, chunk)
        loads.append(pltpu.make_async_copy(weight_hbm.at[:, at, :], w.at[:, at, :], w_sem.at[c]))
    loads.append(pltpu.make_async_copy(table_hbm, table, table_sem))
    for copy in reads + loads:
        copy.start()

    def row_step(i, carry):
        at = pl.ds(pl.multiple_of(i * step, step), step)
        total = jnp.zeros((step, width), jnp.float32)
        for c in range(D // width):
            v = normed_ref[at, c * width : (c + 1) * width].astype(jnp.float32)
            total = total + v * v
        part[at, :] = functools.reduce(jnp.add, [total[:, c * 128 : (c + 1) * 128] for c in range(width // 128)])
        return carry

    for i, copy in enumerate(reads):
        copy.wait()
        lax.fori_loop(i * (span // step), (i + 1) * (span // step), row_step, 0)
    for copy in loads:
        copy.wait()
    mean = jnp.sum(part[...], axis=1, keepdims=True) * (1.0 / D)
    part[...] = jnp.broadcast_to(lax.rsqrt(mean + norm_eps), part.shape)

    def columns(c):
        return pl.ds(pl.multiple_of(c * chunk, chunk), chunk)

    def normalise(c):
        for i in range(tokens // step):
            rows = slice(i * step, (i + 1) * step)
            scale = jnp.concatenate([part[rows, :]] * (chunk // 128), axis=1)
            normed_ref[rows, columns(c)] = (normed_ref[rows, columns(c)].astype(jnp.float32) * scale).astype(jnp.bfloat16)

    def multiply(c, carry):
        for i in (0, 1):
            acc[i] += dot(normed_ref[:, columns(c)], w[i, columns(c), :], NN)

        @pl.when(c + 1 < D // chunk)
        def _():
            normalise(c + 1)

        return carry

    acc[...] = jnp.zeros_like(acc)
    normalise(0)
    lax.fori_loop(0, D // chunk, multiply, 0)
    store_heads(acc, table[0], table[1], key_ref, value_ref)


def norm_project(idx, hidden, weights, tables):
    tokens = hidden.shape[0]
    cols = weights.shape[2]
    return pl.pallas_call(
        norm_project_kernel,
        in_specs=[SMEM, HBM, HBM, HBM],
        out_specs=[VMEM, VMEM, VMEM],
        out_shape=[
            pltpu.VMEM((tokens, D), jnp.bfloat16),
            pltpu.VMEM((tokens, cols), jnp.bfloat16),
            pltpu.VMEM((tokens, cols), jnp.bfloat16),
        ],
        scratch_shapes=[
            pltpu.VMEM((2, D, cols), jnp.bfloat16),
            pltpu.VMEM((2, tokens, cols), jnp.float32),
            pltpu.VMEM((tokens, 128), jnp.float32),
            pltpu.VMEM(tables.shape, jnp.float32),
            pltpu.SemaphoreType.DMA((tokens // 128,)),
            pltpu.SemaphoreType.DMA((D // 1024,)),
            pltpu.SemaphoreType.DMA,
        ],
        compiler_params=params(16),
        cost_estimate=COST,
        name="norm_project",
    )(idx, in_hbm(hidden), in_hbm(weights), in_hbm(tables))


def is_whole(mask):
    return len(bits_of(mask >> 1)) < 2


def read_rows(sources, target, sems):
    if len(sources) == 1:
        return [pltpu.make_async_copy(sources[0], target, sems[0])]
    if len(sources[0].shape) == 2:
        return [pltpu.make_async_copy(sources[i], target.at[i], sems[i]) for i in (0, 1)]
    half = sources[0].shape[1]
    return [pltpu.make_async_copy(sources[h], target.at[:, pl.ds(h * half, half), :], sems[h]) for h in (0, 1)]


def project_kernel(masks, first, last, idx_ref, x_ref, *refs):
    refs = list(refs)
    count = len(masks)
    pieces = [[refs.pop(0) for _ in range(1 if is_whole(m) else 2)] for m in masks]
    held = None if first else refs.pop(0)
    if last:
        table_hbm, key_ref, value_ref, w, acc, table, sem, table_sem = refs
        table_copy = pltpu.make_async_copy(table_hbm, table, table_sem)
        table_copy.start()
    else:
        acc, w, sem = refs
    depth = w.shape[2]
    copies = [read_rows(pieces[n], w.at[n], [sem.at[i, n] for i in (0, 1)]) for n in range(count)]
    for group in copies:
        for copy in group:
            copy.start()
    for n in range(count):
        for copy in copies[n]:
            copy.wait()
        col = pl.multiple_of((idx_ref[0] ^ masks[n]) * depth, depth)
        x = x_ref[:, pl.ds(col, depth)]
        for i in (0, 1):
            term = dot(x, w[n, i], NN)
            if n:
                term = acc[i] + term
            elif not first:
                term = held[i] + term
            acc[i] = term
    if last:
        table_copy.wait()
        store_heads(acc, table[0], table[1], key_ref, value_ref)


def project(idx, normed, masks, pieces, held, tables):
    tokens = normed.shape[0]
    rows, cols = pieces[masks[0]][0].shape[-2:]
    first, last = held is None, tables is not None
    count = len(masks)
    args = [idx, resident(normed)] + [w for m in masks for w in pieces[m]]
    in_specs = [SMEM, VMEM] + [HBM] * (len(args) - 2)
    if not first:
        in_specs.append(VMEM)
        args.append(resident(held))
    acc_shape = (2, tokens, cols)
    scratch = [pltpu.VMEM((count, 2, rows, cols), jnp.bfloat16), pltpu.SemaphoreType.DMA((2, count))]
    if last:
        in_specs.append(HBM)
        args.append(in_hbm(tables))
        out_specs = [VMEM] * 2
        out_shape = [pltpu.VMEM((tokens, cols), jnp.bfloat16)] * 2
        scratch.insert(1, pltpu.VMEM(acc_shape, jnp.float32))
        scratch.insert(2, pltpu.VMEM(tables.shape, jnp.float32))
        scratch.append(pltpu.SemaphoreType.DMA)
    else:
        out_specs = VMEM
        out_shape = pltpu.VMEM(acc_shape, jnp.float32)
    return pl.pallas_call(
        functools.partial(project_kernel, tuple(masks), first, last),
        in_specs=in_specs,
        out_specs=out_specs,
        out_shape=out_shape,
        scratch_shapes=scratch,
        compiler_params=params(10),
        cost_estimate=COST,
        name="project",
    )(*args)


FORWARD_HEADS = 1
BACKWARD_HEADS = 4


def stacked(ref, row, col, r, first, count):
    rows = pl.ds(pl.multiple_of(row + r * TILE, TILE), TILE)
    at = lambda g: pl.ds(pl.multiple_of(col + g * HD, HD), HD)
    return jnp.concatenate([ref[rows, at(g)] for g in range(first, first + count)], axis=0)


def live_readout(ref, row, col, r, first, count, length):
    x = stacked(ref, row, col, r, first, count).astype(jnp.float32)
    at = lax.broadcasted_iota(jnp.int32, x.shape, 0) % TILE + r * TILE
    return jnp.where(at < length, x, 0.0).astype(jnp.bfloat16)


def places(step, q_ref, k_ref):
    heads = k_ref.shape[1] // HD
    seq, h = step // heads, step % heads
    return seq, h, seq * LEN, pl.multiple_of(h * HD, HD), h * (q_ref.shape[1] // heads)


def attend_kernel(keep, len_ref, q_ref, k_ref, v_ref, ro_ref, *rest):
    groups = q_ref.shape[1] // k_ref.shape[1]
    count = min(groups, FORWARD_HEADS)
    if keep:
        before_ref, margin_ref, prob_ref, delta_ref = rest
    else:
        (margin_ref,) = rest

    def one(step, margin):
        seq, h, row, col, q_col = places(step, q_ref, k_ref)
        length = len_ref[seq]
        score = jnp.zeros((1, count * TILE), jnp.float32)
        j = lax.broadcasted_iota(jnp.int32, (TILE, count * TILE), 0)
        i = lax.broadcasted_iota(jnp.int32, (TILE, count * TILE), 1) % TILE
        base = 0
        for r in range(LEN // TILE):
            n = (r + 1) * TILE
            keys = (pl.ds(pl.multiple_of(row, TILE), n), pl.ds(col, HD))
            for g in range(0, groups, count):
                q = stacked(q_ref, row, q_col, r, g, count)
                ro = live_readout(ro_ref, row, q_col, r, g, count, length)
                s = dot(k_ref[keys], q, NT)
                dp = dot(v_ref[keys], ro, NT)
                s = [s[b * TILE : (b + 1) * TILE] for b in range(r + 1)]
                s[r] = jnp.where(j <= i, s[r], -1e30)
                top = functools.reduce(jnp.maximum, [jnp.max(x, axis=0, keepdims=True) for x in s])
                e = [jnp.exp2((x - top) * (logit_scale * math.log2(math.e))) for x in s]
                inverse = 1.0 / functools.reduce(jnp.add, [jnp.sum(x, axis=0, keepdims=True) for x in e])
                cols = slice(g * TILE, (g + count) * TILE)
                delta = jnp.zeros((1, count * TILE), jnp.float32)
                for b in range(r + 1):
                    p = (e[b] * inverse).astype(jnp.bfloat16)
                    if keep:
                        prob_ref[seq, h, base + b * TILE : base + (b + 1) * TILE, cols] = p
                    delta = delta + jnp.sum(p.astype(jnp.float32) * dp[b * TILE : (b + 1) * TILE], axis=0, keepdims=True)
                if keep:
                    delta_ref[seq, h, r : r + 1, cols] = delta
                score = score + delta
            base += n
        side = jnp.where(seq % 2 == 0, 1.0, -1.0) * (dpo_beta / math.sqrt(QH * HD))
        return margin + jnp.sum(score, axis=1, keepdims=True) * side

    steps = k_ref.shape[0] // LEN * (k_ref.shape[1] // HD)
    start = -before_ref[0:1, 0:1] if keep else jnp.zeros((1, 1), jnp.float32)
    margin_ref[...] = jnp.broadcast_to(lax.fori_loop(0, steps, one, start, unroll=keep), margin_ref.shape)


def attend(lengths, queries, keys, values, readout, before=None):
    seqs = lengths.shape[0]
    heads = keys.shape[1] // HD
    wide = queries.shape[1] // heads
    tiles = LEN // TILE
    span = TILE * tiles * (tiles + 1) // 2
    keep = before is not None
    args = [lengths] + [resident(x) for x in (queries, keys, values, readout)]
    out_shape = [jax.ShapeDtypeStruct((8, 128), jnp.float32)]
    if keep:
        args.append(before)
        out_shape += [pltpu.VMEM((seqs, heads, span, wide), jnp.bfloat16), pltpu.VMEM((seqs, heads, tiles, wide), jnp.float32)]
    return pl.pallas_call(
        functools.partial(attend_kernel, keep),
        in_specs=[SMEM] + [VMEM] * (len(args) - 1),
        out_specs=[VMEM] * len(out_shape),
        out_shape=out_shape,
        compiler_params=params(8),
        cost_estimate=COST,
        name="attend",
    )(*args)


def attend_back_kernel(len_ref, q_ref, v_ref, ro_ref, prob_ref, delta_ref, table_ref, grad_ref):
    tiles = LEN // TILE
    groups = q_ref.shape[1] // v_ref.shape[1]
    count = min(groups, BACKWARD_HEADS)

    def one(step, carry):
        seq, h, row, col, q_col = places(step, q_ref, v_ref)
        length = len_ref[seq]
        dk = [None] * tiles
        dv = [None] * tiles
        base = 0
        for r in range(tiles):
            n = (r + 1) * TILE
            keys = (pl.ds(pl.multiple_of(row, TILE), n), pl.ds(col, HD))
            for g in range(0, groups, count):
                q = stacked(q_ref, row, q_col, r, g, count)
                ro = live_readout(ro_ref, row, q_col, r, g, count, length)
                cols = slice(g * TILE, (g + count) * TILE)
                p = prob_ref[seq, h, base : base + n, cols]
                dp = dot(v_ref[keys], ro, NT)
                ds = (p.astype(jnp.float32) * (dp - delta_ref[seq, h, r : r + 1, cols])).astype(jnp.bfloat16)
                tk = dot(ds, q, NN)
                tv = dot(p, ro, NN)
                for b in range(r + 1):
                    at = slice(b * TILE, (b + 1) * TILE)
                    dk[b] = tk[at] if dk[b] is None else dk[b] + tk[at]
                    dv[b] = tv[at] if dv[b] is None else dv[b] + tv[at]
            base += n
        scale = jnp.where(seq % 2 == 0, -1.0, 1.0) * (1.0 / math.sqrt(QH * HD))
        for b in range(tiles):
            at = slice(b * TILE, (b + 1) * TILE)
            to = (pl.ds(col, HD), pl.ds(pl.multiple_of(row + b * TILE, TILE), TILE))
            k = dk[b] * (scale * logit_scale)
            k = k * table_ref[0, at, :] - pltpu.roll(k, HD // 2, 1) * table_ref[1, at, :]
            grad_ref[(0, *to)] = k.T.astype(jnp.bfloat16)
            grad_ref[(1, *to)] = (dv[b] * scale).T.astype(jnp.bfloat16)
        return carry

    steps = v_ref.shape[0] // LEN * (v_ref.shape[1] // HD)
    lax.fori_loop(0, steps, one, 0, unroll=True)


def attend_back(lengths, queries, values, readout, probs, delta, tables):
    return pl.pallas_call(
        attend_back_kernel,
        in_specs=[SMEM] + [VMEM] * 6,
        out_specs=VMEM,
        out_shape=pltpu.VMEM((2,) + values.shape[::-1], jnp.bfloat16),
        compiler_params=params(8),
        cost_estimate=COST,
        name="attend_back",
    )(lengths, *[resident(x) for x in (queries, values, readout, probs, delta, tables)])


def gradient_tiles(idx, mask, x_ref, cot_ref, rows):
    cols = cot_ref.shape[1]
    both = jnp.concatenate([cot_ref[0], cot_ref[1]], axis=0)
    tile = min(rows, 256)
    for t in range(rows // tile):
        col = pl.multiple_of((idx ^ mask) * rows + t * tile, tile)
        out = dot(both, x_ref[:, pl.ds(col, tile)], NN)
        for i in (0, 1):
            yield i, t * tile, tile, out[i * cols : (i + 1) * cols]


def gradient_kernel(masks, idx_ref, x_ref, cot_ref, *outs):
    outs = outs[len(outs) - len(masks) :]
    for mask, out_ref in zip(masks, outs):
        for i, start, tile, value in gradient_tiles(idx_ref[0], mask, x_ref, cot_ref, out_ref.shape[2]):
            out_ref[i, :, start : start + tile] = value.astype(out_ref.dtype)


def merged_kernel(masks, idx_ref, x_ref, cot_ref, mine_ref, their_ref, *refs):
    count = len(masks)
    theirs_hbm, outs = refs[:count], refs[count : 3 * count]
    theirs, sem = refs[3 * count :]
    rows = theirs.shape[3]
    copies = [pltpu.make_async_copy(theirs_hbm[n], theirs.at[n], sem.at[n]) for n in range(count)]
    for copy in copies:
        copy.start()
    mine, their = (ref[0:1, :] for ref in (mine_ref, their_ref))
    mine, their = (jax.nn.sigmoid(-x) for x in (mine, their))
    for n, mask in enumerate(masks):
        copies[n].wait()
        for i, start, tile, value in gradient_tiles(idx_ref[0], mask, x_ref, cot_ref, rows):
            wide = lambda x: jnp.concatenate([x] * (tile // 128), axis=1)
            value = value * wide(mine) + theirs[n, i, :, start : start + tile].astype(jnp.float32) * wide(their)
            outs[2 * n + i][:, start : start + tile] = value.astype(outs[2 * n + i].dtype)


def gradient_blocks(idx, normed, cot, masks, rows, merge=None, earlier=()):
    _, cols, tokens = cot.shape
    args = [idx, resident(normed), resident(cot)]
    in_specs = [SMEM, VMEM, VMEM]
    scratch = []
    if merge is None:
        kernel, name = gradient_kernel, "gradient_block"
        out_shape = [jax.ShapeDtypeStruct((2, cols, rows), jnp.bfloat16) for m in masks]
        args += earlier
        in_specs += [HBM] * len(earlier)
    else:
        kernel, name = merged_kernel, "merged_block"
        margins, theirs = merge
        args += [*margins] + [theirs[m] for m in masks]
        in_specs += [VMEM] * 2 + [HBM] * len(masks)
        out_shape = [
            jax.ShapeDtypeStruct((cols, rows), jnp.bfloat16) if m else pltpu.VMEM((cols, rows), jnp.float32)
            for m in masks
            for i in (0, 1)
        ]
        scratch = [pltpu.VMEM((len(masks), 2, cols, rows), jnp.bfloat16), pltpu.SemaphoreType.DMA((len(masks),))]
    outs = pl.pallas_call(
        functools.partial(kernel, tuple(masks)),
        in_specs=in_specs,
        out_specs=[VMEM] * len(out_shape),
        out_shape=out_shape,
        scratch_shapes=scratch,
        compiler_params=params(10),
        cost_estimate=COST,
        name=name,
    )(*args)
    return outs if merge is None else [outs[2 * n : 2 * n + 2] for n in range(len(masks))]


def finish_kernel(half, counts, *refs):
    refs = list(refs)
    out_ref, square_ref = refs[-2:]
    refs = refs[:-2]
    square_ref[...] = jnp.zeros_like(square_ref)
    _, rows, cols = out_ref.shape
    for i in (0, 1):
        terms = [refs.pop(0) for _ in range(1 + counts[i])]
        squares = jnp.zeros((1, 128), jnp.float32)
        for c in range(0, cols, 128):
            for r in range(0, rows, 128):
                at = [slice(x, x + 128) for x in (r if t.shape[1] == rows else half * rows + r for t in terms)]
                value = functools.reduce(jnp.add, [t[c : c + 128, x].astype(jnp.float32) for t, x in zip(terms, at)])
                squares = squares + jnp.sum(value * value, axis=0, keepdims=True)
                out_ref[i, r : r + 128, c : c + 128] = value.T.astype(jnp.bfloat16)
        square_ref[i : i + 1, :] = jnp.broadcast_to(jnp.sum(squares, axis=1, keepdims=True), (1, 128))


def finish(base, arrived, half):
    args = [x for i in (0, 1) for x in (resident(base[i]), *arrived[i])]
    cols, rows = base[0].shape
    return pl.pallas_call(
        functools.partial(finish_kernel, half, [len(a) for a in arrived]),
        in_specs=[VMEM] * len(args),
        out_specs=[VMEM] * 2,
        out_shape=[jax.ShapeDtypeStruct((2, rows // 2, cols), jnp.bfloat16), jax.ShapeDtypeStruct((8, 128), jnp.float32)],
        compiler_params=params(8),
        cost_estimate=COST,
        name="finish",
    )(*args)


def hand_on_kernel(count, *refs):
    pass


def hand_on(arrays, earlier):
    count = len(arrays)
    return pl.pallas_call(
        functools.partial(hand_on_kernel, count),
        in_specs=[HBM] * (count + 1),
        out_specs=[HBM] * count,
        out_shape=[jax.ShapeDtypeStruct(x.shape, x.dtype) for x in arrays],
        input_output_aliases={n: n for n in range(count)},
        compiler_params=params(2),
        cost_estimate=COST,
        name="hand_on",
    )(*arrays, earlier)


def gate_kernel(value_ref, margin_ref, *refs):
    out_ref, first_ref = refs[-2:]
    out_ref[...] = value_ref[...]
    first_ref[0] = margin_ref[0, 0]


def gate(value, margin, *earlier):
    return pl.pallas_call(
        gate_kernel,
        in_specs=[VMEM, VMEM] + [HBM] * len(earlier),
        out_specs=[VMEM, SMEM],
        out_shape=[jax.ShapeDtypeStruct(value.shape, value.dtype), jax.ShapeDtypeStruct((1,), jnp.float32)],
        compiler_params=params(2),
        cost_estimate=COST,
        name="gate",
    )(value, margin, *earlier)


def pack_kernel(takes, parts, *refs):
    sources, outs, sem = refs[: parts * len(takes)], refs[-1 - len(takes) : -1], refs[-1]
    copies = []
    for n, i in enumerate(takes):
        half = sources[parts * n].shape[1]
        for h in range(parts):
            source, at = sources[parts * n + h], pl.ds(h * half, half)
            if i is None:
                copies.append(pltpu.make_async_copy(source, outs[n].at[:, at, :], sem.at[n, h]))
            else:
                copies.append(pltpu.make_async_copy(source.at[i], outs[n].at[at, :], sem.at[n, h]))
    for copy in copies:
        copy.start()
    for copy in copies:
        copy.wait()


def pack(sources, takes, *earlier):
    parts = len(sources[0])
    _, half, cols = sources[0][0].shape
    shapes = [(2, parts * half, cols) if i is None else (parts * half, cols) for i in takes]
    return pl.pallas_call(
        functools.partial(pack_kernel, tuple(takes), parts),
        in_specs=[HBM] * (parts * len(takes) + len(earlier)),
        out_specs=[HBM] * len(takes),
        out_shape=[jax.ShapeDtypeStruct(shape, jnp.bfloat16) for shape in shapes],
        scratch_shapes=[pltpu.SemaphoreType.DMA((len(takes), 2))],
        compiler_params=params(2),
        cost_estimate=COST,
        name="pack",
    )(*[x for pair in sources for x in pair], *earlier)


def fetch_kernel(masks, idx_ref, *refs):
    refs = list(refs)
    pieces = [[refs.pop(0) for _ in range(1 if is_whole(m) else 2)] for m in masks]
    ref_hbm, _, w, r, sem = refs
    rows = r.shape[2]
    copies = []
    for n, mask in enumerate(masks):
        at = pl.ds(pl.multiple_of((idx_ref[0] ^ mask) * rows, rows), rows)
        copies += read_rows(pieces[n], w.at[n], [sem.at[i, n] for i in (0, 1)])
        copies.append(pltpu.make_async_copy(ref_hbm.at[:, at, :], r.at[n], sem.at[2, n]))
    for copy in copies:
        copy.start()
    for copy in copies:
        copy.wait()


def fetch(idx, weights, reference, masks, earlier):
    rows, cols = weights[masks[0]][0].shape[-2:]
    count = len(masks)
    args = [idx] + [w for m in masks for w in weights[m]] + [in_hbm(reference), earlier]
    return pl.pallas_call(
        functools.partial(fetch_kernel, tuple(masks)),
        in_specs=[SMEM] + [HBM] * (len(args) - 1),
        out_specs=[VMEM] * 2,
        out_shape=[pltpu.VMEM((count, 2, rows, cols), jnp.bfloat16)] * 2,
        scratch_shapes=[pltpu.SemaphoreType.DMA((3, count))],
        compiler_params=params(4),
        cost_estimate=COST,
        name="fetch",
    )(*args)


def blend_kernel(masks, first, offset, idx_ref, square_ref, *refs):
    refs = list(refs)
    count = len(masks)
    grads = [[refs.pop(0) for _ in range(1 if m & 1 and is_whole(m) else 2)] for m in masks]
    w, r = refs.pop(0), refs.pop(0)
    if not first:
        refs.pop(0)
    out_hbm, token_ref = refs.pop(0), refs.pop(0)
    new_hbm = refs.pop(0) if first else None
    g, o, new, sem, out_sem = refs
    rows, cols = g.shape[2:]
    step = 64
    half = rows // 2
    token_ref[...] = jnp.zeros_like(token_ref)
    here = [not is_whole(m) for m in masks]
    coming = [[] if here[n] else read_rows(grads[n], g.at[n], [sem.at[i, n] for i in (0, 1)]) for n in range(count)]
    for group in coming:
        for copy in group:
            copy.start()
    mean = square_ref[...] * (1.0 / (D * KVH * HD))
    scale = jnp.concatenate([learning_rate * lax.rsqrt(mean + norm_eps)] * (cols // 128), axis=1)
    writes = []
    for n in range(count):
        for copy in coming[n]:
            copy.wait()
        for part in range(2):

            def mix(t, carry):
                j = pl.ds(pl.multiple_of(part * half + t * step, step), step)
                for i in (0, 1):
                    slope = grads[n][i][j, :] if here[n] else g[n, i, j]
                    value = w[offset + n, i, j].astype(jnp.float32) - scale[i : i + 1, :] * slope.astype(jnp.float32)
                    value = value.astype(jnp.bfloat16)
                    if first and n == 0:
                        new[i, j] = value
                    mixed = mix_alpha * value.astype(jnp.float32) + (1.0 - mix_alpha) * r[offset + n, i, j].astype(jnp.float32)
                    o[n, i, j] = mixed.astype(jnp.bfloat16)
                return carry

            lax.fori_loop(0, half // step, mix, 0, unroll=4)
            at = pl.ds(pl.multiple_of((idx_ref[0] ^ masks[n]) * rows + part * half, half), half)
            writes.append(pltpu.make_async_copy(o.at[n, :, pl.ds(part * half, half), :], out_hbm.at[:, at, :], out_sem.at[part, n]))
            writes[-1].start()
        if first and n == 0:
            writes.append(pltpu.make_async_copy(new, new_hbm, out_sem.at[0, count]))
            writes[-1].start()
    for copy in writes:
        copy.wait()


def blend(idx, squares, grads, reference, held, masks, ready, offset):
    w, r = ready
    _, _, rows, cols = w.shape
    count = len(masks)
    first = held is None
    args = [idx, squares] + [x if is_whole(m) else resident(x) for m in masks for x in grads[m]]
    in_specs = [SMEM, VMEM] + [HBM if is_whole(m) else VMEM for m in masks for x in grads[m]]
    args += [resident(w), resident(r)]
    in_specs += [VMEM] * 2
    out_specs = [HBM, VMEM]
    out_shape = [jax.ShapeDtypeStruct(reference.shape, jnp.bfloat16), jax.ShapeDtypeStruct((8, 128), jnp.float32)]
    aliases = {}
    if first:
        out_specs.append(HBM)
        out_shape.append(jax.ShapeDtypeStruct((2, rows, cols), jnp.bfloat16))
    else:
        aliases = {len(args): 0}
        in_specs.append(HBM)
        args.append(held)
    block = pltpu.VMEM((count, 2, rows, cols), jnp.bfloat16)
    return pl.pallas_call(
        functools.partial(blend_kernel, tuple(masks), first, offset),
        in_specs=in_specs,
        out_specs=out_specs,
        out_shape=out_shape,
        scratch_shapes=[
            block,
            block,
            pltpu.VMEM((2, rows, cols) if first else (8, 128), jnp.bfloat16),
            pltpu.SemaphoreType.DMA((2, count)),
            pltpu.SemaphoreType.DMA((2, count + 1)),
        ],
        input_output_aliases=aliases,
        compiler_params=params(12),
        cost_estimate=COST,
        name="blend",
    )(*args)


def bits_of(mask):
    return [1 << b for b in range(mask.bit_length()) if mask >> b & 1]


def after(value, *earlier):
    return lax.optimization_barrier((value, earlier))[0]


def body(shards, tensors, hidden_in, policy_weights, reference_weights, policy_queries, reference_queries, readout, lengths):
    rows = policy_weights.shape[1]
    idx = lax.axis_index("shard").astype(jnp.int32).reshape(1)
    tables = jnp.asarray(rope_tables())

    def swap(x, bit, axis="shard", size=shards):
        return lax.ppermute(x, axis, [(i, i ^ bit) for i in range(size)])

    def powers(size):
        return [1 << b for b in range(size.bit_length() - 1)]

    chips = sorted(range(0, shards, 2), key=lambda m: (len(bits_of(m)), m))
    near = [m for m in chips if len(bits_of(m)) == 1]
    far = [m for m in chips if len(bits_of(m)) > 1]
    link = lambda i, m: bits_of(m)[-1] if i == 0 else bits_of(m)[0]

    def send_near(own):
        got = {m: [swap(own, m)] for m in near}
        got[0] = [own]
        got[1] = [swap(own, 1)]
        return got

    def relay(got, m, *earlier):
        got[m] = [None, None]
        for i in (0, 1):
            via = link(i, m)
            source = got[m ^ via]
            source = source[i] if source[0].ndim == 2 else source[0][i]
            got[m][i] = swap(after(source, *earlier), via)

    def to_core(got, m, *earlier):
        got[m | 1] = [swap(after(g, *earlier), 1) for g in got[m]]

    weights = send_near(policy_weights)
    normed, ref_keys, ref_values = norm_project(idx, hidden_in, reference_weights, tables)
    (ref_margin,) = attend(lengths, reference_queries, ref_keys, ref_values, readout)
    two = [m for m in far if len(bits_of(m)) == 2]
    ends = [(m, i) for m in two for i in (0, 1)]
    packed = {}
    if two:
        packed = dict(zip(ends, pack([weights[m ^ link(i, m)] for m, i in ends], [i for m, i in ends], ref_margin)))
    for m in far:
        weights[m] = [swap(packed[m, i] if m in two else weights[m ^ link(i, m)][i], link(i, m)) for i in (0, 1)]
    for m in near:
        to_core(weights, m, ref_margin)
    held = project(idx, normed, [0, 1], weights, None, None)
    held = project(idx, normed, [m | c for m in near for c in (0, 1)], weights, held, None if far else tables)
    if far:
        for m in far:
            to_core(weights, m, held)
        held = project(idx, normed, far, weights, held, None)
        held = project(idx, normed, [m | 1 for m in far], weights, held, tables)
    pol_keys, pol_values = held
    margin, probs, delta = attend(lengths, policy_queries, pol_keys, pol_values, readout, ref_margin)

    theirs = {}
    order = list(reversed(chips))
    split = max(len(far), 1)

    def other_blocks(masks, margin, other=None):
        blocks = gradient_blocks(idx, normed, cot, [m | 1 for m in masks], rows, None, (margin,))
        if other is not None:
            blocks = hand_on(blocks, other)
        theirs.update({m: swap(block, 1) for m, block in zip(masks, blocks)})
        return blocks

    received = [swap(margin, m, "tensor", tensors) for m in range(1, tensors)]
    cot = attend_back(lengths, policy_queries, pol_values, readout, probs, delta, tables)
    terms = [margin] + [after(x, cot) for x in received]
    while len(terms) > 1:
        terms = [a + b for a, b in zip(terms[::2], terms[1::2])]
    (margin,) = terms
    received = swap(margin, 1)
    margins = (margin, after(received, other_blocks(order[:split], margin)))
    other_blocks(order[split:], margin, margins[1])

    chip_sum = {}
    arrived = {m: ([], []) for m in chips}
    halves = ([[], []], [[], []])
    waiting = []

    def send(m, i, half=None):
        terms = [chip_sum[m][i], *arrived[m][i]]
        if half is not None:
            terms = [t[:, half * rows // 2 : (half + 1) * rows // 2] for t in terms]
        payload = terms[0]
        if len(terms) > 1:
            payload = sum(t.astype(jnp.float32) for t in terms).astype(jnp.bfloat16)
        via = link(i, m)
        received = swap(payload, via)
        if half is None:
            arrived[m ^ via][i].append(received)
        else:
            halves[half][i].append(received)

    for masks in (order[:split], order[split:]):
        chip_sum.update(zip(masks, gradient_blocks(idx, normed, cot, masks, rows, (margins, theirs))))
        for m in masks:
            for i in (0, 1):
                if m and not any(k ^ link(i, k) == m for k in far):
                    send(m, i)
                elif m:
                    waiting.append((m, i))
    for m, i in waiting:
        if m in far:
            send(m, i)

    for half in (0, 1):
        for m, i in waiting:
            if m in near:
                send(m, i, half)
    grads = {m: [] for m in [0] + near}
    parts = []
    for half in (0, 1):
        own, part = finish(chip_sum[0], [arrived[0][i] + halves[half][i] for i in (0, 1)], half)
        parts.append(part)
        grads[0].append(own)
        for m in near:
            grads[m].append(swap(own, m))
    squares = parts[0] + parts[1]
    for bit in powers(tensors):
        squares = squares + swap(squares, bit, "tensor", tensors)
    squares = squares + swap(squares, 1)
    squares, margin_out = gate(squares, margin, *[grads[m][0] for m in near])
    masks = [m | c for m in [0] + near for c in (0, 1)] + [m | c for c in (0, 1) for m in far]
    ready = fetch(idx, weights, reference_weights, masks, squares)
    terms = [squares] + [swap(squares, m) for m in chips[1:]]
    while len(terms) > 1:
        terms = [a + b for a, b in zip(terms[::2], terms[1::2])]
    (squares,) = terms
    two = [m for m in far if len(bits_of(m)) == 2]
    ends = [(m, i) for m in two for i in (0, 1)]
    whole = [0] + near
    packed = pack([grads[m ^ link(i, m)] for m, i in ends] + [grads[m] for m in whole], [i for m, i in ends] + [None] * len(whole), squares, ready[0])
    packed = dict(zip(ends + whole, packed))
    for m in far:
        grads[m] = [swap(packed[m, i] if m in two else grads[m ^ link(i, m)][i], link(i, m)) for i in (0, 1)]
    for m in whole:
        grads[m | 1] = [swap(packed[m], 1)]
    groups = [[0, 1], [m | c for m in near for c in (0, 1)]] + [[m | c for m in far] for c in (0, 1)]
    new_reference, at = None, 0
    for group in groups:
        if group == far and far:
            for m in far:
                to_core(grads, m, token)
        if group:
            outs = blend(idx, squares, grads, reference_weights, new_reference, group, ready, at)
            new_reference, token = outs[:2]
            new_policy = outs[2] if at == 0 else new_policy
            at += len(group)
    return (new_policy, new_reference, margin_out)


def solution(mesh):
    return jax.shard_map(
        functools.partial(body, mesh.shape["shard"], mesh.shape["tensor"]),
        mesh=mesh,
        in_specs=(
            P("shard", None),
            P(None, "shard", "tensor"),
            P(None, None, "tensor"),
            P("shard", "tensor"),
            P("shard", "tensor"),
            P("shard", "tensor"),
            P("shard"),
        ),
        out_specs=(P(None, "shard", "tensor"), P(None, None, "tensor"), P("shard")),
        check_vma=False,
    )
```
